32 devices in a mesh: dp: 8 (over y, x, core), mp: 4 (over z).
Axes of the slice: x: 2, y: 2, z: 4, core: 2. Of those that a mesh axis runs over, the one named last changes fastest.
Arguments:
- tokens: bfloat16 [18944, 1024], P(('dp', 'mp')), may hold values from -6 to 6
- cotangent: bfloat16 [18944, 1024], P(('dp', 'mp')), may hold values from -6 to 6
- timesteps: int32 [8], P('dp'), may hold values from 0 to 999
- item_lengths: int32 [8, 18], P('dp'), may hold values from 0 to 512, as said below
- w_qkv: bfloat16 [1024, 3, 1024], P(None, None, 'mp'), may hold values from -0.1875 to 0.1875
- bias_qv: bfloat16 [2, 1024], P(None, 'mp'), may hold values from -1.796875 to 1.796875
- w_out: bfloat16 [1024, 1024], P('mp'), may hold values from -1 to 1
- w_up: bfloat16 [1024, 4096], P(None, 'mp'), may hold values from -0.1875 to 0.1875
- bias_up: bfloat16 [4096], P('mp'), may hold values from -1.796875 to 1.796875
- w_down: bfloat16 [4096, 1024], P('mp'), may hold values from -0.09375 to 0.09375
- vectors: float32 [8, 1024], replicated
Outputs:
- output: bfloat16 [18944, 1024], P(('dp', 'mp'))
- input_grad: bfloat16 [18944, 1024], P(('dp', 'mp'))
- grad_qkv: float32 [1024, 3, 1024], P('dp', None, 'mp')
- grad_bias_qv: float32 [2, 1024], P(None, 'mp')
- grad_out: float32 [1024, 1024], P('mp', 'dp')
- grad_up: float32 [1024, 4096], P('dp', 'mp')
- grad_bias_up: float32 [4096], P('mp')
- grad_down: float32 [4096, 1024], P('mp', 'dp')
- grad_vectors: float32 [8, 1024], replicated
The draws below stay inside these ranges and needn't reach their ends.
Inputs may be any that keep to these rules, and one draw needn't show every extreme that they name: `item_lengths`: each row lists items of 128 or 512 tokens, then zeros; the items of a row fill 18 * 128 tokens and at least one has 512.
All inputs are finite; a program needn't handle non-finite values.
Results may differ from the reference program's by a relative error of at most 0.02.
The reference program's roundings to bfloat16 on the way count: a program that leaves them out, or rounds other values in their place, can miss the bound.
Values may be sent and summed in bfloat16 or wider, within the bound.
A program may use at most 256 MiB of HBM per device.

```python
from functools import partial
import jax
import jax.numpy as jnp
from jax import lax

D = 1024
HEADS = 16
HD = 64
FF = 4096
SHORT = 128
UNITS = 18
LEN = 2368
SEQS = 8
TOKENS = 18944


def draw_item_lengths(key, part):
    key = jax.random.fold_in(key, 7)
    kinds_key, forced_key = jax.random.split(key)
    picks = jax.random.randint(kinds_key, (SEQS, UNITS), 0, 3)
    forced = jax.random.randint(forced_key, (SEQS,), 0, 4)

    def advance(used, inputs):
        pick_row, slot = inputs
        remain = UNITS - used
        wants = ((pick_row == 0) | (forced == slot)) & (remain >= 4)
        width_units = jnp.where(remain == 0, 0, jnp.where(wants, 4, 1))
        return (used + width_units, width_units * SHORT)
    slots = jnp.arange(UNITS, dtype=jnp.int32)
    used, sizes = lax.scan(advance, jnp.zeros((SEQS,), jnp.int32), (picks.T, slots))
    return sizes.T.astype(jnp.int32)


def draw_vectors(key, part):
    key = jax.random.fold_in(key, 11)
    noise = jnp.clip(jax.random.normal(key, (8, D), jnp.float32), -4.0, 4.0)
    scales = jnp.array([1.0, 0.3, 0.3, 0.3, 0.15, 0.3, 0.15, 0.3], jnp.float32)
    bases = jnp.array([0.0, 0.0, 0.0, 0.0, 1.0, 0.0, 1.0, 0.0], jnp.float32)
    return bases[:, None] + scales[:, None] * noise


def with_ends(drawn, own_key, smallest, high):
    extent = drawn.shape
    spot = [jax.random.randint(jax.random.fold_in(own_key, axis), (), 0, extent[axis]) for axis in range(len(extent))]
    drawn = drawn.at[tuple(spot)].set(smallest)
    longest = extent.index(max(extent))
    spot[longest] = (spot[longest] + 1) % extent[longest]
    return drawn.at[tuple(spot)].set(high)


def raised(values, own_key, source, target, blocks, factor):
    def block_of(position):
        return (jnp.arange(values.shape[position]) // (values.shape[position] // blocks)).reshape((-1,) + (1,) * (values.ndim - 1 - position))

    first = jax.random.permutation(own_key, blocks)[block_of(target)]
    far = (block_of(target) + blocks // 2) % blocks
    return jnp.where((block_of(source) == first) | (block_of(source) == far), factor * values, values)


def block_levels(stream_key, shape, pieces, low, largest):
    def one(axis_at, shards_of):
        heights = jax.random.uniform(jax.random.fold_in(jax.random.fold_in(stream_key, 6), axis_at), (shards_of,), jnp.float32, low / len(pieces), largest / len(pieces))
        return jnp.repeat(jnp.exp(heights), shape[axis_at] // shards_of).reshape((-1,) + (1,) * (len(shape) - axis_at - 1))

    loudness = one(*pieces[0])
    for cut in pieces[1:]:
        loudness = loudness * one(*cut)
    return loudness


def gaussian(stream_key, extent, scale, most, pieces=(), kind=jnp.bfloat16):
    drawn = jax.random.normal(stream_key, extent, jnp.float32) * scale
    if len(pieces) > 0:
        drawn = block_levels(stream_key, extent, pieces, -0.22, 0.18) * drawn
    return jnp.clip(drawn, min=-most, max=most).astype(kind)


def noise_with(stream_key, shape, deviation, limit, cuts, heavy, held_as=jnp.bfloat16):
    drawn = deviation * jax.random.normal(stream_key, shape, jnp.float32)
    if cuts:
        drawn = drawn * block_levels(stream_key, shape, cuts, -0.22, 0.18)
    return jnp.clip(raised(drawn, jax.random.fold_in(stream_key, 3), *heavy), -limit, limit).astype(held_as)


def setup_inputs(seed: int = 0) -> dict:
    seeds = jax.random.split(jax.random.key(seed), 12)
    tokens = gaussian(seeds[0], (TOKENS, D), 1.0, 6.0, ((0, 32),))
    cotangent = noise_with(seeds[1], (TOKENS, D), 1.0, 6.0, ((0, 32),), (0, 1, 32, 2.75))
    timesteps = with_ends(jax.random.randint(seeds[2], (SEQS,), 0, 1000), jax.random.fold_in(seeds[2], 1), 0, 999).astype(jnp.int32)
    item_lengths = draw_item_lengths(jax.random.fold_in(seeds[11], 71), 0)
    w_qkv = gaussian(seeds[4], (D, 3, D), D ** -0.5, 0.1875, ((2, 4),))
    bias_qv = gaussian(seeds[5], (2, D), 0.3, 1.796875, ((1, 4),))
    w_out = gaussian(seeds[6], (D, D), (D // 32) ** -0.5, 1.0, ((0, 4),))
    w_up = gaussian(seeds[7], (D, FF), D ** -0.5, 0.1875, ((1, 4),))
    bias_up = gaussian(seeds[8], (FF,), 0.3, 1.796875, ((0, 4),))
    w_down = gaussian(seeds[9], (FF, D), FF ** -0.5, 0.09375, ((0, 4),))
    vectors = draw_vectors(jax.random.fold_in(seeds[11], 71), 0)
    return {"tokens": tokens, "cotangent": cotangent, "timesteps": timesteps, "item_lengths": item_lengths, "w_qkv": w_qkv, "bias_qv": bias_qv, "w_out": w_out, "w_up": w_up, "bias_up": bias_up, "w_down": w_down, "vectors": vectors}


exact_mode = lax.Precision.HIGHEST

@jax.custom_vjp
def low(v):
    return lax.optimization_barrier(v.astype(jnp.bfloat16)).astype(jnp.float32)

@jax.custom_vjp
def low_back(v):
    return v

def low_keep(v):
    return (low(v), None)

def low_pass(kept, grad):
    return (grad,)

def back_keep(v):
    return (v, None)

def back_low(kept, grad):
    return (low(grad),)
low.defvjp(low_keep, low_pass)
low_back.defvjp(back_keep, back_low)

def product(left, right):
    return jnp.dot(left, right, precision=exact_mode)

def layer_norm(value, gain, shift):
    average = lax.optimization_barrier(jnp.mean(value, axis=-1, keepdims=True))
    centred = value - average
    spread = lax.optimization_barrier(jnp.mean(centred * centred, axis=-1, keepdims=True))
    return centred * lax.rsqrt(spread + 1e-05) * gain + shift

def segment_ids(lengths):
    ends = jnp.cumsum(lengths)
    positions = jnp.arange(LEN, dtype=jnp.int32)
    return lax.optimization_barrier(jnp.sum((positions[:, None] >= ends[None, :]).astype(jnp.int32), axis=1))

def head_attention(inputs, allowed):
    query, keys, values = inputs
    scores = low_back(product(query, keys.T) * HD ** (-0.5))
    scores = jnp.where(allowed, scores, -1e+30)
    highest = lax.optimization_barrier(jnp.max(scores, axis=-1, keepdims=True))
    weights = jnp.exp(scores - highest)
    chances = weights / lax.optimization_barrier(jnp.sum(weights, axis=-1, keepdims=True))
    return product(low(chances), values)

def split_heads(value):
    return value.reshape(LEN, HEADS, HD).transpose(1, 0, 2)

def forward(tokens_in, w_qkv, bias_qv, w_out, w_up, bias_up, w_down, vectors, time_value, allowed):
    lifted = tokens_in + time_value * vectors[0] + vectors[1]
    sent = low(lifted)
    projected = jnp.einsum('td,dce->cte', sent, w_qkv, precision=exact_mode)
    queries = low(low_back(projected[0] + bias_qv[0]))
    keys = low(low_back(projected[1]))
    values = low(low_back(projected[2] + bias_qv[1]))
    attended = lax.map(jax.checkpoint(partial(head_attention, allowed=allowed)), (split_heads(queries), split_heads(keys), split_heads(values)))
    attended = low(low_back(attended.transpose(1, 0, 2).reshape(LEN, D)))
    mixed = low_back(product(attended, w_out)) + vectors[2]
    first = layer_norm(lifted + mixed, vectors[4], vectors[5])
    upper = low_back(product(low(first), w_up) + bias_up)
    activated = low(jax.nn.gelu(upper, approximate=False))
    down = low_back(product(activated, w_down)) + vectors[3]
    return layer_norm(first + down, vectors[6], vectors[7])

def reference(tokens, cotangent, timesteps, item_lengths, w_qkv, bias_qv, w_out, w_up, bias_up, w_down, vectors):
    weights = tuple((value.astype(jnp.float32) for value in (w_qkv, bias_qv, w_out, w_up, bias_up, w_down, vectors)))
    sequences = tokens.astype(jnp.float32).reshape(SEQS, LEN, D)
    seq_cotangent = cotangent.astype(jnp.float32).reshape(SEQS, LEN, D)
    step_times = timesteps.astype(jnp.float32) * 0.001

    def visit_sequence(totals, inputs):
        seq_tokens, seq_grad, time_value, lengths = inputs
        segments = segment_ids(lengths)
        allowed = segments[:, None] == segments[None, :]

        def local_layer(tokens_in, *params):
            return forward(tokens_in, *params, time_value, allowed)
        result, pullback = jax.vjp(local_layer, seq_tokens, *weights)
        gradients = pullback(seq_grad)
        totals = tuple((total + grad for total, grad in zip(totals, gradients[1:])))
        return (totals, (result.astype(jnp.bfloat16), gradients[0].astype(jnp.bfloat16)))
    zeros = tuple((jnp.zeros_like(value) for value in weights))
    totals, (outputs, input_grads) = lax.scan(visit_sequence, zeros, (sequences, seq_cotangent, step_times, item_lengths))
    return (outputs.reshape(TOKENS, D), input_grads.reshape(TOKENS, D), totals[0], totals[1], totals[2], totals[3], totals[4], totals[5], totals[6])
```

```python
import functools

import jax
import jax.numpy as jnp
from jax import lax
from jax.experimental import pallas as pl
from jax.experimental.pallas import tpu as pltpu
from jax.sharding import PartitionSpec as P

D = 1024
HD = 64
FF = 4096
LEN = 2368


def norm_forward(value, gain, shift):
    average = jnp.mean(value, axis=-1, keepdims=True)
    centred = value - average
    inverse = lax.rsqrt(jnp.mean(centred * centred, axis=-1, keepdims=True) + 1e-05)
    normed = centred * inverse
    return (normed * gain + shift, normed, inverse)


def norm_backward(grad, normed, inverse, gain):
    scaled = grad * gain
    result = inverse * (
        scaled
        - jnp.mean(scaled, axis=-1, keepdims=True)
        - normed * jnp.mean(scaled * normed, axis=-1, keepdims=True)
    )
    return (result, jnp.sum(grad * normed, axis=0), jnp.sum(grad, axis=0))


def gelu_exact(value):
    return jax.nn.gelu(value, approximate=False)


def attend_forward(queries, keys, values, segments):
    scale = HD ** (-0.5)
    block_rows = LEN // 4

    def one_block(inputs):
        query_block, segment_block = inputs
        scores = (
            jnp.einsum("bhe,khe->hbk", query_block, keys, preferred_element_type=jnp.float32)
            * scale
        )
        allowed = segment_block[:, None] == segments[None, :]
        scores = jnp.where(allowed[None], scores, -1e30)
        highest = jnp.max(scores, axis=-1, keepdims=True)
        weights = jnp.exp(scores - highest)
        totals = jnp.sum(weights, axis=-1, keepdims=True)
        chances_low = (weights / totals).astype(jnp.bfloat16)
        result = jnp.einsum("hbk,khe->bhe", chances_low, values, preferred_element_type=jnp.float32)
        return (result.astype(jnp.bfloat16), (highest + jnp.log(totals))[..., 0])

    blocks = queries.reshape(4, block_rows, queries.shape[1], queries.shape[2])
    results, logsums = lax.map(one_block, (blocks, segments.reshape(4, block_rows)))
    return (results.reshape(queries.shape), logsums)


def attend_backward(queries, keys, values, out_grads, logsums, segments):
    scale = HD ** (-0.5)
    block_rows = LEN // 4

    def one_block(carry, inputs):
        key_grads, value_grads = carry
        query_block, grad_block, logsum_block, segment_block = inputs
        scores = (
            jnp.einsum("bhe,khe->hbk", query_block, keys, preferred_element_type=jnp.float32)
            * scale
        )
        allowed = segment_block[:, None] == segments[None, :]
        scores = jnp.where(allowed[None], scores, -1e30)
        chances = jnp.exp(scores - logsum_block[..., None])
        chances_low = chances.astype(jnp.bfloat16)
        value_grads = value_grads + jnp.einsum(
            "hbk,bhe->khe", chances_low, grad_block, preferred_element_type=jnp.float32
        )
        flow = jnp.einsum("bhe,khe->hbk", grad_block, values, preferred_element_type=jnp.float32)
        inner = jnp.sum(chances * flow, axis=-1, keepdims=True)
        score_grads = (chances * (flow - inner)).astype(jnp.bfloat16)
        query_grads = (
            jnp.einsum("hbk,khe->bhe", score_grads, keys, preferred_element_type=jnp.float32)
            * scale
        )
        key_grads = (
            key_grads
            + jnp.einsum(
                "hbk,bhe->khe", score_grads, query_block, preferred_element_type=jnp.float32
            )
            * scale
        )
        return ((key_grads, value_grads), query_grads)

    shape_blocks = (4, block_rows, queries.shape[1], queries.shape[2])
    zeros = jnp.zeros(keys.shape, jnp.float32)
    (key_grads, value_grads), query_grads = lax.scan(
        one_block,
        (zeros, zeros),
        (
            queries.reshape(shape_blocks),
            out_grads.reshape(shape_blocks),
            logsums,
            segments.reshape(4, block_rows),
        ),
    )
    return (query_grads.reshape(queries.shape), key_grads, value_grads)


def body(
    tokens,
    cotangent,
    timesteps,
    item_lengths,
    w_qkv,
    bias_qv,
    w_out,
    w_up,
    bias_up,
    w_down,
    vectors,
):
    rows = tokens.shape[0]
    total = rows * lax.axis_size("mp")
    seq_count = timesteps.shape[0]
    local_width = w_qkv.shape[2]
    local_hidden = w_up.shape[1]
    local_heads = local_width // HD
    my_index = lax.axis_index("mp")
    row_ids = my_index * rows + lax.iota(jnp.int32, rows)
    row_owner = row_ids // LEN
    step_times = timesteps.astype(jnp.float32) * 0.001
    time_rows = jnp.sum(
        jnp.where(
            row_owner[:, None] == lax.iota(jnp.int32, seq_count)[None, :], step_times[None, :], 0.0
        ),
        axis=1,
    )
    ends = jnp.cumsum(item_lengths, axis=1)
    segments = jnp.sum(
        (lax.iota(jnp.int32, LEN)[None, :, None] >= ends[:, None, :]).astype(jnp.int32), axis=2
    )
    lifted = tokens.astype(jnp.float32) + time_rows[:, None] * vectors[0] + vectors[1]
    gathered = lax.all_gather(lifted.astype(jnp.bfloat16), "mp", axis=0, tiled=True)
    projected = jnp.einsum("td,dce->cte", gathered, w_qkv, preferred_element_type=jnp.float32)
    shaped = (seq_count, LEN, local_heads, HD)
    head_query = (projected[0] + bias_qv[0]).astype(jnp.bfloat16).reshape(shaped)
    head_key = projected[1].astype(jnp.bfloat16).reshape(shaped)
    head_value = (projected[2] + bias_qv[1]).astype(jnp.bfloat16).reshape(shaped)
    attended, logsums = lax.map(
        lambda items: attend_forward(*items), (head_query, head_key, head_value, segments)
    )
    attended = attended.reshape(total, local_width)
    piece = attended
    mixed = (
        lax.psum_scatter(
            jnp.dot(piece, w_out, preferred_element_type=jnp.float32),
            "mp",
            scatter_dimension=0,
            tiled=True,
        )
        + vectors[2]
    )
    first, normed_one, inverse_one = norm_forward(lifted + mixed, vectors[4], vectors[5])
    hidden_all = lax.all_gather(first.astype(jnp.bfloat16), "mp", axis=0, tiled=True)
    upper = jnp.dot(hidden_all, w_up, preferred_element_type=jnp.float32) + bias_up
    activated, gelu_pull = jax.vjp(gelu_exact, upper)
    activated = activated.astype(jnp.bfloat16)
    piece = activated
    down = (
        lax.psum_scatter(
            jnp.dot(piece, w_down, preferred_element_type=jnp.float32).astype(jnp.bfloat16),
            "mp",
            scatter_dimension=0,
            tiled=True,
        ).astype(jnp.float32)
        + vectors[3]
    )
    output, normed_two, inverse_two = norm_forward(first + down, vectors[6], vectors[7])
    out_grads = cotangent.astype(jnp.float32)
    second_grads, gain_two, shift_two = norm_backward(
        out_grads, normed_two, inverse_two, vectors[6]
    )
    down_all = lax.all_gather(second_grads.astype(jnp.bfloat16), "mp", axis=0, tiled=True)
    grad_down = jnp.einsum("tf,td->fd", activated, down_all, preferred_element_type=jnp.float32)
    act_grads = jnp.einsum("td,fd->tf", down_all, w_down, preferred_element_type=jnp.float32)
    (upper_grads,) = gelu_pull(act_grads)
    upper_low = upper_grads.astype(jnp.bfloat16)
    grad_bias_up = jnp.sum(upper_low, axis=0, dtype=jnp.float32)
    grad_up = jnp.einsum("td,tf->df", hidden_all, upper_low, preferred_element_type=jnp.float32)
    piece = upper_low
    first_part = lax.psum_scatter(
        jnp.einsum("tf,df->td", piece, w_up, preferred_element_type=jnp.float32).astype(
            jnp.bfloat16
        ),
        "mp",
        scatter_dimension=0,
        tiled=True,
    ).astype(jnp.float32)
    first_grads = second_grads + first_part
    mixed_grads, gain_one, shift_one = norm_backward(
        first_grads, normed_one, inverse_one, vectors[4]
    )
    mixed_all = lax.all_gather(mixed_grads.astype(jnp.bfloat16), "mp", axis=0, tiled=True)
    grad_out = jnp.einsum("te,td->ed", attended, mixed_all, preferred_element_type=jnp.float32)
    attended_grads = jnp.einsum(
        "td,ed->te", mixed_all, w_out, preferred_element_type=jnp.float32
    ).astype(jnp.bfloat16)
    query_grads, key_grads, value_grads = lax.map(
        lambda items: attend_backward(*items),
        (head_query, head_key, head_value, attended_grads.reshape(shaped), logsums, segments),
    )
    qkv_low = jnp.stack(
        [
            query_grads.reshape(total, local_width),
            key_grads.reshape(total, local_width),
            value_grads.reshape(total, local_width),
        ],
        axis=1,
    ).astype(jnp.bfloat16)
    grad_bias_qv = jnp.sum(qkv_low[:, 0::2], axis=0, dtype=jnp.float32)
    grad_qkv = jnp.einsum("td,tcf->dcf", gathered, qkv_low, preferred_element_type=jnp.float32)
    piece = qkv_low
    input_part = lax.psum_scatter(
        jnp.einsum("tcf,dcf->td", piece, w_qkv, preferred_element_type=jnp.float32).astype(
            jnp.bfloat16
        ),
        "mp",
        scatter_dimension=0,
        tiled=True,
    ).astype(jnp.float32)
    input_sum = mixed_grads + input_part
    vector_terms = jnp.stack(
        [
            jnp.sum(time_rows[:, None] * input_sum, axis=0),
            jnp.sum(input_sum, axis=0),
            jnp.sum(mixed_grads, axis=0),
            jnp.sum(second_grads, axis=0),
            gain_one,
            shift_one,
            gain_two,
            shift_two,
        ],
        axis=0,
    )
    zero_index = jnp.zeros((), jnp.int32)
    qv_start = my_index * local_width
    up_start = my_index * local_hidden
    qv_placed = lax.dynamic_update_slice(
        jnp.zeros((2, D), jnp.float32), grad_bias_qv, (zero_index, qv_start)
    )
    up_placed = lax.dynamic_update_slice(jnp.zeros((FF,), jnp.float32), grad_bias_up, (up_start,))
    grad_qkv, grad_out, grad_up, grad_down = (
        lax.psum_scatter(
            grad_qkv.astype(jnp.bfloat16), "dp", scatter_dimension=0, tiled=True
        ).astype(jnp.float32),
        lax.psum_scatter(
            grad_out.astype(jnp.bfloat16), "dp", scatter_dimension=1, tiled=True
        ).astype(jnp.float32),
        lax.psum_scatter(
            grad_up.astype(jnp.bfloat16), "dp", scatter_dimension=0, tiled=True
        ).astype(jnp.float32),
        lax.psum_scatter(
            grad_down.astype(jnp.bfloat16), "dp", scatter_dimension=1, tiled=True
        ).astype(jnp.float32),
    )
    grad_vectors, qv_summed, up_summed = lax.psum(
        (vector_terms, qv_placed, up_placed), ("dp", "mp")
    )
    grad_bias_qv = lax.dynamic_slice_in_dim(qv_summed, qv_start, local_width, 1)
    grad_bias_up = lax.dynamic_slice_in_dim(up_summed, up_start, local_hidden, 0)
    return (
        output.astype(jnp.bfloat16),
        input_sum.astype(jnp.bfloat16),
        grad_qkv,
        grad_bias_qv,
        grad_out,
        grad_up,
        grad_bias_up,
        grad_down,
        grad_vectors,
    )


UNIT = 128
LONG = 4
MESH = pl.DeviceIdType.MESH


def fits_local(mesh):
    parts = mesh.shape["mp"]
    return mesh.shape["dp"] == 8 and parts == 4 and LEN % (16 * parts) == 0


def window_plan(rows, parts):
    firsts = [(rows * j) // UNIT - (LONG - 1) for j in range(parts)]
    offsets = [rows * j - UNIT * first for j, first in enumerate(firsts)]
    ends = [
        ((rows * (j + 1) - 1) // UNIT + LONG - firsts[j]) * UNIT for j in range(parts)
    ]
    return firsts, offsets, ends


def pick(table, index):
    value = jnp.int32(table[0])
    for j in range(1, len(table)):
        value = jnp.where(index == j, jnp.int32(table[j]), value)
    return value


def gather_kernel(
    rows, window, parts, tokens, w_qkv, w_out, w_up, w_down, win, f_qkv, f_out, f_up, f_down, send, recv, near, far, own
):
    d = lax.axis_index("dp")
    z = lax.axis_index("mp")
    firsts, offsets, ends = window_plan(rows, parts)
    shards = (w_qkv, w_out, w_up, w_down)
    fulls = (f_qkv, f_out, f_up, f_down)
    sizes = (128, 32, 128, 128)
    others = (1, 3, 2)
    peers = [(d, z ^ k) for k in others] + [(d ^ 1, z), (d ^ 2, z), (d ^ 4, z)]
    barrier = pltpu.get_barrier_semaphore()
    for peer in peers:
        pl.semaphore_signal(barrier, inc=1, device_id=peer, device_id_type=MESH)
    pl.semaphore_wait(barrier, len(peers))

    def part(ref, index, owner, size, half=None):
        start = owner * size
        count = size
        if half is not None:
            count = size // 2
            start = start + half * count
        rows_at = pl.ds(pl.multiple_of(start, 16), count)
        if len(ref.shape) == 4:
            return ref.at[index, :, rows_at, :]
        return ref.at[index, rows_at, :]

    chunks = [(g, k) for g in range(4) for k in others]
    copies = {}

    def remote(i, kind, src, dst, target):
        copy = pltpu.make_async_remote_copy(
            src, dst, send.at[i, kind], recv.at[i, kind], device_id=target, device_id_type=MESH
        )
        copy.start()
        copies[i, kind] = copy

    def first_hop(i):
        g, k = chunks[i]
        size = sizes[g]
        rows_at = pl.ds(pl.multiple_of(d * size, 16), size)
        src = shards[g].at[:, rows_at, :] if g == 0 else shards[g].at[rows_at, :]
        remote(i, 0, src, part(fulls[g], z, d, size), (d, z ^ k))

    def place(i, owner, half=None):
        g, k = chunks[i]
        return part(fulls[g], z ^ k, owner, sizes[g], half)

    for i in range(3):
        first_hop(i)
    left_send = [
        pltpu.make_async_remote_copy(
            tokens.at[pl.ds(0, ends[j] - offsets[j] - rows), :],
            win.at[pl.ds(offsets[j] + rows, ends[j] - offsets[j] - rows), :],
            near.at[0], near.at[1], device_id=(d, j), device_id_type=MESH,
        )
        for j in range(parts - 1)
    ]
    right_send = [
        pltpu.make_async_remote_copy(
            tokens.at[pl.ds(rows - offsets[j], offsets[j]), :],
            win.at[pl.ds(0, offsets[j]), :],
            far.at[0], far.at[1], device_id=(d, j), device_id_type=MESH,
        )
        for j in range(1, parts)
    ]
    for j in range(parts - 1):
        @pl.when(z == j + 1)
        def _(j=j):
            left_send[j].start()
    for j in range(1, parts):
        @pl.when(z == j - 1)
        def _(j=j):
            right_send[j - 1].start()
    locals_ = []
    for g in range(4):
        copy = pltpu.make_async_copy(shards[g], fulls[g].at[z], own.at[g])
        copy.start()
        locals_.append(copy)
    offset = pl.multiple_of(pick(offsets, z), 16)
    copy = pltpu.make_async_copy(tokens, win.at[pl.ds(offset, rows), :], own.at[4])
    copy.start()
    locals_.append(copy)
    fill_first = pltpu.make_async_copy(
        tokens.at[pl.ds(0, offsets[0]), :], win.at[pl.ds(0, offsets[0]), :], own.at[5]
    )
    fills = []
    for j in range(parts):
        begin = ends[j] if j < parts - 1 else offsets[j] + rows
        if begin < window:
            fills.append(
                (j, pltpu.make_async_copy(
                    tokens.at[pl.ds(0, window - begin), :], win.at[pl.ds(begin, window - begin), :], own.at[6]
                ))
            )

    @pl.when(z == 0)
    def _():
        fill_first.start()

    for j, fill in fills:
        @pl.when(z == j)
        def _(fill=fill):
            fill.start()

    for i in range(3, len(chunks)):
        first_hop(i)

    def stage_one(i):
        copies[i, 0].wait_recv()
        remote(i, 1, place(i, d), place(i, d), (d ^ 2, z))
        remote(i, 2, place(i, d), place(i, d), (d ^ 4, z))
        remote(i, 5, place(i, d), place(i, d), (d ^ 1, z))

    def stage_two(i):
        copies[i, 1].wait_recv()
        remote(i, 3, place(i, d ^ 2, 0), place(i, d ^ 2, 0), (d ^ 4, z))
        remote(i, 6, place(i, d ^ 2), place(i, d ^ 2), (d ^ 1, z))
        copies[i, 2].wait_recv()
        remote(i, 4, place(i, d ^ 4, 1), place(i, d ^ 4, 1), (d ^ 2, z))
        remote(i, 7, place(i, d ^ 4), place(i, d ^ 4), (d ^ 1, z))

    def stage_three(i):
        copies[i, 3].wait_recv()
        remote(i, 8, place(i, d ^ 6, 0), place(i, d ^ 6, 0), (d ^ 1, z))
        copies[i, 4].wait_recv()
        remote(i, 9, place(i, d ^ 6, 1), place(i, d ^ 6, 1), (d ^ 1, z))

    n = len(chunks)
    for i in range(n + 2):
        if i < n:
            stage_one(i)
        if 0 <= i - 1 < n:
            stage_two(i - 1)
        if 0 <= i - 2 < n:
            stage_three(i - 2)
    for i in range(n):
        for kind in range(5, 10):
            copies[i, kind].wait_recv()
        for kind in range(10):
            copies[i, kind].wait_send()
    for j in range(parts - 1):
        @pl.when(z == j + 1)
        def _(j=j):
            left_send[j].wait_send()

        @pl.when(z == j)
        def _(j=j):
            left_send[j].wait_recv()
    for j in range(1, parts):
        @pl.when(z == j - 1)
        def _(j=j):
            right_send[j - 1].wait_send()

        @pl.when(z == j)
        def _(j=j):
            right_send[j - 1].wait_recv()
    for copy in locals_:
        copy.wait()

    @pl.when(z == 0)
    def _():
        fill_first.wait()

    for j, fill in fills:
        @pl.when(z == j)
        def _(fill=fill):
            fill.wait()


def gather(tokens, w_qkv, w_out, w_up, w_down, window, parts):
    rows = tokens.shape[0]
    any_ = pl.BlockSpec(memory_space=pl.ANY)
    low = jnp.bfloat16
    return pl.pallas_call(
        functools.partial(gather_kernel, rows, window, parts),
        out_shape=[
            jax.ShapeDtypeStruct((window, D), low),
            jax.ShapeDtypeStruct((parts,) + w_qkv.shape, low),
            jax.ShapeDtypeStruct((parts,) + w_out.shape, low),
            jax.ShapeDtypeStruct((parts,) + w_up.shape, low),
            jax.ShapeDtypeStruct((parts,) + w_down.shape, low),
        ],
        in_specs=[any_] * 5,
        out_specs=[any_] * 5,
        scratch_shapes=[
            pltpu.SemaphoreType.DMA((12, 10)),
            pltpu.SemaphoreType.DMA((12, 10)),
            pltpu.SemaphoreType.DMA((2,)),
            pltpu.SemaphoreType.DMA((2,)),
            pltpu.SemaphoreType.DMA((7,)),
        ],
        compiler_params=pltpu.CompilerParams(collective_id=0, has_side_effects=True),
    )(tokens, w_qkv, w_out, w_up, w_down)


NT = (((1,), (1,)), ((), ()))
TN = (((0,), (0,)), ((), ()))
FIRST_OWN, LAST_OWN = LONG - 1, LONG + 4


def two_heads(block):
    lane = lax.broadcasted_iota(jnp.int32, block.shape, 1)
    zero = jnp.zeros_like(block)
    return jnp.concatenate(
        [jnp.where(lane < HD, block, zero), jnp.where(lane < HD, zero, block)], axis=0
    )


def from_two(flipped):
    both = jnp.concatenate([flipped[:HD, :UNIT], flipped[HD:, UNIT:]], axis=0)
    return both.T


def weights_of(keys, pair, valid):
    scores = lax.dot_general(keys, pair, NT, preferred_element_type=jnp.float32) * HD ** (-0.5)
    if valid is not None:
        scores = jnp.where(valid, scores, -1e30)
    highest = jnp.max(scores, axis=0, keepdims=True)
    weights = jnp.exp(scores - highest)
    return weights * (1.0 / jnp.sum(weights, axis=0, keepdims=True))


def attend_kernel(kind, start, unit_seg, seg, q, k, v, o):
    def unit(u, carry):
        mine = pl.ds(pl.multiple_of(u * UNIT, UNIT), UNIT)

        def run(at, valid):
            pair = two_heads(q[mine, :])
            chances = weights_of(k[at, :], pair, valid).astype(jnp.bfloat16)
            flipped = lax.dot_general(v[at, :], chances, TN, preferred_element_type=jnp.float32)
            o[mine, :] = from_two(flipped).astype(o.dtype)

        @pl.when(kind[u] == 2)
        def _():
            run(pl.ds(pl.multiple_of(start[u], UNIT), LONG * UNIT), None)

        @pl.when(kind[u] == 1)
        def _():
            run(mine, seg[mine, :] == unit_seg[u])

        return carry

    lax.fori_loop(FIRST_OWN, LAST_OWN + 1, unit, 0)


def attend_back_kernel(kind, start, unit_seg, seg, q, k, v, g, dq, dk, dv, k_sum, v_sum):
    k_sum[...] = jnp.zeros_like(k_sum)
    v_sum[...] = jnp.zeros_like(v_sum)
    scale = HD ** (-0.5)

    def unit(u, carry):
        mine = pl.ds(pl.multiple_of(u * UNIT, UNIT), UNIT)

        def run(at, valid):
            pair = two_heads(q[mine, :])
            grads = two_heads(g[mine, :])
            keys = k[at, :]
            chances = weights_of(keys, pair, valid)
            flow = lax.dot_general(v[at, :], grads, NT, preferred_element_type=jnp.float32)
            inner = jnp.sum(chances * flow, axis=0, keepdims=True)
            low = (chances * (flow - inner)).astype(jnp.bfloat16)
            v_sum[at, :] += jnp.dot(chances.astype(jnp.bfloat16), grads, preferred_element_type=jnp.float32)
            k_sum[at, :] += jnp.dot(low, pair, preferred_element_type=jnp.float32)

            @pl.when((u >= FIRST_OWN) & (u <= LAST_OWN))
            def _():
                flipped = lax.dot_general(keys, low, TN, preferred_element_type=jnp.float32)
                dq[mine, :] = (from_two(flipped) * scale).astype(dq.dtype)

        @pl.when(kind[u] == 2)
        def _():
            run(pl.ds(pl.multiple_of(start[u], UNIT), LONG * UNIT), None)

        @pl.when(kind[u] == 1)
        def _():
            run(mine, seg[mine, :] == unit_seg[u])

        return carry

    lax.fori_loop(0, q.shape[0] // UNIT, unit, 0)
    dk[...] = (k_sum[...] * scale).astype(dk.dtype)
    dv[...] = v_sum[...].astype(dv.dtype)


def attention_call(kernel, window, plan, segs, arrays, outs, scratch):
    column = pl.BlockSpec((window, 2 * HD), lambda p, *_: (0, p))
    whole = pl.BlockSpec((window, 1), lambda p, *_: (0, 0))
    return pl.pallas_call(
        kernel,
        grid_spec=pltpu.PrefetchScalarGridSpec(
            num_scalar_prefetch=3,
            grid=(D // (2 * HD),),
            in_specs=[whole] + [column] * len(arrays),
            out_specs=[column] * outs,
            scratch_shapes=[pltpu.VMEM((window, 2 * HD), jnp.float32)] * scratch,
        ),
        out_shape=[jax.ShapeDtypeStruct((window, D), jnp.bfloat16)] * outs,
        compiler_params=pltpu.CompilerParams(vmem_limit_bytes=48 * 2**20),
    )(*plan, segs[:, None], *arrays)


def unit_plan(segs, z, offsets, rows, window):
    units = window // UNIT
    unit_seg = segs[::UNIT]
    same = unit_seg[:, None] == unit_seg[None, :]
    counts = jnp.sum(same.astype(jnp.int32), axis=1)
    inside = unit_seg < 1000
    inside = inside & (unit_seg >= 0)
    index = lax.iota(jnp.int32, units)
    first = jnp.sum((unit_seg[None, :] < unit_seg[:, None]).astype(jnp.int32), axis=1)
    own = (index >= FIRST_OWN) & (index <= LAST_OWN)
    meets = jnp.any(same & own[None, :], axis=1)
    long = inside & (counts == LONG) & meets
    kind = jnp.where(long, 2, jnp.where(own, 1, 0))
    return (
        kind.astype(jnp.int32),
        jnp.where(long, first * UNIT, 0).astype(jnp.int32),
        unit_seg,
    )


def swap(array, axis, bit):
    size = lax.axis_size(axis)
    return lax.ppermute(array, axis, [(i, i ^ bit) for i in range(size)])


def choose(array, index, axis):
    return lax.dynamic_index_in_dim(array, index, axis, keepdims=False)


def add_low(kept, received):
    return (kept.astype(jnp.float32) + received.astype(jnp.float32)).astype(jnp.bfloat16)


def scatter_sum(make, x_first):
    d = lax.axis_index("dp")
    z = lax.axis_index("mp")
    core, x, y = d % 2, (d // 2) % 2, d // 4
    low = jnp.bfloat16
    away = swap(make(1 - core).astype(low), "dp", 1)
    terms = add_low(make(core), away)
    order = [(1, x, 2), (0, y, 4)] if x_first else [(0, y, 4), (1, x, 2)]
    for step, (axis, mine, bit) in enumerate(order):
        axis = axis if step == 0 else 0
        away = swap(choose(terms, 1 - mine, axis), "dp", bit)
        terms = add_low(choose(terms, mine, axis), away)
    total = choose(terms, z, 0).astype(jnp.float32)
    for k in (1, 2, 3):
        total = total + swap(choose(terms, z ^ k, 0), "mp", k).astype(jnp.float32)
    return total


def sum_all(value):
    for axis, bit in (("dp", 1), ("dp", 2), ("dp", 4), ("mp", 1), ("mp", 2)):
        value = value + swap(value, axis, bit)
    return value


def local_body(
    tokens,
    cotangent,
    timesteps,
    item_lengths,
    w_qkv,
    bias_qv,
    w_out,
    w_up,
    bias_up,
    w_down,
    vectors,
):
    rows = tokens.shape[0]
    parts = lax.axis_size("mp")
    z = lax.axis_index("mp")
    low = jnp.bfloat16
    f32 = jnp.float32
    firsts, offsets, ends = window_plan(rows, parts)
    window = -(-max(ends) // UNIT) * UNIT
    win, f_qkv, f_out, f_up, f_down = gather(
        tokens, jnp.transpose(w_qkv, (1, 0, 2)), w_out, w_up, w_down, window, parts
    )
    bias_qv_all = lax.all_gather(bias_qv, "mp", axis=1, tiled=True).astype(f32)
    bias_up_all = lax.all_gather(bias_up, "mp", axis=0, tiled=True).astype(f32)
    offset = pick(offsets, z)
    first_token = UNIT * pick(firsts, z)
    positions = first_token + lax.iota(jnp.int32, window)
    lengths_end = jnp.cumsum(item_lengths[0])
    segs = jnp.sum((positions[:, None] >= lengths_end[None, :]).astype(jnp.int32), axis=1)
    segs = jnp.where(positions < 0, -1, jnp.where(positions >= LEN, 1000, segs))
    plan = unit_plan(segs, z, offsets, rows, window)
    step_time = timesteps[0].astype(f32) * 0.001

    lifted = tokens.astype(f32) + step_time * vectors[0] + vectors[1]
    lifted_low = lifted.astype(low)
    win_low = (win.astype(f32) + step_time * vectors[0] + vectors[1]).astype(low)
    w3 = jnp.transpose(f_qkv, (1, 2, 0, 3)).reshape(3, D, D)
    queries = (jnp.dot(win_low, w3[0], preferred_element_type=f32) + bias_qv_all[0]).astype(low)
    keys = jnp.dot(win_low, w3[1], preferred_element_type=f32).astype(low)
    values = (jnp.dot(win_low, w3[2], preferred_element_type=f32) + bias_qv_all[1]).astype(low)
    attended = attention_call(attend_kernel, window, plan, segs, (queries, keys, values), 1, 0)[0]
    attended = lax.dynamic_slice_in_dim(attended, offset, rows, 0)
    wo = f_out.reshape(D, D)
    mixed = jnp.dot(attended, wo, preferred_element_type=f32) + vectors[2]
    first, normed_one, inverse_one = norm_forward(lifted + mixed, vectors[4], vectors[5])
    first_low = first.astype(low)
    wu = jnp.transpose(f_up, (1, 0, 2)).reshape(D, FF)
    upper = jnp.dot(first_low, wu, preferred_element_type=f32) + bias_up_all
    activated, gelu_pull = jax.vjp(gelu_exact, upper)
    activated = activated.astype(low)
    wd = f_down.reshape(FF, D)
    down = jnp.dot(activated, wd, preferred_element_type=f32) + vectors[3]
    output, normed_two, inverse_two = norm_forward(first + down, vectors[6], vectors[7])
    out_grads = cotangent.astype(f32)
    second_grads, gain_two, shift_two = norm_backward(out_grads, normed_two, inverse_two, vectors[6])
    second_low = second_grads.astype(low)

    cut = D // lax.axis_size("dp")
    fold = (rows, 2, 2, 2, cut)

    def for_core(value, c):
        return choose(value.reshape(fold), c, 3)

    act4 = activated.reshape(rows, parts, FF // parts)
    grad_down = scatter_sum(
        lambda c: jnp.einsum("tzf,tyxk->yxzfk", act4, for_core(second_low, c), preferred_element_type=f32), True
    )
    act_grads = jnp.dot(second_low, wd.T, preferred_element_type=f32)
    (upper_grads,) = gelu_pull(act_grads)
    upper_low = upper_grads.astype(low)
    grad_bias_up = jnp.sum(upper_low, axis=0, dtype=f32)
    upper4 = upper_low.reshape(rows, parts, FF // parts)
    grad_up = scatter_sum(
        lambda c: jnp.einsum("tyxk,tzf->yxzkf", for_core(first_low, c), upper4, preferred_element_type=f32), False
    )
    first_grads = second_grads + jnp.dot(upper_low, wu.T, preferred_element_type=f32)
    mixed_grads, gain_one, shift_one = norm_backward(first_grads, normed_one, inverse_one, vectors[4])
    mixed_low = mixed_grads.astype(low)

    most_left, most_right = max(offsets[1:]), max(e - o - rows for e, o in zip(ends[:-1], offsets[:-1]))
    from_left = lax.ppermute(mixed_low[rows - most_left :], "mp", [(j, j + 1) for j in range(parts - 1)])
    from_right = lax.ppermute(mixed_low[:most_right], "mp", [(j + 1, j) for j in range(parts - 1)])
    tail = jnp.zeros((window - offsets[0] - rows, D), low)
    joined = jnp.concatenate([from_left, mixed_low, from_right, tail], axis=0)
    mixed_win = lax.dynamic_slice_in_dim(joined, most_left - offset, window, 0)

    att4 = attended.reshape(rows, parts, D // parts)
    grad_out = scatter_sum(
        lambda c: jnp.einsum("tze,tyxk->yxzek", att4, for_core(mixed_low, c), preferred_element_type=f32), True
    )
    attended_grads = jnp.dot(mixed_win, wo.T, preferred_element_type=f32).astype(low)
    dq, dk, dv = attention_call(
        attend_back_kernel, window, plan, segs, (queries, keys, values, attended_grads), 3, 2
    )
    dq, dk, dv = (lax.dynamic_slice_in_dim(value, offset, rows, 0) for value in (dq, dk, dv))
    grad_bias_qv = jnp.stack([jnp.sum(dq, axis=0, dtype=f32), jnp.sum(dv, axis=0, dtype=f32)])
    input_sum = (
        mixed_grads
        + jnp.dot(dq, w3[0].T, preferred_element_type=f32)
        + jnp.dot(dk, w3[1].T, preferred_element_type=f32)
        + jnp.dot(dv, w3[2].T, preferred_element_type=f32)
    )

    def qkv_terms(value):
        value4 = value.reshape(rows, parts, D // parts)
        return lambda c: jnp.einsum("tyxk,tzf->yxzkf", for_core(lifted_low, c), value4, preferred_element_type=f32)

    grad_q = scatter_sum(qkv_terms(dq), True)
    grad_k = scatter_sum(qkv_terms(dk), False)
    grad_v = scatter_sum(qkv_terms(dv), False)
    grad_qkv = jnp.stack([grad_q, grad_k, grad_v], axis=1)
    input_total = jnp.sum(input_sum, axis=0)
    rows8 = jnp.stack(
        [
            step_time * input_total,
            input_total,
            jnp.sum(mixed_grads, axis=0),
            jnp.sum(second_grads, axis=0),
            gain_one,
            shift_one,
            gain_two,
            shift_two,
        ],
        axis=0,
    )
    small = sum_all(
        jnp.concatenate([rows8, grad_bias_qv, grad_bias_up.reshape(FF // D, D)], axis=0)
    )
    grad_vectors = small[:8]
    grad_bias_qv = lax.dynamic_slice_in_dim(small[8:10], z * (D // parts), D // parts, 1)
    grad_bias_up = lax.dynamic_slice_in_dim(small[10:].reshape(FF), z * (FF // parts), FF // parts, 0)
    return (
        output.astype(low),
        input_sum.astype(low),
        grad_qkv,
        grad_bias_qv,
        grad_out,
        grad_up,
        grad_bias_up,
        grad_down,
        grad_vectors,
    )


def solution(mesh):
    in_specs = (
        P(("dp", "mp"), None),
        P(("dp", "mp"), None),
        P("dp"),
        P("dp", None),
        P(None, None, "mp"),
        P(None, "mp"),
        P("mp", None),
        P(None, "mp"),
        P("mp"),
        P("mp", None),
        P(),
    )
    out_specs = (
        P(("dp", "mp"), None),
        P(("dp", "mp"), None),
        P("dp", None, "mp"),
        P(None, "mp"),
        P("mp", "dp"),
        P("dp", "mp"),
        P("mp"),
        P("mp", "dp"),
        P(),
    )
    chosen = local_body if fits_local(mesh) else body
    return jax.shard_map(chosen, mesh=mesh, in_specs=in_specs, out_specs=out_specs, check_vma=False)
```

```python
import functools
import heapq

import jax
import jax.numpy as jnp
from jax import lax
from jax.experimental import pallas as pl
from jax.experimental.pallas import tpu as pltpu
from jax.sharding import PartitionSpec as P

D = 1024
HD = 64
FF = 4096
LEN = 2368


def norm_forward(value, gain, shift):
    average = jnp.mean(value, axis=-1, keepdims=True)
    centred = value - average
    inverse = lax.rsqrt(jnp.mean(centred * centred, axis=-1, keepdims=True) + 1e-05)
    normed = centred * inverse
    return (normed * gain + shift, normed, inverse)


def norm_backward(grad, normed, inverse, gain):
    scaled = grad * gain
    result = inverse * (
        scaled
        - jnp.mean(scaled, axis=-1, keepdims=True)
        - normed * jnp.mean(scaled * normed, axis=-1, keepdims=True)
    )
    return (result, jnp.sum(grad * normed, axis=0), jnp.sum(grad, axis=0))


def gelu_exact(value):
    return jax.nn.gelu(value, approximate=False)


def attend_forward(queries, keys, values, segments):
    scale = HD ** (-0.5)
    block_rows = LEN // 4

    def one_block(inputs):
        query_block, segment_block = inputs
        scores = (
            jnp.einsum("bhe,khe->hbk", query_block, keys, preferred_element_type=jnp.float32)
            * scale
        )
        allowed = segment_block[:, None] == segments[None, :]
        scores = jnp.where(allowed[None], scores, -1e30)
        highest = jnp.max(scores, axis=-1, keepdims=True)
        weights = jnp.exp(scores - highest)
        totals = jnp.sum(weights, axis=-1, keepdims=True)
        chances_low = (weights / totals).astype(jnp.bfloat16)
        result = jnp.einsum("hbk,khe->bhe", chances_low, values, preferred_element_type=jnp.float32)
        return (result.astype(jnp.bfloat16), (highest + jnp.log(totals))[..., 0])

    blocks = queries.reshape(4, block_rows, queries.shape[1], queries.shape[2])
    results, logsums = lax.map(one_block, (blocks, segments.reshape(4, block_rows)))
    return (results.reshape(queries.shape), logsums)


def attend_backward(queries, keys, values, out_grads, logsums, segments):
    scale = HD ** (-0.5)
    block_rows = LEN // 4

    def one_block(carry, inputs):
        key_grads, value_grads = carry
        query_block, grad_block, logsum_block, segment_block = inputs
        scores = (
            jnp.einsum("bhe,khe->hbk", query_block, keys, preferred_element_type=jnp.float32)
            * scale
        )
        allowed = segment_block[:, None] == segments[None, :]
        scores = jnp.where(allowed[None], scores, -1e30)
        chances = jnp.exp(scores - logsum_block[..., None])
        chances_low = chances.astype(jnp.bfloat16)
        value_grads = value_grads + jnp.einsum(
            "hbk,bhe->khe", chances_low, grad_block, preferred_element_type=jnp.float32
        )
        flow = jnp.einsum("bhe,khe->hbk", grad_block, values, preferred_element_type=jnp.float32)
        inner = jnp.sum(chances * flow, axis=-1, keepdims=True)
        score_grads = (chances * (flow - inner)).astype(jnp.bfloat16)
        query_grads = (
            jnp.einsum("hbk,khe->bhe", score_grads, keys, preferred_element_type=jnp.float32)
            * scale
        )
        key_grads = (
            key_grads
            + jnp.einsum(
                "hbk,bhe->khe", score_grads, query_block, preferred_element_type=jnp.float32
            )
            * scale
        )
        return ((key_grads, value_grads), query_grads)

    shape_blocks = (4, block_rows, queries.shape[1], queries.shape[2])
    zeros = jnp.zeros(keys.shape, jnp.float32)
    (key_grads, value_grads), query_grads = lax.scan(
        one_block,
        (zeros, zeros),
        (
            queries.reshape(shape_blocks),
            out_grads.reshape(shape_blocks),
            logsums,
            segments.reshape(4, block_rows),
        ),
    )
    return (query_grads.reshape(queries.shape), key_grads, value_grads)


def body(
    tokens,
    cotangent,
    timesteps,
    item_lengths,
    w_qkv,
    bias_qv,
    w_out,
    w_up,
    bias_up,
    w_down,
    vectors,
):
    rows = tokens.shape[0]
    total = rows * lax.axis_size("mp")
    seq_count = timesteps.shape[0]
    local_width = w_qkv.shape[2]
    local_hidden = w_up.shape[1]
    local_heads = local_width // HD
    my_index = lax.axis_index("mp")
    row_ids = my_index * rows + lax.iota(jnp.int32, rows)
    row_owner = row_ids // LEN
    step_times = timesteps.astype(jnp.float32) * 0.001
    time_rows = jnp.sum(
        jnp.where(
            row_owner[:, None] == lax.iota(jnp.int32, seq_count)[None, :], step_times[None, :], 0.0
        ),
        axis=1,
    )
    ends = jnp.cumsum(item_lengths, axis=1)
    segments = jnp.sum(
        (lax.iota(jnp.int32, LEN)[None, :, None] >= ends[:, None, :]).astype(jnp.int32), axis=2
    )
    lifted = tokens.astype(jnp.float32) + time_rows[:, None] * vectors[0] + vectors[1]
    gathered = lax.all_gather(lifted.astype(jnp.bfloat16), "mp", axis=0, tiled=True)
    projected = jnp.einsum("td,dce->cte", gathered, w_qkv, preferred_element_type=jnp.float32)
    shaped = (seq_count, LEN, local_heads, HD)
    head_query = (projected[0] + bias_qv[0]).astype(jnp.bfloat16).reshape(shaped)
    head_key = projected[1].astype(jnp.bfloat16).reshape(shaped)
    head_value = (projected[2] + bias_qv[1]).astype(jnp.bfloat16).reshape(shaped)
    attended, logsums = lax.map(
        lambda items: attend_forward(*items), (head_query, head_key, head_value, segments)
    )
    attended = attended.reshape(total, local_width)
    piece = attended
    mixed = (
        lax.psum_scatter(
            jnp.dot(piece, w_out, preferred_element_type=jnp.float32),
            "mp",
            scatter_dimension=0,
            tiled=True,
        )
        + vectors[2]
    )
    first, normed_one, inverse_one = norm_forward(lifted + mixed, vectors[4], vectors[5])
    hidden_all = lax.all_gather(first.astype(jnp.bfloat16), "mp", axis=0, tiled=True)
    upper = jnp.dot(hidden_all, w_up, preferred_element_type=jnp.float32) + bias_up
    activated, gelu_pull = jax.vjp(gelu_exact, upper)
    activated = activated.astype(jnp.bfloat16)
    piece = activated
    down = (
        lax.psum_scatter(
            jnp.dot(piece, w_down, preferred_element_type=jnp.float32).astype(jnp.bfloat16),
            "mp",
            scatter_dimension=0,
            tiled=True,
        ).astype(jnp.float32)
        + vectors[3]
    )
    output, normed_two, inverse_two = norm_forward(first + down, vectors[6], vectors[7])
    out_grads = cotangent.astype(jnp.float32)
    second_grads, gain_two, shift_two = norm_backward(
        out_grads, normed_two, inverse_two, vectors[6]
    )
    down_all = lax.all_gather(second_grads.astype(jnp.bfloat16), "mp", axis=0, tiled=True)
    grad_down = jnp.einsum("tf,td->fd", activated, down_all, preferred_element_type=jnp.float32)
    act_grads = jnp.einsum("td,fd->tf", down_all, w_down, preferred_element_type=jnp.float32)
    (upper_grads,) = gelu_pull(act_grads)
    upper_low = upper_grads.astype(jnp.bfloat16)
    grad_bias_up = jnp.sum(upper_low, axis=0, dtype=jnp.float32)
    grad_up = jnp.einsum("td,tf->df", hidden_all, upper_low, preferred_element_type=jnp.float32)
    piece = upper_low
    first_part = lax.psum_scatter(
        jnp.einsum("tf,df->td", piece, w_up, preferred_element_type=jnp.float32).astype(
            jnp.bfloat16
        ),
        "mp",
        scatter_dimension=0,
        tiled=True,
    ).astype(jnp.float32)
    first_grads = second_grads + first_part
    mixed_grads, gain_one, shift_one = norm_backward(
        first_grads, normed_one, inverse_one, vectors[4]
    )
    mixed_all = lax.all_gather(mixed_grads.astype(jnp.bfloat16), "mp", axis=0, tiled=True)
    grad_out = jnp.einsum("te,td->ed", attended, mixed_all, preferred_element_type=jnp.float32)
    attended_grads = jnp.einsum(
        "td,ed->te", mixed_all, w_out, preferred_element_type=jnp.float32
    ).astype(jnp.bfloat16)
    query_grads, key_grads, value_grads = lax.map(
        lambda items: attend_backward(*items),
        (head_query, head_key, head_value, attended_grads.reshape(shaped), logsums, segments),
    )
    qkv_low = jnp.stack(
        [
            query_grads.reshape(total, local_width),
            key_grads.reshape(total, local_width),
            value_grads.reshape(total, local_width),
        ],
        axis=1,
    ).astype(jnp.bfloat16)
    grad_bias_qv = jnp.sum(qkv_low[:, 0::2], axis=0, dtype=jnp.float32)
    grad_qkv = jnp.einsum("td,tcf->dcf", gathered, qkv_low, preferred_element_type=jnp.float32)
    piece = qkv_low
    input_part = lax.psum_scatter(
        jnp.einsum("tcf,dcf->td", piece, w_qkv, preferred_element_type=jnp.float32).astype(
            jnp.bfloat16
        ),
        "mp",
        scatter_dimension=0,
        tiled=True,
    ).astype(jnp.float32)
    input_sum = mixed_grads + input_part
    vector_terms = jnp.stack(
        [
            jnp.sum(time_rows[:, None] * input_sum, axis=0),
            jnp.sum(input_sum, axis=0),
            jnp.sum(mixed_grads, axis=0),
            jnp.sum(second_grads, axis=0),
            gain_one,
            shift_one,
            gain_two,
            shift_two,
        ],
        axis=0,
    )
    zero_index = jnp.zeros((), jnp.int32)
    qv_start = my_index * local_width
    up_start = my_index * local_hidden
    qv_placed = lax.dynamic_update_slice(
        jnp.zeros((2, D), jnp.float32), grad_bias_qv, (zero_index, qv_start)
    )
    up_placed = lax.dynamic_update_slice(jnp.zeros((FF,), jnp.float32), grad_bias_up, (up_start,))
    grad_qkv, grad_out, grad_up, grad_down = (
        lax.psum_scatter(
            grad_qkv.astype(jnp.bfloat16), "dp", scatter_dimension=0, tiled=True
        ).astype(jnp.float32),
        lax.psum_scatter(
            grad_out.astype(jnp.bfloat16), "dp", scatter_dimension=1, tiled=True
        ).astype(jnp.float32),
        lax.psum_scatter(
            grad_up.astype(jnp.bfloat16), "dp", scatter_dimension=0, tiled=True
        ).astype(jnp.float32),
        lax.psum_scatter(
            grad_down.astype(jnp.bfloat16), "dp", scatter_dimension=1, tiled=True
        ).astype(jnp.float32),
    )
    grad_vectors, qv_summed, up_summed = lax.psum(
        (vector_terms, qv_placed, up_placed), ("dp", "mp")
    )
    grad_bias_qv = lax.dynamic_slice_in_dim(qv_summed, qv_start, local_width, 1)
    grad_bias_up = lax.dynamic_slice_in_dim(up_summed, up_start, local_hidden, 0)
    return (
        output.astype(jnp.bfloat16),
        input_sum.astype(jnp.bfloat16),
        grad_qkv,
        grad_bias_qv,
        grad_out,
        grad_up,
        grad_bias_up,
        grad_down,
        grad_vectors,
    )


UNIT = 128
LONG = 4
MESH = pl.DeviceIdType.MESH


def fits_local(mesh):
    parts = mesh.shape["mp"]
    return mesh.shape["dp"] == 8 and parts == 4 and LEN % (16 * parts) == 0


def window_plan(rows, parts):
    firsts = [(rows * j) // UNIT - (LONG - 1) for j in range(parts)]
    offsets = [rows * j - UNIT * first for j, first in enumerate(firsts)]
    ends = [
        ((rows * (j + 1) - 1) // UNIT + LONG - firsts[j]) * UNIT for j in range(parts)
    ]
    return firsts, offsets, ends


def pick(table, index):
    value = jnp.int32(table[0])
    for j in range(1, len(table)):
        value = jnp.where(index == j, jnp.int32(table[j]), value)
    return value


def gather_kernel(
    rows, window, parts, tokens, w_qkv, w_out, w_up, w_down, win, f_qkv, f_out, f_up, f_down, send, recv, near, far, own
):
    d = lax.axis_index("dp")
    z = lax.axis_index("mp")
    firsts, offsets, ends = window_plan(rows, parts)
    shards = (w_qkv, w_out, w_up, w_down)
    fulls = (f_qkv, f_out, f_up, f_down)
    sizes = (128, 32, 128, 128)
    others = (1, 3, 2)
    peers = [(d, z ^ k) for k in others] + [(d ^ 1, z), (d ^ 2, z), (d ^ 4, z)]
    barrier = pltpu.get_barrier_semaphore()
    for peer in peers:
        pl.semaphore_signal(barrier, inc=1, device_id=peer, device_id_type=MESH)
    pl.semaphore_wait(barrier, len(peers))

    def part(ref, index, owner, size, half=None):
        start = owner * size
        count = size
        if half is not None:
            count = size // 2
            start = start + half * count
        rows_at = pl.ds(pl.multiple_of(start, 16), count)
        return ref.at[index, rows_at, :]

    chunks = [(g, k) for g in range(4) for k in others]
    copies = {}

    def remote(i, kind, src, dst, target):
        copy = pltpu.make_async_remote_copy(
            src, dst, send.at[i, kind], recv.at[i, kind], device_id=target, device_id_type=MESH
        )
        copy.start()
        copies[i, kind] = copy

    def first_hop(i):
        g, k = chunks[i]
        size = sizes[g]
        rows_at = pl.ds(pl.multiple_of(d * size, 16), size)
        src = shards[g].at[rows_at, :]
        remote(i, 0, src, part(fulls[g], z, d, size), (d, z ^ k))

    def place(i, owner, half=None):
        g, k = chunks[i]
        return part(fulls[g], z ^ k, owner, sizes[g], half)

    for i in range(3):
        first_hop(i)
    left_send = [
        pltpu.make_async_remote_copy(
            tokens.at[pl.ds(0, ends[j] - offsets[j] - rows), :],
            win.at[pl.ds(offsets[j] + rows, ends[j] - offsets[j] - rows), :],
            near.at[0], near.at[1], device_id=(d, j), device_id_type=MESH,
        )
        for j in range(parts - 1)
    ]
    right_send = [
        pltpu.make_async_remote_copy(
            tokens.at[pl.ds(rows - offsets[j], offsets[j]), :],
            win.at[pl.ds(0, offsets[j]), :],
            far.at[0], far.at[1], device_id=(d, j), device_id_type=MESH,
        )
        for j in range(1, parts)
    ]
    for j in range(parts - 1):
        @pl.when(z == j + 1)
        def _(j=j):
            left_send[j].start()
    for j in range(1, parts):
        @pl.when(z == j - 1)
        def _(j=j):
            right_send[j - 1].start()
    locals_ = []
    for g in range(4):
        copy = pltpu.make_async_copy(shards[g], fulls[g].at[z], own.at[g])
        copy.start()
        locals_.append(copy)
    offset = pl.multiple_of(pick(offsets, z), 16)
    copy = pltpu.make_async_copy(tokens, win.at[pl.ds(offset, rows), :], own.at[4])
    copy.start()
    locals_.append(copy)
    fill_first = pltpu.make_async_copy(
        tokens.at[pl.ds(0, offsets[0]), :], win.at[pl.ds(0, offsets[0]), :], own.at[5]
    )
    fills = []
    for j in range(parts):
        begin = ends[j] if j < parts - 1 else offsets[j] + rows
        if begin < window:
            fills.append(
                (j, pltpu.make_async_copy(
                    tokens.at[pl.ds(0, window - begin), :], win.at[pl.ds(begin, window - begin), :], own.at[6]
                ))
            )

    @pl.when(z == 0)
    def _():
        fill_first.start()

    for j, fill in fills:
        @pl.when(z == j)
        def _(fill=fill):
            fill.start()


    def stage_one(i):
        copies[i, 0].wait_recv()
        remote(i, 1, place(i, d), place(i, d), (d ^ 2, z))
        remote(i, 2, place(i, d), place(i, d), (d ^ 4, z))
        remote(i, 5, place(i, d), place(i, d), (d ^ 1, z))

    def stage_two(i):
        copies[i, 1].wait_recv()
        remote(i, 3, place(i, d ^ 2, 0), place(i, d ^ 2, 0), (d ^ 4, z))
        remote(i, 6, place(i, d ^ 2), place(i, d ^ 2), (d ^ 1, z))
        copies[i, 2].wait_recv()
        remote(i, 4, place(i, d ^ 4, 1), place(i, d ^ 4, 1), (d ^ 2, z))
        remote(i, 7, place(i, d ^ 4), place(i, d ^ 4), (d ^ 1, z))

    def stage_three(i):
        copies[i, 3].wait_recv()
        remote(i, 8, place(i, d ^ 6, 0), place(i, d ^ 6, 0), (d ^ 1, z))
        copies[i, 4].wait_recv()
        remote(i, 9, place(i, d ^ 6, 1), place(i, d ^ 6, 1), (d ^ 1, z))

    n = len(chunks)
    for i in range(n + 2):
        if i < n:
            stage_one(i)
            if i + 3 < n:
                first_hop(i + 3)
        if 0 <= i - 1 < n:
            stage_two(i - 1)
        if 0 <= i - 2 < n:
            stage_three(i - 2)
    for i in range(n):
        for kind in range(5, 10):
            copies[i, kind].wait_recv()
        for kind in range(10):
            copies[i, kind].wait_send()
    for j in range(parts - 1):
        @pl.when(z == j + 1)
        def _(j=j):
            left_send[j].wait_send()

        @pl.when(z == j)
        def _(j=j):
            left_send[j].wait_recv()
    for j in range(1, parts):
        @pl.when(z == j - 1)
        def _(j=j):
            right_send[j - 1].wait_send()

        @pl.when(z == j)
        def _(j=j):
            right_send[j - 1].wait_recv()
    for copy in locals_:
        copy.wait()

    @pl.when(z == 0)
    def _():
        fill_first.wait()

    for j, fill in fills:
        @pl.when(z == j)
        def _(fill=fill):
            fill.wait()


def gather(tokens, w_qkv, w_out, w_up, w_down, window, parts):
    rows = tokens.shape[0]
    any_ = pl.BlockSpec(memory_space=pl.ANY)
    low = jnp.bfloat16
    return pl.pallas_call(
        functools.partial(gather_kernel, rows, window, parts),
        out_shape=[
            jax.ShapeDtypeStruct((window, D), low),
            jax.ShapeDtypeStruct((parts,) + w_qkv.shape, low),
            jax.ShapeDtypeStruct((parts,) + w_out.shape, low),
            jax.ShapeDtypeStruct((parts,) + w_up.shape, low),
            jax.ShapeDtypeStruct((parts,) + w_down.shape, low),
        ],
        in_specs=[pl.BlockSpec(memory_space=pltpu.VMEM)] * 5,
        out_specs=[any_] * 5,
        scratch_shapes=[
            pltpu.SemaphoreType.DMA((12, 10)),
            pltpu.SemaphoreType.DMA((12, 10)),
            pltpu.SemaphoreType.DMA((2,)),
            pltpu.SemaphoreType.DMA((2,)),
            pltpu.SemaphoreType.DMA((7,)),
        ],
        compiler_params=pltpu.CompilerParams(collective_id=0, has_side_effects=True, vmem_limit_bytes=32 * 2**20),
    )(tokens, w_qkv, w_out, w_up, w_down)


NT = (((1,), (1,)), ((), ()))
TN = (((0,), (0,)), ((), ()))
FIRST_OWN, LAST_OWN = LONG - 1, LONG + 4


def two_heads(block):
    lane = lax.broadcasted_iota(jnp.int32, block.shape, 1)
    zero = jnp.zeros_like(block)
    return jnp.concatenate(
        [jnp.where(lane < HD, block, zero), jnp.where(lane < HD, zero, block)], axis=0
    )


def from_two(flipped):
    both = jnp.concatenate([flipped[:HD, :UNIT], flipped[HD:, UNIT:]], axis=0)
    return both.T


def weights_of(keys, pair, valid):
    scores = lax.dot_general(keys, pair, NT, preferred_element_type=jnp.float32) * HD ** (-0.5)
    if valid is not None:
        scores = jnp.where(valid, scores, -1e30)
    highest = jnp.max(scores, axis=0, keepdims=True)
    weights = jnp.exp(scores - highest)
    return weights * (1.0 / jnp.sum(weights, axis=0, keepdims=True))


def attend_kernel(kind, start, unit_seg, seg, q, k, v, o):
    def unit(u, carry):
        mine = pl.ds(pl.multiple_of(u * UNIT, UNIT), UNIT)

        def run(at, valid):
            pair = two_heads(q[mine, :])
            chances = weights_of(k[at, :], pair, valid).astype(jnp.bfloat16)
            flipped = lax.dot_general(v[at, :], chances, TN, preferred_element_type=jnp.float32)
            o[mine, :] = from_two(flipped).astype(o.dtype)

        @pl.when(kind[u] == 2)
        def _():
            run(pl.ds(pl.multiple_of(start[u], UNIT), LONG * UNIT), None)

        @pl.when(kind[u] == 1)
        def _():
            run(mine, seg[mine, :] == unit_seg[u])

        return carry

    lax.fori_loop(FIRST_OWN, LAST_OWN + 1, unit, 0)


def attention_call(window, parts, plan, segs, qkv):
    cut = D // parts
    pairs = cut // (2 * HD)
    spec = lambda base: pl.BlockSpec((None, window, 2 * HD), lambda c, p, *_: (c, 0, base * pairs + p))
    whole = pl.BlockSpec((window, 1), lambda c, p, *_: (0, 0))
    return pl.pallas_call(
        attend_kernel,
        grid_spec=pltpu.PrefetchScalarGridSpec(
            num_scalar_prefetch=3,
            grid=(parts, pairs),
            in_specs=[whole, spec(0), spec(1), spec(2)],
            out_specs=pl.BlockSpec((window, 2 * HD), lambda c, p, *_: (0, c * pairs + p)),
        ),
        out_shape=jax.ShapeDtypeStruct((window, D), jnp.bfloat16),
        compiler_params=pltpu.CompilerParams(vmem_limit_bytes=48 * 2**20),
    )(*plan, segs[:, None], qkv, qkv, qkv)


def unit_plan(segs, z, offsets, rows, window):
    units = window // UNIT
    unit_seg = segs[::UNIT]
    same = unit_seg[:, None] == unit_seg[None, :]
    counts = jnp.sum(same.astype(jnp.int32), axis=1)
    inside = unit_seg < 1000
    inside = inside & (unit_seg >= 0)
    index = lax.iota(jnp.int32, units)
    first = jnp.sum((unit_seg[None, :] < unit_seg[:, None]).astype(jnp.int32), axis=1)
    own = (index >= FIRST_OWN) & (index <= LAST_OWN)
    meets = jnp.any(same & own[None, :], axis=1)
    long = inside & (counts == LONG) & meets
    kind = jnp.where(long, 2, jnp.where(own, 1, 0))
    return (
        kind.astype(jnp.int32),
        jnp.where(long, first * UNIT, 0).astype(jnp.int32),
        unit_seg,
    )


def swap(array, axis, bit):
    size = lax.axis_size(axis)
    return lax.ppermute(array, axis, [(i, i ^ bit) for i in range(size)])


class Clock:
    def __init__(self):
        self.now = 0.0
        self.free = {}
        self.queue = []
        self.count = 0

    def send(self, link, size, action, share=1.0):
        rate = {"c": 400e3, "x": 44e3, "y": 44e3, "z": 44e3}[link]
        begin = max(self.now, self.free.get(link, 0.0))
        end = begin + share * size / rate
        self.free[link] = end
        self.count += 1
        heapq.heappush(self.queue, (end + 1.5, self.count, action))

    def work(self, time):
        self.now += time
        while self.queue and self.queue[0][0] <= self.now:
            heapq.heappop(self.queue)[2]()

    def drain(self):
        while self.queue:
            ready, _, action = heapq.heappop(self.queue)
            self.now = max(self.now, ready)
            action()


def block_owners(d, core, x_first):
    x, y = lax.rem(d // 2, 2), d // 4
    if x_first:
        return [4 * b + 2 * a + core for a in (1 - x, x) for b in (1 - y, y)]
    return [4 * b + 2 * a + core for b in (1 - y, y) for a in (1 - x, x)]


RING = (2, 3, 1, 0)


def back_kernel(
    rows, window, parts, perm, back, sec_low, sec2, inverse, gain, small_in, kf, qf,
    first_t, lift_t, second_grads, normed_one, act2, dgelu, att2, qkv, f_qkv, f_out, f_up, f_down,
    input_grad, g_qkv, g_out, g_up, g_down, small_out,
    acc, normed, turned, arena, act, slope, y, up2, w_in, mixed2, stage, mixed_win, small, small_in_far,
    s_down, s_up, s_out, s_qkv, k_down, k_up, k_out, k_qkv,
    r_down, r_up, r_out, r_qkv, t_down, t_up, t_out, t_qkv, z_down, z_up, z_out, z_qkv,
    local, hop_send, hop_recv, pair_send, pair_recv, halo_send, halo_recv, small_send, small_recv,
):
    f32, low = jnp.float32, jnp.bfloat16
    d = lax.axis_index("dp")
    z = lax.axis_index("mp")
    core = lax.rem(d, 2)
    firsts, offsets, ends = window_plan(rows, parts)
    offset = pl.multiple_of(pick(offsets, z), 16)
    partner = (d ^ 1, z)
    peers = [(d, z ^ k) for k in (1, 2, 3)] + [partner, (d ^ 2, z), (d ^ 4, z)]
    barrier = pltpu.get_barrier_semaphore()
    for peer in peers:
        pl.semaphore_signal(barrier, inc=1, device_id=peer, device_id_type=MESH)
    pl.semaphore_wait(barrier, len(peers))
    clock = Clock()
    tail = []

    wide = 2 * rows
    wd = arena.at[pl.ds(0, D), :]
    wu = arena.at[pl.ds(D, D), :]

    def fetch(index, source, target):
        copy = pltpu.make_async_copy(source, target, local.at[index])
        copy.start()
        return copy

    chunk = lambda k: z ^ k
    hidden = lambda k: pl.ds(pl.multiple_of(chunk(k) * D, D), D)
    load_wd = lambda i: fetch(0, f_down.at[chunk(RING[i])], wd)
    load_wu = lambda i: fetch(1, f_up.at[chunk(RING[i])], wu)
    load_act = lambda i: fetch(2, act2.at[:, hidden(RING[i])], act)
    load_slope = lambda i: fetch(3, dgelu.at[:, hidden(RING[i])], slope)
    at_wd, at_slope, at_act, at_wu = load_wd(0), load_slope(0), load_act(0), load_wu(0)
    at_acc = fetch(4, second_grads, acc)
    at_normed = fetch(5, normed_one, normed)
    at_turned = fetch(6, first_t, turned)

    zero = jnp.zeros((16, D), low)
    for j in range(parts):
        spans = []
        if j == 0:
            spans.append((0, offsets[0]))
        begin = ends[j] if j < parts - 1 else offsets[j] + rows
        if begin < window:
            spans.append((begin, window))
        if spans:
            @pl.when(z == j)
            def _(spans=spans):
                for begin, end in spans:
                    def clear(i, c):
                        mixed_win[pl.ds(pl.multiple_of(begin + i * 16, 16), 16), :] = zero
                        return c
                    lax.fori_loop(0, (end - begin) // 16, clear, 0)

    groups = {
        "down": (s_down, k_down, r_down, t_down, z_down, g_down, 0),
        "up": (s_up, k_up, r_up, t_up, z_up, g_up, 1),
        "out": (s_out, k_out, r_out, t_out, z_out, g_out, 2),
        "qkv": (s_qkv, k_qkv, r_qkv, t_qkv, z_qkv, g_qkv, 3),
    }
    hops = {}

    def x_ahead(g, i):
        return (i + groups[g][6]) % 2 == 0

    def put(g, i, j, at, value):
        if not x_ahead(g, i):
            j = (0, 2, 1, 3)[j]
        if j < 2:
            groups[g][0][(i % 2, j) + at] = value
        else:
            groups[g][1][(i, j - 2) + at] = value

    def hop(g, i, kind, source, target, device):
        index = groups[g][6]
        copy = pltpu.make_async_remote_copy(
            source, target, hop_send.at[index, i, kind], hop_recv.at[index, i, kind],
            device_id=device, device_id_type=MESH,
        )
        copy.start()
        hops[g, i, kind] = copy

    def add_into(ref, other):
        count = ref.shape[0]
        step = min(count, 64)

        def body(j, c):
            at = pl.ds(pl.multiple_of(j * step, step), step)
            ref[at, :] = (ref[at, :].astype(f32) + other[at, :].astype(f32)).astype(low)
            return c

        lax.fori_loop(0, count // step, body, 0)

    def launch(g, i):
        s, kept, r, t, zb, out, index = groups[g]
        x_first = x_ahead(g, i)
        n1, n2 = ((d ^ 2, z), (d ^ 4, z)) if x_first else ((d ^ 4, z), (d ^ 2, z))
        l1, l2 = ("x", "y") if x_first else ("y", "x")
        block = s.shape[2] * s.shape[3] * 2
        k = RING[i]
        hop(g, i, 0, s.at[i % 2], r.at[i], n1)

        def second():
            hops[g, i, 0].wait_recv()
            add_into(kept.at[i, 0], r.at[i, 0])
            hop(g, i, 1, kept.at[i, 0], t.at[i], n2)
            clock.send(l2, block, third)
            add_into(kept.at[i, 1], r.at[i, 1])

        def third():
            hops[g, i, 1].wait_recv()
            add_into(kept.at[i, 1], t.at[i])
            if k:
                hop(g, i, 2, kept.at[i, 1], zb.at[k - 1], (d, z ^ k))
                clock.send("z", block, fourth, 1.0 if k == 1 else 2.0)

        def fourth():
            hops[g, i, 2].wait_recv()

        clock.send(l1, 2 * block, second)

    def free_slot(g, i):
        if i >= 2:
            hops[g, i - 2, 0].wait_send()

    def finish(g):
        s, kept, r, t, zb, out, index = groups[g]
        own = RING.index(0)
        count = s.shape[2]
        step = min(count, 64)
        pieces = kept.at[own, 1]

        def body(j, c):
            at = pl.ds(pl.multiple_of(j * step, step), step)
            total = pieces[at, :].astype(f32)
            for k in range(parts - 1):
                total = total + zb[k, at, :].astype(f32)
            out[at, :] = total
            return c

        lax.fori_loop(0, count // step, body, 0)

    def exchange(index, source, target):
        copy = pltpu.make_async_remote_copy(
            source, target, pair_send.at[index], pair_recv.at[index], device_id=partner, device_id_type=MESH
        )
        copy.start()
        return copy

    small[...] = small_in[...]

    pending = {}

    def grad_up_chunk(i):
        pending.pop(i).wait_recv()
        if i == 0:
            at_turned.wait()
        free_slot("up", i)

        def body(n, c):
            at = pl.ds(pl.multiple_of(n * 256, 256), 256)
            tile = jnp.dot(turned[...], up2[i, :, at], preferred_element_type=f32).astype(low)
            for j in range(4):
                put("up", i, j, (slice(None), at), tile[j * 128 : (j + 1) * 128])
            return c

        lax.fori_loop(0, 4, body, 0)
        launch("up", i)
        clock.work(2.0)

    exchanges = []
    loads = {"wd": at_wd, "wu": at_wu, "slope": at_slope, "act": at_act}

    def upper_chunk(i):
        loads["wd"].wait()
        loads["slope"].wait()
        bias_row = chunk(RING[i])

        def body(n, c):
            at = pl.ds(pl.multiple_of(n * 256, 256), 256)
            grads = lax.dot_general(sec_low[...], wd[at, :], NT, preferred_element_type=f32)
            value = (grads * slope[:, at].astype(f32)).astype(low)
            up2[i, pl.ds(0, rows), at] = value
            small[pl.ds(10 + bias_row, 1), at] = jnp.sum(value.astype(f32), axis=0, keepdims=True)
            return c

        lax.fori_loop(0, 4, body, 0)
        pending[i] = exchange(i, up2.at[i, pl.ds(0, rows), :], up2.at[i, pl.ds(rows, rows), :])
        exchanges.append(pending[i])
        clock.work(2.5)
        if i + 1 < parts:
            loads["wd"], loads["slope"] = load_wd(i + 1), load_slope(i + 1)

    def grad_down_chunk(i):
        loads["act"].wait()
        free_slot("down", i)

        def body(n, c):
            at = pl.ds(pl.multiple_of(n * 256, 256), 256)
            tile = lax.dot_general(act[:, at], sec2[...], TN, preferred_element_type=f32).astype(low)
            for j in range(4):
                put("down", i, j, (at, slice(None)), tile[:, j * 128 : (j + 1) * 128])
            return c

        lax.fori_loop(0, 4, body, 0)
        launch("down", i)
        clock.work(2.0)
        if i + 1 < parts:
            loads["act"] = load_act(i + 1)

    def first_chunk(i):
        loads["wu"].wait()
        if i == 0:
            at_acc.wait()

        def body(n, c):
            at = pl.ds(pl.multiple_of(n * 256, 256), 256)
            acc[:, at] += lax.dot_general(
                up2[i, pl.ds(0, rows), :], wu[at, :], NT, preferred_element_type=f32
            )
            return c

        lax.fori_loop(0, 4, body, 0)
        clock.work(2.0)
        if i + 1 < parts:
            loads["wu"] = load_wu(i + 1)

    grad_down_chunk(0)
    for i in range(parts):
        upper_chunk(i)
        first_chunk(i)
        if i == 1:
            grad_down_chunk(1)

    at_normed.wait()
    zero_row = jnp.zeros((16, D), f32)

    def norm_body(i, sums):
        at = pl.ds(pl.multiple_of(i * 16, 16), 16)
        grads, unit = acc[at, :], normed[at, :]
        scaled = grads * gain[0:1, :]
        result = inverse[at, :] * (
            scaled
            - jnp.mean(scaled, axis=-1, keepdims=True)
            - unit * jnp.mean(scaled * unit, axis=-1, keepdims=True)
        )
        acc[at, :] = result
        mixed_win[pl.ds(pl.multiple_of(offset + i * 16, 16), 16), :] = result.astype(low)
        return (sums[0] + grads * unit, sums[1] + grads, sums[2] + result)

    sums = lax.fori_loop(0, rows // 16, norm_body, (zero_row, zero_row, zero_row))
    small[4:5, :] = jnp.sum(sums[0], axis=0, keepdims=True)
    small[5:6, :] = jnp.sum(sums[1], axis=0, keepdims=True)
    small[2:3, :] = jnp.sum(sums[2], axis=0, keepdims=True)
    halos = []
    for j in range(parts - 1):
        count = ends[j] - offsets[j] - rows
        halos.append((j + 1, j, pltpu.make_async_remote_copy(
            mixed_win.at[pl.ds(offsets[j + 1], count), :],
            mixed_win.at[pl.ds(offsets[j] + rows, count), :],
            halo_send.at[0], halo_recv.at[0], device_id=(d, j), device_id_type=MESH,
        )))
    for j in range(1, parts):
        halos.append((j - 1, j, pltpu.make_async_remote_copy(
            mixed_win.at[pl.ds(offsets[j - 1] + rows - offsets[j], offsets[j]), :],
            mixed_win.at[pl.ds(0, offsets[j]), :],
            halo_send.at[1], halo_recv.at[1], device_id=(d, j), device_id_type=MESH,
        )))
    for sender, receiver, copy in halos:
        @pl.when(z == sender)
        def _(copy=copy):
            copy.start()
    clock.work(4.0)
    for i in range(parts):
        grad_up_chunk(i)
        if i + 2 < parts:
            grad_down_chunk(i + 2)
    own_at = pl.ds(offset, rows)
    for j, owner in enumerate(block_owners(d, 1 - core, True)):
        stage[:, j * 128 : (j + 1) * 128] = mixed_win[own_at, pl.ds(pl.multiple_of(owner * 128, 128), 128)]
    exchanges.append(exchange(parts, stage, mixed2.at[pl.ds(rows, rows), :]))
    for j, owner in enumerate(block_owners(d, core, True)):
        mixed2[pl.ds(0, rows), j * 128 : (j + 1) * 128] = mixed_win[
            own_at, pl.ds(pl.multiple_of(owner * 128, 128), 128)
        ]
    clock.work(4.0)

    cut = D // parts
    three = 3 * cut
    pairs = cut // (2 * HD)
    x = arena
    wo = slope.at[pl.ds(0, cut), :]
    load_x = lambda i: fetch(0, qkv.at[chunk(RING[i])], arena.at[pl.ds(0, window), pl.ds(0, three)])
    load_wo = lambda i: fetch(1, f_out.at[chunk(RING[i])], wo)
    load_att = lambda i: fetch(
        2, att2.at[:, pl.ds(pl.multiple_of(chunk(RING[i]) * cut, cut), cut)], act.at[:, pl.ds(0, cut)]
    )
    load_wi = lambda i: fetch(3, f_qkv.at[chunk(RING[i])], w_in)
    at_turned = fetch(6, lift_t, turned)
    at_x, at_wo, at_att, at_wi = load_x(0), load_wo(0), load_att(0), load_wi(0)
    exchanges[-1].wait_recv()
    scale = HD ** (-0.5)

    def take_halo():
        for sender, receiver, copy in halos:
            @pl.when(z == receiver)
            def _(copy=copy):
                copy.wait_recv()

    def grad_qkv_chunk(i):
        pending.pop(i).wait_recv()
        if i == 0:
            at_turned.wait()
        free_slot("qkv", i)

        def body(n, c):
            at = pl.ds(pl.multiple_of(n * 256, 256), 256)
            tile = jnp.dot(turned[...], up2[i, :, at], preferred_element_type=f32).astype(low)
            for j in range(4):
                put("qkv", i, j, (slice(None), at), tile[j * 128 : (j + 1) * 128])
            return c

        lax.fori_loop(0, three // 256, body, 0)
        launch("qkv", i)
        clock.work(1.8)

    for i in range(parts):
        at_att.wait()
        free_slot("out", i)
        tile = lax.dot_general(act[:, 0:cut], mixed2[...], TN, preferred_element_type=f32).astype(low)
        for j in range(4):
            put("out", i, j, (slice(None), slice(None)), tile[:, j * 128 : (j + 1) * 128])
        launch("out", i)
        clock.work(0.8)
        if i == 0:
            take_halo()
        at_wo.wait()
        at_x.wait()

        def flow_body(n, c):
            at = pl.ds(pl.multiple_of(n * 512, 512), 512)
            x[at, three : three + cut] = lax.dot_general(
                mixed_win[at, :], wo[...], NT, preferred_element_type=f32
            ).astype(low)
            return c

        lax.fori_loop(0, window // 512, flow_body, 0)
        clock.work(1.2)
        if i + 1 < parts:
            at_wo, at_att = load_wo(i + 1), load_att(i + 1)

        def attend_body(step, c):
            p, slot = step // 3, lax.rem(step, 3)
            lanes = lambda base: pl.ds(pl.multiple_of(base + p * 2 * HD, 2 * HD), 2 * HD)
            unit_at = [
                pl.ds(perm[slot * LONG + m] * UNIT, UNIT) for m in range(LONG)
            ]
            keys = jnp.concatenate([x[at, lanes(cut)] for at in unit_at], axis=0)
            values = jnp.concatenate([x[at, lanes(2 * cut)] for at in unit_at], axis=0)
            marks = jnp.concatenate([kf[at, :] for at in unit_at], axis=0)
            wide_keys = jnp.concatenate([keys, marks], axis=1)
            k_sum = jnp.zeros((LONG * UNIT, 2 * HD), f32)
            v_sum = jnp.zeros((LONG * UNIT, 2 * HD), f32)
            for m in range(LONG):
                pair = two_heads(x[unit_at[m], lanes(0)])
                grads = two_heads(x[unit_at[m], lanes(three)])
                mark = qf[unit_at[m], :]
                wide_pair = jnp.concatenate([pair, jnp.concatenate([mark, mark], axis=0)], axis=1)
                scores = lax.dot_general(wide_keys, wide_pair, NT, preferred_element_type=f32) * scale
                weights = jnp.exp(scores - jnp.max(scores, axis=0, keepdims=True))
                chances = weights * (1.0 / jnp.sum(weights, axis=0, keepdims=True))
                flow = lax.dot_general(values, grads, NT, preferred_element_type=f32)
                inner = jnp.sum(chances * flow, axis=0, keepdims=True)
                slopes = (chances * (flow - inner)).astype(low)
                v_sum = v_sum + jnp.dot(chances.astype(low), grads, preferred_element_type=f32)
                k_sum = k_sum + jnp.dot(slopes, pair, preferred_element_type=f32)
                flipped = lax.dot_general(keys, slopes, TN, preferred_element_type=f32)
                at = pl.ds(pl.multiple_of(slot * LONG * UNIT + m * UNIT, UNIT), UNIT)
                y[at, lanes(0)] = (from_two(flipped) * scale).astype(low)
            at = pl.ds(pl.multiple_of(slot * LONG * UNIT, UNIT), LONG * UNIT)
            y[at, lanes(cut)] = (k_sum * scale).astype(low)
            y[at, lanes(2 * cut)] = v_sum.astype(low)
            return c

        lax.fori_loop(0, pairs * 3, attend_body, 0)
        clock.work(9.0)
        if i + 1 < parts:
            at_x = load_x(i + 1)
        for u in range(FIRST_OWN, LAST_OWN + 1):
            at = pl.ds(back[u] * UNIT, UNIT)
            act[pl.ds((u - FIRST_OWN) * UNIT, UNIT), cut:] = y[at, :]
        exchanges[i].wait_send()
        inner_at = pl.ds(pl.multiple_of(offset - FIRST_OWN * UNIT, 16), rows)
        up2[i, pl.ds(0, rows), 0:three] = act[inner_at, cut:]
        pending[i] = exchange(
            parts + 1 + i, up2.at[i, pl.ds(0, rows), pl.ds(0, three)], up2.at[i, pl.ds(rows, rows), pl.ds(0, three)]
        )
        exchanges.append(pending[i])
        place = pl.multiple_of(chunk(RING[i]) * cut, cut)
        small[8:9, pl.ds(place, cut)] = jnp.sum(up2[i, pl.ds(0, rows), 0:cut].astype(f32), axis=0, keepdims=True)
        small[9:10, pl.ds(place, cut)] = jnp.sum(
            up2[i, pl.ds(0, rows), 2 * cut : three].astype(f32), axis=0, keepdims=True
        )
        at_wi.wait()

        def input_body(n, c, i=i):
            at = pl.ds(pl.multiple_of(n * 256, 256), 256)
            acc[:, at] += lax.dot_general(
                up2[i, pl.ds(0, rows), 0:three], w_in[at, :], NT, preferred_element_type=f32
            )
            return c

        lax.fori_loop(0, 4, input_body, 0)
        clock.work(2.0)
        if i + 1 < parts:
            at_wi = load_wi(i + 1)
        grad_qkv_chunk(i)

    def last_body(i, total):
        at = pl.ds(pl.multiple_of(i * 16, 16), 16)
        value = acc[at, :]
        arena[at, :] = value.astype(low)
        return total + value

    total = jnp.sum(lax.fori_loop(0, rows // 16, last_body, zero_row), axis=0, keepdims=True)
    store = fetch(4, arena.at[pl.ds(0, rows), :], input_grad)
    small[0:1, :] = total * small_in[15:16, :]
    small[1:2, :] = total
    clock.work(2.0)
    small_copies = []

    def small_step(n):
        copy = pltpu.make_async_remote_copy(
            small, small_in_far.at[n], small_send.at[n], small_recv.at[n],
            device_id=[partner, (d ^ 2, z), (d ^ 4, z), (d, z ^ 1), (d, z ^ 2)][n], device_id_type=MESH,
        )
        copy.start()

        def take():
            copy.wait()
            small[...] += small_in_far[n]
            if n < 4:
                small_step(n + 1)

        clock.send("c", 0.4e6, take)

    small_step(0)
    clock.drain()
    for g in groups:
        finish(g)
    small_out[...] = small[...]
    store.wait()
    for (g, i, kind), copy in hops.items():
        if kind or i >= 2:
            copy.wait_send()
    for copy in exchanges[parts:]:
        copy.wait_send()
    for sender, receiver, copy in halos:
        @pl.when(z == sender)
        def _(copy=copy):
            copy.wait_send()


def back_call(rows, window, parts, perm, back, vmem_in, hbm_in):
    f32, low = jnp.float32, jnp.bfloat16
    any_ = pl.BlockSpec(memory_space=pl.ANY)
    vmem = pl.BlockSpec(memory_space=pltpu.VMEM)
    smem = pl.BlockSpec(memory_space=pltpu.SMEM)
    cut = D // parts
    shapes = {"down": (D, 128), "up": (128, D), "out": (cut, 128), "qkv": (128, 3 * cut)}
    outs = [jax.ShapeDtypeStruct((rows, D), low)]
    outs += [jax.ShapeDtypeStruct(shape, f32) for shape in (shapes["qkv"], shapes["out"], shapes["up"], shapes["down"])]
    outs += [jax.ShapeDtypeStruct((16, D), f32)]
    order = ("down", "up", "out", "qkv")
    buffers = [pltpu.VMEM((2, 2) + shapes[g], low) for g in order]
    buffers += [pltpu.VMEM((parts, 2) + shapes[g], low) for g in order]
    buffers += [pltpu.VMEM((parts, 2) + shapes[g], low) for g in order]
    buffers += [pltpu.VMEM((parts,) + shapes[g], low) for g in order]
    buffers += [pltpu.VMEM((parts - 1,) + shapes[g], low) for g in order]
    dma = pltpu.SemaphoreType.DMA
    return pl.pallas_call(
        functools.partial(back_kernel, rows, window, parts),
        out_shape=outs,
        in_specs=[smem, smem] + [vmem] * len(vmem_in) + [any_] * len(hbm_in),
        out_specs=[any_] + [vmem] * 5,
        scratch_shapes=[
            pltpu.VMEM((rows, D), f32),
            pltpu.VMEM((rows, D), f32),
            pltpu.VMEM((512, 2 * rows), low),
            pltpu.VMEM((2 * D, D), low),
            pltpu.VMEM((2 * rows, D), low),
            pltpu.VMEM((rows, D), low),
            pltpu.VMEM((window, 3 * cut), low),
            pltpu.VMEM((parts, 2 * rows, D), low),
            pltpu.VMEM((D, 3 * cut), low),
            pltpu.VMEM((2 * rows, 512), low),
            pltpu.VMEM((rows, 512), low),
            pltpu.VMEM((window, D), low),
            pltpu.VMEM((16, D), f32),
            pltpu.VMEM((5, 16, D), f32),
        ]
        + buffers
        + [
            dma((7,)),
            dma((4, parts, 3)),
            dma((4, parts, 3)),
            dma((2 * parts + 1,)),
            dma((2 * parts + 1,)),
            dma((2,)),
            dma((2,)),
            dma((5,)),
            dma((5,)),
        ],
        compiler_params=pltpu.CompilerParams(
            collective_id=1, has_side_effects=True, vmem_limit_bytes=60 * 2**20
        ),
    )(perm, back, *vmem_in, *hbm_in)


def unit_order(segs, window):
    units = window // UNIT
    unit_seg = segs[::UNIT]
    index = lax.iota(jnp.int32, units)
    counts = jnp.sum((unit_seg[:, None] == unit_seg[None, :]).astype(jnp.int32), axis=1)
    short = jnp.where((counts == LONG) & (unit_seg >= 0) & (unit_seg < 1000), 0, 1) * units + index
    back = jnp.sum((short[None, :] < short[:, None]).astype(jnp.int32), axis=1)
    perm = jnp.sum(jnp.where(back[None, :] == index[:, None], index[None, :], 0), axis=1)
    return perm.astype(jnp.int32), back.astype(jnp.int32)


def marks_of(segs):
    lane = lax.iota(jnp.int32, 2 * HD)
    seg = jnp.where(segs < 0, 2 * HD - 1, jnp.where(segs >= 1000, 2 * HD - 2, segs))
    same = seg[:, None] == lane[None, :]
    keys = jnp.where(same, 1.0, 0.0).astype(jnp.bfloat16)
    queries = jnp.where(same, 0.0, -8e30).astype(jnp.bfloat16)
    return keys, queries


def local_body(
    tokens,
    cotangent,
    timesteps,
    item_lengths,
    w_qkv,
    bias_qv,
    w_out,
    w_up,
    bias_up,
    w_down,
    vectors,
):
    rows = tokens.shape[0]
    parts = lax.axis_size("mp")
    z = lax.axis_index("mp")
    d = lax.axis_index("dp")
    core = lax.rem(d, 2)
    low = jnp.bfloat16
    f32 = jnp.float32
    cut = D // parts
    firsts, offsets, ends = window_plan(rows, parts)
    window = -(-max(ends) // UNIT) * UNIT
    win, f_qkv, f_out, f_up, f_down = gather(
        tokens, w_qkv.reshape(D, 3 * cut), w_out, w_up, w_down, window, parts
    )
    bias_qv_all = lax.all_gather(bias_qv, "mp", axis=1, tiled=True).astype(f32)
    bias_up_all = lax.all_gather(bias_up, "mp", axis=0, tiled=True).astype(f32)
    offset = pick(offsets, z)
    first_token = UNIT * pick(firsts, z)
    positions = first_token + lax.iota(jnp.int32, window)
    lengths_end = jnp.cumsum(item_lengths[0])
    segs = jnp.sum((positions[:, None] >= lengths_end[None, :]).astype(jnp.int32), axis=1)
    segs = jnp.where(positions < 0, -1, jnp.where(positions >= LEN, 1000, segs))
    plan = unit_plan(segs, z, offsets, rows, window)
    perm, back = unit_order(segs, window)
    kf, qf = marks_of(segs)
    step_time = timesteps[0].astype(f32) * 0.001

    lifted = tokens.astype(f32) + step_time * vectors[0] + vectors[1]
    lifted_low = lifted.astype(low)
    win_low = (win.astype(f32) + step_time * vectors[0] + vectors[1]).astype(low)
    bias3 = jnp.stack([bias_qv_all[0], jnp.zeros((D,), f32), bias_qv_all[1]])
    bias3 = jnp.transpose(bias3.reshape(3, parts, cut), (1, 0, 2)).reshape(parts, 1, 3 * cut)
    qkv = (jnp.einsum("td,zde->zte", win_low, f_qkv, preferred_element_type=f32) + bias3).astype(low)
    attended = attention_call(window, parts, plan, segs, qkv)
    attended = lax.dynamic_slice_in_dim(attended, offset, rows, 0)
    wo = f_out.reshape(D, D)
    mixed = jnp.dot(attended, wo, preferred_element_type=f32) + vectors[2]
    first, normed_one, inverse_one = norm_forward(lifted + mixed, vectors[4], vectors[5])
    first_low = first.astype(low)
    upper = jnp.concatenate(
        [jnp.dot(first_low, f_up[j], preferred_element_type=f32) for j in range(parts)], axis=1
    )
    upper = upper + bias_up_all
    chance = 0.5 * (1.0 + lax.erf(upper * (0.5**0.5)))
    activated = (upper * chance).astype(low)
    slope = (chance + upper * jnp.exp(-0.5 * upper * upper) * (0.5 / jnp.pi) ** 0.5).astype(low)
    wd = f_down.reshape(FF, D)
    down = jnp.dot(activated, wd, preferred_element_type=f32) + vectors[3]
    output, normed_two, inverse_two = norm_forward(first + down, vectors[6], vectors[7])
    out_grads = cotangent.astype(f32)
    second_grads, gain_two, shift_two = norm_backward(out_grads, normed_two, inverse_two, vectors[6])
    second_low = second_grads.astype(low)

    def arranged(value, c):
        return jnp.concatenate(
            [lax.dynamic_slice_in_dim(value, owner * 128, 128, 1) for owner in block_owners(d, c, True)], axis=1
        )

    def both(mine, sent):
        return jnp.concatenate([mine, swap(sent, "dp", 1)], axis=0)

    sec2 = both(arranged(second_low, core), arranged(second_low, 1 - core))
    first_t = both(arranged(first_low, core), arranged(first_low, 1 - core)).T
    lift_t = both(arranged(lifted_low, core), arranged(lifted_low, 1 - core)).T
    act2 = both(activated, activated)
    att2 = both(attended, attended)
    zero_row = jnp.zeros((D,), f32)
    small_in = jnp.stack(
        [zero_row] * 3
        + [jnp.sum(second_grads, axis=0), zero_row, zero_row, gain_two, shift_two]
        + [zero_row] * 7
        + [jnp.broadcast_to(step_time, (D,))]
    )
    input_grad, grad_qkv, grad_out, grad_up, grad_down, small = back_call(
        rows, window, parts, perm, back,
        (second_low, sec2, inverse_one, vectors[4:5], small_in, kf, qf),
        (first_t, lift_t, second_grads, normed_one, act2, slope, att2, qkv, f_qkv, f_out, f_up, f_down),
    )
    grad_bias_qv = lax.dynamic_slice_in_dim(small[8:10], z * cut, cut, 1)
    grad_bias_up = lax.dynamic_slice_in_dim(small[10:14].reshape(FF), z * (FF // parts), FF // parts, 0)
    return (
        output.astype(low),
        input_grad,
        grad_qkv.reshape(-1, 3, cut),
        grad_bias_qv,
        grad_out,
        grad_up,
        grad_bias_up,
        grad_down,
        small[:8],
    )


def solution(mesh):
    in_specs = (
        P(("dp", "mp"), None),
        P(("dp", "mp"), None),
        P("dp"),
        P("dp", None),
        P(None, None, "mp"),
        P(None, "mp"),
        P("mp", None),
        P(None, "mp"),
        P("mp"),
        P("mp", None),
        P(),
    )
    out_specs = (
        P(("dp", "mp"), None),
        P(("dp", "mp"), None),
        P("dp", None, "mp"),
        P(None, "mp"),
        P("mp", "dp"),
        P("dp", "mp"),
        P("mp"),
        P("mp", "dp"),
        P(),
    )
    chosen = local_body if fits_local(mesh) else body
    return jax.shard_map(chosen, mesh=mesh, in_specs=in_specs, out_specs=out_specs, check_vma=False)
```

```python
import functools
import heapq

import jax
import jax.numpy as jnp
from jax import lax
from jax.experimental import pallas as pl
from jax.experimental.pallas import tpu as pltpu
from jax.sharding import PartitionSpec as P

D = 1024
HD = 64
FF = 4096
LEN = 2368


def norm_forward(value, gain, shift):
    average = jnp.mean(value, axis=-1, keepdims=True)
    centred = value - average
    inverse = lax.rsqrt(jnp.mean(centred * centred, axis=-1, keepdims=True) + 1e-05)
    normed = centred * inverse
    return (normed * gain + shift, normed, inverse)


def norm_backward(grad, normed, inverse, gain):
    scaled = grad * gain
    result = inverse * (
        scaled
        - jnp.mean(scaled, axis=-1, keepdims=True)
        - normed * jnp.mean(scaled * normed, axis=-1, keepdims=True)
    )
    return (result, jnp.sum(grad * normed, axis=0), jnp.sum(grad, axis=0))


def gelu_exact(value):
    return jax.nn.gelu(value, approximate=False)


def attend_forward(queries, keys, values, segments):
    scale = HD ** (-0.5)
    block_rows = LEN // 4

    def one_block(inputs):
        query_block, segment_block = inputs
        scores = (
            jnp.einsum("bhe,khe->hbk", query_block, keys, preferred_element_type=jnp.float32)
            * scale
        )
        allowed = segment_block[:, None] == segments[None, :]
        scores = jnp.where(allowed[None], scores, -1e30)
        highest = jnp.max(scores, axis=-1, keepdims=True)
        weights = jnp.exp(scores - highest)
        totals = jnp.sum(weights, axis=-1, keepdims=True)
        chances_low = (weights / totals).astype(jnp.bfloat16)
        result = jnp.einsum("hbk,khe->bhe", chances_low, values, preferred_element_type=jnp.float32)
        return (result.astype(jnp.bfloat16), (highest + jnp.log(totals))[..., 0])

    blocks = queries.reshape(4, block_rows, queries.shape[1], queries.shape[2])
    results, logsums = lax.map(one_block, (blocks, segments.reshape(4, block_rows)))
    return (results.reshape(queries.shape), logsums)


def attend_backward(queries, keys, values, out_grads, logsums, segments):
    scale = HD ** (-0.5)
    block_rows = LEN // 4

    def one_block(carry, inputs):
        key_grads, value_grads = carry
        query_block, grad_block, logsum_block, segment_block = inputs
        scores = (
            jnp.einsum("bhe,khe->hbk", query_block, keys, preferred_element_type=jnp.float32)
            * scale
        )
        allowed = segment_block[:, None] == segments[None, :]
        scores = jnp.where(allowed[None], scores, -1e30)
        chances = jnp.exp(scores - logsum_block[..., None])
        chances_low = chances.astype(jnp.bfloat16)
        value_grads = value_grads + jnp.einsum(
            "hbk,bhe->khe", chances_low, grad_block, preferred_element_type=jnp.float32
        )
        flow = jnp.einsum("bhe,khe->hbk", grad_block, values, preferred_element_type=jnp.float32)
        inner = jnp.sum(chances * flow, axis=-1, keepdims=True)
        score_grads = (chances * (flow - inner)).astype(jnp.bfloat16)
        query_grads = (
            jnp.einsum("hbk,khe->bhe", score_grads, keys, preferred_element_type=jnp.float32)
            * scale
        )
        key_grads = (
            key_grads
            + jnp.einsum(
                "hbk,bhe->khe", score_grads, query_block, preferred_element_type=jnp.float32
            )
            * scale
        )
        return ((key_grads, value_grads), query_grads)

    shape_blocks = (4, block_rows, queries.shape[1], queries.shape[2])
    zeros = jnp.zeros(keys.shape, jnp.float32)
    (key_grads, value_grads), query_grads = lax.scan(
        one_block,
        (zeros, zeros),
        (
            queries.reshape(shape_blocks),
            out_grads.reshape(shape_blocks),
            logsums,
            segments.reshape(4, block_rows),
        ),
    )
    return (query_grads.reshape(queries.shape), key_grads, value_grads)


def body(
    tokens,
    cotangent,
    timesteps,
    item_lengths,
    w_qkv,
    bias_qv,
    w_out,
    w_up,
    bias_up,
    w_down,
    vectors,
):
    rows = tokens.shape[0]
    total = rows * lax.axis_size("mp")
    seq_count = timesteps.shape[0]
    local_width = w_qkv.shape[2]
    local_hidden = w_up.shape[1]
    local_heads = local_width // HD
    my_index = lax.axis_index("mp")
    row_ids = my_index * rows + lax.iota(jnp.int32, rows)
    row_owner = row_ids // LEN
    step_times = timesteps.astype(jnp.float32) * 0.001
    time_rows = jnp.sum(
        jnp.where(
            row_owner[:, None] == lax.iota(jnp.int32, seq_count)[None, :], step_times[None, :], 0.0
        ),
        axis=1,
    )
    ends = jnp.cumsum(item_lengths, axis=1)
    segments = jnp.sum(
        (lax.iota(jnp.int32, LEN)[None, :, None] >= ends[:, None, :]).astype(jnp.int32), axis=2
    )
    lifted = tokens.astype(jnp.float32) + time_rows[:, None] * vectors[0] + vectors[1]
    gathered = lax.all_gather(lifted.astype(jnp.bfloat16), "mp", axis=0, tiled=True)
    projected = jnp.einsum("td,dce->cte", gathered, w_qkv, preferred_element_type=jnp.float32)
    shaped = (seq_count, LEN, local_heads, HD)
    head_query = (projected[0] + bias_qv[0]).astype(jnp.bfloat16).reshape(shaped)
    head_key = projected[1].astype(jnp.bfloat16).reshape(shaped)
    head_value = (projected[2] + bias_qv[1]).astype(jnp.bfloat16).reshape(shaped)
    attended, logsums = lax.map(
        lambda items: attend_forward(*items), (head_query, head_key, head_value, segments)
    )
    attended = attended.reshape(total, local_width)
    piece = attended
    mixed = (
        lax.psum_scatter(
            jnp.dot(piece, w_out, preferred_element_type=jnp.float32),
            "mp",
            scatter_dimension=0,
            tiled=True,
        )
        + vectors[2]
    )
    first, normed_one, inverse_one = norm_forward(lifted + mixed, vectors[4], vectors[5])
    hidden_all = lax.all_gather(first.astype(jnp.bfloat16), "mp", axis=0, tiled=True)
    upper = jnp.dot(hidden_all, w_up, preferred_element_type=jnp.float32) + bias_up
    activated, gelu_pull = jax.vjp(gelu_exact, upper)
    activated = activated.astype(jnp.bfloat16)
    piece = activated
    down = (
        lax.psum_scatter(
            jnp.dot(piece, w_down, preferred_element_type=jnp.float32).astype(jnp.bfloat16),
            "mp",
            scatter_dimension=0,
            tiled=True,
        ).astype(jnp.float32)
        + vectors[3]
    )
    output, normed_two, inverse_two = norm_forward(first + down, vectors[6], vectors[7])
    out_grads = cotangent.astype(jnp.float32)
    second_grads, gain_two, shift_two = norm_backward(
        out_grads, normed_two, inverse_two, vectors[6]
    )
    down_all = lax.all_gather(second_grads.astype(jnp.bfloat16), "mp", axis=0, tiled=True)
    grad_down = jnp.einsum("tf,td->fd", activated, down_all, preferred_element_type=jnp.float32)
    act_grads = jnp.einsum("td,fd->tf", down_all, w_down, preferred_element_type=jnp.float32)
    (upper_grads,) = gelu_pull(act_grads)
    upper_low = upper_grads.astype(jnp.bfloat16)
    grad_bias_up = jnp.sum(upper_low, axis=0, dtype=jnp.float32)
    grad_up = jnp.einsum("td,tf->df", hidden_all, upper_low, preferred_element_type=jnp.float32)
    piece = upper_low
    first_part = lax.psum_scatter(
        jnp.einsum("tf,df->td", piece, w_up, preferred_element_type=jnp.float32).astype(
            jnp.bfloat16
        ),
        "mp",
        scatter_dimension=0,
        tiled=True,
    ).astype(jnp.float32)
    first_grads = second_grads + first_part
    mixed_grads, gain_one, shift_one = norm_backward(
        first_grads, normed_one, inverse_one, vectors[4]
    )
    mixed_all = lax.all_gather(mixed_grads.astype(jnp.bfloat16), "mp", axis=0, tiled=True)
    grad_out = jnp.einsum("te,td->ed", attended, mixed_all, preferred_element_type=jnp.float32)
    attended_grads = jnp.einsum(
        "td,ed->te", mixed_all, w_out, preferred_element_type=jnp.float32
    ).astype(jnp.bfloat16)
    query_grads, key_grads, value_grads = lax.map(
        lambda items: attend_backward(*items),
        (head_query, head_key, head_value, attended_grads.reshape(shaped), logsums, segments),
    )
    qkv_low = jnp.stack(
        [
            query_grads.reshape(total, local_width),
            key_grads.reshape(total, local_width),
            value_grads.reshape(total, local_width),
        ],
        axis=1,
    ).astype(jnp.bfloat16)
    grad_bias_qv = jnp.sum(qkv_low[:, 0::2], axis=0, dtype=jnp.float32)
    grad_qkv = jnp.einsum("td,tcf->dcf", gathered, qkv_low, preferred_element_type=jnp.float32)
    piece = qkv_low
    input_part = lax.psum_scatter(
        jnp.einsum("tcf,dcf->td", piece, w_qkv, preferred_element_type=jnp.float32).astype(
            jnp.bfloat16
        ),
        "mp",
        scatter_dimension=0,
        tiled=True,
    ).astype(jnp.float32)
    input_sum = mixed_grads + input_part
    vector_terms = jnp.stack(
        [
            jnp.sum(time_rows[:, None] * input_sum, axis=0),
            jnp.sum(input_sum, axis=0),
            jnp.sum(mixed_grads, axis=0),
            jnp.sum(second_grads, axis=0),
            gain_one,
            shift_one,
            gain_two,
            shift_two,
        ],
        axis=0,
    )
    zero_index = jnp.zeros((), jnp.int32)
    qv_start = my_index * local_width
    up_start = my_index * local_hidden
    qv_placed = lax.dynamic_update_slice(
        jnp.zeros((2, D), jnp.float32), grad_bias_qv, (zero_index, qv_start)
    )
    up_placed = lax.dynamic_update_slice(jnp.zeros((FF,), jnp.float32), grad_bias_up, (up_start,))
    grad_qkv, grad_out, grad_up, grad_down = (
        lax.psum_scatter(
            grad_qkv.astype(jnp.bfloat16), "dp", scatter_dimension=0, tiled=True
        ).astype(jnp.float32),
        lax.psum_scatter(
            grad_out.astype(jnp.bfloat16), "dp", scatter_dimension=1, tiled=True
        ).astype(jnp.float32),
        lax.psum_scatter(
            grad_up.astype(jnp.bfloat16), "dp", scatter_dimension=0, tiled=True
        ).astype(jnp.float32),
        lax.psum_scatter(
            grad_down.astype(jnp.bfloat16), "dp", scatter_dimension=1, tiled=True
        ).astype(jnp.float32),
    )
    grad_vectors, qv_summed, up_summed = lax.psum(
        (vector_terms, qv_placed, up_placed), ("dp", "mp")
    )
    grad_bias_qv = lax.dynamic_slice_in_dim(qv_summed, qv_start, local_width, 1)
    grad_bias_up = lax.dynamic_slice_in_dim(up_summed, up_start, local_hidden, 0)
    return (
        output.astype(jnp.bfloat16),
        input_sum.astype(jnp.bfloat16),
        grad_qkv,
        grad_bias_qv,
        grad_out,
        grad_up,
        grad_bias_up,
        grad_down,
        grad_vectors,
    )


UNIT = 128
LONG = 4
MESH = pl.DeviceIdType.MESH


def fits_local(mesh):
    parts = mesh.shape["mp"]
    return mesh.shape["dp"] == 8 and parts == 4 and LEN % (16 * parts) == 0


def window_plan(rows, parts):
    firsts = [(rows * j) // UNIT - (LONG - 1) for j in range(parts)]
    offsets = [rows * j - UNIT * first for j, first in enumerate(firsts)]
    ends = [
        ((rows * (j + 1) - 1) // UNIT + LONG - firsts[j]) * UNIT for j in range(parts)
    ]
    return firsts, offsets, ends


def pick(table, index):
    value = jnp.int32(table[0])
    for j in range(1, len(table)):
        value = jnp.where(index == j, jnp.int32(table[j]), value)
    return value


NT = (((1,), (1,)), ((), ()))
TN = (((0,), (0,)), ((), ()))
FIRST_OWN, LAST_OWN = LONG - 1, LONG + 4


def two_heads(block):
    lane = lax.broadcasted_iota(jnp.int32, block.shape, 1)
    zero = jnp.zeros_like(block)
    return jnp.concatenate(
        [jnp.where(lane < HD, block, zero), jnp.where(lane < HD, zero, block)], axis=0
    )


def from_two(flipped):
    both = jnp.concatenate([flipped[:HD, :UNIT], flipped[HD:, UNIT:]], axis=0)
    return both.T


class Clock:
    def __init__(self):
        self.now = 0.0
        self.free = {}
        self.queue = []
        self.count = 0

    def send(self, link, size, action, share=1.0):
        rate = {"c": 400e3, "x": 44e3, "y": 44e3, "z": 44e3}[link]
        begin = max(self.now, self.free.get(link, 0.0))
        end = begin + share * size / rate
        self.free[link] = end
        self.count += 1
        heapq.heappush(self.queue, (end + 1.5, self.count, action))

    def work(self, time):
        self.now += time
        while self.queue and self.queue[0][0] <= self.now:
            heapq.heappop(self.queue)[2]()

    def step(self):
        ready, _, action = heapq.heappop(self.queue)
        self.now = max(self.now, ready)
        action()

    def drain(self):
        while self.queue:
            self.step()


def block_owners(d, core, x_first):
    x, y = lax.rem(d // 2, 2), d // 4
    if x_first:
        return [4 * b + 2 * a + core for a in (1 - x, x) for b in (1 - y, y)]
    return [4 * b + 2 * a + core for b in (1 - y, y) for a in (1 - x, x)]


RING = (2, 3, 1, 0)
FORE = (0, 1, 3, 2)


def fore_kernel(
    rows, window, parts, perm, back, tokens, cotangent, w_qkv, w_out, w_up, w_down, biases, vectors, kf, qf,
    f_qkv, f_out, f_up, f_down, qkv, lse, att2, act2, slopes, first_t, lift_t, sec2, normed_out, second_low,
    second_grads, output, inverse, small,
    win, xq, yq, own_rows, attended, mixed, first, first_low, down, in_low, out_low, wu, wd, wq, wo, act, slope, lift2, first2,
    turned, stage, bias_all, send, recv, near, far, own, bias_send, bias_recv, local, pair_send, pair_recv,
):
    f32, low = jnp.float32, jnp.bfloat16
    d = lax.axis_index("dp")
    z = lax.axis_index("mp")
    core = lax.rem(d, 2)
    cut = D // parts
    three = 3 * cut
    pairs = cut // (2 * HD)
    firsts, offsets, ends = window_plan(rows, parts)
    offset = pl.multiple_of(pick(offsets, z), 16)
    shards = (w_qkv, w_out, w_up, w_down)
    fulls = (f_qkv, f_out, f_up, f_down)
    sizes = tuple(shard.shape[0] // 8 for shard in shards)
    partner = (d ^ 1, z)
    peers = [(d, z ^ k) for k in (1, 2, 3)] + [partner, (d ^ 2, z), (d ^ 4, z)]
    barrier = pltpu.get_barrier_semaphore()
    for peer in peers:
        pl.semaphore_signal(barrier, inc=1, device_id=peer, device_id_type=MESH)
    pl.semaphore_wait(barrier, len(peers))
    clock = Clock()

    others = (1, 3, 2)
    chunks = [(g, k) for k in others for g in (0, 1)] + [(g, k) for k in others for g in (2, 3)]
    index_of = {chunk: i for i, chunk in enumerate(chunks)}
    copies, done = {}, {}

    def part(ref, index, owner, size, half=None):
        start, count = owner * size, size
        if half is not None:
            count = size // 2
            start = start + half * count
        return ref.at[index, pl.ds(pl.multiple_of(start, 16), count), :]

    def remote(i, kind, src, dst, target):
        copy = pltpu.make_async_remote_copy(
            src, dst, send.at[i, kind], recv.at[i, kind], device_id=target, device_id_type=MESH
        )
        copy.start()
        copies[i, kind] = copy

    def place(i, owner, half=None):
        g, k = chunks[i]
        return part(fulls[g], z ^ k, owner, sizes[g], half)

    def bytes_of(i):
        g, k = chunks[i]
        return sizes[g] * shards[g].shape[1] * 2

    def pass_on(i, kind, owner, target, half=None):
        remote(i, kind, place(i, owner, half), place(i, owner, half), target)

    def hop_one(i):
        g, k = chunks[i]
        rows_at = pl.ds(pl.multiple_of(d * sizes[g], 16), sizes[g])
        remote(i, 0, shards[g].at[rows_at, :], part(fulls[g], z, d, sizes[g]), (d, z ^ k))
        clock.send("z", bytes_of(i), lambda: hop_two(i), 1.0 if k == 1 else 1.5)

    def hop_two(i):
        copies[i, 0].wait_recv()
        if i + 4 < len(chunks):
            hop_one(i + 4)
        pass_on(i, 1, d, (d ^ 2, z))
        pass_on(i, 2, d, (d ^ 4, z))
        pass_on(i, 5, d, partner)
        clock.send("c", bytes_of(i), lambda: None)
        clock.send("x", bytes_of(i), lambda: hop_three(i))
        clock.send("y", bytes_of(i), lambda: hop_four(i))

    def hop_three(i):
        copies[i, 1].wait_recv()
        pass_on(i, 3, d ^ 2, (d ^ 4, z), 0)
        pass_on(i, 6, d ^ 2, partner)
        clock.send("y", bytes_of(i) // 2, lambda: hop_five(i))

    def hop_four(i):
        copies[i, 2].wait_recv()
        pass_on(i, 4, d ^ 4, (d ^ 2, z), 1)
        pass_on(i, 7, d ^ 4, partner)
        clock.send("x", bytes_of(i) // 2, lambda: hop_six(i))

    def hop_five(i):
        copies[i, 3].wait_recv()
        pass_on(i, 8, d ^ 6, partner, 0)
        finish(i)

    def hop_six(i):
        copies[i, 4].wait_recv()
        pass_on(i, 9, d ^ 6, partner, 1)
        finish(i)

    def finish(i):
        done[i] = done.get(i, 0) + 1

    def arrive(i):
        while done.get(i, 0) < 2:
            clock.step()
        for kind in range(5, 10):
            copies[i, kind].wait_recv()

    for i in range(4):
        hop_one(i)

    halos = []
    for j in range(parts - 1):
        count = ends[j] - offsets[j] - rows
        halos.append((j + 1, j, pltpu.make_async_remote_copy(
            tokens.at[pl.ds(0, count), :], win.at[pl.ds(offsets[j] + rows, count), :],
            near.at[0], near.at[1], device_id=(d, j), device_id_type=MESH,
        )))
    for j in range(1, parts):
        halos.append((j - 1, j, pltpu.make_async_remote_copy(
            tokens.at[pl.ds(rows - offsets[j], offsets[j]), :], win.at[pl.ds(0, offsets[j]), :],
            far.at[0], far.at[1], device_id=(d, j), device_id_type=MESH,
        )))
    for sender, receiver, copy in halos:
        @pl.when(z == sender)
        def _(copy=copy):
            copy.start()
    bias_copies = []
    for k in (1, 2, 3):
        copy = pltpu.make_async_remote_copy(
            biases, bias_all.at[z], bias_send.at[k - 1], bias_recv.at[k - 1], device_id=(d, z ^ k), device_id_type=MESH
        )
        copy.start()
        bias_copies.append(copy)
    bias_all[pl.ds(z, 1)] = biases[...][None]
    owns = []
    for g in range(4):
        copy = pltpu.make_async_copy(shards[g], fulls[g].at[z], own.at[g])
        copy.start()
        owns.append(copy)

    def lift(value):
        return value.astype(f32) + vectors[8:9, :] + vectors[1:2, :]

    def own_body(i, c):
        at = pl.ds(pl.multiple_of(i * 16, 16), 16)
        win[pl.ds(pl.multiple_of(offset + i * 16, 16), 16), :] = lift(tokens[at, :]).astype(low)
        return c

    lax.fori_loop(0, rows // 16, own_body, 0)
    zero = jnp.zeros((16, D), low)

    def spans_of(j):
        end = ends[j] if j < parts - 1 else offsets[j] + rows
        empty = [(0, offsets[0])] if j == 0 else []
        if end < window:
            empty.append((end, window))
        filled = [(0, offsets[j])] if j else []
        if j < parts - 1:
            filled.append((offsets[j] + rows, ends[j]))
        return empty, filled

    for j in range(parts):
        @pl.when(z == j)
        def _(j=j):
            for begin, end in spans_of(j)[0]:
                def clear(i, c, begin=begin):
                    win[pl.ds(pl.multiple_of(begin + i * 16, 16), 16), :] = zero
                    return c
                lax.fori_loop(0, (end - begin) // 16, clear, 0)

    pair_copies = []

    def exchange(source, target):
        index = len(pair_copies)
        copy = pltpu.make_async_remote_copy(
            source, target, pair_send.at[index], pair_recv.at[index], device_id=partner, device_id_type=MESH
        )
        copy.start()
        pair_copies.append(copy)
        return copy

    def columns(read, c, write):
        for j, owner in enumerate(block_owners(d, c, True)):
            write(slice(j * 128, (j + 1) * 128), read(pl.ds(pl.multiple_of(owner * 128, 128), 128)))

    own_at = pl.ds(offset, rows)
    mine = pl.ds(0, rows)
    theirs = pl.ds(rows, rows)
    columns(lambda at: win[own_at, at], 1 - core, lambda at, v: stage.__setitem__((0, slice(None), at), v))
    lift_copy = exchange(stage.at[0], lift2.at[theirs, :])
    columns(lambda at: win[own_at, at], core, lambda at, v: lift2.__setitem__((mine, at), v))

    def fetch(index, source, target):
        copy = pltpu.make_async_copy(source, target, local.at[index])
        copy.start()
        return copy

    clock.work(4.0)
    for copy in bias_copies:
        copy.wait_recv()
    while clock.now < 30.0 and clock.queue:
        clock.step()
    for sender, receiver, copy in halos:
        @pl.when(z == receiver)
        def _(copy=copy):
            copy.wait_recv()
    for j in range(parts):
        @pl.when(z == j)
        def _(j=j):
            for begin, end in spans_of(j)[1]:
                def convert(i, c, begin=begin):
                    at = pl.ds(pl.multiple_of(begin + i * 16, 16), 16)
                    win[at, :] = lift(win[at, :]).astype(low)
                    return c
                lax.fori_loop(0, (end - begin) // 16, convert, 0)
    clock.work(2.0)
    lift_copy.wait_recv()
    turned[...] = lift2[...].T
    turned_out = fetch(0, turned, lift_t)
    clock.work(2.0)

    stores = {}
    for i in range(parts):
        k = FORE[i]
        at_z = z ^ k
        if k == 0:
            wq_ref, wo_ref = w_qkv, w_out
        else:
            arrive(index_of[0, k])
            arrive(index_of[1, k])
            load_q, load_o = fetch(1, f_qkv.at[at_z], wq), fetch(2, f_out.at[at_z], wo)
            wq_ref, wo_ref = wq, wo
            load_q.wait()
        slot_i = i % 2
        if i >= 2:
            stores[i - 2].wait()
        row = bias_all.at[at_z]

        def project(n, c):
            at = pl.ds(pl.multiple_of(n * 512, 512), 512)
            for c3 in range(3):
                lanes = slice(c3 * cut, (c3 + 1) * cut)
                value = jnp.dot(win[at, :], wq_ref[:, lanes], preferred_element_type=f32)
                value = (value + row[1:2, lanes]).astype(low)
                if c3 == 0:
                    value = value * jnp.array(HD ** (-0.5), low)
                xq[slot_i, at, lanes] = value
            return c

        lax.fori_loop(0, window // 512, project, 0)
        stores[i] = fetch(3 + slot_i, xq.at[slot_i], qkv.at[at_z])
        clock.work(4.0)

        def attend(step, c):
            p, slot = step // 3, lax.rem(step, 3)
            lanes = lambda base: pl.ds(pl.multiple_of(base + p * 2 * HD, 2 * HD), 2 * HD)
            unit_at = [pl.ds(perm[slot * LONG + m] * UNIT, UNIT) for m in range(LONG)]
            keys = jnp.concatenate([xq[slot_i, at, lanes(cut)] for at in unit_at], axis=0)
            values = jnp.concatenate([xq[slot_i, at, lanes(2 * cut)] for at in unit_at], axis=0)
            marks = jnp.concatenate([kf[at, :] for at in unit_at], axis=0)
            wide_keys = jnp.concatenate([keys, marks], axis=1)
            for m in range(LONG):
                pair = two_heads(xq[slot_i, unit_at[m], lanes(0)])
                mark = qf[unit_at[m], :]
                wide_pair = jnp.concatenate([pair, jnp.concatenate([mark, mark], axis=0)], axis=1)
                scores = lax.dot_general(wide_keys, wide_pair, NT, preferred_element_type=f32)
                highest = jnp.max(scores, axis=0, keepdims=True)
                weights = jnp.exp(scores - highest)
                total = jnp.sum(weights, axis=0, keepdims=True)
                chances = (weights * (1.0 / total)).astype(low)
                flipped = lax.dot_general(values, chances, TN, preferred_element_type=f32)
                at = pl.ds(pl.multiple_of(slot * LONG * UNIT + m * UNIT, UNIT), UNIT)
                yq[at, lanes(0)] = from_two(flipped).astype(low)
                lse[at_z, pl.ds(step * LONG + m, 1), :] = highest + jnp.log(total)
            return c

        lax.fori_loop(0, pairs * 3, attend, 0)
        clock.work(9.0)
        for u in range(FIRST_OWN, LAST_OWN + 1):
            own_rows[pl.ds((u - FIRST_OWN) * UNIT, UNIT), :] = yq[pl.ds(back[u] * UNIT, UNIT), :]
        lanes_z = pl.ds(pl.multiple_of(at_z * cut, cut), cut)
        attended[i] = own_rows[pl.ds(pl.multiple_of(offset - FIRST_OWN * UNIT, 16), rows), :]
        exchange(attended.at[i], att2.at[theirs, lanes_z])
        stores["a", i] = fetch(5 + i, attended.at[i], att2.at[mine, lanes_z])
        if k:
            load_o.wait()

        def out_body(n, c):
            at = pl.ds(pl.multiple_of(n * 256, 256), 256)
            value = jnp.dot(attended[i], wo_ref[:, at], preferred_element_type=f32)
            if i == 0:
                mixed[:, at] = value
            else:
                mixed[:, at] += value
            return c

        lax.fori_loop(0, D // 256, out_body, 0)
        clock.work(1.0)

    def norm_one(i, c):
        at = pl.ds(pl.multiple_of(i * 16, 16), 16)
        value = lift(tokens[at, :]) + (mixed[at, :] + vectors[2:3, :])
        centred = value - jnp.mean(value, axis=-1, keepdims=True)
        scale = lax.rsqrt(jnp.mean(centred * centred, axis=-1, keepdims=True) + 1e-05)
        normed = centred * scale
        mixed[at, :] = normed
        inverse[at, :] = scale
        result = normed * vectors[4:5, :] + vectors[5:6, :]
        first[at, :] = result
        first_low[at, :] = result.astype(low)
        return c

    lax.fori_loop(0, rows // 16, norm_one, 0)
    normed_store = fetch(9, mixed, normed_out)
    columns(lambda at: first_low[:, at], 1 - core, lambda at, v: stage.__setitem__((1, slice(None), at), v))
    first_copy = exchange(stage.at[1], first2.at[theirs, :])
    columns(lambda at: first_low[:, at], core, lambda at, v: first2.__setitem__((mine, at), v))
    clock.work(4.0)

    for i in range(parts):
        k = FORE[i]
        at_z = z ^ k
        slot_i = i % 2
        if k == 0:
            up_ref, down_ref = w_up, w_down
        else:
            arrive(index_of[2, k])
            load_u = fetch(1, f_up.at[at_z], wu)
            arrive(index_of[3, k])
            load_d = fetch(2, f_down.at[at_z], wd)
            up_ref, down_ref = wu, wd
            load_u.wait()
        if i >= 2:
            for copy in stores["f", i - 2]:
                copy.wait()
            stores["r", i - 2].wait_send()
        row = bias_all.at[at_z]

        def upper_body(n, c):
            at = pl.ds(pl.multiple_of(n * 256, 256), 256)
            value = jnp.dot(first_low[...], up_ref[:, at], preferred_element_type=f32) + row[0:1, at]
            chance = 0.5 + 0.5 * lax.erf(value * (0.5**0.5))
            act[slot_i, :, at] = (value * chance).astype(low)
            density = jnp.exp(-0.5 * value * value) * (0.5 / jnp.pi) ** 0.5
            slope[slot_i, :, at] = (chance + value * density).astype(low)
            return c

        lax.fori_loop(0, D // 256, upper_body, 0)
        hidden = pl.ds(pl.multiple_of(at_z * D, D), D)
        stores["r", i] = exchange(act.at[slot_i], act2.at[theirs, hidden])
        stores["f", i] = (
            fetch(14 + slot_i, act.at[slot_i], act2.at[mine, hidden]),
            fetch(10 + slot_i, slope.at[slot_i], slopes.at[:, hidden]),
        )
        clock.work(4.0)
        if k:
            load_d.wait()

        def down_body(n, c):
            at = pl.ds(pl.multiple_of(n * 256, 256), 256)
            value = jnp.dot(act[slot_i], down_ref[:, at], preferred_element_type=f32)
            if i == 0:
                down[:, at] = value
            else:
                down[:, at] += value
            return c

        lax.fori_loop(0, D // 256, down_body, 0)
        clock.work(2.0)
        if i == 0:
            first_copy.wait_recv()
            turned_out.wait()
            turned[...] = first2[...].T
            turned_out = fetch(0, turned, first_t)
            clock.work(2.0)

    zero_row = jnp.zeros((16, D), f32)

    def norm_two(i, sums):
        at = pl.ds(pl.multiple_of(i * 16, 16), 16)
        value = first[at, :] + (down[at, :] + vectors[3:4, :])
        centred = value - jnp.mean(value, axis=-1, keepdims=True)
        scale = lax.rsqrt(jnp.mean(centred * centred, axis=-1, keepdims=True) + 1e-05)
        normed = centred * scale
        out_low[at, :] = (normed * vectors[6:7, :] + vectors[7:8, :]).astype(low)
        grads = cotangent[at, :].astype(f32)
        scaled = grads * vectors[6:7, :]
        result = scale * (
            scaled
            - jnp.mean(scaled, axis=-1, keepdims=True)
            - normed * jnp.mean(scaled * normed, axis=-1, keepdims=True)
        )
        down[at, :] = result
        in_low[at, :] = result.astype(low)
        return (sums[0] + result, sums[1] + grads * normed, sums[2] + grads)

    sums = lax.fori_loop(0, rows // 16, norm_two, (zero_row, zero_row, zero_row))
    last = [fetch(1, out_low, output), fetch(2, in_low, second_low), fetch(12, down, second_grads)]
    small[...] = jnp.zeros_like(small)
    small[3:4, :] = jnp.sum(sums[0], axis=0, keepdims=True)
    small[6:7, :] = jnp.sum(sums[1], axis=0, keepdims=True)
    small[7:8, :] = jnp.sum(sums[2], axis=0, keepdims=True)
    small[15:16, :] = vectors[9:10, :]
    columns(lambda at: in_low[:, at], 1 - core, lambda at, v: stage.__setitem__((2, slice(None), at), v))
    exchange(stage.at[2], sec2.at[theirs, :])
    columns(lambda at: in_low[:, at], core, lambda at, v: stage.__setitem__((3, slice(None), at), v))
    last.append(fetch(13, stage.at[3], sec2.at[mine, :]))
    clock.drain()
    for copy in last + owns + [turned_out, normed_store, stores[2], stores[3]]:
        copy.wait()
    for i in range(parts):
        stores["a", i].wait()
        if i >= 2:
            for copy in stores["f", i]:
                copy.wait()
    waited = [stores["r", 0], stores["r", 1]]
    for copy in pair_copies:
        if not any(copy is other for other in waited):
            copy.wait_send()
        if copy is not lift_copy and copy is not first_copy:
            copy.wait_recv()
    for copy in copies.values():
        copy.wait_send()
    for copy in bias_copies:
        copy.wait_send()
    for sender, receiver, copy in halos:
        @pl.when(z == sender)
        def _(copy=copy):
            copy.wait_send()


def fore_call(rows, window, parts, perm, back, *arrays):
    f32, low = jnp.float32, jnp.bfloat16
    any_ = pl.BlockSpec(memory_space=pl.ANY)
    vmem = pl.BlockSpec(memory_space=pltpu.VMEM)
    smem = pl.BlockSpec(memory_space=pltpu.SMEM)
    cut = D // parts
    three = 3 * cut
    shape = jax.ShapeDtypeStruct
    marks = cut // (2 * HD) * 3 * LONG
    dma = pltpu.SemaphoreType.DMA
    return pl.pallas_call(
        functools.partial(fore_kernel, rows, window, parts),
        out_shape=[
            shape((parts, D, three), low),
            shape((parts, cut, D), low),
            shape((parts, D, D), low),
            shape((parts, D, D), low),
            shape((parts, window, three), low),
            shape((parts, marks, 2 * UNIT), f32),
            shape((2 * rows, D), low),
            shape((2 * rows, FF), low),
            shape((rows, FF), low),
            shape((512, 2 * rows), low),
            shape((512, 2 * rows), low),
            shape((2 * rows, 512), low),
            shape((rows, D), f32),
            shape((rows, D), low),
            shape((rows, D), f32),
            shape((rows, D), low),
            shape((rows, 1), f32),
            shape((16, D), f32),
        ],
        in_specs=[smem, smem] + [vmem] * len(arrays),
        out_specs=[any_] * 5 + [vmem] + [any_] * 10 + [vmem] * 2,
        scratch_shapes=[
            pltpu.VMEM((window, D), low),
            pltpu.VMEM((2, window, three), low),
            pltpu.VMEM((window, cut), low),
            pltpu.VMEM(((LAST_OWN + 1 - FIRST_OWN) * UNIT, cut), low),
            pltpu.VMEM((parts, rows, cut), low),
            pltpu.VMEM((rows, D), f32),
            pltpu.VMEM((rows, D), f32),
            pltpu.VMEM((rows, D), low),
            pltpu.VMEM((rows, D), f32),
            pltpu.VMEM((rows, D), low),
            pltpu.VMEM((rows, D), low),
            pltpu.VMEM((D, D), low),
            pltpu.VMEM((D, D), low),
            pltpu.VMEM((D, three), low),
            pltpu.VMEM((cut, D), low),
            pltpu.VMEM((2, rows, D), low),
            pltpu.VMEM((2, rows, D), low),
            pltpu.VMEM((2 * rows, 512), low),
            pltpu.VMEM((2 * rows, 512), low),
            pltpu.VMEM((512, 2 * rows), low),
            pltpu.VMEM((4, rows, 512), low),
            pltpu.VMEM((parts, 8, D), f32),
            dma((12, 10)),
            dma((12, 10)),
            dma((2,)),
            dma((2,)),
            dma((4,)),
            dma((3,)),
            dma((3,)),
            dma((16,)),
            dma((2 * parts + 3,)),
            dma((2 * parts + 3,)),
        ],
        compiler_params=pltpu.CompilerParams(
            collective_id=0, has_side_effects=True, vmem_limit_bytes=56 * 2**20
        ),
    )(perm, back, *arrays)


def back_kernel(
    rows, window, parts, perm, back, sec_low, sec2, inverse, gain, small_in, kf, qf, lse,
    first_t, lift_t, second_grads, normed_one, act2, dgelu, att2, qkv, f_qkv, f_out, f_up, f_down,
    input_grad, g_qkv, g_out, g_up, g_down, small_out,
    acc, normed, turned, arena, act, slope, y, up2, w_in, mixed2, stage, mixed_win, small, small_in_far,
    s_down, s_up, s_out, s_qkv, k_down, k_up, k_out, k_qkv,
    r_down, r_up, r_out, r_qkv, t_down, t_up, t_out, t_qkv, z_down, z_up, z_out, z_qkv,
    local, hop_send, hop_recv, pair_send, pair_recv, halo_send, halo_recv, small_send, small_recv,
):
    f32, low = jnp.float32, jnp.bfloat16
    d = lax.axis_index("dp")
    z = lax.axis_index("mp")
    core = lax.rem(d, 2)
    firsts, offsets, ends = window_plan(rows, parts)
    offset = pl.multiple_of(pick(offsets, z), 16)
    partner = (d ^ 1, z)
    peers = [(d, z ^ k) for k in (1, 2, 3)] + [partner, (d ^ 2, z), (d ^ 4, z)]
    barrier = pltpu.get_barrier_semaphore()
    for peer in peers:
        pl.semaphore_signal(barrier, inc=1, device_id=peer, device_id_type=MESH)
    pl.semaphore_wait(barrier, len(peers))
    clock = Clock()
    tail = []

    wide = 2 * rows
    wd = arena.at[pl.ds(0, D), :]
    wu = arena.at[pl.ds(D, D), :]

    def fetch(index, source, target):
        copy = pltpu.make_async_copy(source, target, local.at[index])
        copy.start()
        return copy

    chunk = lambda k: z ^ k
    hidden = lambda k: pl.ds(pl.multiple_of(chunk(k) * D, D), D)
    load_wd = lambda i: fetch(0, f_down.at[chunk(RING[i])], wd)
    load_wu = lambda i: fetch(1, f_up.at[chunk(RING[i])], wu)
    load_act = lambda i: fetch(2, act2.at[:, hidden(RING[i])], act)
    load_slope = lambda i: fetch(3, dgelu.at[:, hidden(RING[i])], slope)
    at_wd, at_slope, at_act, at_wu = load_wd(0), load_slope(0), load_act(0), load_wu(0)
    at_acc = fetch(4, second_grads, acc)
    at_normed = fetch(5, normed_one, normed)
    at_turned = fetch(6, first_t, turned)

    zero = jnp.zeros((16, D), low)
    for j in range(parts):
        spans = []
        if j == 0:
            spans.append((0, offsets[0]))
        begin = ends[j] if j < parts - 1 else offsets[j] + rows
        if begin < window:
            spans.append((begin, window))
        if spans:
            @pl.when(z == j)
            def _(spans=spans):
                for begin, end in spans:
                    def clear(i, c):
                        mixed_win[pl.ds(pl.multiple_of(begin + i * 16, 16), 16), :] = zero
                        return c
                    lax.fori_loop(0, (end - begin) // 16, clear, 0)

    groups = {
        "down": (s_down, k_down, r_down, t_down, z_down, g_down, 0),
        "up": (s_up, k_up, r_up, t_up, z_up, g_up, 1),
        "out": (s_out, k_out, r_out, t_out, z_out, g_out, 2),
        "qkv": (s_qkv, k_qkv, r_qkv, t_qkv, z_qkv, g_qkv, 3),
    }
    hops = {}

    def x_ahead(g, i):
        return (i + groups[g][6]) % 2 == 0

    def put(g, i, j, at, value):
        if not x_ahead(g, i):
            j = (0, 2, 1, 3)[j]
        if j < 2:
            groups[g][0][(i % 2, j) + at] = value
        else:
            groups[g][1][(i, j - 2) + at] = value

    def hop(g, i, kind, source, target, device):
        index = groups[g][6]
        copy = pltpu.make_async_remote_copy(
            source, target, hop_send.at[index, i, kind], hop_recv.at[index, i, kind],
            device_id=device, device_id_type=MESH,
        )
        copy.start()
        hops[g, i, kind] = copy

    def add_into(ref, other):
        count = ref.shape[0]
        step = min(count, 64)

        def body(j, c):
            at = pl.ds(pl.multiple_of(j * step, step), step)
            ref[at, :] = (ref[at, :].astype(f32) + other[at, :].astype(f32)).astype(low)
            return c

        lax.fori_loop(0, count // step, body, 0)

    def launch(g, i):
        s, kept, r, t, zb, out, index = groups[g]
        x_first = x_ahead(g, i)
        n1, n2 = ((d ^ 2, z), (d ^ 4, z)) if x_first else ((d ^ 4, z), (d ^ 2, z))
        l1, l2 = ("x", "y") if x_first else ("y", "x")
        block = s.shape[2] * s.shape[3] * 2
        k = RING[i]
        hop(g, i, 0, s.at[i % 2], r.at[i], n1)

        def second():
            hops[g, i, 0].wait_recv()
            add_into(kept.at[i, 0], r.at[i, 0])
            hop(g, i, 1, kept.at[i, 0], t.at[i], n2)
            clock.send(l2, block, third)
            add_into(kept.at[i, 1], r.at[i, 1])

        def third():
            hops[g, i, 1].wait_recv()
            add_into(kept.at[i, 1], t.at[i])
            if k:
                hop(g, i, 2, kept.at[i, 1], zb.at[k - 1], (d, z ^ k))
                clock.send("z", block, fourth, 1.0 if k == 1 else 2.0)

        def fourth():
            hops[g, i, 2].wait_recv()

        clock.send(l1, 2 * block, second)

    def free_slot(g, i):
        if i >= 2:
            hops[g, i - 2, 0].wait_send()

    def finish(g):
        s, kept, r, t, zb, out, index = groups[g]
        own = RING.index(0)
        count = s.shape[2]
        step = min(count, 64)
        pieces = kept.at[own, 1]

        def body(j, c):
            at = pl.ds(pl.multiple_of(j * step, step), step)
            total = pieces[at, :].astype(f32)
            for k in range(parts - 1):
                total = total + zb[k, at, :].astype(f32)
            out[at, :] = total
            return c

        lax.fori_loop(0, count // step, body, 0)

    def exchange(index, source, target):
        copy = pltpu.make_async_remote_copy(
            source, target, pair_send.at[index], pair_recv.at[index], device_id=partner, device_id_type=MESH
        )
        copy.start()
        return copy

    small[...] = small_in[...]

    pending = {}

    def grad_up_chunk(i):
        pending.pop(i).wait_recv()
        if i == 0:
            at_turned.wait()
        free_slot("up", i)

        def body(n, c):
            at = pl.ds(pl.multiple_of(n * 256, 256), 256)
            tile = jnp.dot(turned[...], up2[i, :, at], preferred_element_type=f32).astype(low)
            for j in range(4):
                put("up", i, j, (slice(None), at), tile[j * 128 : (j + 1) * 128])
            return c

        lax.fori_loop(0, 4, body, 0)
        launch("up", i)
        clock.work(2.0)

    exchanges = []
    loads = {"wd": at_wd, "wu": at_wu, "slope": at_slope, "act": at_act}

    def upper_chunk(i):
        loads["wd"].wait()
        loads["slope"].wait()
        bias_row = chunk(RING[i])

        def body(n, c):
            at = pl.ds(pl.multiple_of(n * 256, 256), 256)
            grads = lax.dot_general(sec_low[...], wd[at, :], NT, preferred_element_type=f32)
            value = (grads * slope[:, at].astype(f32)).astype(low)
            up2[i, pl.ds(0, rows), at] = value
            small[pl.ds(10 + bias_row, 1), at] = jnp.sum(value.astype(f32), axis=0, keepdims=True)
            return c

        lax.fori_loop(0, 4, body, 0)
        pending[i] = exchange(i, up2.at[i, pl.ds(0, rows), :], up2.at[i, pl.ds(rows, rows), :])
        exchanges.append(pending[i])
        clock.work(2.5)
        if i + 1 < parts:
            loads["wd"], loads["slope"] = load_wd(i + 1), load_slope(i + 1)

    def grad_down_chunk(i):
        loads["act"].wait()
        free_slot("down", i)

        def body(n, c):
            at = pl.ds(pl.multiple_of(n * 256, 256), 256)
            tile = lax.dot_general(act[:, at], sec2[...], TN, preferred_element_type=f32).astype(low)
            for j in range(4):
                put("down", i, j, (at, slice(None)), tile[:, j * 128 : (j + 1) * 128])
            return c

        lax.fori_loop(0, 4, body, 0)
        launch("down", i)
        clock.work(2.0)
        if i + 1 < parts:
            loads["act"] = load_act(i + 1)

    def first_chunk(i):
        loads["wu"].wait()
        if i == 0:
            at_acc.wait()

        def body(n, c):
            at = pl.ds(pl.multiple_of(n * 256, 256), 256)
            acc[:, at] += lax.dot_general(
                up2[i, pl.ds(0, rows), :], wu[at, :], NT, preferred_element_type=f32
            )
            return c

        lax.fori_loop(0, 4, body, 0)
        clock.work(2.0)
        if i + 1 < parts:
            loads["wu"] = load_wu(i + 1)

    grad_down_chunk(0)
    for i in range(parts):
        upper_chunk(i)
        first_chunk(i)
        if i == 1:
            grad_down_chunk(1)

    at_normed.wait()
    zero_row = jnp.zeros((16, D), f32)

    def norm_body(i, sums):
        at = pl.ds(pl.multiple_of(i * 16, 16), 16)
        grads, unit = acc[at, :], normed[at, :]
        scaled = grads * gain[0:1, :]
        result = inverse[at, :] * (
            scaled
            - jnp.mean(scaled, axis=-1, keepdims=True)
            - unit * jnp.mean(scaled * unit, axis=-1, keepdims=True)
        )
        acc[at, :] = result
        mixed_win[pl.ds(pl.multiple_of(offset + i * 16, 16), 16), :] = result.astype(low)
        return (sums[0] + grads * unit, sums[1] + grads, sums[2] + result)

    sums = lax.fori_loop(0, rows // 16, norm_body, (zero_row, zero_row, zero_row))
    small[4:5, :] = jnp.sum(sums[0], axis=0, keepdims=True)
    small[5:6, :] = jnp.sum(sums[1], axis=0, keepdims=True)
    small[2:3, :] = jnp.sum(sums[2], axis=0, keepdims=True)
    halos = []
    for j in range(parts - 1):
        count = ends[j] - offsets[j] - rows
        halos.append((j + 1, j, pltpu.make_async_remote_copy(
            mixed_win.at[pl.ds(offsets[j + 1], count), :],
            mixed_win.at[pl.ds(offsets[j] + rows, count), :],
            halo_send.at[0], halo_recv.at[0], device_id=(d, j), device_id_type=MESH,
        )))
    for j in range(1, parts):
        halos.append((j - 1, j, pltpu.make_async_remote_copy(
            mixed_win.at[pl.ds(offsets[j - 1] + rows - offsets[j], offsets[j]), :],
            mixed_win.at[pl.ds(0, offsets[j]), :],
            halo_send.at[1], halo_recv.at[1], device_id=(d, j), device_id_type=MESH,
        )))
    for sender, receiver, copy in halos:
        @pl.when(z == sender)
        def _(copy=copy):
            copy.start()
    clock.work(4.0)
    for i in range(parts):
        grad_up_chunk(i)
        if i + 2 < parts:
            grad_down_chunk(i + 2)
    own_at = pl.ds(offset, rows)
    for j, owner in enumerate(block_owners(d, 1 - core, True)):
        stage[:, j * 128 : (j + 1) * 128] = mixed_win[own_at, pl.ds(pl.multiple_of(owner * 128, 128), 128)]
    exchanges.append(exchange(parts, stage, mixed2.at[pl.ds(rows, rows), :]))
    for j, owner in enumerate(block_owners(d, core, True)):
        mixed2[pl.ds(0, rows), j * 128 : (j + 1) * 128] = mixed_win[
            own_at, pl.ds(pl.multiple_of(owner * 128, 128), 128)
        ]
    clock.work(4.0)

    cut = D // parts
    three = 3 * cut
    pairs = cut // (2 * HD)
    x = arena
    wo = slope.at[pl.ds(0, cut), :]
    load_x = lambda i: fetch(0, qkv.at[chunk(RING[i])], arena.at[pl.ds(0, window), pl.ds(0, three)])
    load_wo = lambda i: fetch(1, f_out.at[chunk(RING[i])], wo)
    load_att = lambda i: fetch(
        2, att2.at[:, pl.ds(pl.multiple_of(chunk(RING[i]) * cut, cut), cut)], act.at[:, pl.ds(0, cut)]
    )
    load_wi = lambda i: fetch(3, f_qkv.at[chunk(RING[i])], w_in)
    at_turned = fetch(6, lift_t, turned)
    at_x, at_wo, at_att, at_wi = load_x(0), load_wo(0), load_att(0), load_wi(0)
    exchanges[-1].wait_recv()
    scale = HD ** (-0.5)

    def take_halo():
        for sender, receiver, copy in halos:
            @pl.when(z == receiver)
            def _(copy=copy):
                copy.wait_recv()

    def grad_qkv_chunk(i):
        pending.pop(i).wait_recv()
        if i == 0:
            at_turned.wait()
        free_slot("qkv", i)

        def body(n, c):
            at = pl.ds(pl.multiple_of(n * 256, 256), 256)
            tile = jnp.dot(turned[...], up2[i, :, at], preferred_element_type=f32).astype(low)
            for j in range(4):
                put("qkv", i, j, (slice(None), at), tile[j * 128 : (j + 1) * 128])
            return c

        lax.fori_loop(0, three // 256, body, 0)
        launch("qkv", i)
        clock.work(1.8)

    for i in range(parts):
        at_att.wait()
        free_slot("out", i)
        tile = lax.dot_general(act[:, 0:cut], mixed2[...], TN, preferred_element_type=f32).astype(low)
        for j in range(4):
            put("out", i, j, (slice(None), slice(None)), tile[:, j * 128 : (j + 1) * 128])
        launch("out", i)
        clock.work(0.8)
        if i == 0:
            take_halo()
        at_wo.wait()
        at_x.wait()

        def flow_body(n, c):
            at = pl.ds(pl.multiple_of(n * 512, 512), 512)
            x[at, three : three + cut] = lax.dot_general(
                mixed_win[at, :], wo[...], NT, preferred_element_type=f32
            ).astype(low)
            return c

        lax.fori_loop(0, window // 512, flow_body, 0)
        clock.work(1.2)
        if i + 1 < parts:
            at_wo, at_att = load_wo(i + 1), load_att(i + 1)

        def attend_body(step, c):
            p, slot = step // 3, lax.rem(step, 3)
            lanes = lambda base: pl.ds(pl.multiple_of(base + p * 2 * HD, 2 * HD), 2 * HD)
            unit_at = [
                pl.ds(perm[slot * LONG + m] * UNIT, UNIT) for m in range(LONG)
            ]
            keys = jnp.concatenate([x[at, lanes(cut)] for at in unit_at], axis=0)
            values = jnp.concatenate([x[at, lanes(2 * cut)] for at in unit_at], axis=0)
            marks = jnp.concatenate([kf[at, :] for at in unit_at], axis=0)
            wide_keys = jnp.concatenate([keys, marks], axis=1)
            k_sum = jnp.zeros((LONG * UNIT, 2 * HD), f32)
            v_sum = jnp.zeros((LONG * UNIT, 2 * HD), f32)
            for m in range(LONG):
                pair = two_heads(x[unit_at[m], lanes(0)])
                grads = two_heads(x[unit_at[m], lanes(three)])
                mark = qf[unit_at[m], :]
                wide_pair = jnp.concatenate([pair, jnp.concatenate([mark, mark], axis=0)], axis=1)
                scores = lax.dot_general(wide_keys, wide_pair, NT, preferred_element_type=f32)
                chances = jnp.exp(scores - lse[chunk(RING[i]), pl.ds(step * LONG + m, 1), :])
                flow = lax.dot_general(values, grads, NT, preferred_element_type=f32)
                inner = jnp.sum(chances * flow, axis=0, keepdims=True)
                slopes = (chances * (flow - inner)).astype(low)
                v_sum = v_sum + jnp.dot(chances.astype(low), grads, preferred_element_type=f32)
                k_sum = k_sum + jnp.dot(slopes, pair, preferred_element_type=f32)
                flipped = lax.dot_general(keys, slopes, TN, preferred_element_type=f32)
                at = pl.ds(pl.multiple_of(slot * LONG * UNIT + m * UNIT, UNIT), UNIT)
                y[at, lanes(0)] = (from_two(flipped) * scale).astype(low)
            at = pl.ds(pl.multiple_of(slot * LONG * UNIT, UNIT), LONG * UNIT)
            y[at, lanes(cut)] = k_sum.astype(low)
            y[at, lanes(2 * cut)] = v_sum.astype(low)
            return c

        lax.fori_loop(0, pairs * 3, attend_body, 0)
        clock.work(9.0)
        if i + 1 < parts:
            at_x = load_x(i + 1)
        for u in range(FIRST_OWN, LAST_OWN + 1):
            at = pl.ds(back[u] * UNIT, UNIT)
            act[pl.ds((u - FIRST_OWN) * UNIT, UNIT), cut:] = y[at, :]
        exchanges[i].wait_send()
        inner_at = pl.ds(pl.multiple_of(offset - FIRST_OWN * UNIT, 16), rows)
        up2[i, pl.ds(0, rows), 0:three] = act[inner_at, cut:]
        pending[i] = exchange(
            parts + 1 + i, up2.at[i, pl.ds(0, rows), pl.ds(0, three)], up2.at[i, pl.ds(rows, rows), pl.ds(0, three)]
        )
        exchanges.append(pending[i])
        place = pl.multiple_of(chunk(RING[i]) * cut, cut)
        small[8:9, pl.ds(place, cut)] = jnp.sum(up2[i, pl.ds(0, rows), 0:cut].astype(f32), axis=0, keepdims=True)
        small[9:10, pl.ds(place, cut)] = jnp.sum(
            up2[i, pl.ds(0, rows), 2 * cut : three].astype(f32), axis=0, keepdims=True
        )
        at_wi.wait()

        def input_body(n, c, i=i):
            at = pl.ds(pl.multiple_of(n * 256, 256), 256)
            acc[:, at] += lax.dot_general(
                up2[i, pl.ds(0, rows), 0:three], w_in[at, :], NT, preferred_element_type=f32
            )
            return c

        lax.fori_loop(0, 4, input_body, 0)
        clock.work(2.0)
        if i + 1 < parts:
            at_wi = load_wi(i + 1)
        grad_qkv_chunk(i)

    def last_body(i, total):
        at = pl.ds(pl.multiple_of(i * 16, 16), 16)
        value = acc[at, :]
        arena[at, :] = value.astype(low)
        return total + value

    total = jnp.sum(lax.fori_loop(0, rows // 16, last_body, zero_row), axis=0, keepdims=True)
    store = fetch(4, arena.at[pl.ds(0, rows), :], input_grad)
    small[0:1, :] = total * small_in[15:16, :]
    small[1:2, :] = total
    clock.work(2.0)
    small_copies = []

    def small_step(n):
        copy = pltpu.make_async_remote_copy(
            small, small_in_far.at[n], small_send.at[n], small_recv.at[n],
            device_id=[partner, (d ^ 2, z), (d ^ 4, z), (d, z ^ 1), (d, z ^ 2)][n], device_id_type=MESH,
        )
        copy.start()

        def take():
            copy.wait()
            small[...] += small_in_far[n]
            if n < 4:
                small_step(n + 1)

        clock.send("c", 0.4e6, take)

    small_step(0)
    clock.drain()
    for g in groups:
        finish(g)
    small_out[...] = small[...]
    store.wait()
    for (g, i, kind), copy in hops.items():
        if kind or i >= 2:
            copy.wait_send()
    for copy in exchanges[parts:]:
        copy.wait_send()
    for sender, receiver, copy in halos:
        @pl.when(z == sender)
        def _(copy=copy):
            copy.wait_send()


def back_call(rows, window, parts, perm, back, vmem_in, hbm_in):
    f32, low = jnp.float32, jnp.bfloat16
    any_ = pl.BlockSpec(memory_space=pl.ANY)
    vmem = pl.BlockSpec(memory_space=pltpu.VMEM)
    smem = pl.BlockSpec(memory_space=pltpu.SMEM)
    cut = D // parts
    shapes = {"down": (D, 128), "up": (128, D), "out": (cut, 128), "qkv": (128, 3 * cut)}
    outs = [jax.ShapeDtypeStruct((rows, D), low)]
    outs += [jax.ShapeDtypeStruct(shape, f32) for shape in (shapes["qkv"], shapes["out"], shapes["up"], shapes["down"])]
    outs += [jax.ShapeDtypeStruct((16, D), f32)]
    order = ("down", "up", "out", "qkv")
    buffers = [pltpu.VMEM((2, 2) + shapes[g], low) for g in order]
    buffers += [pltpu.VMEM((parts, 2) + shapes[g], low) for g in order]
    buffers += [pltpu.VMEM((parts, 2) + shapes[g], low) for g in order]
    buffers += [pltpu.VMEM((parts,) + shapes[g], low) for g in order]
    buffers += [pltpu.VMEM((parts - 1,) + shapes[g], low) for g in order]
    dma = pltpu.SemaphoreType.DMA
    return pl.pallas_call(
        functools.partial(back_kernel, rows, window, parts),
        out_shape=outs,
        in_specs=[smem, smem] + [vmem] * len(vmem_in) + [any_] * len(hbm_in),
        out_specs=[any_] + [vmem] * 5,
        scratch_shapes=[
            pltpu.VMEM((rows, D), f32),
            pltpu.VMEM((rows, D), f32),
            pltpu.VMEM((512, 2 * rows), low),
            pltpu.VMEM((2 * D, D), low),
            pltpu.VMEM((2 * rows, D), low),
            pltpu.VMEM((rows, D), low),
            pltpu.VMEM((window, 3 * cut), low),
            pltpu.VMEM((parts, 2 * rows, D), low),
            pltpu.VMEM((D, 3 * cut), low),
            pltpu.VMEM((2 * rows, 512), low),
            pltpu.VMEM((rows, 512), low),
            pltpu.VMEM((window, D), low),
            pltpu.VMEM((16, D), f32),
            pltpu.VMEM((5, 16, D), f32),
        ]
        + buffers
        + [
            dma((7,)),
            dma((4, parts, 3)),
            dma((4, parts, 3)),
            dma((2 * parts + 1,)),
            dma((2 * parts + 1,)),
            dma((2,)),
            dma((2,)),
            dma((5,)),
            dma((5,)),
        ],
        compiler_params=pltpu.CompilerParams(
            collective_id=1, has_side_effects=True, vmem_limit_bytes=60 * 2**20
        ),
    )(perm, back, *vmem_in, *hbm_in)


def unit_order(segs, window):
    units = window // UNIT
    unit_seg = segs[::UNIT]
    index = lax.iota(jnp.int32, units)
    counts = jnp.sum((unit_seg[:, None] == unit_seg[None, :]).astype(jnp.int32), axis=1)
    short = jnp.where((counts == LONG) & (unit_seg >= 0) & (unit_seg < 1000), 0, 1) * units + index
    back = jnp.sum((short[None, :] < short[:, None]).astype(jnp.int32), axis=1)
    perm = jnp.sum(jnp.where(back[None, :] == index[:, None], index[None, :], 0), axis=1)
    return perm.astype(jnp.int32), back.astype(jnp.int32)


def marks_of(segs):
    lane = lax.iota(jnp.int32, 2 * HD)
    seg = jnp.where(segs < 0, 2 * HD - 1, jnp.where(segs >= 1000, 2 * HD - 2, segs))
    same = seg[:, None] == lane[None, :]
    keys = jnp.where(same, 1.0, 0.0).astype(jnp.bfloat16)
    queries = jnp.where(same, 0.0, -1e30).astype(jnp.bfloat16)
    return keys, queries


def local_body(
    tokens,
    cotangent,
    timesteps,
    item_lengths,
    w_qkv,
    bias_qv,
    w_out,
    w_up,
    bias_up,
    w_down,
    vectors,
):
    rows = tokens.shape[0]
    parts = lax.axis_size("mp")
    z = lax.axis_index("mp")
    low = jnp.bfloat16
    f32 = jnp.float32
    cut = D // parts
    firsts, offsets, ends = window_plan(rows, parts)
    window = -(-max(ends) // UNIT) * UNIT
    first_token = UNIT * pick(firsts, z)
    positions = first_token + lax.iota(jnp.int32, window)
    lengths_end = jnp.cumsum(item_lengths[0])
    segs = jnp.sum((positions[:, None] >= lengths_end[None, :]).astype(jnp.int32), axis=1)
    segs = jnp.where(positions < 0, -1, jnp.where(positions >= LEN, 1000, segs))
    perm, back = unit_order(segs, window)
    kf, qf = marks_of(segs)
    step_time = timesteps[0].astype(f32) * 0.001
    bias_q, bias_v = bias_qv[0].astype(f32), bias_qv[1].astype(f32)
    bias_row = jnp.concatenate([bias_q, jnp.zeros((cut,), f32), bias_v, jnp.zeros((D - 3 * cut,), f32)])
    biases = jnp.concatenate([jnp.stack([bias_up.astype(f32), bias_row]), jnp.zeros((6, D), f32)])
    rows16 = jnp.concatenate(
        [vectors, (step_time * vectors[0])[None], jnp.full((7, D), step_time, f32)], axis=0
    )
    (
        f_qkv, f_out, f_up, f_down, qkv, lse, att2, act2, slope, first_t, lift_t, sec2, normed_one,
        second_low, second_grads, output, inverse_one, small_in,
    ) = fore_call(
        rows, window, parts, perm, back, tokens, cotangent,
        w_qkv.reshape(D, 3 * cut), w_out, w_up, w_down, biases, rows16, kf, qf,
    )
    input_grad, grad_qkv, grad_out, grad_up, grad_down, small = back_call(
        rows, window, parts, perm, back,
        (second_low, sec2, inverse_one, vectors[4:5], small_in, kf, qf, lse),
        (first_t, lift_t, second_grads, normed_one, act2, slope, att2, qkv, f_qkv, f_out, f_up, f_down),
    )
    grad_bias_qv = lax.dynamic_slice_in_dim(small[8:10], z * cut, cut, 1)
    grad_bias_up = lax.dynamic_slice_in_dim(small[10:14].reshape(FF), z * (FF // parts), FF // parts, 0)
    return (
        output,
        input_grad,
        grad_qkv.reshape(-1, 3, cut),
        grad_bias_qv,
        grad_out,
        grad_up,
        grad_bias_up,
        grad_down,
        small[:8],
    )


def solution(mesh):
    in_specs = (
        P(("dp", "mp"), None),
        P(("dp", "mp"), None),
        P("dp"),
        P("dp", None),
        P(None, None, "mp"),
        P(None, "mp"),
        P("mp", None),
        P(None, "mp"),
        P("mp"),
        P("mp", None),
        P(),
    )
    out_specs = (
        P(("dp", "mp"), None),
        P(("dp", "mp"), None),
        P("dp", None, "mp"),
        P(None, "mp"),
        P("mp", "dp"),
        P("dp", "mp"),
        P("mp"),
        P("mp", "dp"),
        P(),
    )
    chosen = local_body if fits_local(mesh) else body
    return jax.shard_map(chosen, mesh=mesh, in_specs=in_specs, out_specs=out_specs, check_vma=False)
```

```python
import functools
import heapq

import jax
import jax.numpy as jnp
from jax import lax
from jax.experimental import pallas as pl
from jax.experimental.pallas import tpu as pltpu
from jax.sharding import PartitionSpec as P

D = 1024
HD = 64
FF = 4096
LEN = 2368


def norm_forward(value, gain, shift):
    average = jnp.mean(value, axis=-1, keepdims=True)
    centred = value - average
    inverse = lax.rsqrt(jnp.mean(centred * centred, axis=-1, keepdims=True) + 1e-05)
    normed = centred * inverse
    return (normed * gain + shift, normed, inverse)


def norm_backward(grad, normed, inverse, gain):
    scaled = grad * gain
    result = inverse * (
        scaled
        - jnp.mean(scaled, axis=-1, keepdims=True)
        - normed * jnp.mean(scaled * normed, axis=-1, keepdims=True)
    )
    return (result, jnp.sum(grad * normed, axis=0), jnp.sum(grad, axis=0))


def gelu_exact(value):
    return jax.nn.gelu(value, approximate=False)


def attend_forward(queries, keys, values, segments):
    scale = HD ** (-0.5)
    block_rows = LEN // 4

    def one_block(inputs):
        query_block, segment_block = inputs
        scores = (
            jnp.einsum("bhe,khe->hbk", query_block, keys, preferred_element_type=jnp.float32)
            * scale
        )
        allowed = segment_block[:, None] == segments[None, :]
        scores = jnp.where(allowed[None], scores, -1e30)
        highest = jnp.max(scores, axis=-1, keepdims=True)
        weights = jnp.exp(scores - highest)
        totals = jnp.sum(weights, axis=-1, keepdims=True)
        chances_low = (weights / totals).astype(jnp.bfloat16)
        result = jnp.einsum("hbk,khe->bhe", chances_low, values, preferred_element_type=jnp.float32)
        return (result.astype(jnp.bfloat16), (highest + jnp.log(totals))[..., 0])

    blocks = queries.reshape(4, block_rows, queries.shape[1], queries.shape[2])
    results, logsums = lax.map(one_block, (blocks, segments.reshape(4, block_rows)))
    return (results.reshape(queries.shape), logsums)


def attend_backward(queries, keys, values, out_grads, logsums, segments):
    scale = HD ** (-0.5)
    block_rows = LEN // 4

    def one_block(carry, inputs):
        key_grads, value_grads = carry
        query_block, grad_block, logsum_block, segment_block = inputs
        scores = (
            jnp.einsum("bhe,khe->hbk", query_block, keys, preferred_element_type=jnp.float32)
            * scale
        )
        allowed = segment_block[:, None] == segments[None, :]
        scores = jnp.where(allowed[None], scores, -1e30)
        chances = jnp.exp(scores - logsum_block[..., None])
        chances_low = chances.astype(jnp.bfloat16)
        value_grads = value_grads + jnp.einsum(
            "hbk,bhe->khe", chances_low, grad_block, preferred_element_type=jnp.float32
        )
        flow = jnp.einsum("bhe,khe->hbk", grad_block, values, preferred_element_type=jnp.float32)
        inner = jnp.sum(chances * flow, axis=-1, keepdims=True)
        score_grads = (chances * (flow - inner)).astype(jnp.bfloat16)
        query_grads = (
            jnp.einsum("hbk,khe->bhe", score_grads, keys, preferred_element_type=jnp.float32)
            * scale
        )
        key_grads = (
            key_grads
            + jnp.einsum(
                "hbk,bhe->khe", score_grads, query_block, preferred_element_type=jnp.float32
            )
            * scale
        )
        return ((key_grads, value_grads), query_grads)

    shape_blocks = (4, block_rows, queries.shape[1], queries.shape[2])
    zeros = jnp.zeros(keys.shape, jnp.float32)
    (key_grads, value_grads), query_grads = lax.scan(
        one_block,
        (zeros, zeros),
        (
            queries.reshape(shape_blocks),
            out_grads.reshape(shape_blocks),
            logsums,
            segments.reshape(4, block_rows),
        ),
    )
    return (query_grads.reshape(queries.shape), key_grads, value_grads)


def body(
    tokens,
    cotangent,
    timesteps,
    item_lengths,
    w_qkv,
    bias_qv,
    w_out,
    w_up,
    bias_up,
    w_down,
    vectors,
):
    rows = tokens.shape[0]
    total = rows * lax.axis_size("mp")
    seq_count = timesteps.shape[0]
    local_width = w_qkv.shape[2]
    local_hidden = w_up.shape[1]
    local_heads = local_width // HD
    my_index = lax.axis_index("mp")
    row_ids = my_index * rows + lax.iota(jnp.int32, rows)
    row_owner = row_ids // LEN
    step_times = timesteps.astype(jnp.float32) * 0.001
    time_rows = jnp.sum(
        jnp.where(
            row_owner[:, None] == lax.iota(jnp.int32, seq_count)[None, :], step_times[None, :], 0.0
        ),
        axis=1,
    )
    ends = jnp.cumsum(item_lengths, axis=1)
    segments = jnp.sum(
        (lax.iota(jnp.int32, LEN)[None, :, None] >= ends[:, None, :]).astype(jnp.int32), axis=2
    )
    lifted = tokens.astype(jnp.float32) + time_rows[:, None] * vectors[0] + vectors[1]
    gathered = lax.all_gather(lifted.astype(jnp.bfloat16), "mp", axis=0, tiled=True)
    projected = jnp.einsum("td,dce->cte", gathered, w_qkv, preferred_element_type=jnp.float32)
    shaped = (seq_count, LEN, local_heads, HD)
    head_query = (projected[0] + bias_qv[0]).astype(jnp.bfloat16).reshape(shaped)
    head_key = projected[1].astype(jnp.bfloat16).reshape(shaped)
    head_value = (projected[2] + bias_qv[1]).astype(jnp.bfloat16).reshape(shaped)
    attended, logsums = lax.map(
        lambda items: attend_forward(*items), (head_query, head_key, head_value, segments)
    )
    attended = attended.reshape(total, local_width)
    piece = attended
    mixed = (
        lax.psum_scatter(
            jnp.dot(piece, w_out, preferred_element_type=jnp.float32),
            "mp",
            scatter_dimension=0,
            tiled=True,
        )
        + vectors[2]
    )
    first, normed_one, inverse_one = norm_forward(lifted + mixed, vectors[4], vectors[5])
    hidden_all = lax.all_gather(first.astype(jnp.bfloat16), "mp", axis=0, tiled=True)
    upper = jnp.dot(hidden_all, w_up, preferred_element_type=jnp.float32) + bias_up
    activated, gelu_pull = jax.vjp(gelu_exact, upper)
    activated = activated.astype(jnp.bfloat16)
    piece = activated
    down = (
        lax.psum_scatter(
            jnp.dot(piece, w_down, preferred_element_type=jnp.float32).astype(jnp.bfloat16),
            "mp",
            scatter_dimension=0,
            tiled=True,
        ).astype(jnp.float32)
        + vectors[3]
    )
    output, normed_two, inverse_two = norm_forward(first + down, vectors[6], vectors[7])
    out_grads = cotangent.astype(jnp.float32)
    second_grads, gain_two, shift_two = norm_backward(
        out_grads, normed_two, inverse_two, vectors[6]
    )
    down_all = lax.all_gather(second_grads.astype(jnp.bfloat16), "mp", axis=0, tiled=True)
    grad_down = jnp.einsum("tf,td->fd", activated, down_all, preferred_element_type=jnp.float32)
    act_grads = jnp.einsum("td,fd->tf", down_all, w_down, preferred_element_type=jnp.float32)
    (upper_grads,) = gelu_pull(act_grads)
    upper_low = upper_grads.astype(jnp.bfloat16)
    grad_bias_up = jnp.sum(upper_low, axis=0, dtype=jnp.float32)
    grad_up = jnp.einsum("td,tf->df", hidden_all, upper_low, preferred_element_type=jnp.float32)
    piece = upper_low
    first_part = lax.psum_scatter(
        jnp.einsum("tf,df->td", piece, w_up, preferred_element_type=jnp.float32).astype(
            jnp.bfloat16
        ),
        "mp",
        scatter_dimension=0,
        tiled=True,
    ).astype(jnp.float32)
    first_grads = second_grads + first_part
    mixed_grads, gain_one, shift_one = norm_backward(
        first_grads, normed_one, inverse_one, vectors[4]
    )
    mixed_all = lax.all_gather(mixed_grads.astype(jnp.bfloat16), "mp", axis=0, tiled=True)
    grad_out = jnp.einsum("te,td->ed", attended, mixed_all, preferred_element_type=jnp.float32)
    attended_grads = jnp.einsum(
        "td,ed->te", mixed_all, w_out, preferred_element_type=jnp.float32
    ).astype(jnp.bfloat16)
    query_grads, key_grads, value_grads = lax.map(
        lambda items: attend_backward(*items),
        (head_query, head_key, head_value, attended_grads.reshape(shaped), logsums, segments),
    )
    qkv_low = jnp.stack(
        [
            query_grads.reshape(total, local_width),
            key_grads.reshape(total, local_width),
            value_grads.reshape(total, local_width),
        ],
        axis=1,
    ).astype(jnp.bfloat16)
    grad_bias_qv = jnp.sum(qkv_low[:, 0::2], axis=0, dtype=jnp.float32)
    grad_qkv = jnp.einsum("td,tcf->dcf", gathered, qkv_low, preferred_element_type=jnp.float32)
    piece = qkv_low
    input_part = lax.psum_scatter(
        jnp.einsum("tcf,dcf->td", piece, w_qkv, preferred_element_type=jnp.float32).astype(
            jnp.bfloat16
        ),
        "mp",
        scatter_dimension=0,
        tiled=True,
    ).astype(jnp.float32)
    input_sum = mixed_grads + input_part
    vector_terms = jnp.stack(
        [
            jnp.sum(time_rows[:, None] * input_sum, axis=0),
            jnp.sum(input_sum, axis=0),
            jnp.sum(mixed_grads, axis=0),
            jnp.sum(second_grads, axis=0),
            gain_one,
            shift_one,
            gain_two,
            shift_two,
        ],
        axis=0,
    )
    zero_index = jnp.zeros((), jnp.int32)
    qv_start = my_index * local_width
    up_start = my_index * local_hidden
    qv_placed = lax.dynamic_update_slice(
        jnp.zeros((2, D), jnp.float32), grad_bias_qv, (zero_index, qv_start)
    )
    up_placed = lax.dynamic_update_slice(jnp.zeros((FF,), jnp.float32), grad_bias_up, (up_start,))
    grad_qkv, grad_out, grad_up, grad_down = (
        lax.psum_scatter(
            grad_qkv.astype(jnp.bfloat16), "dp", scatter_dimension=0, tiled=True
        ).astype(jnp.float32),
        lax.psum_scatter(
            grad_out.astype(jnp.bfloat16), "dp", scatter_dimension=1, tiled=True
        ).astype(jnp.float32),
        lax.psum_scatter(
            grad_up.astype(jnp.bfloat16), "dp", scatter_dimension=0, tiled=True
        ).astype(jnp.float32),
        lax.psum_scatter(
            grad_down.astype(jnp.bfloat16), "dp", scatter_dimension=1, tiled=True
        ).astype(jnp.float32),
    )
    grad_vectors, qv_summed, up_summed = lax.psum(
        (vector_terms, qv_placed, up_placed), ("dp", "mp")
    )
    grad_bias_qv = lax.dynamic_slice_in_dim(qv_summed, qv_start, local_width, 1)
    grad_bias_up = lax.dynamic_slice_in_dim(up_summed, up_start, local_hidden, 0)
    return (
        output.astype(jnp.bfloat16),
        input_sum.astype(jnp.bfloat16),
        grad_qkv,
        grad_bias_qv,
        grad_out,
        grad_up,
        grad_bias_up,
        grad_down,
        grad_vectors,
    )


UNIT = 128
LONG = 4
MESH = pl.DeviceIdType.MESH


def fits_local(mesh):
    parts = mesh.shape["mp"]
    return mesh.shape["dp"] == 8 and parts == 4 and LEN % (16 * parts) == 0


def window_plan(rows, parts):
    firsts = [(rows * j) // UNIT - (LONG - 1) for j in range(parts)]
    offsets = [rows * j - UNIT * first for j, first in enumerate(firsts)]
    ends = [
        ((rows * (j + 1) - 1) // UNIT + LONG - firsts[j]) * UNIT for j in range(parts)
    ]
    return firsts, offsets, ends


def pick(table, index):
    value = jnp.int32(table[0])
    for j in range(1, len(table)):
        value = jnp.where(index == j, jnp.int32(table[j]), value)
    return value


NT = (((1,), (1,)), ((), ()))
TN = (((0,), (0,)), ((), ()))
FIRST_OWN, LAST_OWN = LONG - 1, LONG + 4


def two_heads(block):
    lane = lax.broadcasted_iota(jnp.int32, block.shape, 1)
    zero = jnp.zeros_like(block)
    return jnp.concatenate(
        [jnp.where(lane < HD, block, zero), jnp.where(lane < HD, zero, block)], axis=0
    )


def from_two(flipped):
    both = jnp.concatenate([flipped[:HD, :UNIT], flipped[HD:, UNIT:]], axis=0)
    return both.T


def by_rows(rows, body, carry):
    count = rows // 32

    def step(i, c):
        return body(pl.multiple_of(i * 32, 32), 32, c)

    carry = lax.fori_loop(0, count, step, carry)
    return body(count * 32, rows - count * 32, carry) if rows % 32 else carry


def fold(value):
    return value if value.shape[0] == 16 else value[:16] + value[16:]


class Clock:
    def __init__(self):
        self.now = 0.0
        self.free = {}
        self.queue = []
        self.count = 0

    def send(self, link, size, action, share=1.0):
        rate = {"c": 400e3, "x": 44e3, "y": 44e3, "z": 44e3}[link]
        begin = max(self.now, self.free.get(link, 0.0))
        end = begin + share * size / rate
        self.free[link] = end
        self.count += 1
        heapq.heappush(self.queue, (end + 1.5, self.count, action))

    def work(self, time):
        self.now += time
        while self.queue and self.queue[0][0] <= self.now:
            heapq.heappop(self.queue)[2]()

    def step(self):
        ready, _, action = heapq.heappop(self.queue)
        self.now = max(self.now, ready)
        action()

    def drain(self):
        while self.queue:
            self.step()


def block_owners(d, core, x_first):
    x, y = lax.rem(d // 2, 2), d // 4
    if x_first:
        return [4 * b + 2 * a + core for a in (1 - x, x) for b in (1 - y, y)]
    return [4 * b + 2 * a + core for b in (1 - y, y) for a in (1 - x, x)]


RING = (2, 3, 1, 0)
HALO_TIME = 34.0


def fore_kernel(
    rows, window, parts, perm, back, tokens, cotangent, w_qkv, w_out, w_up, w_down, biases, vectors, kf, qf,
    f_qkv, f_out, f_up, f_down, qkv, lse, att2, act2, slopes, first_t, lift_t, sec2, normed_out, second_low,
    second_grads, output, inverse, small,
    win, xq, yq, own_rows, attended, mixed, first, first_low, down, in_low, out_low, wu, wd, wq, wo, act, slope, lift2, first2,
    turned, stage, bias_all, send, recv, own_sent, near, far, own, bias_send, bias_recv, local, pair_send, pair_recv,
):
    f32, low = jnp.float32, jnp.bfloat16
    d = lax.axis_index("dp")
    z = lax.axis_index("mp")
    core = lax.rem(d, 2)
    cut = D // parts
    three = 3 * cut
    pairs = cut // (2 * HD)
    firsts, offsets, ends = window_plan(rows, parts)
    offset = pl.multiple_of(pick(offsets, z), 16)
    shards = (w_qkv, w_out, w_up, w_down)
    fulls = (f_qkv, f_out, f_up, f_down)
    sizes = tuple(shard.shape[0] // 8 for shard in shards)
    partner = (d ^ 1, z)
    peers = [(d, z ^ k) for k in (1, 2, 3)] + [partner, (d ^ 2, z), (d ^ 4, z)]
    barrier = pltpu.get_barrier_semaphore()
    for peer in peers:
        pl.semaphore_signal(barrier, inc=1, device_id=peer, device_id_type=MESH)
    pl.semaphore_wait(barrier, len(peers))
    clock = Clock()

    order = [sorted((o for o in range(parts) if o != j), key=lambda o: (abs(o - j), o)) for j in range(parts)]
    source = [pick([order[j][n] for j in range(parts)], z) for n in range(parts - 1)]
    chunks = [(g, n) for n in range(parts - 1) for g in (0, 1)] + [(g, n) for n in range(parts - 1) for g in (2, 3)]
    index_of = {chunk: i for i, chunk in enumerate(chunks)}
    copies, done = {}, {}

    def part(ref, index, owner, size, half=None):
        start, count = owner * size, size
        if half is not None:
            count = size // 2
            start = start + half * count
        return ref.at[index, pl.ds(pl.multiple_of(start, 16), count), :]

    def remote(i, kind, src, dst, target):
        copy = pltpu.make_async_remote_copy(
            src, dst, send.at[i, kind], recv.at[i, kind], device_id=target, device_id_type=MESH
        )
        copy.start()
        copies[i, kind] = copy

    def place(i, owner, half=None):
        g, n = chunks[i]
        return part(fulls[g], source[n], owner, sizes[g], half)

    def bytes_of(i):
        g, n = chunks[i]
        return sizes[g] * shards[g].shape[1] * 2

    def pass_on(i, kind, owner, target, half=None):
        remote(i, kind, place(i, owner, half), place(i, owner, half), target)

    column = []

    def along(owner, place_of, here, there, sent, g):
        i = index_of[g, order[there].index(owner)]
        copy = pltpu.make_async_remote_copy(
            place_of, part(fulls[g], owner, d, sizes[g]), sent, recv.at[i, 0],
            device_id=(d, there), device_id_type=MESH,
        )

        @pl.when(z == here)
        def _():
            copy.start()

        column.append((here, copy))

    def send_own(g):
        rows_at = pl.ds(pl.multiple_of(d * sizes[g], 16), sizes[g])
        for here in range(parts):
            for n, there in enumerate((here - 1, here + 1)):
                if 0 <= there < parts:
                    along(here, shards[g].at[rows_at, :], here, there, own_sent.at[g, n], g)
        for n in range(parts - 1):
            i = index_of[g, n]
            clock.send("z", bytes_of(i), lambda i=i: hop_two(i))

    def hop_two(i):
        g, n = chunks[i]
        pltpu.make_async_remote_copy(
            place(i, d), place(i, d), send.at[i, 0], recv.at[i, 0], device_id=partner, device_id_type=MESH
        ).wait_recv()
        for here in range(parts):
            owner = order[here][n]
            there = here + 1 if owner < here else here - 1
            if 0 <= there < parts:
                along(owner, part(fulls[g], owner, d, sizes[g]), here, there, send.at[i, 0], g)
        if n == 0 and g < 2:
            send_own(g + 2)
        pass_on(i, 1, d, (d ^ 2, z))
        pass_on(i, 2, d, (d ^ 4, z))
        pass_on(i, 5, d, partner)
        clock.send("c", bytes_of(i), lambda: None)
        clock.send("x", bytes_of(i), lambda: hop_three(i))
        clock.send("y", bytes_of(i), lambda: hop_four(i))

    def hop_three(i):
        copies[i, 1].wait_recv()
        pass_on(i, 3, d ^ 2, (d ^ 4, z), 0)
        pass_on(i, 6, d ^ 2, partner)
        clock.send("y", bytes_of(i) // 2, lambda: hop_five(i))

    def hop_four(i):
        copies[i, 2].wait_recv()
        pass_on(i, 4, d ^ 4, (d ^ 2, z), 1)
        pass_on(i, 7, d ^ 4, partner)
        clock.send("x", bytes_of(i) // 2, lambda: hop_six(i))

    def hop_five(i):
        copies[i, 3].wait_recv()
        pass_on(i, 8, d ^ 6, partner, 0)
        finish(i)

    def hop_six(i):
        copies[i, 4].wait_recv()
        pass_on(i, 9, d ^ 6, partner, 1)
        finish(i)

    def finish(i):
        done[i] = done.get(i, 0) + 1

    def arrive(i):
        while done.get(i, 0) < 2:
            clock.step()
        for kind in range(5, 10):
            copies[i, kind].wait_recv()

    send_own(0)
    send_own(1)

    halos = []
    for j in range(parts - 1):
        count = ends[j] - offsets[j] - rows
        halos.append((j + 1, j, pltpu.make_async_remote_copy(
            tokens.at[pl.ds(0, count), :], win.at[pl.ds(offsets[j] + rows, count), :],
            near.at[0], near.at[1], device_id=(d, j), device_id_type=MESH,
        )))
    for j in range(1, parts):
        halos.append((j - 1, j, pltpu.make_async_remote_copy(
            tokens.at[pl.ds(rows - offsets[j], offsets[j]), :], win.at[pl.ds(0, offsets[j]), :],
            far.at[0], far.at[1], device_id=(d, j), device_id_type=MESH,
        )))
    for sender, receiver, copy in halos:
        @pl.when(z == sender)
        def _(copy=copy):
            copy.start()
    clock.send("z", max(offsets) * D * 2, lambda: None)
    bias_copies = []
    for k in (1, 2, 3):
        copy = pltpu.make_async_remote_copy(
            biases, bias_all.at[z], bias_send.at[k - 1], bias_recv.at[k - 1], device_id=(d, z ^ k), device_id_type=MESH
        )
        copy.start()
        bias_copies.append(copy)
    bias_all[pl.ds(z, 1)] = biases[...][None]
    owns = []
    for g in range(4):
        copy = pltpu.make_async_copy(shards[g], fulls[g].at[z], own.at[g])
        copy.start()
        owns.append(copy)

    def lift(value):
        return value.astype(f32) + vectors[8:9, :] + vectors[1:2, :]

    def own_body(i, c):
        at = pl.ds(pl.multiple_of(i * 16, 16), 16)
        win[pl.ds(pl.multiple_of(offset + i * 16, 16), 16), :] = lift(tokens[at, :]).astype(low)
        return c

    lax.fori_loop(0, rows // 16, own_body, 0)
    zero = jnp.zeros((16, D), low)

    def spans_of(j):
        end = ends[j] if j < parts - 1 else offsets[j] + rows
        empty = [(0, offsets[0])] if j == 0 else []
        if end < window:
            empty.append((end, window))
        filled = [(0, offsets[j])] if j else []
        if j < parts - 1:
            filled.append((offsets[j] + rows, ends[j]))
        return empty, filled

    for j in range(parts):
        @pl.when(z == j)
        def _(j=j):
            for begin, end in spans_of(j)[0]:
                def clear(i, c, begin=begin):
                    win[pl.ds(pl.multiple_of(begin + i * 16, 16), 16), :] = zero
                    return c
                lax.fori_loop(0, (end - begin) // 16, clear, 0)

    pair_copies = []

    def exchange(source, target):
        index = len(pair_copies)
        copy = pltpu.make_async_remote_copy(
            source, target, pair_send.at[index], pair_recv.at[index], device_id=partner, device_id_type=MESH
        )
        copy.start()
        pair_copies.append(copy)
        return copy

    def columns(read, c, write):
        for j, owner in enumerate(block_owners(d, c, True)):
            write(slice(j * 128, (j + 1) * 128), read(pl.ds(pl.multiple_of(owner * 128, 128), 128)))

    own_at = pl.ds(offset, rows)
    mine = pl.ds(0, rows)
    theirs = pl.ds(rows, rows)
    columns(lambda at: win[own_at, at], 1 - core, lambda at, v: stage.__setitem__((0, slice(None), at), v))
    lift_copy = exchange(stage.at[0], lift2.at[theirs, :])
    columns(lambda at: win[own_at, at], core, lambda at, v: lift2.__setitem__((mine, at), v))

    def fetch(index, source, target):
        copy = pltpu.make_async_copy(source, target, local.at[index])
        copy.start()
        return copy

    clock.work(4.0)
    for copy in bias_copies:
        copy.wait_recv()
    clock.work(max(0.0, HALO_TIME - clock.now))
    for sender, receiver, copy in halos:
        @pl.when(z == receiver)
        def _(copy=copy):
            copy.wait_recv()
    for j in range(parts):
        @pl.when(z == j)
        def _(j=j):
            for begin, end in spans_of(j)[1]:
                def convert(i, c, begin=begin):
                    at = pl.ds(pl.multiple_of(begin + i * 16, 16), 16)
                    win[at, :] = lift(win[at, :]).astype(low)
                    return c
                lax.fori_loop(0, (end - begin) // 16, convert, 0)
    clock.work(2.0)
    lift_copy.wait_recv()
    turned[...] = lift2[...].T
    turned_out = fetch(0, turned, lift_t)
    clock.work(2.0)

    stores = {}
    for i in range(parts):
        k = i
        at_z = source[i - 1] if i else z
        if k == 0:
            wq_ref, wo_ref = w_qkv, w_out
        else:
            arrive(index_of[0, k - 1])
            arrive(index_of[1, k - 1])
            load_q, load_o = fetch(1, f_qkv.at[at_z], wq), fetch(2, f_out.at[at_z], wo)
            wq_ref, wo_ref = wq, wo
            load_q.wait()
        slot_i = i % 2
        if i >= 2:
            stores[i - 2].wait()
        row = bias_all.at[at_z]

        def project(n, c):
            at = pl.ds(pl.multiple_of(n * 512, 512), 512)
            for c3 in range(3):
                lanes = slice(c3 * cut, (c3 + 1) * cut)
                value = jnp.dot(win[at, :], wq_ref[:, lanes], preferred_element_type=f32)
                value = (value + row[1:2, lanes]).astype(low)
                if c3 == 0:
                    value = value * jnp.array(HD ** (-0.5), low)
                xq[slot_i, at, lanes] = value
            return c

        lax.fori_loop(0, window // 512, project, 0)
        stores[i] = fetch(3 + slot_i, xq.at[slot_i], qkv.at[at_z])
        clock.work(4.0)

        def attend(step, c):
            p, slot = step // 3, lax.rem(step, 3)
            lanes = lambda base: pl.ds(pl.multiple_of(base + p * 2 * HD, 2 * HD), 2 * HD)
            unit_at = [pl.ds(perm[slot * LONG + m] * UNIT, UNIT) for m in range(LONG)]
            keys = jnp.concatenate([xq[slot_i, at, lanes(cut)] for at in unit_at], axis=0)
            values = jnp.concatenate([xq[slot_i, at, lanes(2 * cut)] for at in unit_at], axis=0)
            marks = jnp.concatenate([kf[at, :] for at in unit_at], axis=0)
            wide_keys = jnp.concatenate([keys, marks], axis=1)
            pair = jnp.concatenate([two_heads(xq[slot_i, at, lanes(0)]) for at in unit_at], axis=0)
            mark = jnp.concatenate([qf[at, :] for at in unit_at for _ in range(2)], axis=0)
            wide_pair = jnp.concatenate([pair, mark], axis=1)
            scores = lax.dot_general(wide_keys, wide_pair, NT, preferred_element_type=f32)
            highest = jnp.max(scores, axis=0, keepdims=True)
            weights = jnp.exp(scores - highest)
            total = jnp.sum(weights, axis=0, keepdims=True)
            flipped = lax.dot_general(values, weights.astype(low), TN, preferred_element_type=f32) * (1.0 / total)
            logsum = highest + jnp.log(total)
            for m in range(LONG):
                two = slice(m * 2 * UNIT, (m + 1) * 2 * UNIT)
                at = pl.ds(pl.multiple_of(slot * LONG * UNIT + m * UNIT, UNIT), UNIT)
                yq[at, lanes(0)] = from_two(flipped[:, two]).astype(low)
                lse[at_z, pl.ds(step * LONG + m, 1), :] = logsum[:, two]
            return c

        lax.fori_loop(0, pairs * 3, attend, 0, unroll=2)
        clock.work(7.5)
        for u in range(FIRST_OWN, LAST_OWN + 1):
            own_rows[pl.ds((u - FIRST_OWN) * UNIT, UNIT), :] = yq[pl.ds(back[u] * UNIT, UNIT), :]
        lanes_z = pl.ds(pl.multiple_of(at_z * cut, cut), cut)
        attended[i] = own_rows[pl.ds(pl.multiple_of(offset - FIRST_OWN * UNIT, 16), rows), :]
        exchange(attended.at[i], att2.at[theirs, lanes_z])
        stores["a", i] = fetch(5 + i, attended.at[i], att2.at[mine, lanes_z])
        if k:
            load_o.wait()

        def out_body(n, c):
            at = pl.ds(pl.multiple_of(n * 256, 256), 256)
            value = jnp.dot(attended[i], wo_ref[:, at], preferred_element_type=f32)
            if i == 0:
                mixed[:, at] = value
            else:
                mixed[:, at] += value
            return c

        lax.fori_loop(0, D // 256, out_body, 0)
        clock.work(1.0)

    def norm_one(begin, count, c):
        at = pl.ds(begin, count)
        value = lift(tokens[at, :]) + (mixed[at, :] + vectors[2:3, :])
        centred = value - jnp.mean(value, axis=-1, keepdims=True)
        scale = lax.rsqrt(jnp.mean(centred * centred, axis=-1, keepdims=True) + 1e-05)
        normed = centred * scale
        mixed[at, :] = normed
        inverse[at, :] = scale
        result = normed * vectors[4:5, :] + vectors[5:6, :]
        first[at, :] = result
        first_low[at, :] = result.astype(low)
        return c

    by_rows(rows, norm_one, 0)
    normed_store = fetch(9, mixed, normed_out)
    columns(lambda at: first_low[:, at], 1 - core, lambda at, v: stage.__setitem__((1, slice(None), at), v))
    first_copy = exchange(stage.at[1], first2.at[theirs, :])
    columns(lambda at: first_low[:, at], core, lambda at, v: first2.__setitem__((mine, at), v))
    clock.work(4.0)

    for i in range(parts):
        k = i
        at_z = source[i - 1] if i else z
        slot_i = i % 2
        if k == 0:
            up_ref, down_ref = w_up, w_down
        else:
            arrive(index_of[2, k - 1])
            load_u = fetch(1, f_up.at[at_z], wu)
            arrive(index_of[3, k - 1])
            load_d = fetch(2, f_down.at[at_z], wd)
            up_ref, down_ref = wu, wd
            load_u.wait()
        if i >= 2:
            for copy in stores["f", i - 2]:
                copy.wait()
            stores["r", i - 2].wait_send()
        row = bias_all.at[at_z]

        def upper_body(n, c):
            at = pl.ds(pl.multiple_of(n * 256, 256), 256)
            value = jnp.dot(first_low[...], up_ref[:, at], preferred_element_type=f32) + row[0:1, at]
            chance = 0.5 + 0.5 * lax.erf(value * (0.5**0.5))
            act[slot_i, :, at] = (value * chance).astype(low)
            density = jnp.exp(-0.5 * value * value) * (0.5 / jnp.pi) ** 0.5
            slope[slot_i, :, at] = (chance + value * density).astype(low)
            return c

        lax.fori_loop(0, D // 256, upper_body, 0)
        hidden = pl.ds(pl.multiple_of(at_z * D, D), D)
        stores["r", i] = exchange(act.at[slot_i], act2.at[theirs, hidden])
        stores["f", i] = (
            fetch(14 + slot_i, act.at[slot_i], act2.at[mine, hidden]),
            fetch(10 + slot_i, slope.at[slot_i], slopes.at[:, hidden]),
        )
        clock.work(4.0)
        if k:
            load_d.wait()

        def down_body(n, c):
            at = pl.ds(pl.multiple_of(n * 256, 256), 256)
            value = jnp.dot(act[slot_i], down_ref[:, at], preferred_element_type=f32)
            if i == 0:
                down[:, at] = value
            else:
                down[:, at] += value
            return c

        lax.fori_loop(0, D // 256, down_body, 0)
        clock.work(2.0)
        if i == 0:
            first_copy.wait_recv()
            turned_out.wait()
            turned[...] = first2[...].T
            turned_out = fetch(0, turned, first_t)
            clock.work(2.0)

    zero_row = jnp.zeros((16, D), f32)

    def norm_two(begin, count, sums):
        at = pl.ds(begin, count)
        value = first[at, :] + (down[at, :] + vectors[3:4, :])
        centred = value - jnp.mean(value, axis=-1, keepdims=True)
        scale = lax.rsqrt(jnp.mean(centred * centred, axis=-1, keepdims=True) + 1e-05)
        normed = centred * scale
        out_low[at, :] = (normed * vectors[6:7, :] + vectors[7:8, :]).astype(low)
        grads = cotangent[at, :].astype(f32)
        scaled = grads * vectors[6:7, :]
        result = scale * (
            scaled
            - jnp.mean(scaled, axis=-1, keepdims=True)
            - normed * jnp.mean(scaled * normed, axis=-1, keepdims=True)
        )
        down[at, :] = result
        in_low[at, :] = result.astype(low)
        return (sums[0] + fold(result), sums[1] + fold(grads * normed), sums[2] + fold(grads))

    sums = by_rows(rows, norm_two, (zero_row, zero_row, zero_row))
    last = [fetch(1, out_low, output), fetch(2, in_low, second_low), fetch(12, down, second_grads)]
    small[...] = jnp.zeros_like(small)
    small[3:4, :] = jnp.sum(sums[0], axis=0, keepdims=True)
    small[6:7, :] = jnp.sum(sums[1], axis=0, keepdims=True)
    small[7:8, :] = jnp.sum(sums[2], axis=0, keepdims=True)
    small[15:16, :] = vectors[9:10, :]
    columns(lambda at: in_low[:, at], 1 - core, lambda at, v: stage.__setitem__((2, slice(None), at), v))
    exchange(stage.at[2], sec2.at[theirs, :])
    columns(lambda at: in_low[:, at], core, lambda at, v: stage.__setitem__((3, slice(None), at), v))
    last.append(fetch(13, stage.at[3], sec2.at[mine, :]))
    clock.drain()
    for copy in last + owns + [turned_out, normed_store, stores[2], stores[3]]:
        copy.wait()
    for i in range(parts):
        stores["a", i].wait()
        if i >= 2:
            for copy in stores["f", i]:
                copy.wait()
    waited = [stores["r", 0], stores["r", 1]]
    for copy in pair_copies:
        if not any(copy is other for other in waited):
            copy.wait_send()
        if copy is not lift_copy and copy is not first_copy:
            copy.wait_recv()
    for copy in copies.values():
        copy.wait_send()
    for here, copy in column:
        @pl.when(z == here)
        def _(copy=copy):
            copy.wait_send()
    for copy in bias_copies:
        copy.wait_send()
    for sender, receiver, copy in halos:
        @pl.when(z == sender)
        def _(copy=copy):
            copy.wait_send()


def fore_call(rows, window, parts, perm, back, *arrays):
    f32, low = jnp.float32, jnp.bfloat16
    any_ = pl.BlockSpec(memory_space=pl.ANY)
    vmem = pl.BlockSpec(memory_space=pltpu.VMEM)
    smem = pl.BlockSpec(memory_space=pltpu.SMEM)
    cut = D // parts
    three = 3 * cut
    shape = jax.ShapeDtypeStruct
    marks = cut // (2 * HD) * 3 * LONG
    dma = pltpu.SemaphoreType.DMA
    return pl.pallas_call(
        functools.partial(fore_kernel, rows, window, parts),
        out_shape=[
            shape((parts, D, three), low),
            shape((parts, cut, D), low),
            shape((parts, D, D), low),
            shape((parts, D, D), low),
            shape((parts, window, three), low),
            shape((parts, marks, 2 * UNIT), f32),
            shape((2 * rows, D), low),
            shape((2 * rows, FF), low),
            shape((rows, FF), low),
            shape((512, 2 * rows), low),
            shape((512, 2 * rows), low),
            shape((2 * rows, 512), low),
            shape((rows, D), f32),
            shape((rows, D), low),
            shape((rows, D), f32),
            shape((rows, D), low),
            shape((rows, 1), f32),
            shape((16, D), f32),
        ],
        in_specs=[smem, smem] + [vmem] * len(arrays),
        out_specs=[any_] * 5 + [vmem] + [any_] * 10 + [vmem] * 2,
        scratch_shapes=[
            pltpu.VMEM((window, D), low),
            pltpu.VMEM((2, window, three), low),
            pltpu.VMEM((window, cut), low),
            pltpu.VMEM(((LAST_OWN + 1 - FIRST_OWN) * UNIT, cut), low),
            pltpu.VMEM((parts, rows, cut), low),
            pltpu.VMEM((rows, D), f32),
            pltpu.VMEM((rows, D), f32),
            pltpu.VMEM((rows, D), low),
            pltpu.VMEM((rows, D), f32),
            pltpu.VMEM((rows, D), low),
            pltpu.VMEM((rows, D), low),
            pltpu.VMEM((D, D), low),
            pltpu.VMEM((D, D), low),
            pltpu.VMEM((D, three), low),
            pltpu.VMEM((cut, D), low),
            pltpu.VMEM((2, rows, D), low),
            pltpu.VMEM((2, rows, D), low),
            pltpu.VMEM((2 * rows, 512), low),
            pltpu.VMEM((2 * rows, 512), low),
            pltpu.VMEM((512, 2 * rows), low),
            pltpu.VMEM((4, rows, 512), low),
            pltpu.VMEM((parts, 8, D), f32),
            dma((12, 10)),
            dma((12, 10)),
            dma((4, 2)),
            dma((2,)),
            dma((2,)),
            dma((4,)),
            dma((3,)),
            dma((3,)),
            dma((16,)),
            dma((2 * parts + 3,)),
            dma((2 * parts + 3,)),
        ],
        compiler_params=pltpu.CompilerParams(
            collective_id=0, has_side_effects=True, vmem_limit_bytes=56 * 2**20
        ),
    )(perm, back, *arrays)


def back_kernel(
    rows, window, parts, perm, back, sec_low, sec2, inverse, gain, small_in, kf, qf, lse,
    first_t, lift_t, second_grads, normed_one, act2, dgelu, att2, qkv, f_qkv, f_out, f_up, f_down,
    input_grad, g_qkv, g_out, g_up, g_down, small_out,
    acc, normed, turned, arena, act, slope, y, up2, w_in, mixed2, mixed_win, small, small_in_far,
    s_down, s_up, s_out, s_qkv, k_down, k_up, k_out, k_qkv,
    r_down, r_up, r_out, r_qkv, t_down, t_up, t_out, t_qkv, z_down, z_up, z_out, z_qkv,
    local, hop_send, hop_recv, pair_send, pair_recv, halo_send, halo_recv, small_send, small_recv,
):
    f32, low = jnp.float32, jnp.bfloat16
    d = lax.axis_index("dp")
    z = lax.axis_index("mp")
    core = lax.rem(d, 2)
    firsts, offsets, ends = window_plan(rows, parts)
    offset = pl.multiple_of(pick(offsets, z), 16)
    partner = (d ^ 1, z)
    peers = [(d, z ^ k) for k in (1, 2, 3)] + [partner, (d ^ 2, z), (d ^ 4, z), (d ^ 6, z)]
    barrier = pltpu.get_barrier_semaphore()
    for peer in peers:
        pl.semaphore_signal(barrier, inc=1, device_id=peer, device_id_type=MESH)
    pl.semaphore_wait(barrier, len(peers))
    clock = Clock()
    tail = []

    wide = 2 * rows
    wd = arena.at[pl.ds(0, D), :]
    wu = arena.at[pl.ds(D, D), :]

    def fetch(index, source, target):
        copy = pltpu.make_async_copy(source, target, local.at[index])
        copy.start()
        return copy

    chunk = lambda k: z ^ k
    hidden = lambda k: pl.ds(pl.multiple_of(chunk(k) * D, D), D)
    load_wd = lambda i: fetch(0, f_down.at[chunk(RING[i])], wd)
    load_wu = lambda i: fetch(1, f_up.at[chunk(RING[i])], wu)
    load_act = lambda i: fetch(2, act2.at[:, hidden(RING[i])], act)
    load_slope = lambda i: fetch(3, dgelu.at[:, hidden(RING[i])], slope)
    at_act, at_wd, at_slope, at_wu = load_act(0), load_wd(0), load_slope(0), load_wu(0)
    at_acc = fetch(4, second_grads, acc)
    at_normed = fetch(5, normed_one, normed)
    at_turned = fetch(6, first_t, turned)

    zero = jnp.zeros((16, D), low)
    for j in range(parts):
        spans = []
        if j == 0:
            spans.append((0, offsets[0]))
        begin = ends[j] if j < parts - 1 else offsets[j] + rows
        if begin < window:
            spans.append((begin, window))
        if spans:
            @pl.when(z == j)
            def _(spans=spans):
                for begin, end in spans:
                    def clear(i, c):
                        mixed_win[pl.ds(pl.multiple_of(begin + i * 16, 16), 16), :] = zero
                        return c
                    lax.fori_loop(0, (end - begin) // 16, clear, 0)

    groups = {
        "down": (s_down, k_down, r_down, t_down, z_down, g_down, 0),
        "up": (s_up, k_up, r_up, t_up, z_up, g_up, 1),
        "out": (s_out, k_out, r_out, t_out, z_out, g_out, 2),
        "qkv": (s_qkv, k_qkv, r_qkv, t_qkv, z_qkv, g_qkv, 3),
    }
    hops, finished = {}, {}

    def x_ahead(g, i):
        return (i + groups[g][6]) % 2 == 0

    def put(g, i, j, at, value):
        if not x_ahead(g, i):
            j = (0, 2, 1, 3)[j]
        if j < 2:
            groups[g][0][(i % 2, j) + at] = value
        else:
            groups[g][1][(i, j - 2) + at] = value

    def hop(g, i, kind, source, target, device):
        index = groups[g][6]
        copy = pltpu.make_async_remote_copy(
            source, target, hop_send.at[index, i, kind], hop_recv.at[index, i, kind],
            device_id=device, device_id_type=MESH,
        )
        copy.start()
        hops[g, i, kind] = copy

    def add_into(ref, other):
        count = ref.shape[0]
        step = min(count, 64)

        def body(j, c):
            at = pl.ds(pl.multiple_of(j * step, step), step)
            ref[at, :] = (ref[at, :].astype(f32) + other[at, :].astype(f32)).astype(low)
            return c

        lax.fori_loop(0, count // step, body, 0)

    def launch(g, i):
        s, kept, r, t, zb, out, index = groups[g]
        x_first = x_ahead(g, i)
        n1, n2 = ((d ^ 2, z), (d ^ 4, z)) if x_first else ((d ^ 4, z), (d ^ 2, z))
        l1, l2 = ("x", "y") if x_first else ("y", "x")
        block = s.shape[2] * s.shape[3] * 2
        k = RING[i]
        hop(g, i, 0, s.at[i % 2], r.at[i], n1)

        def second():
            hops[g, i, 0].wait_recv()
            add_into(kept.at[i, 0], r.at[i, 0])
            hop(g, i, 1, kept.at[i, 0], t.at[i], n2)
            clock.send(l2, block, third)
            add_into(kept.at[i, 1], r.at[i, 1])

        def third():
            hops[g, i, 1].wait_recv()
            add_into(kept.at[i, 1], t.at[i])
            if k:
                hop(g, i, 2, kept.at[i, 1], zb.at[k - 1], (d, z ^ k))
                clock.send("z", block, fourth, 1.0 if k == 1 else 2.0)
            else:
                ended()

        def fourth():
            hops[g, i, 2].wait_recv()
            ended()

        def ended():
            finished[g] = finished.get(g, 0) + 1
            if finished[g] == parts:
                finish(g)

        clock.send(l1, 2 * block, second)

    def free_slot(g, i):
        if i >= 2:
            hops[g, i - 2, 0].wait_send()

    def finish(g):
        s, kept, r, t, zb, out, index = groups[g]
        own = RING.index(0)
        count = s.shape[2]
        step = min(count, 64)
        pieces = kept.at[own, 1]

        def body(j, c):
            at = pl.ds(pl.multiple_of(j * step, step), step)
            total = pieces[at, :].astype(f32)
            for k in range(parts - 1):
                total = total + zb[k, at, :].astype(f32)
            out[at, :] = total
            return c

        lax.fori_loop(0, count // step, body, 0)

    def exchange(index, source, target):
        copy = pltpu.make_async_remote_copy(
            source, target, pair_send.at[index], pair_recv.at[index], device_id=partner, device_id_type=MESH
        )
        copy.start()
        return copy

    small[...] = small_in[...]

    pending = {}

    def grad_up_chunk(i):
        pending.pop(i).wait_recv()
        if i == 0:
            at_turned.wait()
        free_slot("up", i)

        def body(n, c):
            at = pl.ds(pl.multiple_of(n * 256, 256), 256)
            tile = jnp.dot(turned[...], up2[i, :, at], preferred_element_type=f32).astype(low)
            for j in range(4):
                put("up", i, j, (slice(None), at), tile[j * 128 : (j + 1) * 128])
            return c

        lax.fori_loop(0, 4, body, 0)
        launch("up", i)
        clock.work(2.0)

    exchanges = []
    loads = {"wd": at_wd, "wu": at_wu, "slope": at_slope, "act": at_act}

    def upper_chunk(i):
        loads["wd"].wait()
        loads["slope"].wait()
        bias_row = chunk(RING[i])

        def body(n, c):
            at = pl.ds(pl.multiple_of(n * 256, 256), 256)
            grads = lax.dot_general(sec_low[...], wd[at, :], NT, preferred_element_type=f32)
            value = (grads * slope[:, at].astype(f32)).astype(low)
            up2[i, pl.ds(0, rows), at] = value
            small[pl.ds(10 + bias_row, 1), at] = jnp.sum(value.astype(f32), axis=0, keepdims=True)
            return c

        lax.fori_loop(0, 4, body, 0)
        pending[i] = exchange(i, up2.at[i, pl.ds(0, rows), :], up2.at[i, pl.ds(rows, rows), :])
        exchanges.append(pending[i])
        clock.work(2.5)
        if i + 1 < parts:
            loads["wd"], loads["slope"] = load_wd(i + 1), load_slope(i + 1)

    def grad_down_chunk(i):
        loads["act"].wait()
        free_slot("down", i)

        def body(n, c):
            at = pl.ds(pl.multiple_of(n * 256, 256), 256)
            tile = lax.dot_general(act[:, at], sec2[...], TN, preferred_element_type=f32).astype(low)
            for j in range(4):
                put("down", i, j, (at, slice(None)), tile[:, j * 128 : (j + 1) * 128])
            return c

        lax.fori_loop(0, 4, body, 0)
        launch("down", i)
        clock.work(2.0)
        if i + 1 < parts:
            loads["act"] = load_act(i + 1)

    def first_chunk(i):
        loads["wu"].wait()
        if i == 0:
            at_acc.wait()

        def body(n, c):
            at = pl.ds(pl.multiple_of(n * 256, 256), 256)
            acc[:, at] += lax.dot_general(
                up2[i, pl.ds(0, rows), :], wu[at, :], NT, preferred_element_type=f32
            )
            return c

        lax.fori_loop(0, 4, body, 0)
        clock.work(2.0)
        if i + 1 < parts:
            loads["wu"] = load_wu(i + 1)

    grad_down_chunk(0)
    for i in range(parts):
        upper_chunk(i)
        first_chunk(i)
        if i == 1:
            grad_down_chunk(1)

    at_normed.wait()
    zero_row = jnp.zeros((16, D), f32)

    def norm_body(begin, count, sums):
        at = pl.ds(begin, count)
        grads, unit = acc[at, :], normed[at, :]
        scaled = grads * gain[0:1, :]
        result = inverse[at, :] * (
            scaled
            - jnp.mean(scaled, axis=-1, keepdims=True)
            - unit * jnp.mean(scaled * unit, axis=-1, keepdims=True)
        )
        acc[at, :] = result
        mixed_win[pl.ds(pl.multiple_of(offset + begin, 16), count), :] = result.astype(low)
        return (sums[0] + fold(grads * unit), sums[1] + fold(grads), sums[2] + fold(result))

    sums = by_rows(rows, norm_body, (zero_row, zero_row, zero_row))
    small[4:5, :] = jnp.sum(sums[0], axis=0, keepdims=True)
    small[5:6, :] = jnp.sum(sums[1], axis=0, keepdims=True)
    small[2:3, :] = jnp.sum(sums[2], axis=0, keepdims=True)
    halos = []
    for j in range(parts - 1):
        count = ends[j] - offsets[j] - rows
        halos.append((j + 1, j, pltpu.make_async_remote_copy(
            mixed_win.at[pl.ds(offsets[j + 1], count), :],
            mixed_win.at[pl.ds(offsets[j] + rows, count), :],
            halo_send.at[0], halo_recv.at[0], device_id=(d, j), device_id_type=MESH,
        )))
    for j in range(1, parts):
        halos.append((j - 1, j, pltpu.make_async_remote_copy(
            mixed_win.at[pl.ds(offsets[j - 1] + rows - offsets[j], offsets[j]), :],
            mixed_win.at[pl.ds(0, offsets[j]), :],
            halo_send.at[1], halo_recv.at[1], device_id=(d, j), device_id_type=MESH,
        )))
    for sender, receiver, copy in halos:
        @pl.when(z == sender)
        def _(copy=copy):
            copy.start()
    clock.work(4.0)
    for i in range(parts):
        grad_up_chunk(i)
        if i + 2 < parts:
            grad_down_chunk(i + 2)
    own_at = pl.ds(offset, rows)
    for j, owner in enumerate(block_owners(d, 1 - core, True)):
        y[0:rows, j * 128 : (j + 1) * 128] = mixed_win[own_at, pl.ds(pl.multiple_of(owner * 128, 128), 128)]
    exchanges.append(exchange(parts, y.at[pl.ds(0, rows), pl.ds(0, 512)], mixed2.at[pl.ds(rows, rows), :]))
    for j, owner in enumerate(block_owners(d, core, True)):
        mixed2[pl.ds(0, rows), j * 128 : (j + 1) * 128] = mixed_win[
            own_at, pl.ds(pl.multiple_of(owner * 128, 128), 128)
        ]
    clock.work(4.0)

    cut = D // parts
    three = 3 * cut
    pairs = cut // (2 * HD)
    x = arena
    wo = slope.at[pl.ds(0, cut), :]
    load_x = lambda i: fetch(0, qkv.at[chunk(RING[i])], arena.at[pl.ds(0, window), pl.ds(0, three)])
    load_wo = lambda i: fetch(1, f_out.at[chunk(RING[i])], wo)
    load_att = lambda i: fetch(
        2, att2.at[:, pl.ds(pl.multiple_of(chunk(RING[i]) * cut, cut), cut)], act.at[:, pl.ds(0, cut)]
    )
    load_wi = lambda i: fetch(3, f_qkv.at[chunk(RING[i])], w_in)
    at_turned = fetch(6, lift_t, turned)
    at_x, at_wo, at_att, at_wi = load_x(0), load_wo(0), load_att(0), load_wi(0)
    exchanges[-1].wait_recv()
    scale = HD ** (-0.5)

    def take_halo():
        for sender, receiver, copy in halos:
            @pl.when(z == receiver)
            def _(copy=copy):
                copy.wait_recv()

    def grad_qkv_chunk(i):
        pending.pop(i).wait_recv()
        if i == 0:
            at_turned.wait()
        free_slot("qkv", i)

        def body(n, c):
            at = pl.ds(pl.multiple_of(n * 256, 256), 256)
            tile = jnp.dot(turned[...], up2[i, :, at], preferred_element_type=f32).astype(low)
            for j in range(4):
                put("qkv", i, j, (slice(None), at), tile[j * 128 : (j + 1) * 128])
            return c

        lax.fori_loop(0, three // 256, body, 0)
        launch("qkv", i)
        clock.work(1.8)

    for i in range(parts):
        at_att.wait()
        free_slot("out", i)
        tile = lax.dot_general(act[:, 0:cut], mixed2[...], TN, preferred_element_type=f32).astype(low)
        for j in range(4):
            put("out", i, j, (slice(None), slice(None)), tile[:, j * 128 : (j + 1) * 128])
        launch("out", i)
        clock.work(0.8)
        if i == 0:
            take_halo()
        at_wo.wait()

        def flow_body(n, c):
            at = pl.ds(pl.multiple_of(n * 512, 512), 512)
            x[at, three : three + cut] = lax.dot_general(
                mixed_win[at, :], wo[...], NT, preferred_element_type=f32
            ).astype(low)
            return c

        lax.fori_loop(0, window // 512, flow_body, 0)
        clock.work(1.5)
        if i:
            grad_qkv_chunk(i - 1)
        at_x.wait()
        if i == 0:
            exchanges[parts].wait_send()
        if i + 1 < parts:
            at_wo, at_att = load_wo(i + 1), load_att(i + 1)

        def attend_body(step, c):
            p, slot = step // 3, lax.rem(step, 3)
            lanes = lambda base: pl.ds(pl.multiple_of(base + p * 2 * HD, 2 * HD), 2 * HD)
            unit_at = [
                pl.ds(perm[slot * LONG + m] * UNIT, UNIT) for m in range(LONG)
            ]
            keys = jnp.concatenate([x[at, lanes(cut)] for at in unit_at], axis=0)
            values = jnp.concatenate([x[at, lanes(2 * cut)] for at in unit_at], axis=0)
            marks = jnp.concatenate([kf[at, :] for at in unit_at], axis=0)
            wide_keys = jnp.concatenate([keys, marks], axis=1)
            pair = jnp.concatenate([two_heads(x[at, lanes(0)]) for at in unit_at], axis=0)
            grads = jnp.concatenate([two_heads(x[at, lanes(three)]) for at in unit_at], axis=0)
            mark = jnp.concatenate([qf[at, :] for at in unit_at for _ in range(2)], axis=0)
            wide_pair = jnp.concatenate([pair, mark], axis=1)
            logsum = jnp.concatenate(
                [lse[chunk(RING[i]), pl.ds(step * LONG + m, 1), :] for m in range(LONG)], axis=1
            )
            scores = lax.dot_general(wide_keys, wide_pair, NT, preferred_element_type=f32)
            chances = jnp.exp(scores - logsum)
            flow = lax.dot_general(values, grads, NT, preferred_element_type=f32)
            terms = chances * flow
            slopes = (chances * (flow - jnp.sum(terms, axis=0, keepdims=True))).astype(low)
            v_sum = jnp.dot(chances.astype(low), grads, preferred_element_type=f32)
            k_sum = jnp.dot(slopes, pair, preferred_element_type=f32)
            flipped = lax.dot_general(keys, slopes, TN, preferred_element_type=f32)
            for m in range(LONG):
                two = slice(m * 2 * UNIT, (m + 1) * 2 * UNIT)
                at = pl.ds(pl.multiple_of(slot * LONG * UNIT + m * UNIT, UNIT), UNIT)
                y[at, lanes(0)] = (from_two(flipped[:, two]) * scale).astype(low)
            at = pl.ds(pl.multiple_of(slot * LONG * UNIT, UNIT), LONG * UNIT)
            y[at, lanes(cut)] = k_sum.astype(low)
            y[at, lanes(2 * cut)] = v_sum.astype(low)
            return c

        lax.fori_loop(0, pairs * 3, attend_body, 0, unroll=2)
        clock.work(10.5)
        if i + 1 < parts:
            at_x = load_x(i + 1)
        for u in range(FIRST_OWN, LAST_OWN + 1):
            at = pl.ds(back[u] * UNIT, UNIT)
            act[pl.ds((u - FIRST_OWN) * UNIT, UNIT), cut:] = y[at, :]
        exchanges[i].wait_send()
        inner_at = pl.ds(pl.multiple_of(offset - FIRST_OWN * UNIT, 16), rows)
        up2[i, pl.ds(0, rows), 0:three] = act[inner_at, cut:]
        pending[i] = exchange(
            parts + 1 + i, up2.at[i, pl.ds(0, rows), pl.ds(0, three)], up2.at[i, pl.ds(rows, rows), pl.ds(0, three)]
        )
        exchanges.append(pending[i])
        place = pl.multiple_of(chunk(RING[i]) * cut, cut)
        small[8:9, pl.ds(place, cut)] = jnp.sum(up2[i, pl.ds(0, rows), 0:cut].astype(f32), axis=0, keepdims=True)
        small[9:10, pl.ds(place, cut)] = jnp.sum(
            up2[i, pl.ds(0, rows), 2 * cut : three].astype(f32), axis=0, keepdims=True
        )
        at_wi.wait()

        def input_body(n, c, i=i):
            at = pl.ds(pl.multiple_of(n * 256, 256), 256)
            acc[:, at] += lax.dot_general(
                up2[i, pl.ds(0, rows), 0:three], w_in[at, :], NT, preferred_element_type=f32
            )
            return c

        lax.fori_loop(0, 4, input_body, 0)
        clock.work(2.0)
        if i + 1 < parts:
            at_wi = load_wi(i + 1)

    def last_body(begin, count, total):
        at = pl.ds(begin, count)
        value = acc[at, :]
        arena[at, :] = value.astype(low)
        return total + fold(value)

    total = jnp.sum(by_rows(rows, last_body, zero_row), axis=0, keepdims=True)
    store = fetch(4, arena.at[pl.ds(0, rows), :], input_grad)
    small[0:1, :] = total * small_in[15:16, :]
    small[1:2, :] = total
    clock.work(2.0)
    stages = [[partner], [(d ^ 2, z), (d ^ 4, z), (d ^ 6, z)], [(d, z ^ k) for k in (1, 2, 3)]]

    def small_stage(n, first_slot):
        sent = []
        for slot, device in enumerate(stages[n], first_slot):
            copy = pltpu.make_async_remote_copy(
                small, small_in_far.at[slot], small_send.at[slot], small_recv.at[slot],
                device_id=device, device_id_type=MESH,
            )
            copy.start()
            sent.append(copy)

        def take():
            for copy in sent:
                copy.wait()
            for slot in range(first_slot, first_slot + len(sent)):
                small[...] += small_in_far[slot]
            if n + 1 < len(stages):
                small_stage(n + 1, first_slot + len(sent))

        clock.send("c", 0.6e6, take)

    small_stage(0, 0)
    grad_qkv_chunk(parts - 1)
    clock.drain()
    assert sum(finished.values()) == 4 * parts
    small_out[...] = small[...]
    store.wait()
    for (g, i, kind), copy in hops.items():
        if kind or i >= 2:
            copy.wait_send()
    for copy in exchanges[parts + 1 :]:
        copy.wait_send()
    for sender, receiver, copy in halos:
        @pl.when(z == sender)
        def _(copy=copy):
            copy.wait_send()


def back_call(rows, window, parts, perm, back, vmem_in, hbm_in):
    f32, low = jnp.float32, jnp.bfloat16
    any_ = pl.BlockSpec(memory_space=pl.ANY)
    vmem = pl.BlockSpec(memory_space=pltpu.VMEM)
    smem = pl.BlockSpec(memory_space=pltpu.SMEM)
    cut = D // parts
    shapes = {"down": (D, 128), "up": (128, D), "out": (cut, 128), "qkv": (128, 3 * cut)}
    outs = [jax.ShapeDtypeStruct((rows, D), low)]
    outs += [jax.ShapeDtypeStruct(shape, f32) for shape in (shapes["qkv"], shapes["out"], shapes["up"], shapes["down"])]
    outs += [jax.ShapeDtypeStruct((16, D), f32)]
    order = ("down", "up", "out", "qkv")
    buffers = [pltpu.VMEM((2, 2) + shapes[g], low) for g in order]
    buffers += [pltpu.VMEM((parts, 2) + shapes[g], low) for g in order]
    buffers += [pltpu.VMEM((parts, 2) + shapes[g], low) for g in order]
    buffers += [pltpu.VMEM((parts,) + shapes[g], low) for g in order]
    buffers += [pltpu.VMEM((parts - 1,) + shapes[g], low) for g in order]
    dma = pltpu.SemaphoreType.DMA
    return pl.pallas_call(
        functools.partial(back_kernel, rows, window, parts),
        out_shape=outs,
        in_specs=[smem, smem] + [vmem] * len(vmem_in) + [any_] * len(hbm_in),
        out_specs=[any_] + [vmem] * 5,
        scratch_shapes=[
            pltpu.VMEM((rows, D), f32),
            pltpu.VMEM((rows, D), f32),
            pltpu.VMEM((512, 2 * rows), low),
            pltpu.VMEM((2 * D, D), low),
            pltpu.VMEM((2 * rows, D), low),
            pltpu.VMEM((rows, D), low),
            pltpu.VMEM((window, 3 * cut), low),
            pltpu.VMEM((parts, 2 * rows, D), low),
            pltpu.VMEM((D, 3 * cut), low),
            pltpu.VMEM((2 * rows, 512), low),
            pltpu.VMEM((window, D), low),
            pltpu.VMEM((16, D), f32),
            pltpu.VMEM((7, 16, D), f32),
        ]
        + buffers
        + [
            dma((7,)),
            dma((4, parts, 3)),
            dma((4, parts, 3)),
            dma((2 * parts + 1,)),
            dma((2 * parts + 1,)),
            dma((2,)),
            dma((2,)),
            dma((7,)),
            dma((7,)),
        ],
        compiler_params=pltpu.CompilerParams(
            collective_id=1, has_side_effects=True, vmem_limit_bytes=60 * 2**20 + 2**19
        ),
    )(perm, back, *vmem_in, *hbm_in)


def unit_order(segs, window):
    units = window // UNIT
    unit_seg = segs[::UNIT]
    index = lax.iota(jnp.int32, units)
    counts = jnp.sum((unit_seg[:, None] == unit_seg[None, :]).astype(jnp.int32), axis=1)
    short = jnp.where((counts == LONG) & (unit_seg >= 0) & (unit_seg < 1000), 0, 1) * units + index
    back = jnp.sum((short[None, :] < short[:, None]).astype(jnp.int32), axis=1)
    perm = jnp.sum(jnp.where(back[None, :] == index[:, None], index[None, :], 0), axis=1)
    return perm.astype(jnp.int32), back.astype(jnp.int32)


def marks_of(segs):
    lane = lax.iota(jnp.int32, 2 * HD)
    seg = jnp.where(segs < 0, 2 * HD - 1, jnp.where(segs >= 1000, 2 * HD - 2, segs))
    same = seg[:, None] == lane[None, :]
    keys = jnp.where(same, 1.0, 0.0).astype(jnp.bfloat16)
    queries = jnp.where(same, 0.0, -1e30).astype(jnp.bfloat16)
    return keys, queries


def local_body(
    tokens,
    cotangent,
    timesteps,
    item_lengths,
    w_qkv,
    bias_qv,
    w_out,
    w_up,
    bias_up,
    w_down,
    vectors,
):
    rows = tokens.shape[0]
    parts = lax.axis_size("mp")
    z = lax.axis_index("mp")
    low = jnp.bfloat16
    f32 = jnp.float32
    cut = D // parts
    firsts, offsets, ends = window_plan(rows, parts)
    window = -(-max(ends) // UNIT) * UNIT
    first_token = UNIT * pick(firsts, z)
    positions = first_token + lax.iota(jnp.int32, window)
    lengths_end = jnp.cumsum(item_lengths[0])
    segs = jnp.sum((positions[:, None] >= lengths_end[None, :]).astype(jnp.int32), axis=1)
    segs = jnp.where(positions < 0, -1, jnp.where(positions >= LEN, 1000, segs))
    perm, back = unit_order(segs, window)
    kf, qf = marks_of(segs)
    step_time = timesteps[0].astype(f32) * 0.001
    bias_q, bias_v = bias_qv[0].astype(f32), bias_qv[1].astype(f32)
    bias_row = jnp.concatenate([bias_q, jnp.zeros((cut,), f32), bias_v, jnp.zeros((D - 3 * cut,), f32)])
    biases = jnp.concatenate([jnp.stack([bias_up.astype(f32), bias_row]), jnp.zeros((6, D), f32)])
    rows16 = jnp.concatenate(
        [vectors, (step_time * vectors[0])[None], jnp.full((7, D), step_time, f32)], axis=0
    )
    (
        f_qkv, f_out, f_up, f_down, qkv, lse, att2, act2, slope, first_t, lift_t, sec2, normed_one,
        second_low, second_grads, output, inverse_one, small_in,
    ) = fore_call(
        rows, window, parts, perm, back, tokens, cotangent,
        w_qkv.reshape(D, 3 * cut), w_out, w_up, w_down, biases, rows16, kf, qf,
    )
    input_grad, grad_qkv, grad_out, grad_up, grad_down, small = back_call(
        rows, window, parts, perm, back,
        (second_low, sec2, inverse_one, vectors[4:5], small_in, kf, qf, lse),
        (first_t, lift_t, second_grads, normed_one, act2, slope, att2, qkv, f_qkv, f_out, f_up, f_down),
    )
    grad_bias_qv = lax.dynamic_slice_in_dim(small[8:10], z * cut, cut, 1)
    grad_bias_up = lax.dynamic_slice_in_dim(small[10:14].reshape(FF), z * (FF // parts), FF // parts, 0)
    return (
        output,
        input_grad,
        grad_qkv.reshape(-1, 3, cut),
        grad_bias_qv,
        grad_out,
        grad_up,
        grad_bias_up,
        grad_down,
        small[:8],
    )


def solution(mesh):
    in_specs = (
        P(("dp", "mp"), None),
        P(("dp", "mp"), None),
        P("dp"),
        P("dp", None),
        P(None, None, "mp"),
        P(None, "mp"),
        P("mp", None),
        P(None, "mp"),
        P("mp"),
        P("mp", None),
        P(),
    )
    out_specs = (
        P(("dp", "mp"), None),
        P(("dp", "mp"), None),
        P("dp", None, "mp"),
        P(None, "mp"),
        P("mp", "dp"),
        P("dp", "mp"),
        P("mp"),
        P("mp", "dp"),
        P(),
    )
    chosen = local_body if fits_local(mesh) else body
    return jax.shard_map(chosen, mesh=mesh, in_specs=in_specs, out_specs=out_specs, check_vma=False)
```

```python
import functools
import heapq

import jax
import jax.numpy as jnp
from jax import lax
from jax.experimental import pallas as pl
from jax.experimental.pallas import tpu as pltpu
from jax.sharding import PartitionSpec as P

D = 1024
HD = 64
FF = 4096
LEN = 2368


def norm_forward(value, gain, shift):
    average = jnp.mean(value, axis=-1, keepdims=True)
    centred = value - average
    inverse = lax.rsqrt(jnp.mean(centred * centred, axis=-1, keepdims=True) + 1e-05)
    normed = centred * inverse
    return (normed * gain + shift, normed, inverse)


def norm_backward(grad, normed, inverse, gain):
    scaled = grad * gain
    result = inverse * (
        scaled
        - jnp.mean(scaled, axis=-1, keepdims=True)
        - normed * jnp.mean(scaled * normed, axis=-1, keepdims=True)
    )
    return (result, jnp.sum(grad * normed, axis=0), jnp.sum(grad, axis=0))


def gelu_exact(value):
    return jax.nn.gelu(value, approximate=False)


def attend_forward(queries, keys, values, segments):
    scale = HD ** (-0.5)
    block_rows = LEN // 4

    def one_block(inputs):
        query_block, segment_block = inputs
        scores = (
            jnp.einsum("bhe,khe->hbk", query_block, keys, preferred_element_type=jnp.float32)
            * scale
        )
        allowed = segment_block[:, None] == segments[None, :]
        scores = jnp.where(allowed[None], scores, -1e30)
        highest = jnp.max(scores, axis=-1, keepdims=True)
        weights = jnp.exp(scores - highest)
        totals = jnp.sum(weights, axis=-1, keepdims=True)
        chances_low = (weights / totals).astype(jnp.bfloat16)
        result = jnp.einsum("hbk,khe->bhe", chances_low, values, preferred_element_type=jnp.float32)
        return (result.astype(jnp.bfloat16), (highest + jnp.log(totals))[..., 0])

    blocks = queries.reshape(4, block_rows, queries.shape[1], queries.shape[2])
    results, logsums = lax.map(one_block, (blocks, segments.reshape(4, block_rows)))
    return (results.reshape(queries.shape), logsums)


def attend_backward(queries, keys, values, out_grads, logsums, segments):
    scale = HD ** (-0.5)
    block_rows = LEN // 4

    def one_block(carry, inputs):
        key_grads, value_grads = carry
        query_block, grad_block, logsum_block, segment_block = inputs
        scores = (
            jnp.einsum("bhe,khe->hbk", query_block, keys, preferred_element_type=jnp.float32)
            * scale
        )
        allowed = segment_block[:, None] == segments[None, :]
        scores = jnp.where(allowed[None], scores, -1e30)
        chances = jnp.exp(scores - logsum_block[..., None])
        chances_low = chances.astype(jnp.bfloat16)
        value_grads = value_grads + jnp.einsum(
            "hbk,bhe->khe", chances_low, grad_block, preferred_element_type=jnp.float32
        )
        flow = jnp.einsum("bhe,khe->hbk", grad_block, values, preferred_element_type=jnp.float32)
        inner = jnp.sum(chances * flow, axis=-1, keepdims=True)
        score_grads = (chances * (flow - inner)).astype(jnp.bfloat16)
        query_grads = (
            jnp.einsum("hbk,khe->bhe", score_grads, keys, preferred_element_type=jnp.float32)
            * scale
        )
        key_grads = (
            key_grads
            + jnp.einsum(
                "hbk,bhe->khe", score_grads, query_block, preferred_element_type=jnp.float32
            )
            * scale
        )
        return ((key_grads, value_grads), query_grads)

    shape_blocks = (4, block_rows, queries.shape[1], queries.shape[2])
    zeros = jnp.zeros(keys.shape, jnp.float32)
    (key_grads, value_grads), query_grads = lax.scan(
        one_block,
        (zeros, zeros),
        (
            queries.reshape(shape_blocks),
            out_grads.reshape(shape_blocks),
            logsums,
            segments.reshape(4, block_rows),
        ),
    )
    return (query_grads.reshape(queries.shape), key_grads, value_grads)


def body(
    tokens,
    cotangent,
    timesteps,
    item_lengths,
    w_qkv,
    bias_qv,
    w_out,
    w_up,
    bias_up,
    w_down,
    vectors,
):
    rows = tokens.shape[0]
    total = rows * lax.axis_size("mp")
    seq_count = timesteps.shape[0]
    local_width = w_qkv.shape[2]
    local_hidden = w_up.shape[1]
    local_heads = local_width // HD
    my_index = lax.axis_index("mp")
    row_ids = my_index * rows + lax.iota(jnp.int32, rows)
    row_owner = row_ids // LEN
    step_times = timesteps.astype(jnp.float32) * 0.001
    time_rows = jnp.sum(
        jnp.where(
            row_owner[:, None] == lax.iota(jnp.int32, seq_count)[None, :], step_times[None, :], 0.0
        ),
        axis=1,
    )
    ends = jnp.cumsum(item_lengths, axis=1)
    segments = jnp.sum(
        (lax.iota(jnp.int32, LEN)[None, :, None] >= ends[:, None, :]).astype(jnp.int32), axis=2
    )
    lifted = tokens.astype(jnp.float32) + time_rows[:, None] * vectors[0] + vectors[1]
    gathered = lax.all_gather(lifted.astype(jnp.bfloat16), "mp", axis=0, tiled=True)
    projected = jnp.einsum("td,dce->cte", gathered, w_qkv, preferred_element_type=jnp.float32)
    shaped = (seq_count, LEN, local_heads, HD)
    head_query = (projected[0] + bias_qv[0]).astype(jnp.bfloat16).reshape(shaped)
    head_key = projected[1].astype(jnp.bfloat16).reshape(shaped)
    head_value = (projected[2] + bias_qv[1]).astype(jnp.bfloat16).reshape(shaped)
    attended, logsums = lax.map(
        lambda items: attend_forward(*items), (head_query, head_key, head_value, segments)
    )
    attended = attended.reshape(total, local_width)
    piece = attended
    mixed = (
        lax.psum_scatter(
            jnp.dot(piece, w_out, preferred_element_type=jnp.float32),
            "mp",
            scatter_dimension=0,
            tiled=True,
        )
        + vectors[2]
    )
    first, normed_one, inverse_one = norm_forward(lifted + mixed, vectors[4], vectors[5])
    hidden_all = lax.all_gather(first.astype(jnp.bfloat16), "mp", axis=0, tiled=True)
    upper = jnp.dot(hidden_all, w_up, preferred_element_type=jnp.float32) + bias_up
    activated, gelu_pull = jax.vjp(gelu_exact, upper)
    activated = activated.astype(jnp.bfloat16)
    piece = activated
    down = (
        lax.psum_scatter(
            jnp.dot(piece, w_down, preferred_element_type=jnp.float32).astype(jnp.bfloat16),
            "mp",
            scatter_dimension=0,
            tiled=True,
        ).astype(jnp.float32)
        + vectors[3]
    )
    output, normed_two, inverse_two = norm_forward(first + down, vectors[6], vectors[7])
    out_grads = cotangent.astype(jnp.float32)
    second_grads, gain_two, shift_two = norm_backward(
        out_grads, normed_two, inverse_two, vectors[6]
    )
    down_all = lax.all_gather(second_grads.astype(jnp.bfloat16), "mp", axis=0, tiled=True)
    grad_down = jnp.einsum("tf,td->fd", activated, down_all, preferred_element_type=jnp.float32)
    act_grads = jnp.einsum("td,fd->tf", down_all, w_down, preferred_element_type=jnp.float32)
    (upper_grads,) = gelu_pull(act_grads)
    upper_low = upper_grads.astype(jnp.bfloat16)
    grad_bias_up = jnp.sum(upper_low, axis=0, dtype=jnp.float32)
    grad_up = jnp.einsum("td,tf->df", hidden_all, upper_low, preferred_element_type=jnp.float32)
    piece = upper_low
    first_part = lax.psum_scatter(
        jnp.einsum("tf,df->td", piece, w_up, preferred_element_type=jnp.float32).astype(
            jnp.bfloat16
        ),
        "mp",
        scatter_dimension=0,
        tiled=True,
    ).astype(jnp.float32)
    first_grads = second_grads + first_part
    mixed_grads, gain_one, shift_one = norm_backward(
        first_grads, normed_one, inverse_one, vectors[4]
    )
    mixed_all = lax.all_gather(mixed_grads.astype(jnp.bfloat16), "mp", axis=0, tiled=True)
    grad_out = jnp.einsum("te,td->ed", attended, mixed_all, preferred_element_type=jnp.float32)
    attended_grads = jnp.einsum(
        "td,ed->te", mixed_all, w_out, preferred_element_type=jnp.float32
    ).astype(jnp.bfloat16)
    query_grads, key_grads, value_grads = lax.map(
        lambda items: attend_backward(*items),
        (head_query, head_key, head_value, attended_grads.reshape(shaped), logsums, segments),
    )
    qkv_low = jnp.stack(
        [
            query_grads.reshape(total, local_width),
            key_grads.reshape(total, local_width),
            value_grads.reshape(total, local_width),
        ],
        axis=1,
    ).astype(jnp.bfloat16)
    grad_bias_qv = jnp.sum(qkv_low[:, 0::2], axis=0, dtype=jnp.float32)
    grad_qkv = jnp.einsum("td,tcf->dcf", gathered, qkv_low, preferred_element_type=jnp.float32)
    piece = qkv_low
    input_part = lax.psum_scatter(
        jnp.einsum("tcf,dcf->td", piece, w_qkv, preferred_element_type=jnp.float32).astype(
            jnp.bfloat16
        ),
        "mp",
        scatter_dimension=0,
        tiled=True,
    ).astype(jnp.float32)
    input_sum = mixed_grads + input_part
    vector_terms = jnp.stack(
        [
            jnp.sum(time_rows[:, None] * input_sum, axis=0),
            jnp.sum(input_sum, axis=0),
            jnp.sum(mixed_grads, axis=0),
            jnp.sum(second_grads, axis=0),
            gain_one,
            shift_one,
            gain_two,
            shift_two,
        ],
        axis=0,
    )
    zero_index = jnp.zeros((), jnp.int32)
    qv_start = my_index * local_width
    up_start = my_index * local_hidden
    qv_placed = lax.dynamic_update_slice(
        jnp.zeros((2, D), jnp.float32), grad_bias_qv, (zero_index, qv_start)
    )
    up_placed = lax.dynamic_update_slice(jnp.zeros((FF,), jnp.float32), grad_bias_up, (up_start,))
    grad_qkv, grad_out, grad_up, grad_down = (
        lax.psum_scatter(
            grad_qkv.astype(jnp.bfloat16), "dp", scatter_dimension=0, tiled=True
        ).astype(jnp.float32),
        lax.psum_scatter(
            grad_out.astype(jnp.bfloat16), "dp", scatter_dimension=1, tiled=True
        ).astype(jnp.float32),
        lax.psum_scatter(
            grad_up.astype(jnp.bfloat16), "dp", scatter_dimension=0, tiled=True
        ).astype(jnp.float32),
        lax.psum_scatter(
            grad_down.astype(jnp.bfloat16), "dp", scatter_dimension=1, tiled=True
        ).astype(jnp.float32),
    )
    grad_vectors, qv_summed, up_summed = lax.psum(
        (vector_terms, qv_placed, up_placed), ("dp", "mp")
    )
    grad_bias_qv = lax.dynamic_slice_in_dim(qv_summed, qv_start, local_width, 1)
    grad_bias_up = lax.dynamic_slice_in_dim(up_summed, up_start, local_hidden, 0)
    return (
        output.astype(jnp.bfloat16),
        input_sum.astype(jnp.bfloat16),
        grad_qkv,
        grad_bias_qv,
        grad_out,
        grad_up,
        grad_bias_up,
        grad_down,
        grad_vectors,
    )


UNIT = 128
LONG = 4
MESH = pl.DeviceIdType.MESH


def fits_local(mesh):
    parts = mesh.shape["mp"]
    return mesh.shape["dp"] == 8 and parts == 4 and LEN % (16 * parts) == 0


def window_plan(rows, parts):
    firsts = [(rows * j) // UNIT - (LONG - 1) for j in range(parts)]
    offsets = [rows * j - UNIT * first for j, first in enumerate(firsts)]
    ends = [
        ((rows * (j + 1) - 1) // UNIT + LONG - firsts[j]) * UNIT for j in range(parts)
    ]
    return firsts, offsets, ends


def pick(table, index):
    value = jnp.int32(table[0])
    for j in range(1, len(table)):
        value = jnp.where(index == j, jnp.int32(table[j]), value)
    return value


NT = (((1,), (1,)), ((), ()))
TN = (((0,), (0,)), ((), ()))
FIRST_OWN, LAST_OWN = LONG - 1, LONG + 4


def two_heads(block):
    lane = lax.broadcasted_iota(jnp.int32, block.shape, 1)
    zero = jnp.zeros_like(block)
    return jnp.concatenate(
        [jnp.where(lane < HD, block, zero), jnp.where(lane < HD, zero, block)], axis=0
    )


def from_two(flipped):
    both = jnp.concatenate([flipped[:HD, :UNIT], flipped[HD:, UNIT:]], axis=0)
    return both.T


def by_rows(rows, body, carry):
    count = rows // 32

    def step(i, c):
        return body(pl.multiple_of(i * 32, 32), 32, c)

    carry = lax.fori_loop(0, count, step, carry)
    return body(count * 32, rows - count * 32, carry) if rows % 32 else carry


def fold(value):
    return value if value.shape[0] == 16 else value[:16] + value[16:]


class Clock:
    def __init__(self, rate):
        self.rate = {"c": 400e3, "x": rate, "y": rate, "z": rate}
        self.now = 0.0
        self.free = {}
        self.queue = []
        self.count = 0

    def send(self, link, size, action, share=1.0):
        begin = max(self.now, self.free.get(link, 0.0))
        end = begin + share * size / self.rate[link]
        self.free[link] = end
        self.count += 1
        heapq.heappush(self.queue, (end + 1.5, self.count, action))

    def work(self, time):
        self.now += time
        while self.queue and self.queue[0][0] <= self.now:
            heapq.heappop(self.queue)[2]()

    def step(self):
        ready, _, action = heapq.heappop(self.queue)
        self.now = max(self.now, ready)
        action()

    def drain(self):
        while self.queue:
            self.step()


def block_owners(d, core, x_first):
    x, y = lax.rem(d // 2, 2), d // 4
    if x_first:
        return [4 * b + 2 * a + core for a in (1 - x, x) for b in (1 - y, y)]
    return [4 * b + 2 * a + core for b in (1 - y, y) for a in (1 - x, x)]


RING = (2, 3, 1, 0)
HALO_TIME = 25.0


def fore_kernel(
    rows, window, parts, perm, back, tokens, cotangent, w_qkv, w_out, w_up, w_down, biases, vectors, kf, qf,
    f_qkv, f_out, f_up, f_down, qkv, lse, att2, act2, slopes, first_t, lift_t, sec2, normed_out, second_low,
    second_grads, output, inverse, small,
    win, xq, yq, own_rows, attended, mixed, first, first_low, down, in_low, out_low, wu, wd, wq, wo, act, slope, lift2, first2,
    turned, stage, bias_all, send, recv, own_sent, near, far, own, bias_send, bias_recv, local, pair_send, pair_recv,
):
    f32, low = jnp.float32, jnp.bfloat16
    d = lax.axis_index("dp")
    z = lax.axis_index("mp")
    core = lax.rem(d, 2)
    cut = D // parts
    three = 3 * cut
    pairs = cut // (2 * HD)
    firsts, offsets, ends = window_plan(rows, parts)
    offset = pl.multiple_of(pick(offsets, z), 16)
    shards = (w_qkv, w_out, w_up, w_down)
    fulls = (f_qkv, f_out, f_up, f_down)
    sizes = tuple(shard.shape[0] // 8 for shard in shards)
    partner = (d ^ 1, z)
    peers = [(d, z ^ k) for k in (1, 2, 3)] + [partner, (d ^ 2, z), (d ^ 4, z)]
    barrier = pltpu.get_barrier_semaphore()
    for peer in peers:
        pl.semaphore_signal(barrier, inc=1, device_id=peer, device_id_type=MESH)
    pl.semaphore_wait(barrier, len(peers))
    clock = Clock(44e3)

    order = [sorted((o for o in range(parts) if o != j), key=lambda o: (abs(o - j), o)) for j in range(parts)]
    source = [pick([order[j][n] for j in range(parts)], z) for n in range(parts - 1)]
    chunks = [(g, n) for n in range(parts - 1) for g in (0, 1)] + [(g, n) for n in range(parts - 1) for g in (2, 3)]
    index_of = {chunk: i for i, chunk in enumerate(chunks)}
    copies, done = {}, {}

    def part(ref, index, owner, size, half=None):
        start, count = owner * size, size
        if half is not None:
            count = size // 2
            start = start + half * count
        return ref.at[index, pl.ds(pl.multiple_of(start, 16), count), :]

    def remote(i, kind, src, dst, target):
        copy = pltpu.make_async_remote_copy(
            src, dst, send.at[i, kind], recv.at[i, kind], device_id=target, device_id_type=MESH
        )
        copy.start()
        copies[i, kind] = copy

    def place(i, owner, half=None):
        g, n = chunks[i]
        return part(fulls[g], source[n], owner, sizes[g], half)

    def bytes_of(i):
        g, n = chunks[i]
        return sizes[g] * shards[g].shape[1] * 2

    def pass_on(i, kind, owner, target, half=None):
        remote(i, kind, place(i, owner, half), place(i, owner, half), target)

    column = []

    def along(owner, place_of, here, there, sent, g):
        i = index_of[g, order[there].index(owner)]
        copy = pltpu.make_async_remote_copy(
            place_of, part(fulls[g], owner, d, sizes[g]), sent, recv.at[i, 0],
            device_id=(d, there), device_id_type=MESH,
        )

        @pl.when(z == here)
        def _():
            copy.start()

        column.append((here, copy))

    def send_own(g):
        rows_at = pl.ds(pl.multiple_of(d * sizes[g], 16), sizes[g])
        for here in range(parts):
            for n, there in enumerate((here - 1, here + 1)):
                if 0 <= there < parts:
                    along(here, shards[g].at[rows_at, :], here, there, own_sent.at[g, n], g)
        for n in range(parts - 1):
            i = index_of[g, n]
            clock.send("z", bytes_of(i), lambda i=i: hop_two(i))

    def hop_two(i):
        g, n = chunks[i]
        pltpu.make_async_remote_copy(
            place(i, d), place(i, d), send.at[i, 0], recv.at[i, 0], device_id=partner, device_id_type=MESH
        ).wait_recv()
        for here in range(parts):
            owner = order[here][n]
            there = here + 1 if owner < here else here - 1
            if 0 <= there < parts:
                along(owner, part(fulls[g], owner, d, sizes[g]), here, there, send.at[i, 0], g)
        if g == 2 and n == 0:
            send_own(3)
        pass_on(i, 1, d, (d ^ 2, z))
        pass_on(i, 2, d, (d ^ 4, z))
        pass_on(i, 5, d, partner)
        clock.send("c", bytes_of(i), lambda: None)
        clock.send("x", bytes_of(i), lambda: hop_three(i))
        clock.send("y", bytes_of(i), lambda: hop_four(i))

    def hop_three(i):
        copies[i, 1].wait_recv()
        pass_on(i, 3, d ^ 2, (d ^ 4, z), 0)
        pass_on(i, 6, d ^ 2, partner)
        clock.send("y", bytes_of(i) // 2, lambda: hop_five(i))

    def hop_four(i):
        copies[i, 2].wait_recv()
        pass_on(i, 4, d ^ 4, (d ^ 2, z), 1)
        pass_on(i, 7, d ^ 4, partner)
        clock.send("x", bytes_of(i) // 2, lambda: hop_six(i))

    def hop_five(i):
        copies[i, 3].wait_recv()
        pass_on(i, 8, d ^ 6, partner, 0)
        finish(i)

    def hop_six(i):
        copies[i, 4].wait_recv()
        pass_on(i, 9, d ^ 6, partner, 1)
        finish(i)

    def finish(i):
        done[i] = done.get(i, 0) + 1

    def arrive(i):
        while done.get(i, 0) < 2:
            clock.step()
        for kind in range(5, 10):
            copies[i, kind].wait_recv()

    halos = []
    for j in range(parts - 1):
        count = ends[j] - offsets[j] - rows
        halos.append((j + 1, j, pltpu.make_async_remote_copy(
            tokens.at[pl.ds(0, count), :], win.at[pl.ds(offsets[j] + rows, count), :],
            near.at[0], near.at[1], device_id=(d, j), device_id_type=MESH,
        )))
    for j in range(1, parts):
        halos.append((j - 1, j, pltpu.make_async_remote_copy(
            tokens.at[pl.ds(rows - offsets[j], offsets[j]), :], win.at[pl.ds(0, offsets[j]), :],
            far.at[0], far.at[1], device_id=(d, j), device_id_type=MESH,
        )))
    for sender, receiver, copy in halos:
        @pl.when(z == sender)
        def _(copy=copy):
            copy.start()
    clock.send("z", max(offsets) * D * 2, lambda: None)
    send_own(0)
    send_own(1)
    bias_copies = []
    for k in (1, 2, 3):
        copy = pltpu.make_async_remote_copy(
            biases, bias_all.at[z], bias_send.at[k - 1], bias_recv.at[k - 1], device_id=(d, z ^ k), device_id_type=MESH
        )
        copy.start()
        bias_copies.append(copy)
    bias_all[pl.ds(z, 1)] = biases[...][None]
    owns = []
    for g in range(4):
        copy = pltpu.make_async_copy(shards[g], fulls[g].at[z], own.at[g])
        copy.start()
        owns.append(copy)

    def lift(value):
        return value.astype(f32) + vectors[8:9, :] + vectors[1:2, :]

    def own_body(i, c):
        at = pl.ds(pl.multiple_of(i * 16, 16), 16)
        win[pl.ds(pl.multiple_of(offset + i * 16, 16), 16), :] = lift(tokens[at, :]).astype(low)
        return c

    lax.fori_loop(0, rows // 16, own_body, 0)
    zero = jnp.zeros((16, D), low)

    def spans_of(j):
        end = ends[j] if j < parts - 1 else offsets[j] + rows
        empty = [(0, offsets[0])] if j == 0 else []
        if end < window:
            empty.append((end, window))
        filled = [(0, offsets[j])] if j else []
        if j < parts - 1:
            filled.append((offsets[j] + rows, ends[j]))
        return empty, filled

    for j in range(parts):
        @pl.when(z == j)
        def _(j=j):
            for begin, end in spans_of(j)[0]:
                def clear(i, c, begin=begin):
                    win[pl.ds(pl.multiple_of(begin + i * 16, 16), 16), :] = zero
                    return c
                lax.fori_loop(0, (end - begin) // 16, clear, 0)

    pair_copies = []

    def exchange(source, target):
        index = len(pair_copies)
        copy = pltpu.make_async_remote_copy(
            source, target, pair_send.at[index], pair_recv.at[index], device_id=partner, device_id_type=MESH
        )
        copy.start()
        pair_copies.append(copy)
        return copy

    def columns(read, c, write):
        for j, owner in enumerate(block_owners(d, c, True)):
            write(slice(j * 128, (j + 1) * 128), read(pl.ds(pl.multiple_of(owner * 128, 128), 128)))

    own_at = pl.ds(offset, rows)
    mine = pl.ds(0, rows)
    theirs = pl.ds(rows, rows)
    columns(lambda at: win[own_at, at], 1 - core, lambda at, v: stage.__setitem__((0, slice(None), at), v))
    lift_copy = exchange(stage.at[0], lift2.at[theirs, :])
    columns(lambda at: win[own_at, at], core, lambda at, v: lift2.__setitem__((mine, at), v))

    def fetch(index, source, target):
        copy = pltpu.make_async_copy(source, target, local.at[index])
        copy.start()
        return copy

    clock.work(4.0)
    for copy in bias_copies:
        copy.wait_recv()
    clock.work(max(0.0, HALO_TIME - clock.now))
    for sender, receiver, copy in halos:
        @pl.when(z == receiver)
        def _(copy=copy):
            copy.wait_recv()
    send_own(2)
    for j in range(parts):
        @pl.when(z == j)
        def _(j=j):
            for begin, end in spans_of(j)[1]:
                def convert(i, c, begin=begin):
                    at = pl.ds(pl.multiple_of(begin + i * 16, 16), 16)
                    win[at, :] = lift(win[at, :]).astype(low)
                    return c
                lax.fori_loop(0, (end - begin) // 16, convert, 0)
    clock.work(2.0)
    lift_copy.wait_recv()
    turned[...] = lift2[...].T
    turned_out = fetch(0, turned, lift_t)
    clock.work(2.0)

    stores = {}
    for i in range(parts):
        k = i
        at_z = source[i - 1] if i else z
        if k == 0:
            wq_ref, wo_ref = w_qkv, w_out
        else:
            wq_ref, wo_ref = wq, wo
            load_q.wait()
        slot_i = i % 2
        if i >= 2:
            stores[i - 2].wait()
        row = bias_all.at[at_z]

        def project(n, c):
            at = pl.ds(pl.multiple_of(n * 512, 512), 512)
            for c3 in range(3):
                lanes = slice(c3 * cut, (c3 + 1) * cut)
                value = jnp.dot(win[at, :], wq_ref[:, lanes], preferred_element_type=f32)
                value = (value + row[1:2, lanes]).astype(low)
                if c3 == 0:
                    value = value * jnp.array(HD ** (-0.5), low)
                xq[slot_i, at, lanes] = value
            return c

        lax.fori_loop(0, window // 512, project, 0)
        stores[i] = fetch(3 + slot_i, xq.at[slot_i], qkv.at[at_z])
        clock.work(3.5)
        if i + 1 < parts:
            arrive(index_of[0, i])
            load_q = fetch(1, f_qkv.at[source[i]], wq)

        def attend(step, c):
            p, slot = step // 3, lax.rem(step, 3)
            lanes = lambda base: pl.ds(pl.multiple_of(base + p * 2 * HD, 2 * HD), 2 * HD)
            unit_at = [pl.ds(perm[slot * LONG + m] * UNIT, UNIT) for m in range(LONG)]
            keys = jnp.concatenate([xq[slot_i, at, lanes(cut)] for at in unit_at], axis=0)
            values = jnp.concatenate([xq[slot_i, at, lanes(2 * cut)] for at in unit_at], axis=0)
            marks = jnp.concatenate([kf[at, :] for at in unit_at], axis=0)
            wide_keys = jnp.concatenate([keys, marks], axis=1)
            pair = jnp.concatenate([two_heads(xq[slot_i, at, lanes(0)]) for at in unit_at], axis=0)
            mark = jnp.concatenate([qf[at, :] for at in unit_at for _ in range(2)], axis=0)
            wide_pair = jnp.concatenate([pair, mark], axis=1)
            scores = lax.dot_general(wide_keys, wide_pair, NT, preferred_element_type=f32)
            highest = jnp.max(scores, axis=0, keepdims=True)
            weights = jnp.exp(scores - highest)
            total = jnp.sum(weights, axis=0, keepdims=True)
            flipped = lax.dot_general(values, weights.astype(low), TN, preferred_element_type=f32) * (1.0 / total)
            logsum = highest + jnp.log(total)
            for m in range(LONG):
                two = slice(m * 2 * UNIT, (m + 1) * 2 * UNIT)
                at = pl.ds(pl.multiple_of(slot * LONG * UNIT + m * UNIT, UNIT), UNIT)
                yq[at, lanes(0)] = from_two(flipped[:, two]).astype(low)
                lse[at_z, pl.ds(step * LONG + m, 1), :] = logsum[:, two]
            return c

        lax.fori_loop(0, pairs * 3, attend, 0, unroll=2)
        clock.work(7.5)
        for u in range(FIRST_OWN, LAST_OWN + 1):
            own_rows[pl.ds((u - FIRST_OWN) * UNIT, UNIT), :] = yq[pl.ds(back[u] * UNIT, UNIT), :]
        lanes_z = pl.ds(pl.multiple_of(at_z * cut, cut), cut)
        attended[i] = own_rows[pl.ds(pl.multiple_of(offset - FIRST_OWN * UNIT, 16), rows), :]
        exchange(attended.at[i], att2.at[theirs, lanes_z])
        stores["a", i] = fetch(5 + i, attended.at[i], att2.at[mine, lanes_z])
        if k:
            load_o.wait()

        def out_body(n, c):
            at = pl.ds(pl.multiple_of(n * 256, 256), 256)
            value = jnp.dot(attended[i], wo_ref[:, at], preferred_element_type=f32)
            if i == 0:
                mixed[:, at] = value
            else:
                mixed[:, at] += value
            return c

        lax.fori_loop(0, D // 256, out_body, 0)
        clock.work(1.5)
        if i + 1 < parts:
            arrive(index_of[1, i])
            load_o = fetch(2, f_out.at[source[i]], wo)

    def norm_one(begin, count, c):
        at = pl.ds(begin, count)
        value = lift(tokens[at, :]) + (mixed[at, :] + vectors[2:3, :])
        centred = value - jnp.mean(value, axis=-1, keepdims=True)
        scale = lax.rsqrt(jnp.mean(centred * centred, axis=-1, keepdims=True) + 1e-05)
        normed = centred * scale
        mixed[at, :] = normed
        inverse[at, :] = scale
        result = normed * vectors[4:5, :] + vectors[5:6, :]
        first[at, :] = result
        first_low[at, :] = result.astype(low)
        return c

    by_rows(rows, norm_one, 0)
    normed_store = fetch(9, mixed, normed_out)
    columns(lambda at: first_low[:, at], 1 - core, lambda at, v: stage.__setitem__((1, slice(None), at), v))
    first_copy = exchange(stage.at[1], first2.at[theirs, :])
    columns(lambda at: first_low[:, at], core, lambda at, v: first2.__setitem__((mine, at), v))
    clock.work(4.0)

    for i in range(parts):
        k = i
        at_z = source[i - 1] if i else z
        slot_i = i % 2
        if k == 0:
            up_ref, down_ref = w_up, w_down
        else:
            up_ref, down_ref = wu, wd
            load_u.wait()
        if i >= 2:
            for copy in stores["f", i - 2]:
                copy.wait()
            stores["r", i - 2].wait_send()
        row = bias_all.at[at_z]

        def upper_body(n, c):
            at = pl.ds(pl.multiple_of(n * 256, 256), 256)
            value = jnp.dot(first_low[...], up_ref[:, at], preferred_element_type=f32) + row[0:1, at]
            chance = 0.5 + 0.5 * lax.erf(value * (0.5**0.5))
            act[slot_i, :, at] = (value * chance).astype(low)
            density = jnp.exp(-0.5 * value * value) * (0.5 / jnp.pi) ** 0.5
            slope[slot_i, :, at] = (chance + value * density).astype(low)
            return c

        lax.fori_loop(0, D // 256, upper_body, 0)
        hidden = pl.ds(pl.multiple_of(at_z * D, D), D)
        stores["r", i] = exchange(act.at[slot_i], act2.at[theirs, hidden])
        stores["f", i] = (
            fetch(14 + slot_i, act.at[slot_i], act2.at[mine, hidden]),
            fetch(10 + slot_i, slope.at[slot_i], slopes.at[:, hidden]),
        )
        clock.work(4.0)
        if i + 1 < parts:
            arrive(index_of[2, i])
            load_u = fetch(1, f_up.at[source[i]], wu)
        if k:
            load_d.wait()

        def down_body(n, c):
            at = pl.ds(pl.multiple_of(n * 256, 256), 256)
            value = jnp.dot(act[slot_i], down_ref[:, at], preferred_element_type=f32)
            if i == 0:
                down[:, at] = value
            else:
                down[:, at] += value
            return c

        lax.fori_loop(0, D // 256, down_body, 0)
        clock.work(2.0)
        if i + 1 < parts:
            arrive(index_of[3, i])
            load_d = fetch(2, f_down.at[source[i]], wd)
        if i == 0:
            first_copy.wait_recv()
            turned_out.wait()
            turned[...] = first2[...].T
            turned_out = fetch(0, turned, first_t)
            clock.work(2.0)

    zero_row = jnp.zeros((16, D), f32)

    def norm_two(begin, count, sums):
        at = pl.ds(begin, count)
        value = first[at, :] + (down[at, :] + vectors[3:4, :])
        centred = value - jnp.mean(value, axis=-1, keepdims=True)
        scale = lax.rsqrt(jnp.mean(centred * centred, axis=-1, keepdims=True) + 1e-05)
        normed = centred * scale
        out_low[at, :] = (normed * vectors[6:7, :] + vectors[7:8, :]).astype(low)
        grads = cotangent[at, :].astype(f32)
        scaled = grads * vectors[6:7, :]
        result = scale * (
            scaled
            - jnp.mean(scaled, axis=-1, keepdims=True)
            - normed * jnp.mean(scaled * normed, axis=-1, keepdims=True)
        )
        down[at, :] = result
        in_low[at, :] = result.astype(low)
        return (sums[0] + fold(result), sums[1] + fold(grads * normed), sums[2] + fold(grads))

    sums = by_rows(rows, norm_two, (zero_row, zero_row, zero_row))
    last = [fetch(1, out_low, output), fetch(2, in_low, second_low), fetch(12, down, second_grads)]
    small[...] = jnp.zeros_like(small)
    small[3:4, :] = jnp.sum(sums[0], axis=0, keepdims=True)
    small[6:7, :] = jnp.sum(sums[1], axis=0, keepdims=True)
    small[7:8, :] = jnp.sum(sums[2], axis=0, keepdims=True)
    small[15:16, :] = vectors[9:10, :]
    columns(lambda at: in_low[:, at], 1 - core, lambda at, v: stage.__setitem__((2, slice(None), at), v))
    exchange(stage.at[2], sec2.at[theirs, :])
    columns(lambda at: in_low[:, at], core, lambda at, v: stage.__setitem__((3, slice(None), at), v))
    last.append(fetch(13, stage.at[3], sec2.at[mine, :]))
    clock.drain()
    for copy in last + owns + [turned_out, normed_store, stores[2], stores[3]]:
        copy.wait()
    for i in range(parts):
        stores["a", i].wait()
        if i >= 2:
            for copy in stores["f", i]:
                copy.wait()
    waited = [stores["r", 0], stores["r", 1]]
    for copy in pair_copies:
        if not any(copy is other for other in waited):
            copy.wait_send()
        if copy is not lift_copy and copy is not first_copy:
            copy.wait_recv()
    for copy in copies.values():
        copy.wait_send()
    for here, copy in column:
        @pl.when(z == here)
        def _(copy=copy):
            copy.wait_send()
    for copy in bias_copies:
        copy.wait_send()
    for sender, receiver, copy in halos:
        @pl.when(z == sender)
        def _(copy=copy):
            copy.wait_send()


def fore_call(rows, window, parts, perm, back, *arrays):
    f32, low = jnp.float32, jnp.bfloat16
    any_ = pl.BlockSpec(memory_space=pl.ANY)
    vmem = pl.BlockSpec(memory_space=pltpu.VMEM)
    smem = pl.BlockSpec(memory_space=pltpu.SMEM)
    cut = D // parts
    three = 3 * cut
    shape = jax.ShapeDtypeStruct
    marks = cut // (2 * HD) * 3 * LONG
    dma = pltpu.SemaphoreType.DMA
    return pl.pallas_call(
        functools.partial(fore_kernel, rows, window, parts),
        out_shape=[
            shape((parts, D, three), low),
            shape((parts, cut, D), low),
            shape((parts, D, D), low),
            shape((parts, D, D), low),
            shape((parts, window, three), low),
            shape((parts, marks, 2 * UNIT), f32),
            shape((2 * rows, D), low),
            shape((2 * rows, FF), low),
            shape((rows, FF), low),
            shape((512, 2 * rows), low),
            shape((512, 2 * rows), low),
            shape((2 * rows, 512), low),
            shape((rows, D), f32),
            shape((rows, D), low),
            shape((rows, D), f32),
            shape((rows, D), low),
            shape((rows, 1), f32),
            shape((16, D), f32),
        ],
        in_specs=[smem, smem] + [vmem] * len(arrays),
        out_specs=[any_] * 5 + [vmem] + [any_] * 10 + [vmem] * 2,
        scratch_shapes=[
            pltpu.VMEM((window, D), low),
            pltpu.VMEM((2, window, three), low),
            pltpu.VMEM((window, cut), low),
            pltpu.VMEM(((LAST_OWN + 1 - FIRST_OWN) * UNIT, cut), low),
            pltpu.VMEM((parts, rows, cut), low),
            pltpu.VMEM((rows, D), f32),
            pltpu.VMEM((rows, D), f32),
            pltpu.VMEM((rows, D), low),
            pltpu.VMEM((rows, D), f32),
            pltpu.VMEM((rows, D), low),
            pltpu.VMEM((rows, D), low),
            pltpu.VMEM((D, D), low),
            pltpu.VMEM((D, D), low),
            pltpu.VMEM((D, three), low),
            pltpu.VMEM((cut, D), low),
            pltpu.VMEM((2, rows, D), low),
            pltpu.VMEM((2, rows, D), low),
            pltpu.VMEM((2 * rows, 512), low),
            pltpu.VMEM((2 * rows, 512), low),
            pltpu.VMEM((512, 2 * rows), low),
            pltpu.VMEM((4, rows, 512), low),
            pltpu.VMEM((parts, 8, D), f32),
            dma((12, 10)),
            dma((12, 10)),
            dma((4, 2)),
            dma((2,)),
            dma((2,)),
            dma((4,)),
            dma((3,)),
            dma((3,)),
            dma((16,)),
            dma((2 * parts + 3,)),
            dma((2 * parts + 3,)),
        ],
        compiler_params=pltpu.CompilerParams(
            collective_id=0, has_side_effects=True, vmem_limit_bytes=56 * 2**20
        ),
    )(perm, back, *arrays)


def back_kernel(
    rows, window, parts, perm, back, sec_low, sec2, inverse, gain, small_in, kf, qf, lse,
    first_t, lift_t, second_grads, normed_one, act2, dgelu, att2, qkv, f_qkv, f_out, f_up, f_down,
    input_grad, g_qkv, g_out, g_up, g_down, small_out,
    acc, normed, turned, arena, act, slope, y, up2, w_in, mixed2, mixed_win, small, small_in_far,
    s_down, s_up, s_out, s_qkv, k_down, k_up, k_out, k_qkv,
    r_down, r_up, r_out, r_qkv, t_down, t_up, t_out, t_qkv, z_down, z_up, z_out, z_qkv,
    local, hop_send, hop_recv, pair_send, pair_recv, halo_send, halo_recv, small_send, small_recv,
):
    f32, low = jnp.float32, jnp.bfloat16
    d = lax.axis_index("dp")
    z = lax.axis_index("mp")
    core = lax.rem(d, 2)
    firsts, offsets, ends = window_plan(rows, parts)
    offset = pl.multiple_of(pick(offsets, z), 16)
    partner = (d ^ 1, z)
    peers = [(d, z ^ k) for k in (1, 2, 3)] + [partner, (d ^ 2, z), (d ^ 4, z), (d ^ 6, z)]
    barrier = pltpu.get_barrier_semaphore()
    for peer in peers:
        pl.semaphore_signal(barrier, inc=1, device_id=peer, device_id_type=MESH)
    pl.semaphore_wait(barrier, len(peers))
    clock = Clock(48e3)
    tail = []

    wide = 2 * rows
    wd = arena.at[pl.ds(0, D), :]
    wu = arena.at[pl.ds(D, D), :]

    def fetch(index, source, target):
        copy = pltpu.make_async_copy(source, target, local.at[index])
        copy.start()
        return copy

    chunk = lambda k: z ^ k
    hidden = lambda k: pl.ds(pl.multiple_of(chunk(k) * D, D), D)
    load_wd = lambda i: fetch(0, f_down.at[chunk(RING[i])], wd)
    load_wu = lambda i: fetch(1, f_up.at[chunk(RING[i])], wu)
    load_act = lambda i: fetch(2, act2.at[:, hidden(RING[i])], act)
    load_slope = lambda i: fetch(3, dgelu.at[:, hidden(RING[i])], slope)
    at_act, at_wd, at_slope, at_wu = load_act(0), load_wd(0), load_slope(0), load_wu(0)
    at_acc = fetch(4, second_grads, acc)
    at_normed = fetch(5, normed_one, normed)
    at_turned = fetch(6, first_t, turned)

    zero = jnp.zeros((16, D), low)
    for j in range(parts):
        spans = []
        if j == 0:
            spans.append((0, offsets[0]))
        begin = ends[j] if j < parts - 1 else offsets[j] + rows
        if begin < window:
            spans.append((begin, window))
        if spans:
            @pl.when(z == j)
            def _(spans=spans):
                for begin, end in spans:
                    def clear(i, c):
                        mixed_win[pl.ds(pl.multiple_of(begin + i * 16, 16), 16), :] = zero
                        return c
                    lax.fori_loop(0, (end - begin) // 16, clear, 0)

    groups = {
        "down": (s_down, k_down, r_down, t_down, z_down, g_down, 0),
        "up": (s_up, k_up, r_up, t_up, z_up, g_up, 1),
        "out": (s_out, k_out, r_out, t_out, z_out, g_out, 2),
        "qkv": (s_qkv, k_qkv, r_qkv, t_qkv, z_qkv, g_qkv, 3),
    }
    hops, finished = {}, {}

    def x_ahead(g, i):
        return (i + groups[g][6]) % 2 == 0

    def put(g, i, j, at, value):
        if not x_ahead(g, i):
            j = (0, 2, 1, 3)[j]
        if j < 2:
            groups[g][0][(i % 2, j) + at] = value
        else:
            groups[g][1][(i, j - 2) + at] = value

    def hop(g, i, kind, source, target, device):
        index = groups[g][6]
        copy = pltpu.make_async_remote_copy(
            source, target, hop_send.at[index, i, kind], hop_recv.at[index, i, kind],
            device_id=device, device_id_type=MESH,
        )
        copy.start()
        hops[g, i, kind] = copy

    def add_into(ref, other):
        count = ref.shape[0]
        step = min(count, 64)

        def body(j, c):
            at = pl.ds(pl.multiple_of(j * step, step), step)
            ref[at, :] = (ref[at, :].astype(f32) + other[at, :].astype(f32)).astype(low)
            return c

        lax.fori_loop(0, count // step, body, 0)

    def launch(g, i):
        s, kept, r, t, zb, out, index = groups[g]
        x_first = x_ahead(g, i)
        n1, n2 = ((d ^ 2, z), (d ^ 4, z)) if x_first else ((d ^ 4, z), (d ^ 2, z))
        l1, l2 = ("x", "y") if x_first else ("y", "x")
        block = s.shape[2] * s.shape[3] * 2
        k = RING[i]
        hop(g, i, 0, s.at[i % 2], r.at[i], n1)

        def second():
            hops[g, i, 0].wait_recv()
            add_into(kept.at[i, 0], r.at[i, 0])
            hop(g, i, 1, kept.at[i, 0], t.at[i], n2)
            clock.send(l2, block, third)
            add_into(kept.at[i, 1], r.at[i, 1])

        def third():
            hops[g, i, 1].wait_recv()
            add_into(kept.at[i, 1], t.at[i])
            if k:
                hop(g, i, 2, kept.at[i, 1], zb.at[k - 1], (d, z ^ k))
                clock.send("z", block, fourth, 1.0 if k == 1 else 2.0)
            else:
                ended()

        def fourth():
            hops[g, i, 2].wait_recv()
            ended()

        def ended():
            finished[g] = finished.get(g, 0) + 1
            if finished[g] == parts:
                finish(g)

        clock.send(l1, 2 * block, second)

    def free_slot(g, i):
        if i >= 2:
            hops[g, i - 2, 0].wait_send()

    def finish(g):
        s, kept, r, t, zb, out, index = groups[g]
        own = RING.index(0)
        count = s.shape[2]
        step = min(count, 64)
        pieces = kept.at[own, 1]

        def body(j, c):
            at = pl.ds(pl.multiple_of(j * step, step), step)
            total = pieces[at, :].astype(f32)
            for k in range(parts - 1):
                total = total + zb[k, at, :].astype(f32)
            out[at, :] = total
            return c

        lax.fori_loop(0, count // step, body, 0)

    def exchange(index, source, target):
        copy = pltpu.make_async_remote_copy(
            source, target, pair_send.at[index], pair_recv.at[index], device_id=partner, device_id_type=MESH
        )
        copy.start()
        return copy

    small[...] = small_in[...]

    pending = {}

    def grad_up_chunk(i):
        pending.pop(i).wait_recv()
        if i == 0:
            at_turned.wait()
        free_slot("up", i)

        def body(n, c):
            at = pl.ds(pl.multiple_of(n * 256, 256), 256)
            tile = jnp.dot(turned[...], up2[i, :, at], preferred_element_type=f32).astype(low)
            for j in range(4):
                put("up", i, j, (slice(None), at), tile[j * 128 : (j + 1) * 128])
            return c

        lax.fori_loop(0, 4, body, 0)
        launch("up", i)
        clock.work(2.0)

    exchanges = []
    loads = {"wd": at_wd, "wu": at_wu, "slope": at_slope, "act": at_act}

    def upper_chunk(i):
        loads["wd"].wait()
        loads["slope"].wait()
        bias_row = chunk(RING[i])

        def body(n, c):
            at = pl.ds(pl.multiple_of(n * 256, 256), 256)
            grads = lax.dot_general(sec_low[...], wd[at, :], NT, preferred_element_type=f32)
            value = (grads * slope[:, at].astype(f32)).astype(low)
            up2[i, pl.ds(0, rows), at] = value
            small[pl.ds(10 + bias_row, 1), at] = jnp.sum(value.astype(f32), axis=0, keepdims=True)
            return c

        lax.fori_loop(0, 4, body, 0)
        pending[i] = exchange(i, up2.at[i, pl.ds(0, rows), :], up2.at[i, pl.ds(rows, rows), :])
        exchanges.append(pending[i])
        clock.work(2.5)
        if i + 1 < parts:
            loads["wd"], loads["slope"] = load_wd(i + 1), load_slope(i + 1)

    def grad_down_chunk(i):
        loads["act"].wait()
        free_slot("down", i)

        def body(n, c):
            at = pl.ds(pl.multiple_of(n * 256, 256), 256)
            tile = lax.dot_general(act[:, at], sec2[...], TN, preferred_element_type=f32).astype(low)
            for j in range(4):
                put("down", i, j, (at, slice(None)), tile[:, j * 128 : (j + 1) * 128])
            return c

        lax.fori_loop(0, 4, body, 0)
        launch("down", i)
        clock.work(2.0)
        if i + 1 < parts:
            loads["act"] = load_act(i + 1)

    def first_chunk(i):
        loads["wu"].wait()
        if i == 0:
            at_acc.wait()

        def body(n, c):
            at = pl.ds(pl.multiple_of(n * 256, 256), 256)
            acc[:, at] += lax.dot_general(
                up2[i, pl.ds(0, rows), :], wu[at, :], NT, preferred_element_type=f32
            )
            return c

        lax.fori_loop(0, 4, body, 0)
        clock.work(2.0)
        if i + 1 < parts:
            loads["wu"] = load_wu(i + 1)

    grad_down_chunk(0)
    for i in range(parts):
        upper_chunk(i)
        first_chunk(i)
        if i == 1:
            grad_down_chunk(1)

    at_normed.wait()
    zero_row = jnp.zeros((16, D), f32)

    def norm_body(begin, count, sums):
        at = pl.ds(begin, count)
        grads, unit = acc[at, :], normed[at, :]
        scaled = grads * gain[0:1, :]
        result = inverse[at, :] * (
            scaled
            - jnp.mean(scaled, axis=-1, keepdims=True)
            - unit * jnp.mean(scaled * unit, axis=-1, keepdims=True)
        )
        acc[at, :] = result
        mixed_win[pl.ds(pl.multiple_of(offset + begin, 16), count), :] = result.astype(low)
        return (sums[0] + fold(grads * unit), sums[1] + fold(grads), sums[2] + fold(result))

    sums = by_rows(rows, norm_body, (zero_row, zero_row, zero_row))
    small[4:5, :] = jnp.sum(sums[0], axis=0, keepdims=True)
    small[5:6, :] = jnp.sum(sums[1], axis=0, keepdims=True)
    small[2:3, :] = jnp.sum(sums[2], axis=0, keepdims=True)
    halos = []
    for j in range(parts - 1):
        count = ends[j] - offsets[j] - rows
        halos.append((j + 1, j, pltpu.make_async_remote_copy(
            mixed_win.at[pl.ds(offsets[j + 1], count), :],
            mixed_win.at[pl.ds(offsets[j] + rows, count), :],
            halo_send.at[0], halo_recv.at[0], device_id=(d, j), device_id_type=MESH,
        )))
    for j in range(1, parts):
        halos.append((j - 1, j, pltpu.make_async_remote_copy(
            mixed_win.at[pl.ds(offsets[j - 1] + rows - offsets[j], offsets[j]), :],
            mixed_win.at[pl.ds(0, offsets[j]), :],
            halo_send.at[1], halo_recv.at[1], device_id=(d, j), device_id_type=MESH,
        )))
    for sender, receiver, copy in halos:
        @pl.when(z == sender)
        def _(copy=copy):
            copy.start()
    clock.work(4.0)
    for i in range(parts):
        grad_up_chunk(i)
        if i + 2 < parts:
            grad_down_chunk(i + 2)
    own_at = pl.ds(offset, rows)
    for j, owner in enumerate(block_owners(d, 1 - core, True)):
        y[0:rows, j * 128 : (j + 1) * 128] = mixed_win[own_at, pl.ds(pl.multiple_of(owner * 128, 128), 128)]
    exchanges.append(exchange(parts, y.at[pl.ds(0, rows), pl.ds(0, 512)], mixed2.at[pl.ds(rows, rows), :]))
    for j, owner in enumerate(block_owners(d, core, True)):
        mixed2[pl.ds(0, rows), j * 128 : (j + 1) * 128] = mixed_win[
            own_at, pl.ds(pl.multiple_of(owner * 128, 128), 128)
        ]
    clock.work(4.0)

    cut = D // parts
    three = 3 * cut
    pairs = cut // (2 * HD)
    x = arena
    wo = slope.at[pl.ds(0, cut), :]
    load_x = lambda i: fetch(0, qkv.at[chunk(RING[i])], arena.at[pl.ds(0, window), pl.ds(0, three)])
    load_wo = lambda i: fetch(1, f_out.at[chunk(RING[i])], wo)
    load_att = lambda i: fetch(
        2, att2.at[:, pl.ds(pl.multiple_of(chunk(RING[i]) * cut, cut), cut)], act.at[:, pl.ds(0, cut)]
    )
    load_wi = lambda i: fetch(3, f_qkv.at[chunk(RING[i])], w_in)
    at_turned = fetch(6, lift_t, turned)
    at_x, at_wo, at_att, at_wi = load_x(0), load_wo(0), load_att(0), load_wi(0)
    exchanges[-1].wait_recv()
    scale = HD ** (-0.5)

    def take_halo():
        for sender, receiver, copy in halos:
            @pl.when(z == receiver)
            def _(copy=copy):
                copy.wait_recv()

    def grad_qkv_chunk(i):
        pending.pop(i).wait_recv()
        if i == 0:
            at_turned.wait()
        free_slot("qkv", i)

        def body(n, c):
            at = pl.ds(pl.multiple_of(n * 256, 256), 256)
            tile = jnp.dot(turned[...], up2[i, :, at], preferred_element_type=f32).astype(low)
            for j in range(4):
                put("qkv", i, j, (slice(None), at), tile[j * 128 : (j + 1) * 128])
            return c

        lax.fori_loop(0, three // 256, body, 0)
        launch("qkv", i)
        clock.work(1.8)

    for i in range(parts):
        at_att.wait()
        free_slot("out", i)
        tile = lax.dot_general(act[:, 0:cut], mixed2[...], TN, preferred_element_type=f32).astype(low)
        for j in range(4):
            put("out", i, j, (slice(None), slice(None)), tile[:, j * 128 : (j + 1) * 128])
        launch("out", i)
        clock.work(0.8)
        if i == 0:
            take_halo()
        at_wo.wait()

        def flow_body(n, c):
            at = pl.ds(pl.multiple_of(n * 512, 512), 512)
            x[at, three : three + cut] = lax.dot_general(
                mixed_win[at, :], wo[...], NT, preferred_element_type=f32
            ).astype(low)
            return c

        lax.fori_loop(0, window // 512, flow_body, 0)
        clock.work(1.5)
        if i:
            grad_qkv_chunk(i - 1)
        at_x.wait()
        if i == 0:
            exchanges[parts].wait_send()
        if i + 1 < parts:
            at_wo, at_att = load_wo(i + 1), load_att(i + 1)

        def attend_body(step, c):
            p, slot = step // 3, lax.rem(step, 3)
            lanes = lambda base: pl.ds(pl.multiple_of(base + p * 2 * HD, 2 * HD), 2 * HD)
            unit_at = [
                pl.ds(perm[slot * LONG + m] * UNIT, UNIT) for m in range(LONG)
            ]
            keys = jnp.concatenate([x[at, lanes(cut)] for at in unit_at], axis=0)
            values = jnp.concatenate([x[at, lanes(2 * cut)] for at in unit_at], axis=0)
            marks = jnp.concatenate([kf[at, :] for at in unit_at], axis=0)
            wide_keys = jnp.concatenate([keys, marks], axis=1)
            pair = jnp.concatenate([two_heads(x[at, lanes(0)]) for at in unit_at], axis=0)
            grads = jnp.concatenate([two_heads(x[at, lanes(three)]) for at in unit_at], axis=0)
            mark = jnp.concatenate([qf[at, :] for at in unit_at for _ in range(2)], axis=0)
            wide_pair = jnp.concatenate([pair, mark], axis=1)
            logsum = jnp.concatenate(
                [lse[chunk(RING[i]), pl.ds(step * LONG + m, 1), :] for m in range(LONG)], axis=1
            )
            scores = lax.dot_general(wide_keys, wide_pair, NT, preferred_element_type=f32)
            chances = jnp.exp(scores - logsum)
            flow = lax.dot_general(values, grads, NT, preferred_element_type=f32)
            terms = chances * flow
            slopes = (chances * (flow - jnp.sum(terms, axis=0, keepdims=True))).astype(low)
            v_sum = jnp.dot(chances.astype(low), grads, preferred_element_type=f32)
            k_sum = jnp.dot(slopes, pair, preferred_element_type=f32)
            flipped = lax.dot_general(keys, slopes, TN, preferred_element_type=f32)
            for m in range(LONG):
                two = slice(m * 2 * UNIT, (m + 1) * 2 * UNIT)
                at = pl.ds(pl.multiple_of(slot * LONG * UNIT + m * UNIT, UNIT), UNIT)
                y[at, lanes(0)] = (from_two(flipped[:, two]) * scale).astype(low)
            at = pl.ds(pl.multiple_of(slot * LONG * UNIT, UNIT), LONG * UNIT)
            y[at, lanes(cut)] = k_sum.astype(low)
            y[at, lanes(2 * cut)] = v_sum.astype(low)
            return c

        lax.fori_loop(0, pairs * 3, attend_body, 0, unroll=2)
        clock.work(10.5)
        if i + 1 < parts:
            at_x = load_x(i + 1)
        for u in range(FIRST_OWN, LAST_OWN + 1):
            at = pl.ds(back[u] * UNIT, UNIT)
            act[pl.ds((u - FIRST_OWN) * UNIT, UNIT), cut:] = y[at, :]
        exchanges[i].wait_send()
        inner_at = pl.ds(pl.multiple_of(offset - FIRST_OWN * UNIT, 16), rows)
        up2[i, pl.ds(0, rows), 0:three] = act[inner_at, cut:]
        pending[i] = exchange(
            parts + 1 + i, up2.at[i, pl.ds(0, rows), pl.ds(0, three)], up2.at[i, pl.ds(rows, rows), pl.ds(0, three)]
        )
        exchanges.append(pending[i])
        place = pl.multiple_of(chunk(RING[i]) * cut, cut)
        small[8:9, pl.ds(place, cut)] = jnp.sum(up2[i, pl.ds(0, rows), 0:cut].astype(f32), axis=0, keepdims=True)
        small[9:10, pl.ds(place, cut)] = jnp.sum(
            up2[i, pl.ds(0, rows), 2 * cut : three].astype(f32), axis=0, keepdims=True
        )
        at_wi.wait()

        def input_body(n, c, i=i):
            at = pl.ds(pl.multiple_of(n * 256, 256), 256)
            acc[:, at] += lax.dot_general(
                up2[i, pl.ds(0, rows), 0:three], w_in[at, :], NT, preferred_element_type=f32
            )
            return c

        lax.fori_loop(0, 4, input_body, 0)
        clock.work(2.0)
        if i + 1 < parts:
            at_wi = load_wi(i + 1)

    def last_body(begin, count, total):
        at = pl.ds(begin, count)
        value = acc[at, :]
        arena[at, :] = value.astype(low)
        return total + fold(value)

    total = jnp.sum(by_rows(rows, last_body, zero_row), axis=0, keepdims=True)
    store = fetch(4, arena.at[pl.ds(0, rows), :], input_grad)
    small[0:1, :] = total * small_in[15:16, :]
    small[1:2, :] = total
    clock.work(2.0)
    stages = [[partner], [(d ^ 2, z), (d ^ 4, z), (d ^ 6, z)], [(d, z ^ k) for k in (1, 2, 3)]]

    def small_stage(n, first_slot):
        sent = []
        for slot, device in enumerate(stages[n], first_slot):
            copy = pltpu.make_async_remote_copy(
                small, small_in_far.at[slot], small_send.at[slot], small_recv.at[slot],
                device_id=device, device_id_type=MESH,
            )
            copy.start()
            sent.append(copy)

        def take():
            for copy in sent:
                copy.wait()
            for slot in range(first_slot, first_slot + len(sent)):
                small[...] += small_in_far[slot]
            if n + 1 < len(stages):
                small_stage(n + 1, first_slot + len(sent))

        clock.send("c", 0.6e6, take)

    small_stage(0, 0)
    grad_qkv_chunk(parts - 1)
    clock.drain()
    assert sum(finished.values()) == 4 * parts
    small_out[...] = small[...]
    store.wait()
    for (g, i, kind), copy in hops.items():
        if kind or i >= 2:
            copy.wait_send()
    for copy in exchanges[parts + 1 :]:
        copy.wait_send()
    for sender, receiver, copy in halos:
        @pl.when(z == sender)
        def _(copy=copy):
            copy.wait_send()


def back_call(rows, window, parts, perm, back, vmem_in, hbm_in):
    f32, low = jnp.float32, jnp.bfloat16
    any_ = pl.BlockSpec(memory_space=pl.ANY)
    vmem = pl.BlockSpec(memory_space=pltpu.VMEM)
    smem = pl.BlockSpec(memory_space=pltpu.SMEM)
    cut = D // parts
    shapes = {"down": (D, 128), "up": (128, D), "out": (cut, 128), "qkv": (128, 3 * cut)}
    outs = [jax.ShapeDtypeStruct((rows, D), low)]
    outs += [jax.ShapeDtypeStruct(shape, f32) for shape in (shapes["qkv"], shapes["out"], shapes["up"], shapes["down"])]
    outs += [jax.ShapeDtypeStruct((16, D), f32)]
    order = ("down", "up", "out", "qkv")
    buffers = [pltpu.VMEM((2, 2) + shapes[g], low) for g in order]
    buffers += [pltpu.VMEM((parts, 2) + shapes[g], low) for g in order]
    buffers += [pltpu.VMEM((parts, 2) + shapes[g], low) for g in order]
    buffers += [pltpu.VMEM((parts,) + shapes[g], low) for g in order]
    buffers += [pltpu.VMEM((parts - 1,) + shapes[g], low) for g in order]
    dma = pltpu.SemaphoreType.DMA
    return pl.pallas_call(
        functools.partial(back_kernel, rows, window, parts),
        out_shape=outs,
        in_specs=[smem, smem] + [vmem] * len(vmem_in) + [any_] * len(hbm_in),
        out_specs=[any_] + [vmem] * 5,
        scratch_shapes=[
            pltpu.VMEM((rows, D), f32),
            pltpu.VMEM((rows, D), f32),
            pltpu.VMEM((512, 2 * rows), low),
            pltpu.VMEM((2 * D, D), low),
            pltpu.VMEM((2 * rows, D), low),
            pltpu.VMEM((rows, D), low),
            pltpu.VMEM((window, 3 * cut), low),
            pltpu.VMEM((parts, 2 * rows, D), low),
            pltpu.VMEM((D, 3 * cut), low),
            pltpu.VMEM((2 * rows, 512), low),
            pltpu.VMEM((window, D), low),
            pltpu.VMEM((16, D), f32),
            pltpu.VMEM((7, 16, D), f32),
        ]
        + buffers
        + [
            dma((7,)),
            dma((4, parts, 3)),
            dma((4, parts, 3)),
            dma((2 * parts + 1,)),
            dma((2 * parts + 1,)),
            dma((2,)),
            dma((2,)),
            dma((7,)),
            dma((7,)),
        ],
        compiler_params=pltpu.CompilerParams(
            collective_id=1, has_side_effects=True, vmem_limit_bytes=60 * 2**20 + 2**19
        ),
    )(perm, back, *vmem_in, *hbm_in)


def unit_order(segs, window):
    units = window // UNIT
    unit_seg = segs[::UNIT]
    index = lax.iota(jnp.int32, units)
    counts = jnp.sum((unit_seg[:, None] == unit_seg[None, :]).astype(jnp.int32), axis=1)
    short = jnp.where((counts == LONG) & (unit_seg >= 0) & (unit_seg < 1000), 0, 1) * units + index
    back = jnp.sum((short[None, :] < short[:, None]).astype(jnp.int32), axis=1)
    perm = jnp.sum(jnp.where(back[None, :] == index[:, None], index[None, :], 0), axis=1)
    return perm.astype(jnp.int32), back.astype(jnp.int32)


def marks_of(segs):
    lane = lax.iota(jnp.int32, 2 * HD)
    seg = jnp.where(segs < 0, 2 * HD - 1, jnp.where(segs >= 1000, 2 * HD - 2, segs))
    same = seg[:, None] == lane[None, :]
    keys = jnp.where(same, 1.0, 0.0).astype(jnp.bfloat16)
    queries = jnp.where(same, 0.0, -1e30).astype(jnp.bfloat16)
    return keys, queries


def local_body(
    tokens,
    cotangent,
    timesteps,
    item_lengths,
    w_qkv,
    bias_qv,
    w_out,
    w_up,
    bias_up,
    w_down,
    vectors,
):
    rows = tokens.shape[0]
    parts = lax.axis_size("mp")
    z = lax.axis_index("mp")
    low = jnp.bfloat16
    f32 = jnp.float32
    cut = D // parts
    firsts, offsets, ends = window_plan(rows, parts)
    window = -(-max(ends) // UNIT) * UNIT
    first_token = UNIT * pick(firsts, z)
    positions = first_token + lax.iota(jnp.int32, window)
    lengths_end = jnp.cumsum(item_lengths[0])
    segs = jnp.sum((positions[:, None] >= lengths_end[None, :]).astype(jnp.int32), axis=1)
    segs = jnp.where(positions < 0, -1, jnp.where(positions >= LEN, 1000, segs))
    perm, back = unit_order(segs, window)
    kf, qf = marks_of(segs)
    step_time = timesteps[0].astype(f32) * 0.001
    bias_q, bias_v = bias_qv[0].astype(f32), bias_qv[1].astype(f32)
    bias_row = jnp.concatenate([bias_q, jnp.zeros((cut,), f32), bias_v, jnp.zeros((D - 3 * cut,), f32)])
    biases = jnp.concatenate([jnp.stack([bias_up.astype(f32), bias_row]), jnp.zeros((6, D), f32)])
    rows16 = jnp.concatenate(
        [vectors, (step_time * vectors[0])[None], jnp.full((7, D), step_time, f32)], axis=0
    )
    (
        f_qkv, f_out, f_up, f_down, qkv, lse, att2, act2, slope, first_t, lift_t, sec2, normed_one,
        second_low, second_grads, output, inverse_one, small_in,
    ) = fore_call(
        rows, window, parts, perm, back, tokens, cotangent,
        w_qkv.reshape(D, 3 * cut), w_out, w_up, w_down, biases, rows16, kf, qf,
    )
    input_grad, grad_qkv, grad_out, grad_up, grad_down, small = back_call(
        rows, window, parts, perm, back,
        (second_low, sec2, inverse_one, vectors[4:5], small_in, kf, qf, lse),
        (first_t, lift_t, second_grads, normed_one, act2, slope, att2, qkv, f_qkv, f_out, f_up, f_down),
    )
    grad_bias_qv = lax.dynamic_slice_in_dim(small[8:10], z * cut, cut, 1)
    grad_bias_up = lax.dynamic_slice_in_dim(small[10:14].reshape(FF), z * (FF // parts), FF // parts, 0)
    return (
        output,
        input_grad,
        grad_qkv.reshape(-1, 3, cut),
        grad_bias_qv,
        grad_out,
        grad_up,
        grad_bias_up,
        grad_down,
        small[:8],
    )


def solution(mesh):
    in_specs = (
        P(("dp", "mp"), None),
        P(("dp", "mp"), None),
        P("dp"),
        P("dp", None),
        P(None, None, "mp"),
        P(None, "mp"),
        P("mp", None),
        P(None, "mp"),
        P("mp"),
        P("mp", None),
        P(),
    )
    out_specs = (
        P(("dp", "mp"), None),
        P(("dp", "mp"), None),
        P("dp", None, "mp"),
        P(None, "mp"),
        P("mp", "dp"),
        P("dp", "mp"),
        P("mp"),
        P("mp", "dp"),
        P(),
    )
    chosen = local_body if fits_local(mesh) else body
    return jax.shard_map(chosen, mesh=mesh, in_specs=in_specs, out_specs=out_specs, check_vma=False)
```

```python
import functools
import heapq

import jax
import jax.numpy as jnp
from jax import lax
from jax.experimental import pallas as pl
from jax.experimental.pallas import tpu as pltpu
from jax.sharding import PartitionSpec as P

D = 1024
HD = 64
FF = 4096
LEN = 2368


def norm_forward(value, gain, shift):
    average = jnp.mean(value, axis=-1, keepdims=True)
    centred = value - average
    inverse = lax.rsqrt(jnp.mean(centred * centred, axis=-1, keepdims=True) + 1e-05)
    normed = centred * inverse
    return (normed * gain + shift, normed, inverse)


def norm_backward(grad, normed, inverse, gain):
    scaled = grad * gain
    result = inverse * (
        scaled
        - jnp.mean(scaled, axis=-1, keepdims=True)
        - normed * jnp.mean(scaled * normed, axis=-1, keepdims=True)
    )
    return (result, jnp.sum(grad * normed, axis=0), jnp.sum(grad, axis=0))


def gelu_exact(value):
    return jax.nn.gelu(value, approximate=False)


def attend_forward(queries, keys, values, segments):
    scale = HD ** (-0.5)
    block_rows = LEN // 4

    def one_block(inputs):
        query_block, segment_block = inputs
        scores = (
            jnp.einsum("bhe,khe->hbk", query_block, keys, preferred_element_type=jnp.float32)
            * scale
        )
        allowed = segment_block[:, None] == segments[None, :]
        scores = jnp.where(allowed[None], scores, -1e30)
        highest = jnp.max(scores, axis=-1, keepdims=True)
        weights = jnp.exp(scores - highest)
        totals = jnp.sum(weights, axis=-1, keepdims=True)
        chances_low = (weights / totals).astype(jnp.bfloat16)
        result = jnp.einsum("hbk,khe->bhe", chances_low, values, preferred_element_type=jnp.float32)
        return (result.astype(jnp.bfloat16), (highest + jnp.log(totals))[..., 0])

    blocks = queries.reshape(4, block_rows, queries.shape[1], queries.shape[2])
    results, logsums = lax.map(one_block, (blocks, segments.reshape(4, block_rows)))
    return (results.reshape(queries.shape), logsums)


def attend_backward(queries, keys, values, out_grads, logsums, segments):
    scale = HD ** (-0.5)
    block_rows = LEN // 4

    def one_block(carry, inputs):
        key_grads, value_grads = carry
        query_block, grad_block, logsum_block, segment_block = inputs
        scores = (
            jnp.einsum("bhe,khe->hbk", query_block, keys, preferred_element_type=jnp.float32)
            * scale
        )
        allowed = segment_block[:, None] == segments[None, :]
        scores = jnp.where(allowed[None], scores, -1e30)
        chances = jnp.exp(scores - logsum_block[..., None])
        chances_low = chances.astype(jnp.bfloat16)
        value_grads = value_grads + jnp.einsum(
            "hbk,bhe->khe", chances_low, grad_block, preferred_element_type=jnp.float32
        )
        flow = jnp.einsum("bhe,khe->hbk", grad_block, values, preferred_element_type=jnp.float32)
        inner = jnp.sum(chances * flow, axis=-1, keepdims=True)
        score_grads = (chances * (flow - inner)).astype(jnp.bfloat16)
        query_grads = (
            jnp.einsum("hbk,khe->bhe", score_grads, keys, preferred_element_type=jnp.float32)
            * scale
        )
        key_grads = (
            key_grads
            + jnp.einsum(
                "hbk,bhe->khe", score_grads, query_block, preferred_element_type=jnp.float32
            )
            * scale
        )
        return ((key_grads, value_grads), query_grads)

    shape_blocks = (4, block_rows, queries.shape[1], queries.shape[2])
    zeros = jnp.zeros(keys.shape, jnp.float32)
    (key_grads, value_grads), query_grads = lax.scan(
        one_block,
        (zeros, zeros),
        (
            queries.reshape(shape_blocks),
            out_grads.reshape(shape_blocks),
            logsums,
            segments.reshape(4, block_rows),
        ),
    )
    return (query_grads.reshape(queries.shape), key_grads, value_grads)


def body(
    tokens,
    cotangent,
    timesteps,
    item_lengths,
    w_qkv,
    bias_qv,
    w_out,
    w_up,
    bias_up,
    w_down,
    vectors,
):
    rows = tokens.shape[0]
    total = rows * lax.axis_size("mp")
    seq_count = timesteps.shape[0]
    local_width = w_qkv.shape[2]
    local_hidden = w_up.shape[1]
    local_heads = local_width // HD
    my_index = lax.axis_index("mp")
    row_ids = my_index * rows + lax.iota(jnp.int32, rows)
    row_owner = row_ids // LEN
    step_times = timesteps.astype(jnp.float32) * 0.001
    time_rows = jnp.sum(
        jnp.where(
            row_owner[:, None] == lax.iota(jnp.int32, seq_count)[None, :], step_times[None, :], 0.0
        ),
        axis=1,
    )
    ends = jnp.cumsum(item_lengths, axis=1)
    segments = jnp.sum(
        (lax.iota(jnp.int32, LEN)[None, :, None] >= ends[:, None, :]).astype(jnp.int32), axis=2
    )
    lifted = tokens.astype(jnp.float32) + time_rows[:, None] * vectors[0] + vectors[1]
    gathered = lax.all_gather(lifted.astype(jnp.bfloat16), "mp", axis=0, tiled=True)
    projected = jnp.einsum("td,dce->cte", gathered, w_qkv, preferred_element_type=jnp.float32)
    shaped = (seq_count, LEN, local_heads, HD)
    head_query = (projected[0] + bias_qv[0]).astype(jnp.bfloat16).reshape(shaped)
    head_key = projected[1].astype(jnp.bfloat16).reshape(shaped)
    head_value = (projected[2] + bias_qv[1]).astype(jnp.bfloat16).reshape(shaped)
    attended, logsums = lax.map(
        lambda items: attend_forward(*items), (head_query, head_key, head_value, segments)
    )
    attended = attended.reshape(total, local_width)
    piece = attended
    mixed = (
        lax.psum_scatter(
            jnp.dot(piece, w_out, preferred_element_type=jnp.float32),
            "mp",
            scatter_dimension=0,
            tiled=True,
        )
        + vectors[2]
    )
    first, normed_one, inverse_one = norm_forward(lifted + mixed, vectors[4], vectors[5])
    hidden_all = lax.all_gather(first.astype(jnp.bfloat16), "mp", axis=0, tiled=True)
    upper = jnp.dot(hidden_all, w_up, preferred_element_type=jnp.float32) + bias_up
    activated, gelu_pull = jax.vjp(gelu_exact, upper)
    activated = activated.astype(jnp.bfloat16)
    piece = activated
    down = (
        lax.psum_scatter(
            jnp.dot(piece, w_down, preferred_element_type=jnp.float32).astype(jnp.bfloat16),
            "mp",
            scatter_dimension=0,
            tiled=True,
        ).astype(jnp.float32)
        + vectors[3]
    )
    output, normed_two, inverse_two = norm_forward(first + down, vectors[6], vectors[7])
    out_grads = cotangent.astype(jnp.float32)
    second_grads, gain_two, shift_two = norm_backward(
        out_grads, normed_two, inverse_two, vectors[6]
    )
    down_all = lax.all_gather(second_grads.astype(jnp.bfloat16), "mp", axis=0, tiled=True)
    grad_down = jnp.einsum("tf,td->fd", activated, down_all, preferred_element_type=jnp.float32)
    act_grads = jnp.einsum("td,fd->tf", down_all, w_down, preferred_element_type=jnp.float32)
    (upper_grads,) = gelu_pull(act_grads)
    upper_low = upper_grads.astype(jnp.bfloat16)
    grad_bias_up = jnp.sum(upper_low, axis=0, dtype=jnp.float32)
    grad_up = jnp.einsum("td,tf->df", hidden_all, upper_low, preferred_element_type=jnp.float32)
    piece = upper_low
    first_part = lax.psum_scatter(
        jnp.einsum("tf,df->td", piece, w_up, preferred_element_type=jnp.float32).astype(
            jnp.bfloat16
        ),
        "mp",
        scatter_dimension=0,
        tiled=True,
    ).astype(jnp.float32)
    first_grads = second_grads + first_part
    mixed_grads, gain_one, shift_one = norm_backward(
        first_grads, normed_one, inverse_one, vectors[4]
    )
    mixed_all = lax.all_gather(mixed_grads.astype(jnp.bfloat16), "mp", axis=0, tiled=True)
    grad_out = jnp.einsum("te,td->ed", attended, mixed_all, preferred_element_type=jnp.float32)
    attended_grads = jnp.einsum(
        "td,ed->te", mixed_all, w_out, preferred_element_type=jnp.float32
    ).astype(jnp.bfloat16)
    query_grads, key_grads, value_grads = lax.map(
        lambda items: attend_backward(*items),
        (head_query, head_key, head_value, attended_grads.reshape(shaped), logsums, segments),
    )
    qkv_low = jnp.stack(
        [
            query_grads.reshape(total, local_width),
            key_grads.reshape(total, local_width),
            value_grads.reshape(total, local_width),
        ],
        axis=1,
    ).astype(jnp.bfloat16)
    grad_bias_qv = jnp.sum(qkv_low[:, 0::2], axis=0, dtype=jnp.float32)
    grad_qkv = jnp.einsum("td,tcf->dcf", gathered, qkv_low, preferred_element_type=jnp.float32)
    piece = qkv_low
    input_part = lax.psum_scatter(
        jnp.einsum("tcf,dcf->td", piece, w_qkv, preferred_element_type=jnp.float32).astype(
            jnp.bfloat16
        ),
        "mp",
        scatter_dimension=0,
        tiled=True,
    ).astype(jnp.float32)
    input_sum = mixed_grads + input_part
    vector_terms = jnp.stack(
        [
            jnp.sum(time_rows[:, None] * input_sum, axis=0),
            jnp.sum(input_sum, axis=0),
            jnp.sum(mixed_grads, axis=0),
            jnp.sum(second_grads, axis=0),
            gain_one,
            shift_one,
            gain_two,
            shift_two,
        ],
        axis=0,
    )
    zero_index = jnp.zeros((), jnp.int32)
    qv_start = my_index * local_width
    up_start = my_index * local_hidden
    qv_placed = lax.dynamic_update_slice(
        jnp.zeros((2, D), jnp.float32), grad_bias_qv, (zero_index, qv_start)
    )
    up_placed = lax.dynamic_update_slice(jnp.zeros((FF,), jnp.float32), grad_bias_up, (up_start,))
    grad_qkv, grad_out, grad_up, grad_down = (
        lax.psum_scatter(
            grad_qkv.astype(jnp.bfloat16), "dp", scatter_dimension=0, tiled=True
        ).astype(jnp.float32),
        lax.psum_scatter(
            grad_out.astype(jnp.bfloat16), "dp", scatter_dimension=1, tiled=True
        ).astype(jnp.float32),
        lax.psum_scatter(
            grad_up.astype(jnp.bfloat16), "dp", scatter_dimension=0, tiled=True
        ).astype(jnp.float32),
        lax.psum_scatter(
            grad_down.astype(jnp.bfloat16), "dp", scatter_dimension=1, tiled=True
        ).astype(jnp.float32),
    )
    grad_vectors, qv_summed, up_summed = lax.psum(
        (vector_terms, qv_placed, up_placed), ("dp", "mp")
    )
    grad_bias_qv = lax.dynamic_slice_in_dim(qv_summed, qv_start, local_width, 1)
    grad_bias_up = lax.dynamic_slice_in_dim(up_summed, up_start, local_hidden, 0)
    return (
        output.astype(jnp.bfloat16),
        input_sum.astype(jnp.bfloat16),
        grad_qkv,
        grad_bias_qv,
        grad_out,
        grad_up,
        grad_bias_up,
        grad_down,
        grad_vectors,
    )


UNIT = 128
LONG = 4
MESH = pl.DeviceIdType.MESH


def fits_local(mesh):
    parts = mesh.shape["mp"]
    return mesh.shape["dp"] == 8 and parts == 4 and LEN % (16 * parts) == 0


def window_plan(rows, parts):
    firsts = [(rows * j) // UNIT - (LONG - 1) for j in range(parts)]
    offsets = [rows * j - UNIT * first for j, first in enumerate(firsts)]
    ends = [
        ((rows * (j + 1) - 1) // UNIT + LONG - firsts[j]) * UNIT for j in range(parts)
    ]
    return firsts, offsets, ends


def pick(table, index):
    value = jnp.int32(table[0])
    for j in range(1, len(table)):
        value = jnp.where(index == j, jnp.int32(table[j]), value)
    return value


NT = (((1,), (1,)), ((), ()))
TN = (((0,), (0,)), ((), ()))
FIRST_OWN, LAST_OWN = LONG - 1, LONG + 4


def two_heads(block):
    lane = lax.broadcasted_iota(jnp.int32, block.shape, 1)
    zero = jnp.zeros_like(block)
    return jnp.concatenate(
        [jnp.where(lane < HD, block, zero), jnp.where(lane < HD, zero, block)], axis=0
    )


def from_two(flipped):
    both = jnp.concatenate([flipped[:HD, :UNIT], flipped[HD:, UNIT:]], axis=0)
    return both.T


def by_rows(rows, body, carry):
    count = rows // 32

    def step(i, c):
        return body(pl.multiple_of(i * 32, 32), 32, c)

    carry = lax.fori_loop(0, count, step, carry)
    return body(count * 32, rows - count * 32, carry) if rows % 32 else carry


def fold(value):
    return value if value.shape[0] == 16 else value[:16] + value[16:]


class Clock:
    def __init__(self, rate):
        self.rate = {"c": 400e3, "x": rate, "y": rate, "z": rate}
        self.now = 0.0
        self.free = {}
        self.queue = []
        self.count = 0

    def send(self, link, size, action, share=1.0):
        begin = max(self.now, self.free.get(link, 0.0))
        end = begin + share * size / self.rate[link]
        self.free[link] = end
        self.count += 1
        heapq.heappush(self.queue, (end + 1.5, self.count, action))

    def work(self, time):
        self.now += time
        while self.queue and self.queue[0][0] <= self.now:
            heapq.heappop(self.queue)[2]()

    def step(self):
        ready, _, action = heapq.heappop(self.queue)
        self.now = max(self.now, ready)
        action()

    def drain(self):
        while self.queue:
            self.step()


def block_owners(d, core, x_first):
    x, y = lax.rem(d // 2, 2), d // 4
    if x_first:
        return [4 * b + 2 * a + core for a in (1 - x, x) for b in (1 - y, y)]
    return [4 * b + 2 * a + core for b in (1 - y, y) for a in (1 - x, x)]


RING = (2, 3, 1, 0)
HALO_TIME = 25.0


def fore_kernel(
    rows, window, parts, perm, back, steps, tokens, cotangent, w_split, w_out, w_up, w_down, bias_up, bias_qv, vectors, kf, qf,
    f_qkv, f_out, f_up, f_down, qkv, lse, att2, act2, slopes, first_t, lift_t, sec2, normed_out, second_low,
    second_grads, output, inverse, small,
    win, xq, yq, own_rows, attended, mixed, first, first_low, down, in_low, out_low, wu, wd, wq, wo, act, slope, lift2, first2,
    turned, stage, w_qkv, biases, bias_all, send, recv, own_sent, near, far, own, bias_send, bias_recv, local, pair_send, pair_recv,
):
    f32, low = jnp.float32, jnp.bfloat16
    d = lax.axis_index("dp")
    z = lax.axis_index("mp")
    core = lax.rem(d, 2)
    cut = D // parts
    three = 3 * cut
    pairs = cut // (2 * HD)
    firsts, offsets, ends = window_plan(rows, parts)
    offset = pl.multiple_of(pick(offsets, z), 16)
    shards = (w_qkv, w_out, w_up, w_down)
    fulls = (f_qkv, f_out, f_up, f_down)
    sizes = tuple(shard.shape[0] // 8 for shard in shards)
    partner = (d ^ 1, z)
    peers = [(d, z ^ k) for k in (1, 2, 3)] + [partner, (d ^ 2, z), (d ^ 4, z)]
    barrier = pltpu.get_barrier_semaphore()
    for peer in peers:
        pl.semaphore_signal(barrier, inc=1, device_id=peer, device_id_type=MESH)
    pl.semaphore_wait(barrier, len(peers))
    clock = Clock(46e3)

    order = [sorted((o for o in range(parts) if o != j), key=lambda o: (abs(o - j), o)) for j in range(parts)]
    source = [pick([order[j][n] for j in range(parts)], z) for n in range(parts - 1)]
    chunks = [(g, n) for n in range(parts - 1) for g in (0, 1)] + [(g, n) for n in range(parts - 1) for g in (2, 3)]
    index_of = {chunk: i for i, chunk in enumerate(chunks)}
    copies, done = {}, {}

    def part(ref, index, owner, size, half=None):
        start, count = owner * size, size
        if half is not None:
            count = size // 2
            start = start + half * count
        return ref.at[index, pl.ds(pl.multiple_of(start, 16), count), :]

    def remote(i, kind, src, dst, target):
        copy = pltpu.make_async_remote_copy(
            src, dst, send.at[i, kind], recv.at[i, kind], device_id=target, device_id_type=MESH
        )
        copy.start()
        copies[i, kind] = copy

    def place(i, owner, half=None):
        g, n = chunks[i]
        return part(fulls[g], source[n], owner, sizes[g], half)

    def bytes_of(i):
        g, n = chunks[i]
        return sizes[g] * shards[g].shape[1] * 2

    def pass_on(i, kind, owner, target, half=None):
        remote(i, kind, place(i, owner, half), place(i, owner, half), target)

    column = []

    def along(owner, place_of, here, there, sent, g):
        i = index_of[g, order[there].index(owner)]
        copy = pltpu.make_async_remote_copy(
            place_of, part(fulls[g], owner, d, sizes[g]), sent, recv.at[i, 0],
            device_id=(d, there), device_id_type=MESH,
        )

        @pl.when(z == here)
        def _():
            copy.start()

        column.append((here, copy))

    def send_own(g):
        rows_at = pl.ds(pl.multiple_of(d * sizes[g], 16), sizes[g])
        for here in range(parts):
            for n, there in enumerate((here - 1, here + 1)):
                if 0 <= there < parts:
                    along(here, shards[g].at[rows_at, :], here, there, own_sent.at[g, n], g)
        for n in range(parts - 1):
            i = index_of[g, n]
            clock.send("z", bytes_of(i), lambda i=i: hop_two(i))

    def hop_two(i):
        g, n = chunks[i]
        pltpu.make_async_remote_copy(
            place(i, d), place(i, d), send.at[i, 0], recv.at[i, 0], device_id=partner, device_id_type=MESH
        ).wait_recv()
        for here in range(parts):
            owner = order[here][n]
            there = here + 1 if owner < here else here - 1
            if 0 <= there < parts:
                along(owner, part(fulls[g], owner, d, sizes[g]), here, there, send.at[i, 0], g)
        if g == 2 and n == 0:
            send_own(3)
        pass_on(i, 1, d, (d ^ 2, z))
        pass_on(i, 2, d, (d ^ 4, z))
        pass_on(i, 5, d, partner)
        clock.send("c", bytes_of(i), lambda: None)
        clock.send("x", bytes_of(i), lambda: hop_three(i))
        clock.send("y", bytes_of(i), lambda: hop_four(i))

    def hop_three(i):
        copies[i, 1].wait_recv()
        pass_on(i, 3, d ^ 2, (d ^ 4, z), 0)
        pass_on(i, 6, d ^ 2, partner)
        clock.send("y", bytes_of(i) // 2, lambda: hop_five(i))

    def hop_four(i):
        copies[i, 2].wait_recv()
        pass_on(i, 4, d ^ 4, (d ^ 2, z), 1)
        pass_on(i, 7, d ^ 4, partner)
        clock.send("x", bytes_of(i) // 2, lambda: hop_six(i))

    def hop_five(i):
        copies[i, 3].wait_recv()
        pass_on(i, 8, d ^ 6, partner, 0)
        finish(i)

    def hop_six(i):
        copies[i, 4].wait_recv()
        pass_on(i, 9, d ^ 6, partner, 1)
        finish(i)

    def finish(i):
        done[i] = done.get(i, 0) + 1

    def arrive(i):
        while done.get(i, 0) < 2:
            clock.step()
        for kind in range(5, 10):
            copies[i, kind].wait_recv()

    halos = []
    for j in range(parts - 1):
        count = ends[j] - offsets[j] - rows
        halos.append((j + 1, j, pltpu.make_async_remote_copy(
            tokens.at[pl.ds(0, count), :], win.at[pl.ds(offsets[j] + rows, count), :],
            near.at[0], near.at[1], device_id=(d, j), device_id_type=MESH,
        )))
    for j in range(1, parts):
        halos.append((j - 1, j, pltpu.make_async_remote_copy(
            tokens.at[pl.ds(rows - offsets[j], offsets[j]), :], win.at[pl.ds(0, offsets[j]), :],
            far.at[0], far.at[1], device_id=(d, j), device_id_type=MESH,
        )))
    for sender, receiver, copy in halos:
        @pl.when(z == sender)
        def _(copy=copy):
            copy.start()
    clock.send("z", max(offsets) * D * 2, lambda: None)

    def join(n, c):
        at = pl.ds(pl.multiple_of(n * 64, 64), 64)
        for c3 in range(3):
            w_qkv[at, c3 * cut : (c3 + 1) * cut] = w_split[c3, at, :]
        return c

    lax.fori_loop(0, D // 64, join, 0)
    send_own(0)
    send_own(1)
    biases[...] = jnp.zeros_like(biases)
    biases[0:1, :] = bias_up[...].astype(f32)
    pair_rows = bias_qv[...].astype(f32)
    biases[1:2, 0:cut] = pair_rows[0:1]
    biases[1:2, 2 * cut : three] = pair_rows[1:2]
    bias_copies = []
    for k in (1, 2, 3):
        copy = pltpu.make_async_remote_copy(
            biases, bias_all.at[z], bias_send.at[k - 1], bias_recv.at[k - 1], device_id=(d, z ^ k), device_id_type=MESH
        )
        copy.start()
        bias_copies.append(copy)
    bias_all[pl.ds(z, 1)] = biases[...][None]
    owns = []
    for g in range(4):
        copy = pltpu.make_async_copy(shards[g], fulls[g].at[z], own.at[g])
        copy.start()
        owns.append(copy)

    step_time = steps[0].astype(f32) * 0.001
    shift = step_time * vectors[0:1, :]

    def lift(value):
        return value.astype(f32) + shift + vectors[1:2, :]

    def own_body(i, c):
        at = pl.ds(pl.multiple_of(i * 16, 16), 16)
        win[pl.ds(pl.multiple_of(offset + i * 16, 16), 16), :] = lift(tokens[at, :]).astype(low)
        return c

    lax.fori_loop(0, rows // 16, own_body, 0)
    zero = jnp.zeros((16, D), low)

    def spans_of(j):
        end = ends[j] if j < parts - 1 else offsets[j] + rows
        empty = [(0, offsets[0])] if j == 0 else []
        if end < window:
            empty.append((end, window))
        filled = [(0, offsets[j])] if j else []
        if j < parts - 1:
            filled.append((offsets[j] + rows, ends[j]))
        return empty, filled

    for j in range(parts):
        @pl.when(z == j)
        def _(j=j):
            for begin, end in spans_of(j)[0]:
                def clear(i, c, begin=begin):
                    win[pl.ds(pl.multiple_of(begin + i * 16, 16), 16), :] = zero
                    return c
                lax.fori_loop(0, (end - begin) // 16, clear, 0)

    pair_copies = []

    def exchange(source, target):
        index = len(pair_copies)
        copy = pltpu.make_async_remote_copy(
            source, target, pair_send.at[index], pair_recv.at[index], device_id=partner, device_id_type=MESH
        )
        copy.start()
        pair_copies.append(copy)
        return copy

    def columns(read, c, write):
        for j, owner in enumerate(block_owners(d, c, True)):
            write(slice(j * 128, (j + 1) * 128), read(pl.ds(pl.multiple_of(owner * 128, 128), 128)))

    own_at = pl.ds(offset, rows)
    mine = pl.ds(0, rows)
    theirs = pl.ds(rows, rows)
    columns(lambda at: win[own_at, at], 1 - core, lambda at, v: stage.__setitem__((0, slice(None), at), v))
    lift_copy = exchange(stage.at[0], lift2.at[theirs, :])
    columns(lambda at: win[own_at, at], core, lambda at, v: lift2.__setitem__((mine, at), v))

    def fetch(index, source, target):
        copy = pltpu.make_async_copy(source, target, local.at[index])
        copy.start()
        return copy

    clock.work(4.0)
    for copy in bias_copies:
        copy.wait_recv()
    clock.work(max(0.0, HALO_TIME - clock.now))
    for sender, receiver, copy in halos:
        @pl.when(z == receiver)
        def _(copy=copy):
            copy.wait_recv()
    send_own(2)
    for j in range(parts):
        @pl.when(z == j)
        def _(j=j):
            for begin, end in spans_of(j)[1]:
                def convert(i, c, begin=begin):
                    at = pl.ds(pl.multiple_of(begin + i * 16, 16), 16)
                    win[at, :] = lift(win[at, :]).astype(low)
                    return c
                lax.fori_loop(0, (end - begin) // 16, convert, 0)
    clock.work(2.0)
    lift_copy.wait_recv()
    turned[...] = lift2[...].T
    turned_out = fetch(0, turned, lift_t)
    clock.work(2.0)

    stores = {}
    for i in range(parts):
        k = i
        at_z = source[i - 1] if i else z
        if k == 0:
            wq_ref, wo_ref = w_qkv, w_out
        else:
            wq_ref, wo_ref = wq, wo
            load_q.wait()
        slot_i = i % 2
        if i >= 2:
            stores[i - 2].wait()
        row = bias_all.at[at_z]

        def project(n, c):
            at = pl.ds(pl.multiple_of(n * 512, 512), 512)
            for c3 in range(3):
                lanes = slice(c3 * cut, (c3 + 1) * cut)
                value = jnp.dot(win[at, :], wq_ref[:, lanes], preferred_element_type=f32)
                value = (value + row[1:2, lanes]).astype(low)
                if c3 == 0:
                    value = value * jnp.array(HD ** (-0.5), low)
                xq[slot_i, at, lanes] = value
            return c

        lax.fori_loop(0, window // 512, project, 0)
        stores[i] = fetch(3 + slot_i, xq.at[slot_i], qkv.at[at_z])
        clock.work(3.5)
        if i + 1 < parts:
            arrive(index_of[0, i])
            load_q = fetch(1, f_qkv.at[source[i]], wq)

        def attend(step, c):
            p, slot = step // 3, lax.rem(step, 3)
            lanes = lambda base: pl.ds(pl.multiple_of(base + p * 2 * HD, 2 * HD), 2 * HD)
            unit_at = [pl.ds(perm[slot * LONG + m] * UNIT, UNIT) for m in range(LONG)]
            keys = jnp.concatenate([xq[slot_i, at, lanes(cut)] for at in unit_at], axis=0)
            values = jnp.concatenate([xq[slot_i, at, lanes(2 * cut)] for at in unit_at], axis=0)
            marks = jnp.concatenate([kf[at, :] for at in unit_at], axis=0)
            wide_keys = jnp.concatenate([keys, marks], axis=1)
            pair = jnp.concatenate([two_heads(xq[slot_i, at, lanes(0)]) for at in unit_at], axis=0)
            mark = jnp.concatenate([qf[at, :] for at in unit_at for _ in range(2)], axis=0)
            wide_pair = jnp.concatenate([pair, mark], axis=1)
            scores = lax.dot_general(wide_keys, wide_pair, NT, preferred_element_type=f32)
            highest = jnp.max(scores, axis=0, keepdims=True)
            weights = jnp.exp(scores - highest)
            total = jnp.sum(weights, axis=0, keepdims=True)
            flipped = lax.dot_general(values, weights.astype(low), TN, preferred_element_type=f32) * (1.0 / total)
            logsum = highest + jnp.log(total)
            for m in range(LONG):
                two = slice(m * 2 * UNIT, (m + 1) * 2 * UNIT)
                at = pl.ds(pl.multiple_of(slot * LONG * UNIT + m * UNIT, UNIT), UNIT)
                yq[at, lanes(0)] = from_two(flipped[:, two]).astype(low)
                lse[at_z, pl.ds(step * LONG + m, 1), :] = logsum[:, two]
            return c

        lax.fori_loop(0, pairs * 3, attend, 0, unroll=2)
        clock.work(7.5)
        for u in range(FIRST_OWN, LAST_OWN + 1):
            own_rows[pl.ds((u - FIRST_OWN) * UNIT, UNIT), :] = yq[pl.ds(back[u] * UNIT, UNIT), :]
        lanes_z = pl.ds(pl.multiple_of(at_z * cut, cut), cut)
        attended[i] = own_rows[pl.ds(pl.multiple_of(offset - FIRST_OWN * UNIT, 16), rows), :]
        exchange(attended.at[i], att2.at[theirs, lanes_z])
        stores["a", i] = fetch(5 + i, attended.at[i], att2.at[mine, lanes_z])
        if k:
            load_o.wait()

        def out_body(n, c):
            at = pl.ds(pl.multiple_of(n * 256, 256), 256)
            value = jnp.dot(attended[i], wo_ref[:, at], preferred_element_type=f32)
            if i == 0:
                mixed[:, at] = value
            else:
                mixed[:, at] += value
            return c

        lax.fori_loop(0, D // 256, out_body, 0)
        clock.work(1.5)
        if i + 1 < parts:
            arrive(index_of[1, i])
            load_o = fetch(2, f_out.at[source[i]], wo)

    def norm_one(begin, count, c):
        at = pl.ds(begin, count)
        value = lift(tokens[at, :]) + (mixed[at, :] + vectors[2:3, :])
        centred = value - jnp.mean(value, axis=-1, keepdims=True)
        scale = lax.rsqrt(jnp.mean(centred * centred, axis=-1, keepdims=True) + 1e-05)
        normed = centred * scale
        mixed[at, :] = normed
        inverse[at, :] = scale
        result = normed * vectors[4:5, :] + vectors[5:6, :]
        first[at, :] = result
        first_low[at, :] = result.astype(low)
        return c

    by_rows(rows, norm_one, 0)
    normed_store = fetch(9, mixed, normed_out)
    columns(lambda at: first_low[:, at], 1 - core, lambda at, v: stage.__setitem__((1, slice(None), at), v))
    first_copy = exchange(stage.at[1], first2.at[theirs, :])
    columns(lambda at: first_low[:, at], core, lambda at, v: first2.__setitem__((mine, at), v))
    clock.work(4.0)

    for i in range(parts):
        k = i
        at_z = source[i - 1] if i else z
        slot_i = i % 2
        if k == 0:
            up_ref, down_ref = w_up, w_down
        else:
            up_ref, down_ref = wu, wd
            load_u.wait()
        if i >= 2:
            for copy in stores["f", i - 2]:
                copy.wait()
            stores["r", i - 2].wait_send()
        row = bias_all.at[at_z]

        def upper_body(n, c):
            at = pl.ds(pl.multiple_of(n * 256, 256), 256)
            value = jnp.dot(first_low[...], up_ref[:, at], preferred_element_type=f32) + row[0:1, at]
            chance = 0.5 + 0.5 * lax.erf(value * (0.5**0.5))
            act[slot_i, :, at] = (value * chance).astype(low)
            density = jnp.exp(-0.5 * value * value) * (0.5 / jnp.pi) ** 0.5
            slope[slot_i, :, at] = (chance + value * density).astype(low)
            return c

        lax.fori_loop(0, D // 256, upper_body, 0)
        hidden = pl.ds(pl.multiple_of(at_z * D, D), D)
        stores["r", i] = exchange(act.at[slot_i], act2.at[theirs, hidden])
        stores["f", i] = (
            fetch(14 + slot_i, act.at[slot_i], act2.at[mine, hidden]),
            fetch(10 + slot_i, slope.at[slot_i], slopes.at[:, hidden]),
        )
        clock.work(4.0)
        if i + 1 < parts:
            arrive(index_of[2, i])
            load_u = fetch(1, f_up.at[source[i]], wu)
        if k:
            load_d.wait()

        def down_body(n, c):
            at = pl.ds(pl.multiple_of(n * 256, 256), 256)
            value = jnp.dot(act[slot_i], down_ref[:, at], preferred_element_type=f32)
            if i == 0:
                down[:, at] = value
            else:
                down[:, at] += value
            return c

        lax.fori_loop(0, D // 256, down_body, 0)
        clock.work(2.0)
        if i + 1 < parts:
            arrive(index_of[3, i])
            load_d = fetch(2, f_down.at[source[i]], wd)
        if i == 0:
            first_copy.wait_recv()
            turned_out.wait()
            turned[...] = first2[...].T
            turned_out = fetch(0, turned, first_t)
            clock.work(2.0)

    zero_row = jnp.zeros((16, D), f32)

    def norm_two(begin, count, sums):
        at = pl.ds(begin, count)
        value = first[at, :] + (down[at, :] + vectors[3:4, :])
        centred = value - jnp.mean(value, axis=-1, keepdims=True)
        scale = lax.rsqrt(jnp.mean(centred * centred, axis=-1, keepdims=True) + 1e-05)
        normed = centred * scale
        out_low[at, :] = (normed * vectors[6:7, :] + vectors[7:8, :]).astype(low)
        grads = cotangent[at, :].astype(f32)
        scaled = grads * vectors[6:7, :]
        result = scale * (
            scaled
            - jnp.mean(scaled, axis=-1, keepdims=True)
            - normed * jnp.mean(scaled * normed, axis=-1, keepdims=True)
        )
        down[at, :] = result
        in_low[at, :] = result.astype(low)
        return (sums[0] + fold(result), sums[1] + fold(grads * normed), sums[2] + fold(grads))

    sums = by_rows(rows, norm_two, (zero_row, zero_row, zero_row))
    last = [fetch(1, out_low, output), fetch(2, in_low, second_low), fetch(12, down, second_grads)]
    small[...] = jnp.zeros_like(small)
    small[3:4, :] = jnp.sum(sums[0], axis=0, keepdims=True)
    small[6:7, :] = jnp.sum(sums[1], axis=0, keepdims=True)
    small[7:8, :] = jnp.sum(sums[2], axis=0, keepdims=True)
    small[15:16, :] = jnp.full((1, D), step_time, f32)
    columns(lambda at: in_low[:, at], 1 - core, lambda at, v: stage.__setitem__((2, slice(None), at), v))
    exchange(stage.at[2], sec2.at[theirs, :])
    columns(lambda at: in_low[:, at], core, lambda at, v: stage.__setitem__((3, slice(None), at), v))
    last.append(fetch(13, stage.at[3], sec2.at[mine, :]))
    clock.drain()
    for copy in last + owns + [turned_out, normed_store, stores[2], stores[3]]:
        copy.wait()
    for i in range(parts):
        stores["a", i].wait()
        if i >= 2:
            for copy in stores["f", i]:
                copy.wait()
    waited = [stores["r", 0], stores["r", 1]]
    for copy in pair_copies:
        if not any(copy is other for other in waited):
            copy.wait_send()
        if copy is not lift_copy and copy is not first_copy:
            copy.wait_recv()
    for copy in copies.values():
        copy.wait_send()
    for here, copy in column:
        @pl.when(z == here)
        def _(copy=copy):
            copy.wait_send()
    for copy in bias_copies:
        copy.wait_send()
    for sender, receiver, copy in halos:
        @pl.when(z == sender)
        def _(copy=copy):
            copy.wait_send()


def fore_call(rows, window, parts, perm, back, steps, *arrays):
    f32, low = jnp.float32, jnp.bfloat16
    any_ = pl.BlockSpec(memory_space=pl.ANY)
    vmem = pl.BlockSpec(memory_space=pltpu.VMEM)
    smem = pl.BlockSpec(memory_space=pltpu.SMEM)
    cut = D // parts
    three = 3 * cut
    shape = jax.ShapeDtypeStruct
    marks = cut // (2 * HD) * 3 * LONG
    dma = pltpu.SemaphoreType.DMA
    return pl.pallas_call(
        functools.partial(fore_kernel, rows, window, parts),
        out_shape=[
            shape((parts, D, three), low),
            shape((parts, cut, D), low),
            shape((parts, D, D), low),
            shape((parts, D, D), low),
            shape((parts, window, three), low),
            shape((parts, marks, 2 * UNIT), f32),
            shape((2 * rows, D), low),
            shape((2 * rows, FF), low),
            shape((rows, FF), low),
            shape((512, 2 * rows), low),
            shape((512, 2 * rows), low),
            shape((2 * rows, 512), low),
            shape((rows, D), f32),
            shape((rows, D), low),
            shape((rows, D), f32),
            shape((rows, D), low),
            shape((rows, 1), f32),
            shape((16, D), f32),
        ],
        in_specs=[smem] * 3 + [vmem] * len(arrays),
        out_specs=[any_] * 5 + [vmem] + [any_] * 10 + [vmem] * 2,
        scratch_shapes=[
            pltpu.VMEM((window, D), low),
            pltpu.VMEM((2, window, three), low),
            pltpu.VMEM((window, cut), low),
            pltpu.VMEM(((LAST_OWN + 1 - FIRST_OWN) * UNIT, cut), low),
            pltpu.VMEM((parts, rows, cut), low),
            pltpu.VMEM((rows, D), f32),
            pltpu.VMEM((rows, D), f32),
            pltpu.VMEM((rows, D), low),
            pltpu.VMEM((rows, D), f32),
            pltpu.VMEM((rows, D), low),
            pltpu.VMEM((rows, D), low),
            pltpu.VMEM((D, D), low),
            pltpu.VMEM((D, D), low),
            pltpu.VMEM((D, three), low),
            pltpu.VMEM((cut, D), low),
            pltpu.VMEM((2, rows, D), low),
            pltpu.VMEM((2, rows, D), low),
            pltpu.VMEM((2 * rows, 512), low),
            pltpu.VMEM((2 * rows, 512), low),
            pltpu.VMEM((512, 2 * rows), low),
            pltpu.VMEM((4, rows, 512), low),
            pltpu.VMEM((D, three), low),
            pltpu.VMEM((8, D), f32),
            pltpu.VMEM((parts, 8, D), f32),
            dma((12, 10)),
            dma((12, 10)),
            dma((4, 2)),
            dma((2,)),
            dma((2,)),
            dma((4,)),
            dma((3,)),
            dma((3,)),
            dma((16,)),
            dma((2 * parts + 3,)),
            dma((2 * parts + 3,)),
        ],
        compiler_params=pltpu.CompilerParams(
            collective_id=0, has_side_effects=True, vmem_limit_bytes=56 * 2**20
        ),
    )(perm, back, steps, *arrays)


def back_kernel(
    rows, window, parts, perm, back, sec_low, sec2, inverse, gain, small_in, kf, qf, lse,
    first_t, lift_t, second_grads, normed_one, act2, dgelu, att2, qkv, f_qkv, f_out, f_up, f_down,
    input_grad, g_qkv, g_out, g_up, g_down, small_out,
    acc, normed, turned, arena, act, slope, y, up2, w_in, mixed2, mixed_win, small, small_in_far,
    s_down, s_up, s_out, s_qkv, k_down, k_up, k_out, k_qkv,
    r_down, r_up, r_out, r_qkv, t_down, t_up, t_out, t_qkv, z_down, z_up, z_out, z_qkv,
    local, hop_send, hop_recv, pair_send, pair_recv, halo_send, halo_recv, small_send, small_recv,
):
    f32, low = jnp.float32, jnp.bfloat16
    d = lax.axis_index("dp")
    z = lax.axis_index("mp")
    core = lax.rem(d, 2)
    firsts, offsets, ends = window_plan(rows, parts)
    offset = pl.multiple_of(pick(offsets, z), 16)
    partner = (d ^ 1, z)
    peers = [(d, z ^ k) for k in (1, 2, 3)] + [partner, (d ^ 2, z), (d ^ 4, z), (d ^ 6, z)]
    barrier = pltpu.get_barrier_semaphore()
    for peer in peers:
        pl.semaphore_signal(barrier, inc=1, device_id=peer, device_id_type=MESH)
    pl.semaphore_wait(barrier, len(peers))
    clock = Clock(47e3)
    tail = []

    wide = 2 * rows
    wd = arena.at[pl.ds(0, D), :]
    wu = arena.at[pl.ds(D, D), :]

    def fetch(index, source, target):
        copy = pltpu.make_async_copy(source, target, local.at[index])
        copy.start()
        return copy

    chunk = lambda k: z ^ k
    hidden = lambda k: pl.ds(pl.multiple_of(chunk(k) * D, D), D)
    load_wd = lambda i: fetch(0, f_down.at[chunk(RING[i])], wd)
    load_wu = lambda i: fetch(1, f_up.at[chunk(RING[i])], wu)
    load_act = lambda i: fetch(2, act2.at[:, hidden(RING[i])], act)
    load_slope = lambda i: fetch(3, dgelu.at[:, hidden(RING[i])], slope)
    at_act, at_wd, at_slope, at_wu = load_act(0), load_wd(0), load_slope(0), load_wu(0)
    at_acc = fetch(4, second_grads, acc)
    at_normed = fetch(5, normed_one, normed)
    at_turned = fetch(6, first_t, turned)

    zero = jnp.zeros((16, D), low)
    for j in range(parts):
        spans = []
        if j == 0:
            spans.append((0, offsets[0]))
        begin = ends[j] if j < parts - 1 else offsets[j] + rows
        if begin < window:
            spans.append((begin, window))
        if spans:
            @pl.when(z == j)
            def _(spans=spans):
                for begin, end in spans:
                    def clear(i, c):
                        mixed_win[pl.ds(pl.multiple_of(begin + i * 16, 16), 16), :] = zero
                        return c
                    lax.fori_loop(0, (end - begin) // 16, clear, 0)

    groups = {
        "down": (s_down, k_down, r_down, t_down, z_down, g_down, 0),
        "up": (s_up, k_up, r_up, t_up, z_up, g_up, 1),
        "out": (s_out, k_out, r_out, t_out, z_out, g_out, 2),
        "qkv": (s_qkv, k_qkv, r_qkv, t_qkv, z_qkv, g_qkv, 3),
    }
    hops, finished = {}, {}

    def x_ahead(g, i):
        return (i + groups[g][6]) % 2 == 0

    def put(g, i, j, at, value):
        if not x_ahead(g, i):
            j = (0, 2, 1, 3)[j]
        if j < 2:
            groups[g][0][(i % 2, j) + at] = value
        else:
            groups[g][1][(i, j - 2) + at] = value

    def hop(g, i, kind, source, target, device):
        index = groups[g][6]
        copy = pltpu.make_async_remote_copy(
            source, target, hop_send.at[index, i, kind], hop_recv.at[index, i, kind],
            device_id=device, device_id_type=MESH,
        )
        copy.start()
        hops[g, i, kind] = copy

    def add_into(ref, other):
        count = ref.shape[0]
        step = min(count, 64)

        def body(j, c):
            at = pl.ds(pl.multiple_of(j * step, step), step)
            ref[at, :] = (ref[at, :].astype(f32) + other[at, :].astype(f32)).astype(low)
            return c

        lax.fori_loop(0, count // step, body, 0)

    def launch(g, i):
        s, kept, r, t, zb, out, index = groups[g]
        x_first = x_ahead(g, i)
        n1, n2 = ((d ^ 2, z), (d ^ 4, z)) if x_first else ((d ^ 4, z), (d ^ 2, z))
        l1, l2 = ("x", "y") if x_first else ("y", "x")
        block = s.shape[2] * s.shape[3] * 2
        k = RING[i]
        hop(g, i, 0, s.at[i % 2], r.at[i], n1)

        def second():
            hops[g, i, 0].wait_recv()
            add_into(kept.at[i, 0], r.at[i, 0])
            hop(g, i, 1, kept.at[i, 0], t.at[i], n2)
            clock.send(l2, block, third)
            add_into(kept.at[i, 1], r.at[i, 1])

        def third():
            hops[g, i, 1].wait_recv()
            add_into(kept.at[i, 1], t.at[i])
            if k:
                hop(g, i, 2, kept.at[i, 1], zb.at[k - 1], (d, z ^ k))
                clock.send("z", block, fourth, 1.0 if k == 1 else 2.0)
            else:
                ended()

        def fourth():
            hops[g, i, 2].wait_recv()
            ended()

        def ended():
            finished[g] = finished.get(g, 0) + 1
            if finished[g] == parts:
                finish(g)

        clock.send(l1, 2 * block, second)

    def free_slot(g, i):
        if i >= 2:
            hops[g, i - 2, 0].wait_send()

    def finish(g):
        s, kept, r, t, zb, out, index = groups[g]
        own = RING.index(0)
        count = s.shape[2]
        step = min(count, 64)
        pieces = kept.at[own, 1]

        def body(j, c):
            at = pl.ds(pl.multiple_of(j * step, step), step)
            total = pieces[at, :].astype(f32)
            for k in range(parts - 1):
                total = total + zb[k, at, :].astype(f32)
            if g == "qkv":
                for c3 in range(3):
                    out[c3, at, :] = total[:, c3 * out.shape[2] : (c3 + 1) * out.shape[2]]
            else:
                out[at, :] = total
            return c

        lax.fori_loop(0, count // step, body, 0)

    def exchange(index, source, target):
        copy = pltpu.make_async_remote_copy(
            source, target, pair_send.at[index], pair_recv.at[index], device_id=partner, device_id_type=MESH
        )
        copy.start()
        return copy

    small[...] = small_in[...]

    pending = {}

    def grad_up_chunk(i):
        pending.pop(i).wait_recv()
        if i == 0:
            at_turned.wait()
        free_slot("up", i)

        def body(n, c):
            at = pl.ds(pl.multiple_of(n * 256, 256), 256)
            tile = jnp.dot(turned[...], up2[i, :, at], preferred_element_type=f32).astype(low)
            for j in range(4):
                put("up", i, j, (slice(None), at), tile[j * 128 : (j + 1) * 128])
            return c

        lax.fori_loop(0, 4, body, 0)
        launch("up", i)
        clock.work(2.0)

    exchanges = []
    loads = {"wd": at_wd, "wu": at_wu, "slope": at_slope, "act": at_act}

    def upper_chunk(i):
        loads["wd"].wait()
        loads["slope"].wait()
        bias_row = chunk(RING[i])

        def body(n, c):
            at = pl.ds(pl.multiple_of(n * 256, 256), 256)
            grads = lax.dot_general(sec_low[...], wd[at, :], NT, preferred_element_type=f32)
            value = (grads * slope[:, at].astype(f32)).astype(low)
            up2[i, pl.ds(0, rows), at] = value
            small[pl.ds(10 + bias_row, 1), at] = jnp.sum(value.astype(f32), axis=0, keepdims=True)
            return c

        lax.fori_loop(0, 4, body, 0)
        pending[i] = exchange(i, up2.at[i, pl.ds(0, rows), :], up2.at[i, pl.ds(rows, rows), :])
        exchanges.append(pending[i])
        clock.work(2.5)
        if i + 1 < parts:
            loads["wd"], loads["slope"] = load_wd(i + 1), load_slope(i + 1)

    def grad_down_chunk(i):
        loads["act"].wait()
        free_slot("down", i)

        def body(n, c):
            at = pl.ds(pl.multiple_of(n * 256, 256), 256)
            tile = lax.dot_general(act[:, at], sec2[...], TN, preferred_element_type=f32).astype(low)
            for j in range(4):
                put("down", i, j, (at, slice(None)), tile[:, j * 128 : (j + 1) * 128])
            return c

        lax.fori_loop(0, 4, body, 0)
        launch("down", i)
        clock.work(2.0)
        if i + 1 < parts:
            loads["act"] = load_act(i + 1)

    def first_chunk(i):
        loads["wu"].wait()
        if i == 0:
            at_acc.wait()

        def body(n, c):
            at = pl.ds(pl.multiple_of(n * 256, 256), 256)
            acc[:, at] += lax.dot_general(
                up2[i, pl.ds(0, rows), :], wu[at, :], NT, preferred_element_type=f32
            )
            return c

        lax.fori_loop(0, 4, body, 0)
        clock.work(2.0)
        if i + 1 < parts:
            loads["wu"] = load_wu(i + 1)

    grad_down_chunk(0)
    for i in range(parts):
        upper_chunk(i)
        first_chunk(i)
        if i == 1:
            grad_down_chunk(1)

    at_normed.wait()
    zero_row = jnp.zeros((16, D), f32)

    def norm_body(begin, count, sums):
        at = pl.ds(begin, count)
        grads, unit = acc[at, :], normed[at, :]
        scaled = grads * gain[4:5, :]
        result = inverse[at, :] * (
            scaled
            - jnp.mean(scaled, axis=-1, keepdims=True)
            - unit * jnp.mean(scaled * unit, axis=-1, keepdims=True)
        )
        acc[at, :] = result
        mixed_win[pl.ds(pl.multiple_of(offset + begin, 16), count), :] = result.astype(low)
        return (sums[0] + fold(grads * unit), sums[1] + fold(grads), sums[2] + fold(result))

    sums = by_rows(rows, norm_body, (zero_row, zero_row, zero_row))
    small[4:5, :] = jnp.sum(sums[0], axis=0, keepdims=True)
    small[5:6, :] = jnp.sum(sums[1], axis=0, keepdims=True)
    small[2:3, :] = jnp.sum(sums[2], axis=0, keepdims=True)
    halos = []
    for j in range(parts - 1):
        count = ends[j] - offsets[j] - rows
        halos.append((j + 1, j, pltpu.make_async_remote_copy(
            mixed_win.at[pl.ds(offsets[j + 1], count), :],
            mixed_win.at[pl.ds(offsets[j] + rows, count), :],
            halo_send.at[0], halo_recv.at[0], device_id=(d, j), device_id_type=MESH,
        )))
    for j in range(1, parts):
        halos.append((j - 1, j, pltpu.make_async_remote_copy(
            mixed_win.at[pl.ds(offsets[j - 1] + rows - offsets[j], offsets[j]), :],
            mixed_win.at[pl.ds(0, offsets[j]), :],
            halo_send.at[1], halo_recv.at[1], device_id=(d, j), device_id_type=MESH,
        )))
    for sender, receiver, copy in halos:
        @pl.when(z == sender)
        def _(copy=copy):
            copy.start()
    clock.work(4.0)
    for i in range(parts):
        grad_up_chunk(i)
        if i + 2 < parts:
            grad_down_chunk(i + 2)
    own_at = pl.ds(offset, rows)
    for j, owner in enumerate(block_owners(d, 1 - core, True)):
        y[0:rows, j * 128 : (j + 1) * 128] = mixed_win[own_at, pl.ds(pl.multiple_of(owner * 128, 128), 128)]
    exchanges.append(exchange(parts, y.at[pl.ds(0, rows), pl.ds(0, 512)], mixed2.at[pl.ds(rows, rows), :]))
    for j, owner in enumerate(block_owners(d, core, True)):
        mixed2[pl.ds(0, rows), j * 128 : (j + 1) * 128] = mixed_win[
            own_at, pl.ds(pl.multiple_of(owner * 128, 128), 128)
        ]
    clock.work(4.0)

    cut = D // parts
    three = 3 * cut
    pairs = cut // (2 * HD)
    x = arena
    wo = slope.at[pl.ds(0, cut), :]
    load_x = lambda i: fetch(0, qkv.at[chunk(RING[i])], arena.at[pl.ds(0, window), pl.ds(0, three)])
    load_wo = lambda i: fetch(1, f_out.at[chunk(RING[i])], wo)
    load_att = lambda i: fetch(
        2, att2.at[:, pl.ds(pl.multiple_of(chunk(RING[i]) * cut, cut), cut)], act.at[:, pl.ds(0, cut)]
    )
    load_wi = lambda i: fetch(3, f_qkv.at[chunk(RING[i])], w_in)
    at_turned = fetch(6, lift_t, turned)
    at_x, at_wo, at_att, at_wi = load_x(0), load_wo(0), load_att(0), load_wi(0)
    exchanges[-1].wait_recv()
    scale = HD ** (-0.5)

    def take_halo():
        for sender, receiver, copy in halos:
            @pl.when(z == receiver)
            def _(copy=copy):
                copy.wait_recv()

    def grad_qkv_chunk(i):
        pending.pop(i).wait_recv()
        if i == 0:
            at_turned.wait()
        free_slot("qkv", i)

        def body(n, c):
            at = pl.ds(pl.multiple_of(n * 256, 256), 256)
            tile = jnp.dot(turned[...], up2[i, :, at], preferred_element_type=f32).astype(low)
            for j in range(4):
                put("qkv", i, j, (slice(None), at), tile[j * 128 : (j + 1) * 128])
            return c

        lax.fori_loop(0, three // 256, body, 0)
        launch("qkv", i)
        clock.work(1.8)

    for i in range(parts):
        at_att.wait()
        free_slot("out", i)
        tile = lax.dot_general(act[:, 0:cut], mixed2[...], TN, preferred_element_type=f32).astype(low)
        for j in range(4):
            put("out", i, j, (slice(None), slice(None)), tile[:, j * 128 : (j + 1) * 128])
        launch("out", i)
        clock.work(0.8)
        if i == 0:
            take_halo()
        at_wo.wait()

        def flow_body(n, c):
            at = pl.ds(pl.multiple_of(n * 512, 512), 512)
            x[at, three : three + cut] = lax.dot_general(
                mixed_win[at, :], wo[...], NT, preferred_element_type=f32
            ).astype(low)
            return c

        lax.fori_loop(0, window // 512, flow_body, 0)
        clock.work(1.5)
        if i:
            grad_qkv_chunk(i - 1)
        at_x.wait()
        if i == 0:
            exchanges[parts].wait_send()
        if i + 1 < parts:
            at_wo, at_att = load_wo(i + 1), load_att(i + 1)

        def attend_body(step, c):
            p, slot = step // 3, lax.rem(step, 3)
            lanes = lambda base: pl.ds(pl.multiple_of(base + p * 2 * HD, 2 * HD), 2 * HD)
            unit_at = [
                pl.ds(perm[slot * LONG + m] * UNIT, UNIT) for m in range(LONG)
            ]
            keys = jnp.concatenate([x[at, lanes(cut)] for at in unit_at], axis=0)
            values = jnp.concatenate([x[at, lanes(2 * cut)] for at in unit_at], axis=0)
            marks = jnp.concatenate([kf[at, :] for at in unit_at], axis=0)
            wide_keys = jnp.concatenate([keys, marks], axis=1)
            pair = jnp.concatenate([two_heads(x[at, lanes(0)]) for at in unit_at], axis=0)
            grads = jnp.concatenate([two_heads(x[at, lanes(three)]) for at in unit_at], axis=0)
            mark = jnp.concatenate([qf[at, :] for at in unit_at for _ in range(2)], axis=0)
            wide_pair = jnp.concatenate([pair, mark], axis=1)
            logsum = jnp.concatenate(
                [lse[chunk(RING[i]), pl.ds(step * LONG + m, 1), :] for m in range(LONG)], axis=1
            )
            scores = lax.dot_general(wide_keys, wide_pair, NT, preferred_element_type=f32)
            chances = jnp.exp(scores - logsum)
            flow = lax.dot_general(values, grads, NT, preferred_element_type=f32)
            terms = chances * flow
            slopes = (chances * (flow - jnp.sum(terms, axis=0, keepdims=True))).astype(low)
            v_sum = jnp.dot(chances.astype(low), grads, preferred_element_type=f32)
            k_sum = jnp.dot(slopes, pair, preferred_element_type=f32)
            flipped = lax.dot_general(keys, slopes, TN, preferred_element_type=f32)
            for m in range(LONG):
                two = slice(m * 2 * UNIT, (m + 1) * 2 * UNIT)
                at = pl.ds(pl.multiple_of(slot * LONG * UNIT + m * UNIT, UNIT), UNIT)
                y[at, lanes(0)] = (from_two(flipped[:, two]) * scale).astype(low)
            at = pl.ds(pl.multiple_of(slot * LONG * UNIT, UNIT), LONG * UNIT)
            y[at, lanes(cut)] = k_sum.astype(low)
            y[at, lanes(2 * cut)] = v_sum.astype(low)
            return c

        lax.fori_loop(0, pairs * 3, attend_body, 0, unroll=2)
        clock.work(10.5)
        if i + 1 < parts:
            at_x = load_x(i + 1)
        for u in range(FIRST_OWN, LAST_OWN + 1):
            at = pl.ds(back[u] * UNIT, UNIT)
            act[pl.ds((u - FIRST_OWN) * UNIT, UNIT), cut:] = y[at, :]
        exchanges[i].wait_send()
        inner_at = pl.ds(pl.multiple_of(offset - FIRST_OWN * UNIT, 16), rows)
        up2[i, pl.ds(0, rows), 0:three] = act[inner_at, cut:]
        pending[i] = exchange(
            parts + 1 + i, up2.at[i, pl.ds(0, rows), pl.ds(0, three)], up2.at[i, pl.ds(rows, rows), pl.ds(0, three)]
        )
        exchanges.append(pending[i])
        place = pl.multiple_of(chunk(RING[i]) * cut, cut)
        small[8:9, pl.ds(place, cut)] = jnp.sum(up2[i, pl.ds(0, rows), 0:cut].astype(f32), axis=0, keepdims=True)
        small[9:10, pl.ds(place, cut)] = jnp.sum(
            up2[i, pl.ds(0, rows), 2 * cut : three].astype(f32), axis=0, keepdims=True
        )
        at_wi.wait()

        def input_body(n, c, i=i):
            at = pl.ds(pl.multiple_of(n * 256, 256), 256)
            acc[:, at] += lax.dot_general(
                up2[i, pl.ds(0, rows), 0:three], w_in[at, :], NT, preferred_element_type=f32
            )
            return c

        lax.fori_loop(0, 4, input_body, 0)
        clock.work(2.0)
        if i + 1 < parts:
            at_wi = load_wi(i + 1)

    def last_body(begin, count, total):
        at = pl.ds(begin, count)
        value = acc[at, :]
        arena[at, :] = value.astype(low)
        return total + fold(value)

    total = jnp.sum(by_rows(rows, last_body, zero_row), axis=0, keepdims=True)
    store = fetch(4, arena.at[pl.ds(0, rows), :], input_grad)
    small[0:1, :] = total * small_in[15:16, :]
    small[1:2, :] = total
    clock.work(2.0)
    stages = [[partner], [(d ^ 2, z), (d ^ 4, z), (d ^ 6, z)], [(d, z ^ k) for k in (1, 2, 3)]]

    def small_stage(n, first_slot):
        sent = []
        for slot, device in enumerate(stages[n], first_slot):
            copy = pltpu.make_async_remote_copy(
                small, small_in_far.at[slot], small_send.at[slot], small_recv.at[slot],
                device_id=device, device_id_type=MESH,
            )
            copy.start()
            sent.append(copy)

        def take():
            for copy in sent:
                copy.wait()
            for slot in range(first_slot, first_slot + len(sent)):
                small[...] += small_in_far[slot]
            if n + 1 < len(stages):
                small_stage(n + 1, first_slot + len(sent))

        clock.send("c", 0.6e6, take)

    small_stage(0, 0)
    grad_qkv_chunk(parts - 1)
    clock.drain()
    assert sum(finished.values()) == 4 * parts
    small_out[...] = small[...]
    store.wait()
    for (g, i, kind), copy in hops.items():
        if kind or i >= 2:
            copy.wait_send()
    for copy in exchanges[parts + 1 :]:
        copy.wait_send()
    for sender, receiver, copy in halos:
        @pl.when(z == sender)
        def _(copy=copy):
            copy.wait_send()


def back_call(rows, window, parts, perm, back, vmem_in, hbm_in):
    f32, low = jnp.float32, jnp.bfloat16
    any_ = pl.BlockSpec(memory_space=pl.ANY)
    vmem = pl.BlockSpec(memory_space=pltpu.VMEM)
    smem = pl.BlockSpec(memory_space=pltpu.SMEM)
    cut = D // parts
    shapes = {"down": (D, 128), "up": (128, D), "out": (cut, 128), "qkv": (128, 3 * cut)}
    outs = [jax.ShapeDtypeStruct((rows, D), low)]
    outs += [jax.ShapeDtypeStruct(shape, f32) for shape in ((3, 128, cut), shapes["out"], shapes["up"], shapes["down"])]
    outs += [jax.ShapeDtypeStruct((16, D), f32)]
    order = ("down", "up", "out", "qkv")
    buffers = [pltpu.VMEM((2, 2) + shapes[g], low) for g in order]
    buffers += [pltpu.VMEM((parts, 2) + shapes[g], low) for g in order]
    buffers += [pltpu.VMEM((parts, 2) + shapes[g], low) for g in order]
    buffers += [pltpu.VMEM((parts,) + shapes[g], low) for g in order]
    buffers += [pltpu.VMEM((parts - 1,) + shapes[g], low) for g in order]
    dma = pltpu.SemaphoreType.DMA
    return pl.pallas_call(
        functools.partial(back_kernel, rows, window, parts),
        out_shape=outs,
        in_specs=[smem, smem] + [vmem] * len(vmem_in) + [any_] * len(hbm_in),
        out_specs=[any_] + [vmem] * 5,
        scratch_shapes=[
            pltpu.VMEM((rows, D), f32),
            pltpu.VMEM((rows, D), f32),
            pltpu.VMEM((512, 2 * rows), low),
            pltpu.VMEM((2 * D, D), low),
            pltpu.VMEM((2 * rows, D), low),
            pltpu.VMEM((rows, D), low),
            pltpu.VMEM((window, 3 * cut), low),
            pltpu.VMEM((parts, 2 * rows, D), low),
            pltpu.VMEM((D, 3 * cut), low),
            pltpu.VMEM((2 * rows, 512), low),
            pltpu.VMEM((window, D), low),
            pltpu.VMEM((16, D), f32),
            pltpu.VMEM((7, 16, D), f32),
        ]
        + buffers
        + [
            dma((7,)),
            dma((4, parts, 3)),
            dma((4, parts, 3)),
            dma((2 * parts + 1,)),
            dma((2 * parts + 1,)),
            dma((2,)),
            dma((2,)),
            dma((7,)),
            dma((7,)),
        ],
        compiler_params=pltpu.CompilerParams(
            collective_id=1, has_side_effects=True, vmem_limit_bytes=60 * 2**20 + 2**19
        ),
    )(perm, back, *vmem_in, *hbm_in)


def unit_order(segs, window):
    units = window // UNIT
    unit_seg = segs[::UNIT]
    index = lax.iota(jnp.int32, units)
    counts = jnp.sum((unit_seg[:, None] == unit_seg[None, :]).astype(jnp.int32), axis=1)
    short = jnp.where((counts == LONG) & (unit_seg >= 0) & (unit_seg < 1000), 0, 1) * units + index
    back = jnp.sum((short[None, :] < short[:, None]).astype(jnp.int32), axis=1)
    perm = jnp.sum(jnp.where(back[None, :] == index[:, None], index[None, :], 0), axis=1)
    return perm.astype(jnp.int32), back.astype(jnp.int32)


def marks_of(segs):
    lane = lax.iota(jnp.int32, 2 * HD)
    seg = jnp.where(segs < 0, 2 * HD - 1, jnp.where(segs >= 1000, 2 * HD - 2, segs))
    same = seg[:, None] == lane[None, :]
    keys = jnp.where(same, 1.0, 0.0).astype(jnp.bfloat16)
    queries = jnp.where(same, 0.0, -1e30).astype(jnp.bfloat16)
    return keys, queries


def local_body(
    tokens,
    cotangent,
    timesteps,
    item_lengths,
    w_qkv,
    bias_qv,
    w_out,
    w_up,
    bias_up,
    w_down,
    vectors,
):
    rows = tokens.shape[0]
    parts = lax.axis_size("mp")
    z = lax.axis_index("mp")
    low = jnp.bfloat16
    f32 = jnp.float32
    cut = D // parts
    firsts, offsets, ends = window_plan(rows, parts)
    window = -(-max(ends) // UNIT) * UNIT
    first_token = UNIT * pick(firsts, z)
    positions = first_token + lax.iota(jnp.int32, window)
    lengths_end = jnp.cumsum(item_lengths[0])
    segs = jnp.sum((positions[:, None] >= lengths_end[None, :]).astype(jnp.int32), axis=1)
    segs = jnp.where(positions < 0, -1, jnp.where(positions >= LEN, 1000, segs))
    perm, back = unit_order(segs, window)
    kf, qf = marks_of(segs)
    (
        f_qkv, f_out, f_up, f_down, qkv, lse, att2, act2, slope, first_t, lift_t, sec2, normed_one,
        second_low, second_grads, output, inverse_one, small_in,
    ) = fore_call(
        rows, window, parts, perm, back, timesteps, tokens, cotangent,
        jnp.transpose(w_qkv, (1, 0, 2)), w_out, w_up, w_down, bias_up[None], bias_qv, vectors, kf, qf,
    )
    input_grad, grad_qkv, grad_out, grad_up, grad_down, small = back_call(
        rows, window, parts, perm, back,
        (second_low, sec2, inverse_one, vectors, small_in, kf, qf, lse),
        (first_t, lift_t, second_grads, normed_one, act2, slope, att2, qkv, f_qkv, f_out, f_up, f_down),
    )
    grad_bias_qv = lax.dynamic_slice_in_dim(small[8:10], z * cut, cut, 1)
    grad_bias_up = lax.dynamic_slice_in_dim(small[10:14].reshape(FF), z * (FF // parts), FF // parts, 0)
    return (
        output,
        input_grad,
        jnp.transpose(grad_qkv, (1, 0, 2)),
        grad_bias_qv,
        grad_out,
        grad_up,
        grad_bias_up,
        grad_down,
        small[:8],
    )


def solution(mesh):
    in_specs = (
        P(("dp", "mp"), None),
        P(("dp", "mp"), None),
        P("dp"),
        P("dp", None),
        P(None, None, "mp"),
        P(None, "mp"),
        P("mp", None),
        P(None, "mp"),
        P("mp"),
        P("mp", None),
        P(),
    )
    out_specs = (
        P(("dp", "mp"), None),
        P(("dp", "mp"), None),
        P("dp", None, "mp"),
        P(None, "mp"),
        P("mp", "dp"),
        P("dp", "mp"),
        P("mp"),
        P("mp", "dp"),
        P(),
    )
    chosen = local_body if fits_local(mesh) else body
    return jax.shard_map(chosen, mesh=mesh, in_specs=in_specs, out_specs=out_specs, check_vma=False)
```

```python
import functools
import heapq

import jax
import jax.numpy as jnp
from jax import lax
from jax.experimental import pallas as pl
from jax.experimental.pallas import tpu as pltpu
from jax.sharding import PartitionSpec as P

D = 1024
HD = 64
FF = 4096
LEN = 2368


def norm_forward(value, gain, shift):
    average = jnp.mean(value, axis=-1, keepdims=True)
    centred = value - average
    inverse = lax.rsqrt(jnp.mean(centred * centred, axis=-1, keepdims=True) + 1e-05)
    normed = centred * inverse
    return (normed * gain + shift, normed, inverse)


def norm_backward(grad, normed, inverse, gain):
    scaled = grad * gain
    result = inverse * (
        scaled
        - jnp.mean(scaled, axis=-1, keepdims=True)
        - normed * jnp.mean(scaled * normed, axis=-1, keepdims=True)
    )
    return (result, jnp.sum(grad * normed, axis=0), jnp.sum(grad, axis=0))


def gelu_exact(value):
    return jax.nn.gelu(value, approximate=False)


def attend_forward(queries, keys, values, segments):
    scale = HD ** (-0.5)
    block_rows = LEN // 4

    def one_block(inputs):
        query_block, segment_block = inputs
        scores = (
            jnp.einsum("bhe,khe->hbk", query_block, keys, preferred_element_type=jnp.float32)
            * scale
        )
        allowed = segment_block[:, None] == segments[None, :]
        scores = jnp.where(allowed[None], scores, -1e30)
        highest = jnp.max(scores, axis=-1, keepdims=True)
        weights = jnp.exp(scores - highest)
        totals = jnp.sum(weights, axis=-1, keepdims=True)
        chances_low = (weights / totals).astype(jnp.bfloat16)
        result = jnp.einsum("hbk,khe->bhe", chances_low, values, preferred_element_type=jnp.float32)
        return (result.astype(jnp.bfloat16), (highest + jnp.log(totals))[..., 0])

    blocks = queries.reshape(4, block_rows, queries.shape[1], queries.shape[2])
    results, logsums = lax.map(one_block, (blocks, segments.reshape(4, block_rows)))
    return (results.reshape(queries.shape), logsums)


def attend_backward(queries, keys, values, out_grads, logsums, segments):
    scale = HD ** (-0.5)
    block_rows = LEN // 4

    def one_block(carry, inputs):
        key_grads, value_grads = carry
        query_block, grad_block, logsum_block, segment_block = inputs
        scores = (
            jnp.einsum("bhe,khe->hbk", query_block, keys, preferred_element_type=jnp.float32)
            * scale
        )
        allowed = segment_block[:, None] == segments[None, :]
        scores = jnp.where(allowed[None], scores, -1e30)
        chances = jnp.exp(scores - logsum_block[..., None])
        chances_low = chances.astype(jnp.bfloat16)
        value_grads = value_grads + jnp.einsum(
            "hbk,bhe->khe", chances_low, grad_block, preferred_element_type=jnp.float32
        )
        flow = jnp.einsum("bhe,khe->hbk", grad_block, values, preferred_element_type=jnp.float32)
        inner = jnp.sum(chances * flow, axis=-1, keepdims=True)
        score_grads = (chances * (flow - inner)).astype(jnp.bfloat16)
        query_grads = (
            jnp.einsum("hbk,khe->bhe", score_grads, keys, preferred_element_type=jnp.float32)
            * scale
        )
        key_grads = (
            key_grads
            + jnp.einsum(
                "hbk,bhe->khe", score_grads, query_block, preferred_element_type=jnp.float32
            )
            * scale
        )
        return ((key_grads, value_grads), query_grads)

    shape_blocks = (4, block_rows, queries.shape[1], queries.shape[2])
    zeros = jnp.zeros(keys.shape, jnp.float32)
    (key_grads, value_grads), query_grads = lax.scan(
        one_block,
        (zeros, zeros),
        (
            queries.reshape(shape_blocks),
            out_grads.reshape(shape_blocks),
            logsums,
            segments.reshape(4, block_rows),
        ),
    )
    return (query_grads.reshape(queries.shape), key_grads, value_grads)


def body(
    tokens,
    cotangent,
    timesteps,
    item_lengths,
    w_qkv,
    bias_qv,
    w_out,
    w_up,
    bias_up,
    w_down,
    vectors,
):
    rows = tokens.shape[0]
    total = rows * lax.axis_size("mp")
    seq_count = timesteps.shape[0]
    local_width = w_qkv.shape[2]
    local_hidden = w_up.shape[1]
    local_heads = local_width // HD
    my_index = lax.axis_index("mp")
    row_ids = my_index * rows + lax.iota(jnp.int32, rows)
    row_owner = row_ids // LEN
    step_times = timesteps.astype(jnp.float32) * 0.001
    time_rows = jnp.sum(
        jnp.where(
            row_owner[:, None] == lax.iota(jnp.int32, seq_count)[None, :], step_times[None, :], 0.0
        ),
        axis=1,
    )
    ends = jnp.cumsum(item_lengths, axis=1)
    segments = jnp.sum(
        (lax.iota(jnp.int32, LEN)[None, :, None] >= ends[:, None, :]).astype(jnp.int32), axis=2
    )
    lifted = tokens.astype(jnp.float32) + time_rows[:, None] * vectors[0] + vectors[1]
    gathered = lax.all_gather(lifted.astype(jnp.bfloat16), "mp", axis=0, tiled=True)
    projected = jnp.einsum("td,dce->cte", gathered, w_qkv, preferred_element_type=jnp.float32)
    shaped = (seq_count, LEN, local_heads, HD)
    head_query = (projected[0] + bias_qv[0]).astype(jnp.bfloat16).reshape(shaped)
    head_key = projected[1].astype(jnp.bfloat16).reshape(shaped)
    head_value = (projected[2] + bias_qv[1]).astype(jnp.bfloat16).reshape(shaped)
    attended, logsums = lax.map(
        lambda items: attend_forward(*items), (head_query, head_key, head_value, segments)
    )
    attended = attended.reshape(total, local_width)
    piece = attended
    mixed = (
        lax.psum_scatter(
            jnp.dot(piece, w_out, preferred_element_type=jnp.float32),
            "mp",
            scatter_dimension=0,
            tiled=True,
        )
        + vectors[2]
    )
    first, normed_one, inverse_one = norm_forward(lifted + mixed, vectors[4], vectors[5])
    hidden_all = lax.all_gather(first.astype(jnp.bfloat16), "mp", axis=0, tiled=True)
    upper = jnp.dot(hidden_all, w_up, preferred_element_type=jnp.float32) + bias_up
    activated, gelu_pull = jax.vjp(gelu_exact, upper)
    activated = activated.astype(jnp.bfloat16)
    piece = activated
    down = (
        lax.psum_scatter(
            jnp.dot(piece, w_down, preferred_element_type=jnp.float32).astype(jnp.bfloat16),
            "mp",
            scatter_dimension=0,
            tiled=True,
        ).astype(jnp.float32)
        + vectors[3]
    )
    output, normed_two, inverse_two = norm_forward(first + down, vectors[6], vectors[7])
    out_grads = cotangent.astype(jnp.float32)
    second_grads, gain_two, shift_two = norm_backward(
        out_grads, normed_two, inverse_two, vectors[6]
    )
    down_all = lax.all_gather(second_grads.astype(jnp.bfloat16), "mp", axis=0, tiled=True)
    grad_down = jnp.einsum("tf,td->fd", activated, down_all, preferred_element_type=jnp.float32)
    act_grads = jnp.einsum("td,fd->tf", down_all, w_down, preferred_element_type=jnp.float32)
    (upper_grads,) = gelu_pull(act_grads)
    upper_low = upper_grads.astype(jnp.bfloat16)
    grad_bias_up = jnp.sum(upper_low, axis=0, dtype=jnp.float32)
    grad_up = jnp.einsum("td,tf->df", hidden_all, upper_low, preferred_element_type=jnp.float32)
    piece = upper_low
    first_part = lax.psum_scatter(
        jnp.einsum("tf,df->td", piece, w_up, preferred_element_type=jnp.float32).astype(
            jnp.bfloat16
        ),
        "mp",
        scatter_dimension=0,
        tiled=True,
    ).astype(jnp.float32)
    first_grads = second_grads + first_part
    mixed_grads, gain_one, shift_one = norm_backward(
        first_grads, normed_one, inverse_one, vectors[4]
    )
    mixed_all = lax.all_gather(mixed_grads.astype(jnp.bfloat16), "mp", axis=0, tiled=True)
    grad_out = jnp.einsum("te,td->ed", attended, mixed_all, preferred_element_type=jnp.float32)
    attended_grads = jnp.einsum(
        "td,ed->te", mixed_all, w_out, preferred_element_type=jnp.float32
    ).astype(jnp.bfloat16)
    query_grads, key_grads, value_grads = lax.map(
        lambda items: attend_backward(*items),
        (head_query, head_key, head_value, attended_grads.reshape(shaped), logsums, segments),
    )
    qkv_low = jnp.stack(
        [
            query_grads.reshape(total, local_width),
            key_grads.reshape(total, local_width),
            value_grads.reshape(total, local_width),
        ],
        axis=1,
    ).astype(jnp.bfloat16)
    grad_bias_qv = jnp.sum(qkv_low[:, 0::2], axis=0, dtype=jnp.float32)
    grad_qkv = jnp.einsum("td,tcf->dcf", gathered, qkv_low, preferred_element_type=jnp.float32)
    piece = qkv_low
    input_part = lax.psum_scatter(
        jnp.einsum("tcf,dcf->td", piece, w_qkv, preferred_element_type=jnp.float32).astype(
            jnp.bfloat16
        ),
        "mp",
        scatter_dimension=0,
        tiled=True,
    ).astype(jnp.float32)
    input_sum = mixed_grads + input_part
    vector_terms = jnp.stack(
        [
            jnp.sum(time_rows[:, None] * input_sum, axis=0),
            jnp.sum(input_sum, axis=0),
            jnp.sum(mixed_grads, axis=0),
            jnp.sum(second_grads, axis=0),
            gain_one,
            shift_one,
            gain_two,
            shift_two,
        ],
        axis=0,
    )
    zero_index = jnp.zeros((), jnp.int32)
    qv_start = my_index * local_width
    up_start = my_index * local_hidden
    qv_placed = lax.dynamic_update_slice(
        jnp.zeros((2, D), jnp.float32), grad_bias_qv, (zero_index, qv_start)
    )
    up_placed = lax.dynamic_update_slice(jnp.zeros((FF,), jnp.float32), grad_bias_up, (up_start,))
    grad_qkv, grad_out, grad_up, grad_down = (
        lax.psum_scatter(
            grad_qkv.astype(jnp.bfloat16), "dp", scatter_dimension=0, tiled=True
        ).astype(jnp.float32),
        lax.psum_scatter(
            grad_out.astype(jnp.bfloat16), "dp", scatter_dimension=1, tiled=True
        ).astype(jnp.float32),
        lax.psum_scatter(
            grad_up.astype(jnp.bfloat16), "dp", scatter_dimension=0, tiled=True
        ).astype(jnp.float32),
        lax.psum_scatter(
            grad_down.astype(jnp.bfloat16), "dp", scatter_dimension=1, tiled=True
        ).astype(jnp.float32),
    )
    grad_vectors, qv_summed, up_summed = lax.psum(
        (vector_terms, qv_placed, up_placed), ("dp", "mp")
    )
    grad_bias_qv = lax.dynamic_slice_in_dim(qv_summed, qv_start, local_width, 1)
    grad_bias_up = lax.dynamic_slice_in_dim(up_summed, up_start, local_hidden, 0)
    return (
        output.astype(jnp.bfloat16),
        input_sum.astype(jnp.bfloat16),
        grad_qkv,
        grad_bias_qv,
        grad_out,
        grad_up,
        grad_bias_up,
        grad_down,
        grad_vectors,
    )


UNIT = 128
LONG = 4
MESH = pl.DeviceIdType.MESH


def fits_local(mesh):
    parts = mesh.shape["mp"]
    return mesh.shape["dp"] == 8 and parts == 4 and LEN % (16 * parts) == 0


def window_plan(rows, parts):
    firsts = [(rows * j) // UNIT - (LONG - 1) for j in range(parts)]
    offsets = [rows * j - UNIT * first for j, first in enumerate(firsts)]
    ends = [
        ((rows * (j + 1) - 1) // UNIT + LONG - firsts[j]) * UNIT for j in range(parts)
    ]
    return firsts, offsets, ends


def pick(table, index):
    value = jnp.int32(table[0])
    for j in range(1, len(table)):
        value = jnp.where(index == j, jnp.int32(table[j]), value)
    return value


NT = (((1,), (1,)), ((), ()))
TN = (((0,), (0,)), ((), ()))
FIRST_OWN, LAST_OWN = LONG - 1, LONG + 4


def two_heads(block):
    lane = lax.broadcasted_iota(jnp.int32, block.shape, 1)
    zero = jnp.zeros_like(block)
    return jnp.concatenate(
        [jnp.where(lane < HD, block, zero), jnp.where(lane < HD, zero, block)], axis=0
    )


def from_two(flipped):
    both = jnp.concatenate([flipped[:HD, :UNIT], flipped[HD:, UNIT:]], axis=0)
    return both.T


def by_rows(rows, body, carry):
    count = rows // 32

    def step(i, c):
        return body(pl.multiple_of(i * 32, 32), 32, c)

    carry = lax.fori_loop(0, count, step, carry)
    return body(count * 32, rows - count * 32, carry) if rows % 32 else carry


def fold(value):
    return value if value.shape[0] == 16 else value[:16] + value[16:]


class Clock:
    def __init__(self, rate):
        self.rate = {"c": 400e3, "x": rate, "y": rate, "z": rate}
        self.now = 0.0
        self.free = {}
        self.queue = []
        self.count = 0

    def send(self, link, size, action, share=1.0):
        begin = max(self.now, self.free.get(link, 0.0))
        end = begin + share * size / self.rate[link]
        self.free[link] = end
        self.count += 1
        heapq.heappush(self.queue, (end + 1.5, self.count, action))

    def work(self, time):
        self.now += time
        while self.queue and self.queue[0][0] <= self.now:
            heapq.heappop(self.queue)[2]()

    def step(self):
        ready, _, action = heapq.heappop(self.queue)
        self.now = max(self.now, ready)
        action()

    def drain(self):
        while self.queue:
            self.step()


def block_owners(d, core, x_first):
    x, y = lax.rem(d // 2, 2), d // 4
    if x_first:
        return [4 * b + 2 * a + core for a in (1 - x, x) for b in (1 - y, y)]
    return [4 * b + 2 * a + core for b in (1 - y, y) for a in (1 - x, x)]


RING = (2, 3, 1, 0)
HALO_TIME = 25.0


def fore_kernel(
    rows, window, parts, perm, back, steps, tokens, cotangent, w_qkv, w_out, w_up, w_down, bias_up, bias_qv, vectors, kf, qf,
    f_qkv, f_out, f_up, f_down, qkv, lse, att2, act2, slopes, first_t, lift_t, sec2, normed_out, second_low,
    second_grads, output, inverse, small,
    win, xq, yq, own_rows, attended, mixed, first, first_low, down, in_low, out_low, wu, wd, wq, wo, act, slope, lift2, first2,
    turned, stage, biases, bias_all, send, recv, own_sent, near, far, own, bias_send, bias_recv, local, pair_send, pair_recv,
):
    f32, low = jnp.float32, jnp.bfloat16
    d = lax.axis_index("dp")
    z = lax.axis_index("mp")
    core = lax.rem(d, 2)
    cut = D // parts
    three = 3 * cut
    pairs = cut // (2 * HD)
    firsts, offsets, ends = window_plan(rows, parts)
    offset = pl.multiple_of(pick(offsets, z), 16)
    shards = (w_qkv, w_out, w_up, w_down)
    fulls = (f_qkv, f_out, f_up, f_down)
    sizes = tuple(shard.shape[0] // 8 for shard in shards)
    partner = (d ^ 1, z)
    peers = [(d, z ^ k) for k in (1, 2, 3)] + [partner, (d ^ 2, z), (d ^ 4, z)]
    barrier = pltpu.get_barrier_semaphore()
    for peer in peers:
        pl.semaphore_signal(barrier, inc=1, device_id=peer, device_id_type=MESH)
    pl.semaphore_wait(barrier, len(peers))
    clock = Clock(46e3)

    order = [sorted((o for o in range(parts) if o != j), key=lambda o: (abs(o - j), o)) for j in range(parts)]
    source = [pick([order[j][n] for j in range(parts)], z) for n in range(parts - 1)]
    chunks = [(g, n) for n in range(parts - 1) for g in (0, 1)] + [(g, n) for n in range(parts - 1) for g in (2, 3)]
    index_of = {chunk: i for i, chunk in enumerate(chunks)}
    copies, done = {}, {}

    def part(ref, index, owner, size, half=None):
        start, count = owner * size, size
        if half is not None:
            count = size // 2
            start = start + half * count
        return ref.at[index, pl.ds(pl.multiple_of(start, 16), count), :]

    def remote(i, kind, src, dst, target):
        copy = pltpu.make_async_remote_copy(
            src, dst, send.at[i, kind], recv.at[i, kind], device_id=target, device_id_type=MESH
        )
        copy.start()
        copies[i, kind] = copy

    def place(i, owner, half=None):
        g, n = chunks[i]
        return part(fulls[g], source[n], owner, sizes[g], half)

    def bytes_of(i):
        g, n = chunks[i]
        return sizes[g] * shards[g].shape[1] * 2

    def pass_on(i, kind, owner, target, half=None):
        remote(i, kind, place(i, owner, half), place(i, owner, half), target)

    column = []

    def along(owner, place_of, here, there, sent, g):
        i = index_of[g, order[there].index(owner)]
        copy = pltpu.make_async_remote_copy(
            place_of, part(fulls[g], owner, d, sizes[g]), sent, recv.at[i, 0],
            device_id=(d, there), device_id_type=MESH,
        )

        @pl.when(z == here)
        def _():
            copy.start()

        column.append((here, copy))

    def send_own(g):
        rows_at = pl.ds(pl.multiple_of(d * sizes[g], 16), sizes[g])
        for here in range(parts):
            for n, there in enumerate((here - 1, here + 1)):
                if 0 <= there < parts:
                    along(here, shards[g].at[rows_at, :], here, there, own_sent.at[g, n], g)
        for n in range(parts - 1):
            i = index_of[g, n]
            clock.send("z", bytes_of(i), lambda i=i: hop_two(i))

    def hop_two(i):
        g, n = chunks[i]
        pltpu.make_async_remote_copy(
            place(i, d), place(i, d), send.at[i, 0], recv.at[i, 0], device_id=partner, device_id_type=MESH
        ).wait_recv()
        for here in range(parts):
            owner = order[here][n]
            there = here + 1 if owner < here else here - 1
            if 0 <= there < parts:
                along(owner, part(fulls[g], owner, d, sizes[g]), here, there, send.at[i, 0], g)
        if g == 2 and n == 0:
            send_own(3)
        pass_on(i, 1, d, (d ^ 2, z))
        pass_on(i, 2, d, (d ^ 4, z))
        pass_on(i, 5, d, partner)
        clock.send("c", bytes_of(i), lambda: None)
        clock.send("x", bytes_of(i), lambda: hop_three(i))
        clock.send("y", bytes_of(i), lambda: hop_four(i))

    def hop_three(i):
        copies[i, 1].wait_recv()
        pass_on(i, 3, d ^ 2, (d ^ 4, z), 0)
        pass_on(i, 6, d ^ 2, partner)
        clock.send("y", bytes_of(i) // 2, lambda: hop_five(i))

    def hop_four(i):
        copies[i, 2].wait_recv()
        pass_on(i, 4, d ^ 4, (d ^ 2, z), 1)
        pass_on(i, 7, d ^ 4, partner)
        clock.send("x", bytes_of(i) // 2, lambda: hop_six(i))

    def hop_five(i):
        copies[i, 3].wait_recv()
        pass_on(i, 8, d ^ 6, partner, 0)
        finish(i)

    def hop_six(i):
        copies[i, 4].wait_recv()
        pass_on(i, 9, d ^ 6, partner, 1)
        finish(i)

    def finish(i):
        done[i] = done.get(i, 0) + 1

    def arrive(i):
        while done.get(i, 0) < 2:
            clock.step()
        for kind in range(5, 10):
            copies[i, kind].wait_recv()

    halos = []
    for j in range(parts - 1):
        count = ends[j] - offsets[j] - rows
        halos.append((j + 1, j, pltpu.make_async_remote_copy(
            tokens.at[pl.ds(0, count), :], win.at[pl.ds(offsets[j] + rows, count), :],
            near.at[0], near.at[1], device_id=(d, j), device_id_type=MESH,
        )))
    for j in range(1, parts):
        halos.append((j - 1, j, pltpu.make_async_remote_copy(
            tokens.at[pl.ds(rows - offsets[j], offsets[j]), :], win.at[pl.ds(0, offsets[j]), :],
            far.at[0], far.at[1], device_id=(d, j), device_id_type=MESH,
        )))
    for sender, receiver, copy in halos:
        @pl.when(z == sender)
        def _(copy=copy):
            copy.start()
    clock.send("z", max(offsets) * D * 2, lambda: None)
    send_own(0)
    send_own(1)
    biases[...] = jnp.zeros_like(biases)
    biases[0:1, :] = bias_up[...].astype(f32)
    pair_rows = bias_qv[...].astype(f32)
    biases[1:2, 0:cut] = pair_rows[0:1]
    biases[1:2, 2 * cut : three] = pair_rows[1:2]
    bias_copies = []
    for k in (1, 2, 3):
        copy = pltpu.make_async_remote_copy(
            biases, bias_all.at[z], bias_send.at[k - 1], bias_recv.at[k - 1], device_id=(d, z ^ k), device_id_type=MESH
        )
        copy.start()
        bias_copies.append(copy)
    bias_all[pl.ds(z, 1)] = biases[...][None]
    owns = []
    for g in range(4):
        copy = pltpu.make_async_copy(shards[g], fulls[g].at[z], own.at[g])
        copy.start()
        owns.append(copy)

    step_time = steps[0].astype(f32) * 0.001
    shift = step_time * vectors[0:1, :]

    def lift(value):
        return value.astype(f32) + shift + vectors[1:2, :]

    def own_body(i, c):
        at = pl.ds(pl.multiple_of(i * 16, 16), 16)
        win[pl.ds(pl.multiple_of(offset + i * 16, 16), 16), :] = lift(tokens[at, :]).astype(low)
        return c

    lax.fori_loop(0, rows // 16, own_body, 0)
    zero = jnp.zeros((16, D), low)

    def spans_of(j):
        end = ends[j] if j < parts - 1 else offsets[j] + rows
        empty = [(0, offsets[0])] if j == 0 else []
        if end < window:
            empty.append((end, window))
        filled = [(0, offsets[j])] if j else []
        if j < parts - 1:
            filled.append((offsets[j] + rows, ends[j]))
        return empty, filled

    for j in range(parts):
        @pl.when(z == j)
        def _(j=j):
            for begin, end in spans_of(j)[0]:
                def clear(i, c, begin=begin):
                    win[pl.ds(pl.multiple_of(begin + i * 16, 16), 16), :] = zero
                    return c
                lax.fori_loop(0, (end - begin) // 16, clear, 0)

    pair_copies = []

    def exchange(source, target):
        index = len(pair_copies)
        copy = pltpu.make_async_remote_copy(
            source, target, pair_send.at[index], pair_recv.at[index], device_id=partner, device_id_type=MESH
        )
        copy.start()
        pair_copies.append(copy)
        return copy

    def columns(read, c, write):
        for j, owner in enumerate(block_owners(d, c, True)):
            write(slice(j * 128, (j + 1) * 128), read(pl.ds(pl.multiple_of(owner * 128, 128), 128)))

    own_at = pl.ds(offset, rows)
    mine = pl.ds(0, rows)
    theirs = pl.ds(rows, rows)
    columns(lambda at: win[own_at, at], 1 - core, lambda at, v: stage.__setitem__((0, slice(None), at), v))
    lift_copy = exchange(stage.at[0], lift2.at[theirs, :])
    columns(lambda at: win[own_at, at], core, lambda at, v: lift2.__setitem__((mine, at), v))

    def fetch(index, source, target):
        copy = pltpu.make_async_copy(source, target, local.at[index])
        copy.start()
        return copy

    clock.work(4.0)
    for copy in bias_copies:
        copy.wait_recv()
    clock.work(max(0.0, HALO_TIME - clock.now))
    for sender, receiver, copy in halos:
        @pl.when(z == receiver)
        def _(copy=copy):
            copy.wait_recv()
    send_own(2)
    for j in range(parts):
        @pl.when(z == j)
        def _(j=j):
            for begin, end in spans_of(j)[1]:
                def convert(i, c, begin=begin):
                    at = pl.ds(pl.multiple_of(begin + i * 16, 16), 16)
                    win[at, :] = lift(win[at, :]).astype(low)
                    return c
                lax.fori_loop(0, (end - begin) // 16, convert, 0)
    clock.work(2.0)
    lift_copy.wait_recv()
    turned[...] = lift2[...].T
    turned_out = fetch(0, turned, lift_t)
    clock.work(2.0)

    stores = {}
    for i in range(parts):
        k = i
        at_z = source[i - 1] if i else z
        if k == 0:
            wq_ref, wo_ref = w_qkv, w_out
        else:
            wq_ref, wo_ref = wq, wo
            load_q.wait()
        slot_i = i % 2
        if i >= 2:
            stores[i - 2].wait()
        row = bias_all.at[at_z]

        def project(n, c):
            at = pl.ds(pl.multiple_of(n * 512, 512), 512)
            for c3 in range(3):
                lanes = slice(c3 * cut, (c3 + 1) * cut)
                value = jnp.dot(win[at, :], wq_ref[:, lanes], preferred_element_type=f32)
                value = (value + row[1:2, lanes]).astype(low)
                if c3 == 0:
                    value = value * jnp.array(HD ** (-0.5), low)
                xq[slot_i, at, lanes] = value
            return c

        lax.fori_loop(0, window // 512, project, 0)
        stores[i] = fetch(3 + slot_i, xq.at[slot_i], qkv.at[at_z])
        clock.work(3.5)
        if i + 1 < parts:
            arrive(index_of[0, i])
            load_q = fetch(1, f_qkv.at[source[i]], wq)

        def attend(step, c):
            p, slot = step // 3, lax.rem(step, 3)
            lanes = lambda base: pl.ds(pl.multiple_of(base + p * 2 * HD, 2 * HD), 2 * HD)
            unit_at = [pl.ds(perm[slot * LONG + m] * UNIT, UNIT) for m in range(LONG)]
            keys = jnp.concatenate([xq[slot_i, at, lanes(cut)] for at in unit_at], axis=0)
            values = jnp.concatenate([xq[slot_i, at, lanes(2 * cut)] for at in unit_at], axis=0)
            marks = jnp.concatenate([kf[at, :] for at in unit_at], axis=0)
            wide_keys = jnp.concatenate([keys, marks], axis=1)
            pair = jnp.concatenate([two_heads(xq[slot_i, at, lanes(0)]) for at in unit_at], axis=0)
            mark = jnp.concatenate([qf[at, :] for at in unit_at for _ in range(2)], axis=0)
            wide_pair = jnp.concatenate([pair, mark], axis=1)
            scores = lax.dot_general(wide_keys, wide_pair, NT, preferred_element_type=f32)
            highest = jnp.max(scores, axis=0, keepdims=True)
            weights = jnp.exp(scores - highest)
            total = jnp.sum(weights, axis=0, keepdims=True)
            flipped = lax.dot_general(values, weights.astype(low), TN, preferred_element_type=f32) * (1.0 / total)
            logsum = highest + jnp.log(total)
            for m in range(LONG):
                two = slice(m * 2 * UNIT, (m + 1) * 2 * UNIT)
                at = pl.ds(pl.multiple_of(slot * LONG * UNIT + m * UNIT, UNIT), UNIT)
                yq[at, lanes(0)] = from_two(flipped[:, two]).astype(low)
                lse[at_z, pl.ds(step * LONG + m, 1), :] = logsum[:, two]
            return c

        lax.fori_loop(0, pairs * 3, attend, 0, unroll=2)
        clock.work(7.5)
        for u in range(FIRST_OWN, LAST_OWN + 1):
            own_rows[pl.ds((u - FIRST_OWN) * UNIT, UNIT), :] = yq[pl.ds(back[u] * UNIT, UNIT), :]
        lanes_z = pl.ds(pl.multiple_of(at_z * cut, cut), cut)
        attended[i] = own_rows[pl.ds(pl.multiple_of(offset - FIRST_OWN * UNIT, 16), rows), :]
        exchange(attended.at[i], att2.at[theirs, lanes_z])
        stores["a", i] = fetch(5 + i, attended.at[i], att2.at[mine, lanes_z])
        if k:
            load_o.wait()

        def out_body(n, c):
            at = pl.ds(pl.multiple_of(n * 256, 256), 256)
            value = jnp.dot(attended[i], wo_ref[:, at], preferred_element_type=f32)
            if i == 0:
                mixed[:, at] = value
            else:
                mixed[:, at] += value
            return c

        lax.fori_loop(0, D // 256, out_body, 0)
        clock.work(1.5)
        if i + 1 < parts:
            arrive(index_of[1, i])
            load_o = fetch(2, f_out.at[source[i]], wo)

    def norm_one(begin, count, c):
        at = pl.ds(begin, count)
        value = lift(tokens[at, :]) + (mixed[at, :] + vectors[2:3, :])
        centred = value - jnp.mean(value, axis=-1, keepdims=True)
        scale = lax.rsqrt(jnp.mean(centred * centred, axis=-1, keepdims=True) + 1e-05)
        normed = centred * scale
        mixed[at, :] = normed
        inverse[at, :] = scale
        result = normed * vectors[4:5, :] + vectors[5:6, :]
        first[at, :] = result
        first_low[at, :] = result.astype(low)
        return c

    by_rows(rows, norm_one, 0)
    normed_store = fetch(9, mixed, normed_out)
    columns(lambda at: first_low[:, at], 1 - core, lambda at, v: stage.__setitem__((1, slice(None), at), v))
    first_copy = exchange(stage.at[1], first2.at[theirs, :])
    columns(lambda at: first_low[:, at], core, lambda at, v: first2.__setitem__((mine, at), v))
    clock.work(4.0)

    for i in range(parts):
        k = i
        at_z = source[i - 1] if i else z
        slot_i = i % 2
        if k == 0:
            up_ref, down_ref = w_up, w_down
        else:
            up_ref, down_ref = wu, wd
            load_u.wait()
        if i >= 2:
            for copy in stores["f", i - 2]:
                copy.wait()
            stores["r", i - 2].wait_send()
        row = bias_all.at[at_z]

        def upper_body(n, c):
            at = pl.ds(pl.multiple_of(n * 256, 256), 256)
            value = jnp.dot(first_low[...], up_ref[:, at], preferred_element_type=f32) + row[0:1, at]
            chance = 0.5 + 0.5 * lax.erf(value * (0.5**0.5))
            act[slot_i, :, at] = (value * chance).astype(low)
            density = jnp.exp(-0.5 * value * value) * (0.5 / jnp.pi) ** 0.5
            slope[slot_i, :, at] = (chance + value * density).astype(low)
            return c

        lax.fori_loop(0, D // 256, upper_body, 0)
        hidden = pl.ds(pl.multiple_of(at_z * D, D), D)
        stores["r", i] = exchange(act.at[slot_i], act2.at[theirs, hidden])
        stores["f", i] = (
            fetch(14 + slot_i, act.at[slot_i], act2.at[mine, hidden]),
            fetch(10 + slot_i, slope.at[slot_i], slopes.at[:, hidden]),
        )
        clock.work(4.0)
        if i + 1 < parts:
            arrive(index_of[2, i])
            load_u = fetch(1, f_up.at[source[i]], wu)
        if k:
            load_d.wait()

        def down_body(n, c):
            at = pl.ds(pl.multiple_of(n * 256, 256), 256)
            value = jnp.dot(act[slot_i], down_ref[:, at], preferred_element_type=f32)
            if i == 0:
                down[:, at] = value
            else:
                down[:, at] += value
            return c

        lax.fori_loop(0, D // 256, down_body, 0)
        clock.work(2.0)
        if i + 1 < parts:
            arrive(index_of[3, i])
            load_d = fetch(2, f_down.at[source[i]], wd)
        if i == 0:
            first_copy.wait_recv()
            turned_out.wait()
            turned[...] = first2[...].T
            turned_out = fetch(0, turned, first_t)
            clock.work(2.0)

    zero_row = jnp.zeros((16, D), f32)

    def norm_two(begin, count, sums):
        at = pl.ds(begin, count)
        value = first[at, :] + (down[at, :] + vectors[3:4, :])
        centred = value - jnp.mean(value, axis=-1, keepdims=True)
        scale = lax.rsqrt(jnp.mean(centred * centred, axis=-1, keepdims=True) + 1e-05)
        normed = centred * scale
        out_low[at, :] = (normed * vectors[6:7, :] + vectors[7:8, :]).astype(low)
        grads = cotangent[at, :].astype(f32)
        scaled = grads * vectors[6:7, :]
        result = scale * (
            scaled
            - jnp.mean(scaled, axis=-1, keepdims=True)
            - normed * jnp.mean(scaled * normed, axis=-1, keepdims=True)
        )
        down[at, :] = result
        in_low[at, :] = result.astype(low)
        return (sums[0] + fold(result), sums[1] + fold(grads * normed), sums[2] + fold(grads))

    sums = by_rows(rows, norm_two, (zero_row, zero_row, zero_row))
    last = [fetch(1, out_low, output), fetch(2, in_low, second_low), fetch(12, down, second_grads)]
    small[...] = jnp.zeros_like(small)
    small[3:4, :] = jnp.sum(sums[0], axis=0, keepdims=True)
    small[6:7, :] = jnp.sum(sums[1], axis=0, keepdims=True)
    small[7:8, :] = jnp.sum(sums[2], axis=0, keepdims=True)
    small[15:16, :] = jnp.full((1, D), step_time, f32)
    columns(lambda at: in_low[:, at], 1 - core, lambda at, v: stage.__setitem__((2, slice(None), at), v))
    exchange(stage.at[2], sec2.at[theirs, :])
    columns(lambda at: in_low[:, at], core, lambda at, v: stage.__setitem__((3, slice(None), at), v))
    last.append(fetch(13, stage.at[3], sec2.at[mine, :]))
    clock.drain()
    for copy in last + owns + [turned_out, normed_store, stores[2], stores[3]]:
        copy.wait()
    for i in range(parts):
        stores["a", i].wait()
        if i >= 2:
            for copy in stores["f", i]:
                copy.wait()
    waited = [stores["r", 0], stores["r", 1]]
    for copy in pair_copies:
        if not any(copy is other for other in waited):
            copy.wait_send()
        if copy is not lift_copy and copy is not first_copy:
            copy.wait_recv()
    for copy in copies.values():
        copy.wait_send()
    for here, copy in column:
        @pl.when(z == here)
        def _(copy=copy):
            copy.wait_send()
    for copy in bias_copies:
        copy.wait_send()
    for sender, receiver, copy in halos:
        @pl.when(z == sender)
        def _(copy=copy):
            copy.wait_send()


def fore_call(rows, window, parts, perm, back, steps, *arrays):
    f32, low = jnp.float32, jnp.bfloat16
    any_ = pl.BlockSpec(memory_space=pl.ANY)
    vmem = pl.BlockSpec(memory_space=pltpu.VMEM)
    smem = pl.BlockSpec(memory_space=pltpu.SMEM)
    cut = D // parts
    three = 3 * cut
    shape = jax.ShapeDtypeStruct
    marks = cut // (2 * HD) * 3 * LONG
    dma = pltpu.SemaphoreType.DMA
    return pl.pallas_call(
        functools.partial(fore_kernel, rows, window, parts),
        out_shape=[
            shape((parts, D, three), low),
            shape((parts, cut, D), low),
            shape((parts, D, D), low),
            shape((parts, D, D), low),
            shape((parts, window, three), low),
            shape((parts, marks, 2 * UNIT), f32),
            shape((2 * rows, D), low),
            shape((2 * rows, FF), low),
            shape((rows, FF), low),
            shape((512, 2 * rows), low),
            shape((512, 2 * rows), low),
            shape((2 * rows, 512), low),
            shape((rows, D), f32),
            shape((rows, D), low),
            shape((rows, D), f32),
            shape((rows, D), low),
            shape((rows, 1), f32),
            shape((16, D), f32),
        ],
        in_specs=[smem] * 3 + [vmem] * len(arrays),
        out_specs=[any_] * 5 + [vmem] + [any_] * 10 + [vmem] * 2,
        scratch_shapes=[
            pltpu.VMEM((window, D), low),
            pltpu.VMEM((2, window, three), low),
            pltpu.VMEM((window, cut), low),
            pltpu.VMEM(((LAST_OWN + 1 - FIRST_OWN) * UNIT, cut), low),
            pltpu.VMEM((parts, rows, cut), low),
            pltpu.VMEM((rows, D), f32),
            pltpu.VMEM((rows, D), f32),
            pltpu.VMEM((rows, D), low),
            pltpu.VMEM((rows, D), f32),
            pltpu.VMEM((rows, D), low),
            pltpu.VMEM((rows, D), low),
            pltpu.VMEM((D, D), low),
            pltpu.VMEM((D, D), low),
            pltpu.VMEM((D, three), low),
            pltpu.VMEM((cut, D), low),
            pltpu.VMEM((2, rows, D), low),
            pltpu.VMEM((2, rows, D), low),
            pltpu.VMEM((2 * rows, 512), low),
            pltpu.VMEM((2 * rows, 512), low),
            pltpu.VMEM((512, 2 * rows), low),
            pltpu.VMEM((4, rows, 512), low),
            pltpu.VMEM((8, D), f32),
            pltpu.VMEM((parts, 8, D), f32),
            dma((12, 10)),
            dma((12, 10)),
            dma((4, 2)),
            dma((2,)),
            dma((2,)),
            dma((4,)),
            dma((3,)),
            dma((3,)),
            dma((16,)),
            dma((2 * parts + 3,)),
            dma((2 * parts + 3,)),
        ],
        compiler_params=pltpu.CompilerParams(
            collective_id=0, has_side_effects=True, vmem_limit_bytes=56 * 2**20
        ),
    )(perm, back, steps, *arrays)


def back_kernel(
    rows, window, parts, perm, back, sec_low, sec2, inverse, gain, small_in, kf, qf, lse,
    first_t, lift_t, second_grads, normed_one, act2, dgelu, att2, qkv, f_qkv, f_out, f_up, f_down,
    input_grad, g_qkv, g_out, g_up, g_down, small_out,
    acc, normed, turned, arena, act, slope, y, up2, w_in, mixed2, mixed_win, small, small_in_far,
    s_down, s_up, s_out, s_qkv, k_down, k_up, k_out, k_qkv,
    r_down, r_up, r_out, r_qkv, t_down, t_up, t_out, t_qkv, z_down, z_up, z_out, z_qkv,
    local, hop_send, hop_recv, pair_send, pair_recv, halo_send, halo_recv, small_send, small_recv,
):
    f32, low = jnp.float32, jnp.bfloat16
    d = lax.axis_index("dp")
    z = lax.axis_index("mp")
    core = lax.rem(d, 2)
    firsts, offsets, ends = window_plan(rows, parts)
    offset = pl.multiple_of(pick(offsets, z), 16)
    partner = (d ^ 1, z)
    peers = [(d, z ^ k) for k in (1, 2, 3)] + [partner, (d ^ 2, z), (d ^ 4, z), (d ^ 6, z)]
    barrier = pltpu.get_barrier_semaphore()
    for peer in peers:
        pl.semaphore_signal(barrier, inc=1, device_id=peer, device_id_type=MESH)
    pl.semaphore_wait(barrier, len(peers))
    clock = Clock(47e3)
    tail = []

    wide = 2 * rows
    wd = arena.at[pl.ds(0, D), :]
    wu = arena.at[pl.ds(D, D), :]

    def fetch(index, source, target):
        copy = pltpu.make_async_copy(source, target, local.at[index])
        copy.start()
        return copy

    chunk = lambda k: z ^ k
    hidden = lambda k: pl.ds(pl.multiple_of(chunk(k) * D, D), D)
    load_wd = lambda i: fetch(0, f_down.at[chunk(RING[i])], wd)
    load_wu = lambda i: fetch(1, f_up.at[chunk(RING[i])], wu)
    load_act = lambda i: fetch(2, act2.at[:, hidden(RING[i])], act)
    load_slope = lambda i: fetch(3, dgelu.at[:, hidden(RING[i])], slope)
    at_act, at_wd, at_slope, at_wu = load_act(0), load_wd(0), load_slope(0), load_wu(0)
    at_acc = fetch(4, second_grads, acc)
    at_normed = fetch(5, normed_one, normed)
    at_turned = fetch(6, first_t, turned)

    zero = jnp.zeros((16, D), low)
    for j in range(parts):
        spans = []
        if j == 0:
            spans.append((0, offsets[0]))
        begin = ends[j] if j < parts - 1 else offsets[j] + rows
        if begin < window:
            spans.append((begin, window))
        if spans:
            @pl.when(z == j)
            def _(spans=spans):
                for begin, end in spans:
                    def clear(i, c):
                        mixed_win[pl.ds(pl.multiple_of(begin + i * 16, 16), 16), :] = zero
                        return c
                    lax.fori_loop(0, (end - begin) // 16, clear, 0)

    groups = {
        "down": (s_down, k_down, r_down, t_down, z_down, g_down, 0),
        "up": (s_up, k_up, r_up, t_up, z_up, g_up, 1),
        "out": (s_out, k_out, r_out, t_out, z_out, g_out, 2),
        "qkv": (s_qkv, k_qkv, r_qkv, t_qkv, z_qkv, g_qkv, 3),
    }
    hops, finished = {}, {}

    def x_ahead(g, i):
        return (i + groups[g][6]) % 2 == 0

    def put(g, i, j, at, value):
        if not x_ahead(g, i):
            j = (0, 2, 1, 3)[j]
        if j < 2:
            groups[g][0][(i % 2, j) + at] = value
        else:
            groups[g][1][(i, j - 2) + at] = value

    def hop(g, i, kind, source, target, device):
        index = groups[g][6]
        copy = pltpu.make_async_remote_copy(
            source, target, hop_send.at[index, i, kind], hop_recv.at[index, i, kind],
            device_id=device, device_id_type=MESH,
        )
        copy.start()
        hops[g, i, kind] = copy

    def add_into(ref, other):
        count = ref.shape[0]
        step = min(count, 64)

        def body(j, c):
            at = pl.ds(pl.multiple_of(j * step, step), step)
            ref[at, :] = (ref[at, :].astype(f32) + other[at, :].astype(f32)).astype(low)
            return c

        lax.fori_loop(0, count // step, body, 0)

    def launch(g, i):
        s, kept, r, t, zb, out, index = groups[g]
        x_first = x_ahead(g, i)
        n1, n2 = ((d ^ 2, z), (d ^ 4, z)) if x_first else ((d ^ 4, z), (d ^ 2, z))
        l1, l2 = ("x", "y") if x_first else ("y", "x")
        block = s.shape[2] * s.shape[3] * 2
        k = RING[i]
        hop(g, i, 0, s.at[i % 2], r.at[i], n1)

        def second():
            hops[g, i, 0].wait_recv()
            add_into(kept.at[i, 0], r.at[i, 0])
            hop(g, i, 1, kept.at[i, 0], t.at[i], n2)
            clock.send(l2, block, third)
            add_into(kept.at[i, 1], r.at[i, 1])

        def third():
            hops[g, i, 1].wait_recv()
            add_into(kept.at[i, 1], t.at[i])
            if k:
                hop(g, i, 2, kept.at[i, 1], zb.at[k - 1], (d, z ^ k))
                clock.send("z", block, fourth, 1.0 if k == 1 else 2.0)
            else:
                ended()

        def fourth():
            hops[g, i, 2].wait_recv()
            ended()

        def ended():
            finished[g] = finished.get(g, 0) + 1
            if finished[g] == parts:
                finish(g)

        clock.send(l1, 2 * block, second)

    def free_slot(g, i):
        if i >= 2:
            hops[g, i - 2, 0].wait_send()

    def finish(g):
        s, kept, r, t, zb, out, index = groups[g]
        own = RING.index(0)
        count = s.shape[2]
        step = min(count, 64)
        pieces = kept.at[own, 1]

        def body(j, c):
            at = pl.ds(pl.multiple_of(j * step, step), step)
            total = pieces[at, :].astype(f32)
            for k in range(parts - 1):
                total = total + zb[k, at, :].astype(f32)
            out[at, :] = total
            return c

        lax.fori_loop(0, count // step, body, 0)

    def exchange(index, source, target):
        copy = pltpu.make_async_remote_copy(
            source, target, pair_send.at[index], pair_recv.at[index], device_id=partner, device_id_type=MESH
        )
        copy.start()
        return copy

    small[...] = small_in[...]

    pending = {}

    def grad_up_chunk(i):
        pending.pop(i).wait_recv()
        if i == 0:
            at_turned.wait()
        free_slot("up", i)

        def body(n, c):
            at = pl.ds(pl.multiple_of(n * 256, 256), 256)
            tile = jnp.dot(turned[...], up2[i, :, at], preferred_element_type=f32).astype(low)
            for j in range(4):
                put("up", i, j, (slice(None), at), tile[j * 128 : (j + 1) * 128])
            return c

        lax.fori_loop(0, 4, body, 0)
        launch("up", i)
        clock.work(2.0)

    exchanges = []
    loads = {"wd": at_wd, "wu": at_wu, "slope": at_slope, "act": at_act}

    def upper_chunk(i):
        loads["wd"].wait()
        loads["slope"].wait()
        bias_row = chunk(RING[i])

        def body(n, c):
            at = pl.ds(pl.multiple_of(n * 256, 256), 256)
            grads = lax.dot_general(sec_low[...], wd[at, :], NT, preferred_element_type=f32)
            value = (grads * slope[:, at].astype(f32)).astype(low)
            up2[i, pl.ds(0, rows), at] = value
            small[pl.ds(10 + bias_row, 1), at] = jnp.sum(value.astype(f32), axis=0, keepdims=True)
            return c

        lax.fori_loop(0, 4, body, 0)
        pending[i] = exchange(i, up2.at[i, pl.ds(0, rows), :], up2.at[i, pl.ds(rows, rows), :])
        exchanges.append(pending[i])
        clock.work(2.5)
        if i + 1 < parts:
            loads["wd"], loads["slope"] = load_wd(i + 1), load_slope(i + 1)

    def grad_down_chunk(i):
        loads["act"].wait()
        free_slot("down", i)

        def body(n, c):
            at = pl.ds(pl.multiple_of(n * 256, 256), 256)
            tile = lax.dot_general(act[:, at], sec2[...], TN, preferred_element_type=f32).astype(low)
            for j in range(4):
                put("down", i, j, (at, slice(None)), tile[:, j * 128 : (j + 1) * 128])
            return c

        lax.fori_loop(0, 4, body, 0)
        launch("down", i)
        clock.work(2.0)
        if i + 1 < parts:
            loads["act"] = load_act(i + 1)

    def first_chunk(i):
        loads["wu"].wait()
        if i == 0:
            at_acc.wait()

        def body(n, c):
            at = pl.ds(pl.multiple_of(n * 256, 256), 256)
            acc[:, at] += lax.dot_general(
                up2[i, pl.ds(0, rows), :], wu[at, :], NT, preferred_element_type=f32
            )
            return c

        lax.fori_loop(0, 4, body, 0)
        clock.work(2.0)
        if i + 1 < parts:
            loads["wu"] = load_wu(i + 1)

    grad_down_chunk(0)
    for i in range(parts):
        upper_chunk(i)
        first_chunk(i)
        if i == 1:
            grad_down_chunk(1)

    at_normed.wait()
    zero_row = jnp.zeros((16, D), f32)

    def norm_body(begin, count, sums):
        at = pl.ds(begin, count)
        grads, unit = acc[at, :], normed[at, :]
        scaled = grads * gain[4:5, :]
        result = inverse[at, :] * (
            scaled
            - jnp.mean(scaled, axis=-1, keepdims=True)
            - unit * jnp.mean(scaled * unit, axis=-1, keepdims=True)
        )
        acc[at, :] = result
        mixed_win[pl.ds(pl.multiple_of(offset + begin, 16), count), :] = result.astype(low)
        return (sums[0] + fold(grads * unit), sums[1] + fold(grads), sums[2] + fold(result))

    sums = by_rows(rows, norm_body, (zero_row, zero_row, zero_row))
    small[4:5, :] = jnp.sum(sums[0], axis=0, keepdims=True)
    small[5:6, :] = jnp.sum(sums[1], axis=0, keepdims=True)
    small[2:3, :] = jnp.sum(sums[2], axis=0, keepdims=True)
    halos = []
    for j in range(parts - 1):
        count = ends[j] - offsets[j] - rows
        halos.append((j + 1, j, pltpu.make_async_remote_copy(
            mixed_win.at[pl.ds(offsets[j + 1], count), :],
            mixed_win.at[pl.ds(offsets[j] + rows, count), :],
            halo_send.at[0], halo_recv.at[0], device_id=(d, j), device_id_type=MESH,
        )))
    for j in range(1, parts):
        halos.append((j - 1, j, pltpu.make_async_remote_copy(
            mixed_win.at[pl.ds(offsets[j - 1] + rows - offsets[j], offsets[j]), :],
            mixed_win.at[pl.ds(0, offsets[j]), :],
            halo_send.at[1], halo_recv.at[1], device_id=(d, j), device_id_type=MESH,
        )))
    for sender, receiver, copy in halos:
        @pl.when(z == sender)
        def _(copy=copy):
            copy.start()
    clock.work(4.0)
    for i in range(parts):
        grad_up_chunk(i)
        if i + 2 < parts:
            grad_down_chunk(i + 2)
    own_at = pl.ds(offset, rows)
    for j, owner in enumerate(block_owners(d, 1 - core, True)):
        y[0:rows, j * 128 : (j + 1) * 128] = mixed_win[own_at, pl.ds(pl.multiple_of(owner * 128, 128), 128)]
    exchanges.append(exchange(parts, y.at[pl.ds(0, rows), pl.ds(0, 512)], mixed2.at[pl.ds(rows, rows), :]))
    for j, owner in enumerate(block_owners(d, core, True)):
        mixed2[pl.ds(0, rows), j * 128 : (j + 1) * 128] = mixed_win[
            own_at, pl.ds(pl.multiple_of(owner * 128, 128), 128)
        ]
    clock.work(4.0)

    cut = D // parts
    three = 3 * cut
    pairs = cut // (2 * HD)
    x = arena
    wo = slope.at[pl.ds(0, cut), :]
    load_x = lambda i: fetch(0, qkv.at[chunk(RING[i])], arena.at[pl.ds(0, window), pl.ds(0, three)])
    load_wo = lambda i: fetch(1, f_out.at[chunk(RING[i])], wo)
    load_att = lambda i: fetch(
        2, att2.at[:, pl.ds(pl.multiple_of(chunk(RING[i]) * cut, cut), cut)], act.at[:, pl.ds(0, cut)]
    )
    load_wi = lambda i: fetch(3, f_qkv.at[chunk(RING[i])], w_in)
    at_turned = fetch(6, lift_t, turned)
    at_x, at_wo, at_att, at_wi = load_x(0), load_wo(0), load_att(0), load_wi(0)
    exchanges[-1].wait_recv()
    scale = HD ** (-0.5)

    def take_halo():
        for sender, receiver, copy in halos:
            @pl.when(z == receiver)
            def _(copy=copy):
                copy.wait_recv()

    def grad_qkv_chunk(i):
        pending.pop(i).wait_recv()
        if i == 0:
            at_turned.wait()
        free_slot("qkv", i)

        def body(n, c):
            at = pl.ds(pl.multiple_of(n * 256, 256), 256)
            tile = jnp.dot(turned[...], up2[i, :, at], preferred_element_type=f32).astype(low)
            for j in range(4):
                put("qkv", i, j, (slice(None), at), tile[j * 128 : (j + 1) * 128])
            return c

        lax.fori_loop(0, three // 256, body, 0)
        launch("qkv", i)
        clock.work(1.8)

    for i in range(parts):
        at_att.wait()
        free_slot("out", i)
        tile = lax.dot_general(act[:, 0:cut], mixed2[...], TN, preferred_element_type=f32).astype(low)
        for j in range(4):
            put("out", i, j, (slice(None), slice(None)), tile[:, j * 128 : (j + 1) * 128])
        launch("out", i)
        clock.work(0.8)
        if i == 0:
            take_halo()
        at_wo.wait()

        def flow_body(n, c):
            at = pl.ds(pl.multiple_of(n * 512, 512), 512)
            x[at, three : three + cut] = lax.dot_general(
                mixed_win[at, :], wo[...], NT, preferred_element_type=f32
            ).astype(low)
            return c

        lax.fori_loop(0, window // 512, flow_body, 0)
        clock.work(1.5)
        if i:
            grad_qkv_chunk(i - 1)
        at_x.wait()
        if i == 0:
            exchanges[parts].wait_send()
        if i + 1 < parts:
            at_wo, at_att = load_wo(i + 1), load_att(i + 1)

        def attend_body(step, c):
            p, slot = step // 3, lax.rem(step, 3)
            lanes = lambda base: pl.ds(pl.multiple_of(base + p * 2 * HD, 2 * HD), 2 * HD)
            unit_at = [
                pl.ds(perm[slot * LONG + m] * UNIT, UNIT) for m in range(LONG)
            ]
            keys = jnp.concatenate([x[at, lanes(cut)] for at in unit_at], axis=0)
            values = jnp.concatenate([x[at, lanes(2 * cut)] for at in unit_at], axis=0)
            marks = jnp.concatenate([kf[at, :] for at in unit_at], axis=0)
            wide_keys = jnp.concatenate([keys, marks], axis=1)
            pair = jnp.concatenate([two_heads(x[at, lanes(0)]) for at in unit_at], axis=0)
            grads = jnp.concatenate([two_heads(x[at, lanes(three)]) for at in unit_at], axis=0)
            mark = jnp.concatenate([qf[at, :] for at in unit_at for _ in range(2)], axis=0)
            wide_pair = jnp.concatenate([pair, mark], axis=1)
            logsum = jnp.concatenate(
                [lse[chunk(RING[i]), pl.ds(step * LONG + m, 1), :] for m in range(LONG)], axis=1
            )
            scores = lax.dot_general(wide_keys, wide_pair, NT, preferred_element_type=f32)
            chances = jnp.exp(scores - logsum)
            flow = lax.dot_general(values, grads, NT, preferred_element_type=f32)
            terms = chances * flow
            slopes = (chances * (flow - jnp.sum(terms, axis=0, keepdims=True))).astype(low)
            v_sum = jnp.dot(chances.astype(low), grads, preferred_element_type=f32)
            k_sum = jnp.dot(slopes, pair, preferred_element_type=f32)
            flipped = lax.dot_general(keys, slopes, TN, preferred_element_type=f32)
            for m in range(LONG):
                two = slice(m * 2 * UNIT, (m + 1) * 2 * UNIT)
                at = pl.ds(pl.multiple_of(slot * LONG * UNIT + m * UNIT, UNIT), UNIT)
                y[at, lanes(0)] = (from_two(flipped[:, two]) * scale).astype(low)
            at = pl.ds(pl.multiple_of(slot * LONG * UNIT, UNIT), LONG * UNIT)
            y[at, lanes(cut)] = k_sum.astype(low)
            y[at, lanes(2 * cut)] = v_sum.astype(low)
            return c

        lax.fori_loop(0, pairs * 3, attend_body, 0, unroll=2)
        clock.work(10.5)
        if i + 1 < parts:
            at_x = load_x(i + 1)
        for u in range(FIRST_OWN, LAST_OWN + 1):
            at = pl.ds(back[u] * UNIT, UNIT)
            act[pl.ds((u - FIRST_OWN) * UNIT, UNIT), cut:] = y[at, :]
        exchanges[i].wait_send()
        inner_at = pl.ds(pl.multiple_of(offset - FIRST_OWN * UNIT, 16), rows)
        up2[i, pl.ds(0, rows), 0:three] = act[inner_at, cut:]
        pending[i] = exchange(
            parts + 1 + i, up2.at[i, pl.ds(0, rows), pl.ds(0, three)], up2.at[i, pl.ds(rows, rows), pl.ds(0, three)]
        )
        exchanges.append(pending[i])
        place = pl.multiple_of(chunk(RING[i]) * cut, cut)
        small[8:9, pl.ds(place, cut)] = jnp.sum(up2[i, pl.ds(0, rows), 0:cut].astype(f32), axis=0, keepdims=True)
        small[9:10, pl.ds(place, cut)] = jnp.sum(
            up2[i, pl.ds(0, rows), 2 * cut : three].astype(f32), axis=0, keepdims=True
        )
        at_wi.wait()

        def input_body(n, c, i=i):
            at = pl.ds(pl.multiple_of(n * 256, 256), 256)
            acc[:, at] += lax.dot_general(
                up2[i, pl.ds(0, rows), 0:three], w_in[at, :], NT, preferred_element_type=f32
            )
            return c

        lax.fori_loop(0, 4, input_body, 0)
        clock.work(2.0)
        if i + 1 < parts:
            at_wi = load_wi(i + 1)

    def last_body(begin, count, total):
        at = pl.ds(begin, count)
        value = acc[at, :]
        arena[at, :] = value.astype(low)
        return total + fold(value)

    total = jnp.sum(by_rows(rows, last_body, zero_row), axis=0, keepdims=True)
    store = fetch(4, arena.at[pl.ds(0, rows), :], input_grad)
    small[0:1, :] = total * small_in[15:16, :]
    small[1:2, :] = total
    clock.work(2.0)
    stages = [[partner], [(d ^ 2, z), (d ^ 4, z), (d ^ 6, z)], [(d, z ^ k) for k in (1, 2, 3)]]

    def small_stage(n, first_slot):
        sent = []
        for slot, device in enumerate(stages[n], first_slot):
            copy = pltpu.make_async_remote_copy(
                small, small_in_far.at[slot], small_send.at[slot], small_recv.at[slot],
                device_id=device, device_id_type=MESH,
            )
            copy.start()
            sent.append(copy)

        def take():
            for copy in sent:
                copy.wait()
            for slot in range(first_slot, first_slot + len(sent)):
                small[...] += small_in_far[slot]
            if n + 1 < len(stages):
                small_stage(n + 1, first_slot + len(sent))

        clock.send("c", 0.6e6, take)

    small_stage(0, 0)
    grad_qkv_chunk(parts - 1)
    clock.drain()
    assert sum(finished.values()) == 4 * parts
    small_out[...] = small[...]
    store.wait()
    for (g, i, kind), copy in hops.items():
        if kind or i >= 2:
            copy.wait_send()
    for copy in exchanges[parts + 1 :]:
        copy.wait_send()
    for sender, receiver, copy in halos:
        @pl.when(z == sender)
        def _(copy=copy):
            copy.wait_send()


def back_call(rows, window, parts, perm, back, vmem_in, hbm_in):
    f32, low = jnp.float32, jnp.bfloat16
    any_ = pl.BlockSpec(memory_space=pl.ANY)
    vmem = pl.BlockSpec(memory_space=pltpu.VMEM)
    smem = pl.BlockSpec(memory_space=pltpu.SMEM)
    cut = D // parts
    shapes = {"down": (D, 128), "up": (128, D), "out": (cut, 128), "qkv": (128, 3 * cut)}
    outs = [jax.ShapeDtypeStruct((rows, D), low)]
    outs += [jax.ShapeDtypeStruct(shape, f32) for shape in (shapes["qkv"], shapes["out"], shapes["up"], shapes["down"])]
    outs += [jax.ShapeDtypeStruct((16, D), f32)]
    order = ("down", "up", "out", "qkv")
    buffers = [pltpu.VMEM((2, 2) + shapes[g], low) for g in order]
    buffers += [pltpu.VMEM((parts, 2) + shapes[g], low) for g in order]
    buffers += [pltpu.VMEM((parts, 2) + shapes[g], low) for g in order]
    buffers += [pltpu.VMEM((parts,) + shapes[g], low) for g in order]
    buffers += [pltpu.VMEM((parts - 1,) + shapes[g], low) for g in order]
    dma = pltpu.SemaphoreType.DMA
    return pl.pallas_call(
        functools.partial(back_kernel, rows, window, parts),
        out_shape=outs,
        in_specs=[smem, smem] + [vmem] * len(vmem_in) + [any_] * len(hbm_in),
        out_specs=[any_] + [vmem] * 5,
        scratch_shapes=[
            pltpu.VMEM((rows, D), f32),
            pltpu.VMEM((rows, D), f32),
            pltpu.VMEM((512, 2 * rows), low),
            pltpu.VMEM((2 * D, D), low),
            pltpu.VMEM((2 * rows, D), low),
            pltpu.VMEM((rows, D), low),
            pltpu.VMEM((window, 3 * cut), low),
            pltpu.VMEM((parts, 2 * rows, D), low),
            pltpu.VMEM((D, 3 * cut), low),
            pltpu.VMEM((2 * rows, 512), low),
            pltpu.VMEM((window, D), low),
            pltpu.VMEM((16, D), f32),
            pltpu.VMEM((7, 16, D), f32),
        ]
        + buffers
        + [
            dma((7,)),
            dma((4, parts, 3)),
            dma((4, parts, 3)),
            dma((2 * parts + 1,)),
            dma((2 * parts + 1,)),
            dma((2,)),
            dma((2,)),
            dma((7,)),
            dma((7,)),
        ],
        compiler_params=pltpu.CompilerParams(
            collective_id=1, has_side_effects=True, vmem_limit_bytes=60 * 2**20 + 2**19
        ),
    )(perm, back, *vmem_in, *hbm_in)


def unit_order(segs, window):
    units = window // UNIT
    unit_seg = segs[::UNIT]
    index = lax.iota(jnp.int32, units)
    counts = jnp.sum((unit_seg[:, None] == unit_seg[None, :]).astype(jnp.int32), axis=1)
    short = jnp.where((counts == LONG) & (unit_seg >= 0) & (unit_seg < 1000), 0, 1) * units + index
    back = jnp.sum((short[None, :] < short[:, None]).astype(jnp.int32), axis=1)
    perm = jnp.sum(jnp.where(back[None, :] == index[:, None], index[None, :], 0), axis=1)
    return perm.astype(jnp.int32), back.astype(jnp.int32)


def marks_of(segs):
    lane = lax.iota(jnp.int32, 2 * HD)
    seg = jnp.where(segs < 0, 2 * HD - 1, jnp.where(segs >= 1000, 2 * HD - 2, segs))
    same = seg[:, None] == lane[None, :]
    keys = jnp.where(same, 1.0, 0.0).astype(jnp.bfloat16)
    queries = jnp.where(same, 0.0, -1e30).astype(jnp.bfloat16)
    return keys, queries


def local_body(
    tokens,
    cotangent,
    timesteps,
    item_lengths,
    w_qkv,
    bias_qv,
    w_out,
    w_up,
    bias_up,
    w_down,
    vectors,
):
    rows = tokens.shape[0]
    parts = lax.axis_size("mp")
    z = lax.axis_index("mp")
    low = jnp.bfloat16
    f32 = jnp.float32
    cut = D // parts
    firsts, offsets, ends = window_plan(rows, parts)
    window = -(-max(ends) // UNIT) * UNIT
    first_token = UNIT * pick(firsts, z)
    positions = first_token + lax.iota(jnp.int32, window)
    lengths_end = jnp.cumsum(item_lengths[0])
    segs = jnp.sum((positions[:, None] >= lengths_end[None, :]).astype(jnp.int32), axis=1)
    segs = jnp.where(positions < 0, -1, jnp.where(positions >= LEN, 1000, segs))
    perm, back = unit_order(segs, window)
    kf, qf = marks_of(segs)
    (
        f_qkv, f_out, f_up, f_down, qkv, lse, att2, act2, slope, first_t, lift_t, sec2, normed_one,
        second_low, second_grads, output, inverse_one, small_in,
    ) = fore_call(
        rows, window, parts, perm, back, timesteps, tokens, cotangent,
        w_qkv.reshape(D, 3 * cut), w_out, w_up, w_down, bias_up[None], bias_qv, vectors, kf, qf,
    )
    input_grad, grad_qkv, grad_out, grad_up, grad_down, small = back_call(
        rows, window, parts, perm, back,
        (second_low, sec2, inverse_one, vectors, small_in, kf, qf, lse),
        (first_t, lift_t, second_grads, normed_one, act2, slope, att2, qkv, f_qkv, f_out, f_up, f_down),
    )
    grad_bias_qv = lax.dynamic_slice_in_dim(small[8:10], z * cut, cut, 1)
    grad_bias_up = lax.dynamic_slice_in_dim(small[10:14].reshape(FF), z * (FF // parts), FF // parts, 0)
    return (
        output,
        input_grad,
        grad_qkv.reshape(-1, 3, cut),
        grad_bias_qv,
        grad_out,
        grad_up,
        grad_bias_up,
        grad_down,
        small[:8],
    )


def solution(mesh):
    in_specs = (
        P(("dp", "mp"), None),
        P(("dp", "mp"), None),
        P("dp"),
        P("dp", None),
        P(None, None, "mp"),
        P(None, "mp"),
        P("mp", None),
        P(None, "mp"),
        P("mp"),
        P("mp", None),
        P(),
    )
    out_specs = (
        P(("dp", "mp"), None),
        P(("dp", "mp"), None),
        P("dp", None, "mp"),
        P(None, "mp"),
        P("mp", "dp"),
        P("dp", "mp"),
        P("mp"),
        P("mp", "dp"),
        P(),
    )
    chosen = local_body if fits_local(mesh) else body
    return jax.shard_map(chosen, mesh=mesh, in_specs=in_specs, out_specs=out_specs, check_vma=False)
```
